32 devices in a mesh: wide: 8 (over z, y), narrow: 4 (over x, core).
Axes of the slice: x: 2, y: 2, z: 4, core: 2. Of those that a mesh axis runs over, the one named last changes fastest.
Arguments:
- tokens: bfloat16 [32768, 767], P(('wide', 'narrow')), may hold values from -6 to 6
- lengths: int32 [32, 3], P(('wide', 'narrow')), may hold values from 1 to 768, 960 in all within a row
- gain_one: bfloat16 [768], P(('wide', 'narrow')), may hold values from 0.5 to 1.5
- w_qkv: bfloat16 [768, 2304], P(('wide', 'narrow')), may hold values from -0.21875 to 0.21875
- w_out: bfloat16 [768, 768], P(('wide', 'narrow')), may hold values from -0.875 to 0.875
- gain_two: bfloat16 [768], P(('wide', 'narrow')), may hold values from 0.5 to 1.5
- w_up: bfloat16 [768, 3072], P(('wide', 'narrow')), may hold values from -0.21875 to 0.21875
- b_up: bfloat16 [3072], P(('wide', 'narrow')), may hold values from -3 to 3
- w_down: bfloat16 [3072, 768], P(('wide', 'narrow')), may hold values from -0.15625 to 0.15625
- cotangent: bfloat16 [32768, 767], P(('wide', 'narrow')), may hold values from -6 to 6
Outputs:
- out: bfloat16 [32768, 767], P(('wide', 'narrow'))
- d_tokens: bfloat16 [32768, 767], P(('wide', 'narrow'))
- d_gain_one: float32 [768], P(('wide', 'narrow'))
- d_w_qkv: float32 [768, 2304], P(('wide', 'narrow'))
- d_w_out: float32 [768, 768], P(('wide', 'narrow'))
- d_gain_two: float32 [768], P(('wide', 'narrow'))
- d_w_up: float32 [768, 3072], P(('wide', 'narrow'))
- d_b_up: float32 [3072], P(('wide', 'narrow'))
- d_w_down: float32 [3072, 768], P(('wide', 'narrow'))
The draws below stay inside these ranges and needn't reach their ends.
Inputs may be any that keep to these rules, and one draw needn't show every extreme that they name: In each device's row the 3 lengths sum to 960 and the largest is exactly 768; the last 64 slots of each device are padding.
All inputs are finite; a program needn't handle non-finite values.
Results may differ from the reference program's by a relative error of at most 0.012.
Values may be sent and summed in bfloat16 or wider, within the bound.
No kernel may reach another device: no remote copies, remote signals or barrier semaphores. Data moves between devices by JAX's collectives and lax.ppermute only.
A program may use at most 192 MiB of HBM per device.

```python
import math
import jax
import jax.numpy as jnp
import numpy as np
from jax import lax

D = 768
DC = 767
HEADS = 12
HEAD_DIM = 64
FF = 3072
TOK_DEV = 1024
DOCS = 3
LIVE = 960
MOST = 768
TOKENS = 32768
DEVICES = 32


def block_scale(rng, extent, shards, low, top_value):
    gain = 1.0
    for position, blocks in shards:
        steps = jax.random.uniform(jax.random.fold_in(jax.random.fold_in(rng, 6), position), (blocks,), jnp.float32, low / len(shards), top_value / len(shards))
        gain = gain * jnp.repeat(jnp.exp(steps), extent[position] // blocks).reshape((-1,) + (1,) * (len(extent) - 1 - position))
    return gain


def split_up(number_of, total, most, lean):
    loads = [(1 << 20) // math.isqrt(grade ** lean) + 1 for grade in range(2, number_of + 1)]
    surplus, given = total - most - (number_of - 1), [1] * (number_of - 1)
    while surplus > 0:
        movable = [i for i in range(number_of - 1) if given[i] < most]
        whole, budget = sum([loads[i] for i in movable]), surplus
        for i in movable:
            more = min(most - given[i], max(1, budget * loads[i] // whole), surplus)
            given[i] = given[i] + more
            surplus = surplus - more
    return np.array([most] + given)


def ragged(key, amount, total, most, lean):
    if amount == 2:
        one = jax.random.randint(key, (), max(1, total - most), min(most, total - 1) + 1)
        return jnp.stack([one, total - one])
    sizes = jnp.asarray(split_up(amount, total, most, lean), jnp.int32)
    pairs = (amount - 1) // 2
    donor, sink = sizes[1:1 + 2 * pairs:2], sizes[2:2 + 2 * pairs:2]
    room = jnp.minimum(donor - 1, most - sink)
    moved = jax.random.randint(jax.random.fold_in(key, 1), (pairs,), 0, 1 << 20) % (room + 1)
    sizes = sizes.at[1:1 + 2 * pairs:2].set(donor - moved).at[2:2 + 2 * pairs:2].set(sink + moved)
    return sizes[jax.random.permutation(jax.random.fold_in(key, 2), amount)]


def normal_values(own_key, shape, spread, reach, shards=(), held_as=jnp.bfloat16):
    drawn = jax.random.normal(own_key, shape, jnp.float32) * spread
    if len(shards) > 0:
        drawn = block_scale(own_key, shape, shards, -0.22, 0.18) * drawn
    return jnp.clip(drawn, min=-reach, max=reach).astype(held_as)


def setup_inputs(seed: int = 0) -> dict:
    key_list = jax.random.split(jax.random.key(seed), 11)
    tokens = normal_values(key_list[0], (TOKENS, DC), 1.0, 6.0, ((0, 32),))
    lengths = jax.vmap(lambda own: ragged(own, DOCS, LIVE, MOST, 2))(jax.random.split(key_list[1], DEVICES)).reshape((DEVICES, DOCS)).astype(jnp.int32)
    gain_one = jnp.clip(1.0 + 0.1 * jax.random.normal(key_list[2], (D,), jnp.float32), 0.5, 1.5).astype(jnp.bfloat16)
    w_qkv = normal_values(key_list[3], (D, 3 * D), D ** -0.5, 0.21875, ((0, 32),))
    w_out = normal_values(key_list[4], (D, D), (D // 16) ** -0.5, 0.875, ((0, 32),))
    gain_two = jnp.clip(1.0 + 0.1 * jax.random.normal(key_list[5], (D,), jnp.float32), 0.5, 1.5).astype(jnp.bfloat16)
    w_up = normal_values(key_list[6], (D, FF), D ** -0.5, 0.21875, ((0, 32),))
    b_up = normal_values(key_list[7], (FF,), 0.5, 3.0, ((0, 32),))
    w_down = normal_values(key_list[8], (FF, D), (FF // 2) ** -0.5, 0.15625, ((0, 32),))
    cotangent = normal_values(key_list[9], (TOKENS, DC), 1.0, 6.0, ((0, 32),))
    return {"tokens": tokens, "lengths": lengths, "gain_one": gain_one, "w_qkv": w_qkv, "w_out": w_out, "gain_two": gain_two, "w_up": w_up, "b_up": b_up, "w_down": w_down, "cotangent": cotangent}


epsilon = 1e-05
highest = lax.Precision.HIGHEST

@jax.custom_vjp
def low(v):
    return lax.optimization_barrier(v.astype(jnp.bfloat16)).astype(jnp.float32)

@jax.custom_vjp
def low_back(v):
    return v

def low_keep(v):
    return (low(v), None)

def low_pass(kept, grad):
    return (grad,)

def back_keep(v):
    return (v, None)

def back_low(kept, grad):
    return (low(grad),)
low.defvjp(low_keep, low_pass)
low_back.defvjp(back_keep, back_low)

def compressed_norm(row_data, gain_vec):
    row_sum = lax.optimization_barrier(jnp.sum(row_data, axis=1, keepdims=True))
    square_sum = lax.optimization_barrier(jnp.sum(row_data * row_data, axis=1, keepdims=True))
    inverse = lax.rsqrt((square_sum + row_sum * row_sum) / gain_vec.shape[0] + epsilon)
    expanded = jnp.concatenate([row_data, -row_sum], axis=1)
    return expanded * inverse * gain_vec

def compress(branch):
    centred = branch - lax.optimization_barrier(jnp.mean(branch, axis=1, keepdims=True))
    return centred[:, :-1]

def attend_block(pieces):
    qkv_rows, segments = pieces
    heads_view = qkv_rows.reshape(TOK_DEV, 3, HEADS, HEAD_DIM)
    queries = heads_view[:, 0]
    keys_in = heads_view[:, 1]
    values = heads_view[:, 2]
    scores = jnp.einsum('qhd,khd->hqk', queries, keys_in, precision=highest) * HEAD_DIM ** (-0.5)
    scores = low_back(scores)
    places = jnp.arange(TOK_DEV, dtype=jnp.int32)
    allowed = (segments[:, None] == segments[None, :]) & (places[None, :] <= places[:, None])
    weights = low(jax.nn.softmax(jnp.where(allowed[None], scores, -1e+30), axis=-1))
    mixed = jnp.einsum('hqk,khd->qhd', weights, values, precision=highest)
    return mixed.reshape(TOK_DEV, D)

def reference(tokens, lengths, gain_one, w_qkv, w_out, gain_two, w_up, b_up, w_down, cotangent):
    places = jnp.arange(TOK_DEV, dtype=jnp.int32)
    bounds = jnp.cumsum(lengths, axis=1).astype(jnp.int32)
    segments = lax.optimization_barrier(jnp.sum((places[None, :, None] >= bounds[:, None, :]).astype(jnp.int32), axis=2))

    def forward(residual, norm_one, qkv_weight, out_weight, norm_two, up_weight, up_bias, down_weight):
        normed = low(compressed_norm(residual, norm_one))
        qkv = low_back(low(jnp.dot(normed, qkv_weight, precision=highest)))
        blocks = qkv.reshape(DEVICES, TOK_DEV, 3 * D)
        attended = lax.map(jax.checkpoint(attend_block), (blocks, segments)).reshape(DEVICES * TOK_DEV, D)
        attended = low_back(low(attended))
        mixed = low_back(jnp.dot(attended, out_weight, precision=highest))
        middle = residual + compress(mixed)
        second = low(compressed_norm(middle, norm_two))
        hidden = low_back(jnp.dot(second, up_weight, precision=highest) + up_bias)
        active = low(jax.nn.gelu(hidden, approximate=True))
        branch = low_back(jnp.dot(active, down_weight, precision=highest))
        return middle + compress(branch)
    inputs = [operand.astype(jnp.float32) for operand in (tokens, gain_one, w_qkv, w_out, gain_two, w_up, b_up, w_down)]
    result, pullback = jax.vjp(forward, *inputs)
    gradients = pullback(cotangent.astype(jnp.float32))
    return (result.astype(jnp.bfloat16), gradients[0].astype(jnp.bfloat16), gradients[1], gradients[2], gradients[3], gradients[4], gradients[5], gradients[6], gradients[7])
```

```python
import functools

import jax
import jax.numpy as jnp
from jax import lax
from jax.experimental import pallas as pl
from jax.experimental.pallas import tpu as pltpu
from jax.sharding import PartitionSpec as P

AXES = ("wide", "narrow")
EPSILON = 1e-05
BF = jnp.bfloat16
F32 = jnp.float32
WIDTH = 768
HIDDEN = 3072
ROWS = 1024
TILE = 256
BIG = 768
PAIRS = 6
HEAD = 64
PROB_COLS = 1792
CHIPS = 16
BLOCK = 48
LIMIT = 56 * 1024 * 1024


def mm(left, right):
    return lax.dot_general(left, right, (((1,), (0,)), ((), ())), preferred_element_type=F32)


def mm_nt(left, right):
    return lax.dot_general(left, right, (((1,), (1,)), ((), ())), preferred_element_type=F32)


def mm_tn(left, right):
    return lax.dot_general(left, right, (((0,), (0,)), ((), ())), preferred_element_type=F32)


def lanes(width=WIDTH):
    return lax.broadcasted_iota(jnp.int32, (1, width), 1)


def norm_parts(rows):
    total = jnp.sum(rows, axis=1, keepdims=True)
    squares = jnp.sum(rows * rows, axis=1, keepdims=True)
    inverse = lax.rsqrt((squares + total * total) * (1.0 / WIDTH) + EPSILON)
    expanded = jnp.where(lanes() == WIDTH - 1, -total, rows)
    return inverse, expanded


def norm_back(weighted, inverse, expanded):
    inner = jnp.sum(weighted * expanded, axis=1, keepdims=True) * (1.0 / WIDTH)
    full = inverse * (weighted - (inverse * inverse * inner) * expanded)
    last = full[:, WIDTH - 1 :]
    return jnp.where(lanes() == WIDTH - 1, 0.0, full - last)


def turn(start, first_row, count, forward):
    rows = lax.broadcasted_iota(jnp.int32, (count, ROWS), 0) + first_row
    cols = lax.broadcasted_iota(jnp.int32, (count, ROWS), 1)
    if forward:
        source = rows + start
        source = jnp.where(source >= ROWS, source - ROWS, source)
    else:
        source = rows - start
        source = jnp.where(source < 0, source + ROWS, source)
    return jnp.where(cols == source, 1.0, 0.0).astype(BF)


def params(**more):
    return pltpu.CompilerParams(vmem_limit_bytes=LIMIT, **more)


def cost(flops, nbytes, transcendentals=0):
    return pl.CostEstimate(flops=flops, bytes_accessed=nbytes, transcendentals=transcendentals)


HBM = pl.BlockSpec(memory_space=pl.ANY)


def whole(*shape):
    return pl.BlockSpec(shape, lambda *i: (0,) * len(shape))


def row_tile(width, tile=TILE):
    return pl.BlockSpec((tile, width), lambda i, *s: (i, 0))


def col_tile(rows, width):
    return pl.BlockSpec((rows, width), lambda i, *s: (0, i))


def copies(table, pieces, target, only=None):
    core = table[2 * CHIPS]
    for side in range(2):
        for half in range(2):
            quarter = 2 * (core ^ side) + half

            def start(side=side, half=half, quarter=quarter):
                for part in range(2):
                    source = pieces[4 * side + 2 * half + part]
                    for j in range(CHIPS // 2):
                        block = table[half * CHIPS + part * (CHIPS // 2) + j]
                        place, semaphore = target(quarter, block)
                        pltpu.make_async_copy(
                            source.at[pl.ds(j * BLOCK, BLOCK)], place, semaphore
                        ).start()

            if only is None:
                start()
            elif half == only & 1:
                pl.when(quarter == only)(start)


def by_cols(store, sems):
    def target(quarter, block):
        return store.at[quarter, pl.ds(pl.multiple_of(block * BLOCK, 16), BLOCK)], sems.at[quarter]

    return target


def one_col(store, semaphore):
    def target(quarter, block):
        return store.at[pl.ds(pl.multiple_of(block * BLOCK, 16), BLOCK)], semaphore

    return target


def by_rows(store, sems):
    def target(quarter, block):
        first = pl.multiple_of((block & 3) * (4 * BLOCK) + quarter * BLOCK, 16)
        return store.at[block >> 2, pl.ds(first, BLOCK)], sems.at[block >> 2]

    return target


def arrived(ref, semaphore):
    pltpu.make_async_copy(ref, ref, semaphore).wait()


SLOTS = pltpu.VMEM((4, WIDTH, WIDTH), BF)
SLOT_SEMS = pltpu.SemaphoreType.DMA((4,))


def before_kernel(info, tok_ref, cot_ref, x_ref, up_ref, down_ref):
    pick = turn(info[0], pl.program_id(0) * TILE, TILE, True)
    x_ref[...] = mm(pick, tok_ref[...]).astype(BF)
    grads = mm(pick, cot_ref[...])
    up_ref[...] = grads.astype(BF)
    down_ref[...] = (grads - jnp.sum(grads, axis=1, keepdims=True) * (1.0 / WIDTH)).astype(BF)


def before(info, tokens, cotangent):
    shape = jax.ShapeDtypeStruct((ROWS, WIDTH), BF)
    return pl.pallas_call(
        before_kernel,
        grid_spec=pltpu.PrefetchScalarGridSpec(
            num_scalar_prefetch=1,
            grid=(ROWS // TILE,),
            in_specs=[whole(ROWS, WIDTH)] * 2,
            out_specs=[row_tile(WIDTH)] * 3,
        ),
        out_shape=[shape] * 3,
        compiler_params=params(),
        cost_estimate=cost(4 * ROWS * ROWS * WIDTH, 10 * ROWS * WIDTH),
        name="before",
    )(info, tokens, cotangent)


def qkv_kernel(table, x_ref, gain_ref, *rest):
    pieces, (normed_ref, out_ref, store, sems) = rest[:8], rest[8:]
    step = pl.program_id(0)

    @pl.when(step == 0)
    def _():
        copies(table, pieces, by_cols(store, sems))
        inverse, expanded = norm_parts(x_ref[...].astype(F32))
        normed_ref[...] = (expanded * inverse * gain_ref[...]).astype(BF)

    arrived(store.at[step], sems.at[step])
    out_ref[...] = mm(normed_ref[...], store[step]).astype(BF)

    @pl.when(step == 2)
    def _():
        arrived(store.at[3], sems.at[3])


def project_qkv(table, x, gain, pieces):
    return pl.pallas_call(
        qkv_kernel,
        grid_spec=pltpu.PrefetchScalarGridSpec(
            num_scalar_prefetch=1,
            grid=(3,),
            in_specs=[whole(ROWS, WIDTH), whole(1, WIDTH)] + [HBM] * 8,
            out_specs=[whole(ROWS, WIDTH), col_tile(ROWS, WIDTH)],
            scratch_shapes=[SLOTS, SLOT_SEMS],
        ),
        out_shape=[
            jax.ShapeDtypeStruct((ROWS, WIDTH), BF),
            jax.ShapeDtypeStruct((ROWS, 3 * WIDTH), BF),
        ],
        compiler_params=params(),
        cost_estimate=cost(6 * ROWS * WIDTH * WIDTH, 14 * ROWS * WIDTH),
        name="project_qkv",
    )(table, x, gain, *pieces)


SPANS = ((0, 0, 256, 0), (256, 0, 512, 256), (512, 0, 768, 768), (768, 768, 256, 1536))


def tail_segments(info, axis):
    shape = (TILE, 1) if axis == 0 else (1, TILE)
    place = lax.broadcasted_iota(jnp.int32, shape, axis) + BIG + info[0]
    place = jnp.where(place >= ROWS, place - ROWS, place)
    found = jnp.zeros(shape, jnp.int32)
    for j in range(3):
        found = found + jnp.where(place >= info[1 + j], 1, 0)
    return found


def head_mask(head):
    place = lanes(2 * HEAD)
    return (place < HEAD) if head == 0 else (place >= HEAD)


def attend_kernel(info, q_ref, k_ref, v_ref, out_ref, prob_ref):
    causal = lax.broadcasted_iota(jnp.int32, (TILE, TILE), 0) >= lax.broadcasted_iota(
        jnp.int32, (TILE, TILE), 1
    )
    for first, key_first, key_count, place in SPANS:
        queries = q_ref[first : first + TILE, :]
        keys = k_ref[key_first : key_first + key_count, :]
        values = v_ref[key_first : key_first + key_count, :]
        allowed = causal
        if first == BIG:
            allowed = causal & (tail_segments(info, 0) == tail_segments(info, 1))
        mixed = []
        for head in range(2):
            mine = jnp.where(head_mask(head), queries, 0) * BF(HEAD**-0.5)
            scores = mm_nt(mine, keys)
            last = jnp.where(allowed, scores[:, key_count - TILE :], -1e30)
            largest = jnp.max(last, axis=1, keepdims=True)
            if key_count > TILE:
                early = scores[:, : key_count - TILE]
                largest = jnp.maximum(largest, jnp.max(early, axis=1, keepdims=True))
                early = jnp.exp(early - largest)
            last = jnp.exp(last - largest)
            normal = jnp.sum(last, axis=1, keepdims=True)
            if key_count > TILE:
                normal = normal + jnp.sum(early, axis=1, keepdims=True)
            scale = 1.0 / normal
            if key_count > TILE:
                prob_ref[head, :, place : place + key_count - TILE] = (early * scale).astype(BF)
            prob_ref[head, :, place + key_count - TILE : place + key_count] = (
                last * scale
            ).astype(BF)
            mixed.append(mm(prob_ref[head, :, place : place + key_count], values))
        out_ref[first : first + TILE, :] = jnp.where(head_mask(0), mixed[0], mixed[1]).astype(BF)


def pair_cols(offset):
    return pl.BlockSpec((ROWS, 2 * HEAD), lambda i, *s: (0, offset + i))


PROB_SPEC = pl.BlockSpec((2, TILE, PROB_COLS), lambda i, *s: (i, 0, 0))
PART = 3
PART_COLS = PART * 2 * HEAD


def attend(info, qkv, part):
    first = PART * part
    return pl.pallas_call(
        attend_kernel,
        grid_spec=pltpu.PrefetchScalarGridSpec(
            num_scalar_prefetch=1,
            grid=(PART,),
            in_specs=[pair_cols(first), pair_cols(PAIRS + first), pair_cols(2 * PAIRS + first)],
            out_specs=[pair_cols(0), PROB_SPEC],
        ),
        out_shape=[
            jax.ShapeDtypeStruct((ROWS, PART_COLS), BF),
            jax.ShapeDtypeStruct((2 * PART, TILE, PROB_COLS), BF),
        ],
        compiler_params=params(),
        cost_estimate=cost(4 * 6 * 7 * TILE * TILE * 256, 4 * ROWS * WIDTH + 5505024, 2752512),
        name=f"attend_{part}",
    )(info, qkv, qkv, qkv)


def middle_kernel(table, first_ref, second_ref, x_ref, gain_ref, *rest):
    pieces, (middle_ref, normed_ref, store, semaphore) = rest[:8], rest[8:]

    @pl.when(pl.program_id(0) == 0)
    def _():
        copies(table, pieces, one_col(store, semaphore), 3)
        arrived(store, semaphore)

    mixed = mm(first_ref[...], store[:PART_COLS]) + mm(second_ref[...], store[PART_COLS:])
    mixed = mixed - jnp.sum(mixed, axis=1, keepdims=True) * (1.0 / WIDTH)
    rows = x_ref[...].astype(F32) + jnp.where(lanes() == WIDTH - 1, 0.0, mixed)
    inverse, expanded = norm_parts(rows)
    middle_ref[...] = rows
    normed_ref[...] = (expanded * inverse * gain_ref[...]).astype(BF)


def make_middle(table, attended, x, gain, pieces):
    return pl.pallas_call(
        middle_kernel,
        grid_spec=pltpu.PrefetchScalarGridSpec(
            num_scalar_prefetch=1,
            grid=(ROWS // TILE,),
            in_specs=[row_tile(PART_COLS)] * 2 + [row_tile(WIDTH), whole(1, WIDTH)] + [HBM] * 8,
            out_specs=[row_tile(WIDTH)] * 2,
            scratch_shapes=[pltpu.VMEM((WIDTH, WIDTH), BF), pltpu.SemaphoreType.DMA],
        ),
        out_shape=[
            jax.ShapeDtypeStruct((ROWS, WIDTH), F32),
            jax.ShapeDtypeStruct((ROWS, WIDTH), BF),
        ],
        compiler_params=params(),
        cost_estimate=cost(2 * ROWS * WIDTH * WIDTH, 14 * ROWS * WIDTH),
        name="make_middle",
    )(table, *attended, x, gain, *pieces)


GELU_A = 0.7978845608028654
GELU_B = 0.044715


def feed_kernel(inverse, table, second_ref, down_in_ref, bias_ref, *rest):
    pieces, outs = rest[:8], rest[10:14]
    act_ref, slope_ref = rest[8:10]
    store, sems, stage, out_sem = rest[14:]
    step = pl.program_id(0)
    core = inverse[2 * CHIPS]

    @pl.when(step == 0)
    def _():
        copies(table, pieces, by_cols(store, sems))

    arrived(store.at[step], sems.at[step])
    for i in range(ROWS // TILE):
        rows = slice(i * TILE, (i + 1) * TILE)
        hidden = mm(second_ref[rows, :], store[step]) + bias_ref[...]
        square = hidden * hidden
        bent = jnp.tanh(hidden * (GELU_A + (GELU_A * GELU_B) * square))
        half = 0.5 + 0.5 * bent
        act_ref[rows, :] = (hidden * half).astype(BF)
        tilt = hidden * (0.5 * GELU_A + (1.5 * GELU_A * GELU_B) * square)
        slope_ref[rows, :] = (half + tilt * (1.0 - bent * bent)).astype(BF)
    grads = mm_tn(act_ref[...], down_in_ref[...])
    for i in range(8):
        slot = 8 * step + i
        stage[slot] = grads[96 * i : 96 * (i + 1)].astype(BF)
        mine = core == (i & 1)

        def put(first, slot=slot, chip=4 * step + (i >> 1)):
            for half in range(2):
                pltpu.make_async_copy(
                    stage.at[slot, :, pl.ds(half * HALF, HALF)],
                    outs[first + 2 * half].at[inverse[half * CHIPS + chip]],
                    out_sem,
                ).start()

        pl.when(mine)(functools.partial(put, 0))
        pl.when(jnp.logical_not(mine))(functools.partial(put, 1))

    @pl.when(step == 3)
    def _():
        arrived(stage, out_sem)


HALF = WIDTH // 2


def feed(inverse, table, second, down_in, bias, pieces):
    return pl.pallas_call(
        feed_kernel,
        grid_spec=pltpu.PrefetchScalarGridSpec(
            num_scalar_prefetch=2,
            grid=(4,),
            in_specs=[whole(ROWS, WIDTH)] * 2 + [col_tile(1, WIDTH)] + [HBM] * 8,
            out_specs=[col_tile(ROWS, WIDTH)] * 2 + [HBM] * 4,
            scratch_shapes=[SLOTS, SLOT_SEMS, pltpu.VMEM((32, 96, WIDTH), BF), pltpu.SemaphoreType.DMA],
        ),
        out_shape=[jax.ShapeDtypeStruct((ROWS, HIDDEN), BF)] * 2
        + [jax.ShapeDtypeStruct((CHIPS, 96, HALF), BF)] * 4,
        compiler_params=params(),
        cost_estimate=cost(4 * ROWS * WIDTH * HIDDEN, 6 * ROWS * HIDDEN + 4 * WIDTH * HIDDEN),
        name="feed",
    )(inverse, table, second, down_in, bias, *pieces)


SPARE = 128
FIRST_COLS = 2 * WIDTH + HALF + SPARE
SECOND_COLS = 2 * WIDTH + HALF


def spread_out(inverse, half, grads, stage, cols=slice(None)):
    core = inverse[2 * CHIPS]
    for device in range(32):
        place = inverse[half * CHIPS + (device >> 1)]
        stage[core ^ (device & 1), place, :, cols] = grads[24 * device : 24 * (device + 1)].astype(BF)


def back_kernel(inverse, table, down_in_ref, second_ref, slope_ref, gain_ref, *rest):
    att_hbm, middle_hbm, up_hbm = rest[:4][:2], rest[2], rest[3]
    down_pieces, up_pieces, out_pieces = rest[4:12], rest[12:20], rest[20:28]
    outs, total_hbm, grad_att_hbm = rest[28:32], rest[32], rest[33]
    (down_store, down_sems, up_store, up_sems, out_store, att, middle, up, in_sems,
     grads, weighted, stage, out_stage, spare, total, grad_att, out_sem) = rest[34:]
    step = pl.program_id(0)
    core = inverse[2 * CHIPS]
    late = [
        (att_hbm[0], att.at[:, pl.ds(0, PART_COLS)]),
        (att_hbm[1], att.at[:, pl.ds(PART_COLS, PART_COLS)]),
        (middle_hbm, middle),
        (up_hbm, up),
    ]

    @pl.when(step == 0)
    def _():
        copies(table, down_pieces, by_rows(down_store, down_sems))
        copies(table, up_pieces, by_cols(up_store, up_sems))
        copies(table, out_pieces, one_col(out_store, in_sems.at[4]), 3)
        for i, (source, target) in enumerate(late):
            pltpu.make_async_copy(source, target, in_sems.at[i]).start()

    arrived(down_store.at[step], down_sems.at[step])
    sums = jnp.zeros((1, WIDTH), F32)
    for i in range(ROWS // TILE):
        rows = slice(i * TILE, (i + 1) * TILE)
        value = slope_ref[rows, :].astype(F32) * mm_nt(down_in_ref[rows, :], down_store[step])
        value = value.astype(BF)
        grads[rows, :] = value
        sums += jnp.sum(value.astype(F32), axis=0, keepdims=True)
    for i in range(8):
        few = jnp.concatenate([sums[:, 96 * i : 96 * (i + 1)], jnp.zeros((1, 32), F32)], axis=1)
        few = jnp.broadcast_to(few, (24, SPARE)).astype(BF)
        spare[core ^ (i & 1), inverse[4 * step + (i >> 1)]] = few
    arrived(up_store.at[step], up_sems.at[step])

    @pl.when(step == 0)
    def _():
        for i in range(ROWS // TILE):
            rows = slice(i * TILE, (i + 1) * TILE)
            weighted[rows, :] = mm_nt(grads[rows, :], up_store[step])

    @pl.when(step > 0)
    def _():
        for i in range(ROWS // TILE):
            rows = slice(i * TILE, (i + 1) * TILE)
            weighted[rows, :] += mm_nt(grads[rows, :], up_store[step])

    found = mm_tn(second_ref[...], grads[...])
    for half in range(2):

        @pl.when((step >> 1) == half)
        def _(half=half):
            spread_out(inverse, half, found, stage.at[step])
            for which in range(2):
                pltpu.make_async_copy(
                    stage.at[step, which],
                    outs[2 * half + which].at[:, :, pl.ds(pl.multiple_of((step & 1) * WIDTH, 128), WIDTH)],
                    out_sem.at[0],
                ).start()

    @pl.when(step == 3)
    def _():
        for which in range(2):
            pltpu.make_async_copy(
                spare.at[which], outs[which].at[:, :, pl.ds(FIRST_COLS - SPARE, SPARE)], out_sem.at[1]
            ).start()
        for i, (source, target) in enumerate(late):
            pltpu.make_async_copy(source, target, in_sems.at[i]).wait()
        arrived(out_store, in_sems.at[4])
        for i in range(ROWS // TILE):
            rows = slice(i * TILE, (i + 1) * TILE)
            inner, expanded = norm_parts(middle[rows, :])
            value = up[rows, :].astype(F32) + norm_back(
                weighted[rows, :] * gain_ref[...], inner, expanded
            )
            total[rows, :] = value
            mixed = (value - jnp.sum(value, axis=1, keepdims=True) * (1.0 / WIDTH)).astype(BF)
            grads[rows, :] = mixed
            grad_att[rows, :] = mm_nt(mixed, out_store[...]).astype(BF)
        pltpu.make_async_copy(total, total_hbm, out_sem.at[2]).start()
        pltpu.make_async_copy(grad_att, grad_att_hbm, out_sem.at[3]).start()
        for half in range(2):
            found = mm_tn(att[...], grads[:, half * HALF : (half + 1) * HALF])
            spread_out(inverse, half, found, out_stage.at[half])
            for which in range(2):
                pltpu.make_async_copy(
                    out_stage.at[half, which],
                    outs[2 * half + which].at[:, :, pl.ds(2 * WIDTH, HALF)],
                    out_sem.at[4],
                ).start()
        arrived(stage, out_sem.at[0])
        arrived(spare, out_sem.at[1])
        arrived(total, out_sem.at[2])
        arrived(grad_att, out_sem.at[3])
        arrived(out_stage, out_sem.at[4])


def back(inverse, table, down_in, second, slope, gain, attended, middle, upstream, down_pieces, up_pieces, out_pieces):
    return pl.pallas_call(
        back_kernel,
        grid_spec=pltpu.PrefetchScalarGridSpec(
            num_scalar_prefetch=2,
            grid=(4,),
            in_specs=[whole(ROWS, WIDTH)] * 2 + [col_tile(ROWS, WIDTH), whole(1, WIDTH)] + [HBM] * 28,
            out_specs=[HBM] * 6,
            scratch_shapes=[
                SLOTS, SLOT_SEMS, SLOTS, SLOT_SEMS,
                pltpu.VMEM((WIDTH, WIDTH), BF),
                pltpu.VMEM((ROWS, WIDTH), BF),
                pltpu.VMEM((ROWS, WIDTH), F32),
                pltpu.VMEM((ROWS, WIDTH), BF),
                pltpu.SemaphoreType.DMA((5,)),
                pltpu.VMEM((ROWS, WIDTH), BF),
                pltpu.VMEM((ROWS, WIDTH), F32),
                pltpu.VMEM((4, 2, CHIPS, 24, WIDTH), BF),
                pltpu.VMEM((2, 2, CHIPS, 24, HALF), BF),
                pltpu.VMEM((2, CHIPS, 24, SPARE), BF),
                pltpu.VMEM((ROWS, WIDTH), F32),
                pltpu.VMEM((ROWS, WIDTH), BF),
                pltpu.SemaphoreType.DMA((5,)),
            ],
        ),
        out_shape=[jax.ShapeDtypeStruct((CHIPS, 24, FIRST_COLS), BF)] * 2
        + [jax.ShapeDtypeStruct((CHIPS, 24, SECOND_COLS), BF)] * 2
        + [jax.ShapeDtypeStruct((ROWS, WIDTH), F32), jax.ShapeDtypeStruct((ROWS, WIDTH), BF)],
        compiler_params=params(),
        cost_estimate=cost(6 * ROWS * WIDTH * HIDDEN + 4 * ROWS * WIDTH * WIDTH, 40000000),
        name="back",
    )(inverse, table, down_in, second, slope, gain, *attended, middle, upstream, *down_pieces, *up_pieces, *out_pieces)


def attend_grad_kernel(half, inverse, q_ref, k_ref, v_ref, grad_ref, att_ref, prob_ref, normed_ref,
                       dq_ref, dk_ref, dv_ref, keep_hbm, send_hbm, key_sum, value_sum, kept, stage, out_sem):
    factor = HEAD**-0.5
    key_sum[...] = jnp.zeros_like(key_sum)
    value_sum[...] = jnp.zeros_like(value_sum)
    for first, key_first, key_count, place in SPANS:
        rows = slice(first, first + TILE)
        keys_at = slice(key_first, key_first + key_count)
        queries = q_ref[rows, :]
        grads = grad_ref[rows, :]
        product = grads.astype(F32) * att_ref[rows, :].astype(F32)
        keys = k_ref[keys_at, :]
        values = v_ref[keys_at, :]
        parts = []
        for head in range(2):
            mask = head_mask(head)
            my_grads = jnp.where(mask, grads, 0)
            my_queries = jnp.where(mask, queries, 0)
            probs = prob_ref[head, :, place : place + key_count]
            inner = jnp.sum(jnp.where(mask, product, 0.0), axis=1, keepdims=True)
            slopes = probs.astype(F32) * (mm_nt(my_grads, values) - inner)
            slopes = slopes.astype(BF)
            parts.append(mm(slopes, keys))
            value_sum[:, keys_at] += mm_tn(my_grads, probs)
            key_sum[:, keys_at] += mm_tn(my_queries, slopes)
        dq_ref[rows, :] = (jnp.where(head_mask(0), parts[0], parts[1]) * factor).astype(BF)
    dk_ref[...] = (key_sum[...].T * factor).astype(BF)
    dv_ref[...] = value_sum[...].T.astype(BF)
    step = pl.program_id(0)
    for i, ref in enumerate((dq_ref, dk_ref, dv_ref)):
        kept[i, step] = ref[...]

    @pl.when(step == PART - 1)
    def _():
        for i in range(3):
            value = jnp.concatenate([kept[i, j] for j in range(PART)], axis=1)
            found = mm_tn(normed_ref[...], value)
            spread_out(inverse, half, found, stage.at[i])
            for which, target in enumerate((keep_hbm, send_hbm)):
                pltpu.make_async_copy(
                    stage.at[i, which], target.at[:, :, pl.ds(i * PART_COLS, PART_COLS)], out_sem
                ).start()
        arrived(stage, out_sem)


def attend_grad(inverse, qkv, grad_attended, attended, probs, normed, part):
    first = PART * part
    grads = (CHIPS, 24, 3 * PART_COLS)
    return pl.pallas_call(
        functools.partial(attend_grad_kernel, part),
        grid_spec=pltpu.PrefetchScalarGridSpec(
            num_scalar_prefetch=1,
            grid=(PART,),
            in_specs=[
                pair_cols(first), pair_cols(PAIRS + first), pair_cols(2 * PAIRS + first),
                pair_cols(first), pair_cols(0), PROB_SPEC, whole(ROWS, WIDTH),
            ],
            out_specs=[pair_cols(0)] * 3 + [HBM] * 2,
            scratch_shapes=[pltpu.VMEM((2 * HEAD, ROWS), F32)] * 2
            + [
                pltpu.VMEM((3, PART, ROWS, 2 * HEAD), BF),
                pltpu.VMEM((3, 2, CHIPS, 24, PART_COLS), BF),
                pltpu.SemaphoreType.DMA,
            ],
        ),
        out_shape=[jax.ShapeDtypeStruct((ROWS, PART_COLS), BF)] * 3
        + [jax.ShapeDtypeStruct(grads, BF)] * 2,
        compiler_params=params(),
        cost_estimate=cost(8 * 6 * 7 * TILE * TILE * 256, 8 * ROWS * WIDTH + 5505024),
        name=f"attend_grad_{part}",
    )(inverse, qkv, qkv, qkv, grad_attended, attended, probs, normed)


def token_grad_kernel(table, info, *rest):
    parts, (x_ref, total_ref, gain_ref) = rest[:6], rest[6:9]
    pieces, (out_ref, store, turned, sems) = rest[9:17], rest[17:]
    step = pl.program_id(0)

    @pl.when(step == 0)
    def _():
        copies(table, pieces, by_cols(store, sems))
        for i in range(4):
            arrived(store.at[i], sems.at[i])

    weighted = jnp.zeros((TILE, WIDTH), F32)
    for part in range(2):
        for i in range(3):
            cols = slice(part * PART_COLS, (part + 1) * PART_COLS)
            weighted += mm_nt(parts[3 * part + i][...], store[i, :, cols])
    inverse, expanded = norm_parts(x_ref[...].astype(F32))
    grads = total_ref[...] + norm_back(weighted * gain_ref[...], inverse, expanded)
    turned[pl.ds(pl.multiple_of(step * TILE, TILE), TILE), :] = grads.astype(BF)

    @pl.when(step == ROWS // TILE - 1)
    def _():
        for i in range(ROWS // TILE):
            turn_back = mm(turn(info[0], i * TILE, TILE, False), turned[...])
            out_ref[i * TILE : (i + 1) * TILE, :] = turn_back.astype(BF)[:, : WIDTH - 1]


def token_grad(table, info, parts, x, total, gain, pieces):
    return pl.pallas_call(
        token_grad_kernel,
        grid_spec=pltpu.PrefetchScalarGridSpec(
            num_scalar_prefetch=2,
            grid=(ROWS // TILE,),
            in_specs=[row_tile(PART_COLS)] * 6 + [row_tile(WIDTH)] * 2 + [whole(1, WIDTH)] + [HBM] * 8,
            out_specs=whole(ROWS, WIDTH - 1),
            scratch_shapes=[SLOTS, pltpu.VMEM((ROWS, WIDTH), BF), SLOT_SEMS],
        ),
        out_shape=jax.ShapeDtypeStruct((ROWS, WIDTH - 1), BF),
        compiler_params=params(),
        cost_estimate=cost(8 * ROWS * WIDTH * WIDTH, 20 * ROWS * WIDTH),
        name="token_grad",
    )(table, info, *parts, x, total, gain, *pieces)


def result_kernel(table, info, act_ref, middle_ref, *rest):
    pieces, (out_ref, store, turned, sems) = rest[:8], rest[8:]
    step = pl.program_id(0)

    @pl.when(step == 0)
    def _():
        copies(table, pieces, by_rows(store, sems))
        for i in range(4):
            arrived(store.at[i], sems.at[i])

    branch = mm(act_ref[:, :WIDTH], store[0])
    for i in range(1, 4):
        branch += mm(act_ref[:, i * WIDTH : (i + 1) * WIDTH], store[i])
    branch = branch - jnp.sum(branch, axis=1, keepdims=True) * (1.0 / WIDTH)
    turned[pl.ds(pl.multiple_of(step * TILE, TILE), TILE), :] = (middle_ref[...] + branch).astype(BF)

    @pl.when(step == ROWS // TILE - 1)
    def _():
        for i in range(ROWS // TILE):
            turn_back = mm(turn(info[0], i * TILE, TILE, False), turned[...])
            out_ref[i * TILE : (i + 1) * TILE, :] = turn_back.astype(BF)[:, : WIDTH - 1]


def result(table, info, active, middle, pieces):
    return pl.pallas_call(
        result_kernel,
        grid_spec=pltpu.PrefetchScalarGridSpec(
            num_scalar_prefetch=2,
            grid=(ROWS // TILE,),
            in_specs=[row_tile(HIDDEN), row_tile(WIDTH)] + [HBM] * 8,
            out_specs=whole(ROWS, WIDTH - 1),
            scratch_shapes=[SLOTS, pltpu.VMEM((ROWS, WIDTH), BF), SLOT_SEMS],
        ),
        out_shape=jax.ShapeDtypeStruct((ROWS, WIDTH - 1), BF),
        compiler_params=params(),
        cost_estimate=cost(2 * ROWS * WIDTH * HIDDEN, 2 * ROWS * HIDDEN + 4718592 + 10 * ROWS * WIDTH),
        name="result",
    )(table, info, active, middle, *pieces)


def segment_info(lengths):
    bounds = jnp.cumsum(lengths[0])
    starts = bounds - lengths[0]
    first = jnp.sum(jnp.where(lengths[0] == BIG, starts, 0))
    return jnp.concatenate([first[None], bounds]).astype(jnp.int32)


def swap(value, axis, bits, size):
    return lax.ppermute(value, axis, [(i, i ^ bits) for i in range(size)])


def place_of(offset, half):
    x, y, z = offset & 1, (offset >> 1) & 1, offset >> 2
    return z + 4 * (x + 2 * y if half == 0 else y + 2 * x)


def offset_of(place, half):
    z, low, high = place & 3, (place >> 2) & 1, (place >> 3) & 1
    return 4 * z + (low + 2 * high if half == 0 else high + 2 * low)


WAYS = {
    "core": ("narrow", 1),
    "x": ("narrow", 2),
    "y": ("wide", 1),
    "z1": ("wide", 2),
    "z2": ("wide", 4),
    "z3": ("wide", 6),
}


class Cube:
    def __init__(self, sizes):
        self.sizes = sizes
        wide, narrow = lax.axis_index("wide"), lax.axis_index("narrow")
        self.core = (narrow & 1).astype(jnp.int32)
        self.chip = (wide * 2 + (narrow >> 1)).astype(jnp.int32)
        every = jnp.arange(CHIPS, dtype=jnp.int32)
        blocks = [self.chip ^ offset_of(every, half) for half in range(2)]
        places = [place_of(self.chip ^ every, half) for half in range(2)]
        self.table = jnp.concatenate(blocks + [self.core[None]])
        self.inverse = jnp.concatenate(places + [self.core[None]])

    def hop(self, value, way):
        axis, bits = WAYS[way]
        return swap(value, axis, bits, self.sizes[axis])

    def along_z(self, value):
        return [self.hop(value, way) for way in ("z1", "z2", "z3")]

    def gather_small(self, row):
        row = jnp.pad(row, ((0, 0), (0, -row.shape[1] % 128)))
        other = yield self.hop(row, "core")
        row = jnp.concatenate([row, other])
        others = yield self.along_z(row)
        row = jnp.concatenate([row] + others)
        other = yield self.hop(row, "x")
        row = jnp.concatenate([row, other])
        other = yield self.hop(row, "y")
        row = jnp.concatenate([row, other])
        every = jnp.arange(2 * CHIPS, dtype=jnp.int32)
        return row[place_of((every >> 1) ^ self.chip, 0) * 2 + ((every & 1) ^ self.core)]

    def pair(self, shard):
        half = shard.shape[1] // 2
        other = yield self.hop(shard, "core")
        mine = lax.dynamic_slice_in_dim(shard, self.core * half, half, 1)
        theirs = lax.dynamic_slice_in_dim(other, self.core * half, half, 1)
        return jnp.where(
            self.core == 0, jnp.concatenate([mine, theirs]), jnp.concatenate([theirs, mine])
        )

    def gather(self, block):
        half = block.shape[1] // 2
        others = yield self.along_z(block)
        cols = [slice(i * half, (i + 1) * half) for i in range(2)]
        near = [jnp.concatenate([part[:, c] for part in [block] + others]) for c in cols]
        other = yield [self.hop(part, way) for part, way in zip(near, ("x", "y"))]
        near = [jnp.concatenate(both) for both in zip(near, other)]
        far = yield [self.hop(part, way) for part, way in zip(near, ("y", "x"))]
        own = [near[0], far[0], near[1], far[1]]
        other = yield [self.hop(part, "core") for part in own]
        return own + other

    def gather_cols(self, shard):
        block = yield from self.pair(shard)
        return (yield from self.gather(block))

    def gather_rows(self, shard):
        return (yield from self.gather(jnp.concatenate([shard[:BLOCK], shard[BLOCK:]], axis=1)))

    def reduce(self, keep, send, half):
        got = yield self.hop(send, "core")
        for way in ("yx", "xy")[half]:
            count = keep.shape[0] // 2
            both = [
                (keep[part].astype(F32) + got[part].astype(F32)).astype(BF)
                for part in (slice(0, count), slice(count, None))
            ]
            keep = both[0]
            got = yield self.hop(both[1], way)
        both = [(keep[i].astype(F32) + got[i].astype(F32)).astype(BF) for i in range(4)]
        others = yield [self.hop(both[i], way) for i, way in ((1, "z1"), (2, "z2"), (3, "z3"))]
        return sum([other.astype(F32) for other in others], both[0].astype(F32))


class Plain:
    def __init__(self):
        every = jnp.arange(CHIPS, dtype=jnp.int32)
        self.table = jnp.concatenate([every, every, jnp.zeros((1,), jnp.int32)])
        self.inverse = self.table

    def gather_small(self, row):
        yield ()
        return lax.all_gather(row, AXES, axis=0, tiled=True)

    def gather_cols(self, shard):
        yield ()
        full = lax.all_gather(shard, AXES, axis=0, tiled=True)
        quarters = [full[:, i * WIDTH : (i + 1) * WIDTH] for i in range(4)]
        return [part for quarter in quarters for part in (quarter[:HALF], quarter[HALF:])]

    def gather_rows(self, shard):
        yield ()
        full = lax.all_gather(shard, AXES, axis=0, tiled=True).reshape(CHIPS, 4, BLOCK, WIDTH)
        quarters = [full[:, i].reshape(WIDTH, WIDTH) for i in range(4)]
        return [part for quarter in quarters for part in (quarter[:HALF], quarter[HALF:])]

    def reduce(self, keep, send, half):
        yield ()
        full = jnp.stack([keep, send], axis=1).reshape(-1, keep.shape[2])
        return lax.psum_scatter(full, AXES, scatter_dimension=0, tiled=True).astype(F32)


class Task:
    def __init__(self, steps):
        self.steps, self.flight, self.over, self.result = steps, (), False, None
        self.go(None)

    def go(self, arrived_now):
        try:
            self.flight = self.steps.send(arrived_now)
        except StopIteration as end:
            self.flight, self.over, self.result = (), True, end.value


def meet(values, *tasks):
    tasks = [task for task in tasks if not task.over]
    values, flights = lax.optimization_barrier((values, [task.flight for task in tasks]))
    for task, flight in zip(tasks, flights):
        task.go(flight)
    return values


def finish(values, *tasks):
    while not all(task.over for task in tasks):
        values = meet(values, *tasks)
    return values


def layer(sizes, tokens, lengths, gain_one, w_qkv, w_out, gain_two, w_up, b_up, w_down, cotangent):
    info = segment_info(lengths)
    share, few = b_up.shape[0], gain_one.shape[0]
    links = Cube(sizes) if sizes["wide"] == 8 and sizes["narrow"] == 4 else Plain()
    table, inverse = links.table, links.inverse

    first = Task(links.gather_cols(jnp.concatenate([w_qkv, w_out], axis=1)))
    small = Task(links.gather_small(jnp.concatenate([b_up, gain_one, gain_two])[None]))
    up = Task(links.gather_cols(w_up))
    meet((), first, small)
    side = ((0, 0), (0, 1))
    x, upstream, down_in = before(info, jnp.pad(tokens, side), jnp.pad(cotangent, side))
    x, upstream, down_in, w_down = meet((x, upstream, down_in, w_down), first, small, up)
    w_down = meet(w_down, first, small)
    w_down = meet(w_down, first, small, up)
    down = Task(links.gather_rows(w_down))
    x = finish(x, first, small)
    first = first.result
    small = small.result.astype(F32)
    bias = small[:, :share].reshape(1, HIDDEN)
    norm_one = small[:, share : share + few].reshape(1, WIDTH)
    norm_two = small[:, share + few : share + 2 * few].reshape(1, WIDTH)

    normed, qkv = project_qkv(table, x, norm_one, first)
    qkv = meet(qkv, up)
    att_0, probs_0 = attend(info, qkv, 0)
    att_0, qkv = meet((att_0, qkv), down)
    att_1, probs_1 = attend(info, qkv, 1)
    att_0, att_1 = meet((att_0, att_1), up, down)
    middle, second = make_middle(table, (att_0, att_1), x, norm_two, first)
    second = finish(second, up)
    active, slope, *grad_down = feed(inverse, table, second, down_in, bias, up.result)
    slope, grad_down = meet((slope, grad_down), down)
    downs = [Task(links.reduce(*grad_down[2 * i : 2 * i + 2], i)) for i in range(2)]
    slope = finish(slope, down)
    slope = meet(slope, *downs)
    *grad_up, total, grad_att = back(
        inverse, table, down_in, second, slope, norm_two, (att_0, att_1), middle, upstream,
        down.result, up.result, first,
    )
    grad_att, total, grad_up = meet((grad_att, total, grad_up), *downs)
    ups = [Task(links.reduce(*grad_up[2 * i : 2 * i + 2], i)) for i in range(2)]
    *parts_0, keep, send = attend_grad(inverse, qkv, grad_att, att_0, probs_0, normed, 0)
    grad_att, parts_0, keep, send = meet((grad_att, parts_0, keep, send), *downs, *ups)
    heads_0 = Task(links.reduce(keep, send, 0))
    *parts_1, keep, send = attend_grad(inverse, qkv, grad_att, att_1, probs_1, normed, 1)
    parts_1, keep, send = meet((parts_1, keep, send), *downs, heads_0)
    heads_1 = Task(links.reduce(keep, send, 1))
    active = meet(active, *ups, heads_1)
    output = result(table, info, active, middle, down.result)
    parts_0, output = meet((parts_0, output), *ups, heads_0, heads_1)
    grad_tokens = token_grad(table, info, parts_0 + parts_1, x, total, norm_one, first)
    grad_tokens = finish(grad_tokens, *ups, heads_0, heads_1, *downs)

    grad_down = jnp.concatenate([task.result for task in downs], axis=1)
    one, two = ups[0].result, ups[1].result
    grad_up = jnp.concatenate([one[:, : 2 * WIDTH], two[:, : 2 * WIDTH]], axis=1)
    grad_out = jnp.concatenate(
        [one[:, 2 * WIDTH : 2 * WIDTH + HALF], two[:, 2 * WIDTH : 2 * WIDTH + HALF]], axis=1
    )
    sums = one[:, 2 * WIDTH + HALF : 2 * WIDTH + HALF + 96]
    if few >= 24:
        sums = sums[::24].reshape(-1)
    else:
        index = lax.axis_index("wide") * sizes["narrow"] + lax.axis_index("narrow")
        sums = lax.dynamic_slice_in_dim(sums[0], index % (24 // few) * share, share)
    one, two = heads_0.result, heads_1.result
    grad_qkv = jnp.concatenate(
        [half[:, i * PART_COLS : (i + 1) * PART_COLS] for i in range(3) for half in (one, two)], axis=1
    )
    return (
        output,
        grad_tokens,
        jnp.sum(w_qkv.astype(F32) * grad_qkv, axis=1) / gain_one.astype(F32),
        grad_qkv,
        grad_out,
        jnp.sum(w_up.astype(F32) * grad_up, axis=1) / gain_two.astype(F32),
        grad_up,
        sums,
        grad_down,
    )


def solution(mesh):
    rows, vector = P(AXES, None), P(AXES)
    sizes = dict(mesh.shape)
    return jax.shard_map(
        functools.partial(layer, sizes),
        mesh=mesh,
        in_specs=(rows, rows, vector, rows, rows, vector, rows, vector, rows, rows),
        out_specs=(rows, rows, vector, rows, rows, vector, rows, vector, rows),
        check_vma=False,
    )
```

```python
import functools

import jax
import jax.numpy as jnp
from jax import lax
from jax.experimental import pallas as pl
from jax.experimental.pallas import tpu as pltpu
from jax.sharding import PartitionSpec as P

AXES = ("wide", "narrow")
EPSILON = 1e-05
BF = jnp.bfloat16
F32 = jnp.float32
WIDTH = 768
HIDDEN = 3072
ROWS = 1024
TILE = 256
BIG = 768
PAIRS = 6
HEAD = 64
PROB_COLS = 1792
CHIPS = 16
BLOCK = 48
LIMIT = 56 * 1024 * 1024


def mm(left, right):
    return lax.dot_general(left, right, (((1,), (0,)), ((), ())), preferred_element_type=F32)


def mm_nt(left, right):
    return lax.dot_general(left, right, (((1,), (1,)), ((), ())), preferred_element_type=F32)


def mm_tn(left, right):
    return lax.dot_general(left, right, (((0,), (0,)), ((), ())), preferred_element_type=F32)


def lanes(width=WIDTH):
    return lax.broadcasted_iota(jnp.int32, (1, width), 1)


def norm_parts(rows):
    total = jnp.sum(rows, axis=1, keepdims=True)
    squares = jnp.sum(rows * rows, axis=1, keepdims=True)
    inverse = lax.rsqrt((squares + total * total) * (1.0 / WIDTH) + EPSILON)
    expanded = jnp.where(lanes() == WIDTH - 1, -total, rows)
    return inverse, expanded


def norm_back(weighted, inverse, expanded):
    inner = jnp.sum(weighted * expanded, axis=1, keepdims=True) * (1.0 / WIDTH)
    full = inverse * (weighted - (inverse * inverse * inner) * expanded)
    last = full[:, WIDTH - 1 :]
    return jnp.where(lanes() == WIDTH - 1, 0.0, full - last)


def turn(start, first_row, count, forward):
    rows = lax.broadcasted_iota(jnp.int32, (count, ROWS), 0) + first_row
    cols = lax.broadcasted_iota(jnp.int32, (count, ROWS), 1)
    if forward:
        source = rows + start
        source = jnp.where(source >= ROWS, source - ROWS, source)
    else:
        source = rows - start
        source = jnp.where(source < 0, source + ROWS, source)
    return jnp.where(cols == source, 1.0, 0.0).astype(BF)


def first_row(info):
    return jnp.where(info[2] == BIG, 0, jnp.where(info[3] == BIG, info[2], info[2] + info[3]))


def params(**more):
    return pltpu.CompilerParams(vmem_limit_bytes=LIMIT, **more)


def cost(flops, nbytes, transcendentals=0):
    return pl.CostEstimate(flops=flops, bytes_accessed=nbytes, transcendentals=transcendentals)


HBM = pl.BlockSpec(memory_space=pl.ANY)


def whole(*shape):
    return pl.BlockSpec(shape, lambda *i: (0,) * len(shape))


def row_tile(width, tile=TILE):
    return pl.BlockSpec((tile, width), lambda i, *s: (i, 0))


def col_tile(rows, width):
    return pl.BlockSpec((rows, width), lambda i, *s: (0, i))


def offset_of(place):
    return 4 * (place & 3) + (place >> 2)


def place_at(info, chip):
    offset = info[0] ^ chip
    return (offset >> 2) + 4 * (offset & 3)


def copies(info, pieces, target, cols=None):
    for side in range(2):
        half = info[1] ^ side

        def start(side=side, half=half):
            for place in range(CHIPS):
                source = pieces[4 * side + place // 4].at[pl.ds((place % 4) * BLOCK, BLOCK)]
                if cols is not None:
                    source = source.at[:, pl.ds(*cols)]
                block = pl.multiple_of((info[0] ^ offset_of(place)) * BLOCK, 16)
                pltpu.make_async_copy(source, *target(half, block)).start()

        if cols is None:
            start()
        else:
            pl.when(half == 1)(start)


def by_half(store, sems):
    width = store.shape[1] // 2

    def target(half, first):
        cols = pl.ds(pl.multiple_of(half * width, 128), width)
        return store.at[pl.ds(first, BLOCK), cols], sems.at[half]

    return target


def one_half(store, semaphore):
    return lambda half, first: (store.at[pl.ds(first, BLOCK)], semaphore)


def arrived(ref, semaphore):
    pltpu.make_async_copy(ref, ref, semaphore).wait()


def halves_arrived(store, sems, halves=(0, 1)):
    width = store.shape[1] // 2
    for half in halves:
        arrived(store.at[:, pl.ds(half * width, width)], sems.at[half])


OUT_COLS = (128, WIDTH)
PAIR_SEMS = pltpu.SemaphoreType.DMA((2,))
SLOT_SEMS = pltpu.SemaphoreType.DMA((4,))
PART = 3
PART_COLS = PART * 2 * HEAD
SMALL = 128
A_COLS = 3 * PART_COLS + SMALL
B_COLS = 3 * PART_COLS + WIDTH + SMALL


def pack_kernel(qkv_ref, out_ref, one_ref, two_ref, bias_ref, a_ref, b_ref):
    few, share = one_ref.shape[1], bias_ref.shape[1]
    for part, ref in enumerate((a_ref, b_ref)):
        for i in range(3):
            first = i * WIDTH + part * PART_COLS
            ref[:, i * PART_COLS : (i + 1) * PART_COLS] = qkv_ref[:, first : first + PART_COLS]
    b_ref[:, 3 * PART_COLS : 3 * PART_COLS + WIDTH] = out_ref[...]
    place = lax.broadcasted_iota(jnp.int32, (few, SMALL), 1)

    def column(row, first):
        count = row.shape[1]
        at = lax.broadcasted_iota(jnp.int32, (few, count), 1)
        down = lax.broadcasted_iota(jnp.int32, (few, count), 0) + first
        return jnp.sum(jnp.where(at == down, row.astype(F32), 0.0), axis=1, keepdims=True)

    gains = jnp.where(place == 0, column(one_ref[...], 0), 0.0)
    gains = jnp.where(place == 1, column(two_ref[...], 0), gains)
    a_ref[:, A_COLS - SMALL :] = gains.astype(BF)
    bias = jnp.zeros((few, SMALL), F32)
    for i in range(share // few):
        bias = jnp.where(place == i, column(bias_ref[...], i * few), bias)
    b_ref[:, B_COLS - SMALL :] = bias.astype(BF)


def pack(w_qkv, w_out, gain_one, gain_two, b_up):
    few = w_qkv.shape[0]
    return pl.pallas_call(
        pack_kernel,
        out_shape=[
            jax.ShapeDtypeStruct((few, A_COLS), BF), jax.ShapeDtypeStruct((few, B_COLS), BF)
        ],
        compiler_params=params(),
        name="pack",
    )(w_qkv, w_out, gain_one[None], gain_two[None], b_up[None])


def join_kernel(count, info, *refs):
    for own, other, out in zip(refs[:count], refs[count : 2 * count], refs[2 * count :]):
        half = own.shape[1] // 2
        cols = pl.ds(pl.multiple_of(info[1] * half, 128), half)
        mine, theirs = own[:, cols].astype(F32), other[:, cols].astype(F32)
        first = info[1] == 0
        out[...] = jnp.concatenate(
            [jnp.where(first, mine, theirs), jnp.where(first, theirs, mine)], axis=0
        ).astype(BF)


def join(info, own, other):
    return pl.pallas_call(
        functools.partial(join_kernel, len(own)),
        grid_spec=pltpu.PrefetchScalarGridSpec(
            num_scalar_prefetch=1,
            grid=(1,),
            in_specs=[whole(*v.shape) for v in [*own, *other]],
            out_specs=[whole(2 * v.shape[0], v.shape[1] // 2) for v in own],
        ),
        out_shape=[jax.ShapeDtypeStruct((2 * v.shape[0], v.shape[1] // 2), BF) for v in own],
        compiler_params=params(),
        name="join",
    )(info, *own, *other)


def before_kernel(info, tok_ref, cot_ref, x_ref, up_ref, down_ref, wide):
    pick = turn(first_row(info), pl.program_id(0) * TILE, TILE, True)
    wide[:, WIDTH - 128 :] = jnp.zeros((TILE, 128), F32)
    wide[:, : WIDTH - 1] = mm(pick, tok_ref[...])
    x_ref[...] = wide[...].astype(BF)
    wide[:, : WIDTH - 1] = mm(pick, cot_ref[...])
    grads = wide[...]
    up_ref[...] = grads.astype(BF)
    down_ref[...] = (grads - jnp.sum(grads, axis=1, keepdims=True) * (1.0 / WIDTH)).astype(BF)


def before(info, tokens, cotangent):
    shape = jax.ShapeDtypeStruct((ROWS, WIDTH), BF)
    return pl.pallas_call(
        before_kernel,
        grid_spec=pltpu.PrefetchScalarGridSpec(
            num_scalar_prefetch=1,
            grid=(ROWS // TILE,),
            in_specs=[whole(ROWS, WIDTH - 1)] * 2,
            out_specs=[row_tile(WIDTH)] * 3,
            scratch_shapes=[pltpu.VMEM((TILE, WIDTH), F32)],
        ),
        out_shape=[shape] * 3,
        compiler_params=params(),
        cost_estimate=cost(4 * ROWS * ROWS * WIDTH, 10 * ROWS * WIDTH),
        name="before",
    )(info, tokens, cotangent)


SPANS = ((0, 0, 256, 0), (256, 0, 512, 256), (512, 0, 768, 768), (768, 768, 256, 1536))


def tail_segments(info, axis):
    shape = (TILE, 1) if axis == 0 else (1, TILE)
    place = lax.broadcasted_iota(jnp.int32, shape, axis) + BIG + first_row(info)
    place = jnp.where(place >= ROWS, place - ROWS, place)
    found = jnp.zeros(shape, jnp.int32)
    bound = 0
    for j in range(3):
        bound = bound + info[2 + j]
        found = found + jnp.where(place >= bound, 1, 0)
    return found


def head_mask(head):
    place = lanes(2 * HEAD)
    return (place < HEAD) if head == 0 else (place >= HEAD)


def attend_pair(info, qkv, pair, out_ref, norm_ref, prob_ref):
    cols = [pl.ds(pl.multiple_of(i * PART_COLS + pair * 2 * HEAD, 128), 2 * HEAD) for i in range(3)]
    causal = lax.broadcasted_iota(jnp.int32, (TILE, TILE), 0) >= lax.broadcasted_iota(
        jnp.int32, (TILE, TILE), 1
    )
    for first, key_first, key_count, place in SPANS:
        queries = qkv[first : first + TILE, cols[0]]
        keys = qkv[key_first : key_first + key_count, cols[1]]
        values = qkv[key_first : key_first + key_count, cols[2]]
        values = jnp.concatenate([values, jnp.ones_like(values)], axis=1)
        allowed = causal
        if first == BIG:
            allowed = causal & (tail_segments(info, 0) == tail_segments(info, 1))
        mixed = []
        for head in range(2):
            mine = jnp.where(head_mask(head), queries, 0) * BF(HEAD**-0.5)
            scores = mm_nt(mine, keys)
            split = key_count - TILE
            last = jnp.where(allowed, scores[:, split:], -1e30)
            largest = jnp.max(last, axis=1, keepdims=True)
            if split:
                largest = jnp.maximum(largest, jnp.max(scores[:, :split], axis=1, keepdims=True))
            last = jnp.exp(last - largest).astype(BF)
            prob_ref[head, :, place + split : place + key_count] = last
            both = mm(last, values[split:])
            if split:
                early = jnp.exp(scores[:, :split] - largest).astype(BF)
                prob_ref[head, :, place : place + split] = early
                both += mm(early, values[:split])
            mixed.append(both)
        both = jnp.where(jnp.concatenate([head_mask(0)] * 2, axis=1), mixed[0], mixed[1])
        inverse = 1.0 / both[:, 2 * HEAD :]
        norm_ref[first : first + TILE, :] = inverse
        out_ref[first : first + TILE, :] = (both[:, : 2 * HEAD] * inverse).astype(BF)


def pair_cols(offset):
    return pl.BlockSpec((ROWS, 2 * HEAD), lambda i, *s: (0, offset + i))


PROB_SPEC = pl.BlockSpec((2, TILE, PROB_COLS), lambda i, *s: (i, 0, 0))
HEADS_SHAPES = [
    jax.ShapeDtypeStruct((ROWS, PART_COLS), BF),
    jax.ShapeDtypeStruct((ROWS, PART_COLS), F32),
    jax.ShapeDtypeStruct((2 * PART, TILE, PROB_COLS), BF),
]


def heads_a_kernel(info, x_ref, *rest):
    pieces, (normed_hbm, qkv_hbm, gains_ref, att_ref, norm_ref, prob_ref) = rest[:8], rest[8:14]
    store, normed, qkv, sems, out_sems = rest[14:]
    step = pl.program_id(0)

    @pl.when(step == 0)
    def _():
        copies(info, pieces, by_half(store, sems))
        inverse, expanded = norm_parts(x_ref[...].astype(F32))
        expanded = expanded * inverse
        halves_arrived(store, sems)
        gains = store[:, 3 * PART_COLS :].astype(F32).T[:8]
        gains_ref[...] = gains
        normed[...] = (expanded * gains[:1]).astype(BF)
        pltpu.make_async_copy(normed, normed_hbm, out_sems.at[0]).start()
        for i in range(3):
            cols = slice(i * PART_COLS, (i + 1) * PART_COLS)
            qkv[:, cols] = mm(normed[...], store[:, cols]).astype(BF)
        pltpu.make_async_copy(qkv, qkv_hbm, out_sems.at[1]).start()

    attend_pair(info, qkv, step, att_ref, norm_ref, prob_ref)

    @pl.when(step == PART - 1)
    def _():
        arrived(normed, out_sems.at[0])
        arrived(qkv, out_sems.at[1])


def heads_a(info, x, pieces):
    return pl.pallas_call(
        heads_a_kernel,
        grid_spec=pltpu.PrefetchScalarGridSpec(
            num_scalar_prefetch=1,
            grid=(PART,),
            in_specs=[whole(ROWS, WIDTH)] + [HBM] * 8,
            out_specs=[HBM, HBM, whole(8, WIDTH), pair_cols(0), pair_cols(0), PROB_SPEC],
            scratch_shapes=[
                pltpu.VMEM((WIDTH, A_COLS), BF), pltpu.VMEM((ROWS, WIDTH), BF),
                pltpu.VMEM((ROWS, 3 * PART_COLS), BF), PAIR_SEMS, PAIR_SEMS,
            ],
        ),
        out_shape=[
            jax.ShapeDtypeStruct((ROWS, WIDTH), BF),
            jax.ShapeDtypeStruct((ROWS, 3 * PART_COLS), BF),
            jax.ShapeDtypeStruct((8, WIDTH), F32),
        ]
        + HEADS_SHAPES,
        compiler_params=params(),
        cost_estimate=cost(6 * ROWS * WIDTH * PART_COLS + 4 * 6 * 7 * TILE * TILE * 256, 20000000, 2752512),
        name="heads_a",
    )(info, x, *pieces)


def heads_b_kernel(info, normed_ref, gains_ref, a_att_hbm, x_hbm, *rest):
    pieces, (qkv_hbm, bias_ref, middle_hbm, second_hbm, att_ref, norm_ref, prob_ref) = rest[:8], rest[8:15]
    store, qkv, att, x, middle, second, sems, in_sems, out_sems = rest[15:]
    step = pl.program_id(0)
    late = [
        pltpu.make_async_copy(a_att_hbm, att.at[:, pl.ds(0, PART_COLS)], in_sems.at[0]),
        pltpu.make_async_copy(x_hbm, x, in_sems.at[1]),
    ]

    @pl.when(step == 0)
    def _():
        copies(info, pieces, by_half(store, sems))
        for copy in late:
            copy.start()
        halves_arrived(store, sems)
        for i in range(3):
            cols = slice(i * PART_COLS, (i + 1) * PART_COLS)
            qkv[:, cols] = mm(normed_ref[...], store[:, cols]).astype(BF)
        bias_ref[...] = store[:, B_COLS - SMALL :].astype(F32).T[:8]
        pltpu.make_async_copy(qkv, qkv_hbm, out_sems.at[0]).start()

    attend_pair(info, qkv, step, att_ref, norm_ref, prob_ref)
    att[:, pl.ds(pl.multiple_of(PART_COLS + step * 2 * HEAD, 128), 2 * HEAD)] = att_ref[...]

    @pl.when(step == PART - 1)
    def _():
        for copy in late:
            copy.wait()
        weights = store[:, 3 * PART_COLS : 3 * PART_COLS + WIDTH]
        for i in range(ROWS // TILE):
            rows = slice(i * TILE, (i + 1) * TILE)
            mixed = mm(att[rows, :], weights)
            mixed = mixed - jnp.sum(mixed, axis=1, keepdims=True) * (1.0 / WIDTH)
            value = x[rows, :].astype(F32) + jnp.where(lanes() == WIDTH - 1, 0.0, mixed)
            inverse, expanded = norm_parts(value)
            middle[rows, :] = value
            second[rows, :] = (expanded * inverse * gains_ref[1:2, :]).astype(BF)
            for j, (source, target) in enumerate(((middle, middle_hbm), (second, second_hbm))):
                pltpu.make_async_copy(source.at[rows], target.at[rows], out_sems.at[1 + j]).start()
        arrived(qkv, out_sems.at[0])
        arrived(middle, out_sems.at[1])
        arrived(second, out_sems.at[2])


def heads_b(info, normed, gains, a_att, x, pieces):
    return pl.pallas_call(
        heads_b_kernel,
        grid_spec=pltpu.PrefetchScalarGridSpec(
            num_scalar_prefetch=1,
            grid=(PART,),
            in_specs=[whole(ROWS, WIDTH), whole(8, WIDTH)] + [HBM] * 10,
            out_specs=[HBM, whole(8, WIDTH), HBM, HBM, pair_cols(0), pair_cols(0), PROB_SPEC],
            scratch_shapes=[
                pltpu.VMEM((WIDTH, B_COLS), BF), pltpu.VMEM((ROWS, 3 * PART_COLS), BF),
                pltpu.VMEM((ROWS, WIDTH), BF), pltpu.VMEM((ROWS, WIDTH), BF),
                pltpu.VMEM((ROWS, WIDTH), F32), pltpu.VMEM((ROWS, WIDTH), BF),
                PAIR_SEMS, PAIR_SEMS, pltpu.SemaphoreType.DMA((3,)),
            ],
        ),
        out_shape=[
            jax.ShapeDtypeStruct((ROWS, 3 * PART_COLS), BF),
            jax.ShapeDtypeStruct((8, WIDTH), F32),
            jax.ShapeDtypeStruct((ROWS, WIDTH), F32),
            jax.ShapeDtypeStruct((ROWS, WIDTH), BF),
        ]
        + HEADS_SHAPES,
        compiler_params=params(),
        cost_estimate=cost(
            6 * ROWS * WIDTH * PART_COLS + 2 * ROWS * WIDTH * WIDTH + 4 * 6 * 7 * TILE * TILE * 256,
            25000000, 2752512,
        ),
        name="heads_b",
    )(info, normed, gains, a_att, x, *pieces)


GELU_A = 0.7978845608028654
GELU_B = 0.044715


def feed_kernel(info, second_ref, down_in_ref, bias_ref, *rest):
    pieces, outs = rest[:8], rest[10:12]
    act_ref, slope_ref = rest[8:10]
    store, sems, stage, out_sem = rest[12:]
    step = pl.program_id(0)
    core = info[1]

    @pl.when(step == 0)
    def _():
        copies(info, pieces, by_half(store, sems))
        halves_arrived(store, sems, (0,))

    @pl.when(step == 2)
    def _():
        halves_arrived(store, sems, (1,))

    weights = store[:, pl.ds(pl.multiple_of(step * WIDTH, WIDTH), WIDTH)]
    for i in range(ROWS // TILE):
        rows = slice(i * TILE, (i + 1) * TILE)
        hidden = mm(second_ref[rows, :], weights) + bias_ref[...]
        square = hidden * hidden
        bent = jnp.tanh(hidden * (GELU_A + (GELU_A * GELU_B) * square))
        half = 0.5 + 0.5 * bent
        act_ref[rows, :] = (hidden * half).astype(BF)
        tilt = hidden * (0.5 * GELU_A + (1.5 * GELU_A * GELU_B) * square)
        slope_ref[rows, :] = (half + tilt * (1.0 - bent * bent)).astype(BF)
    grads = mm_tn(act_ref[...], down_in_ref[...])
    for i in range(8):
        slot = 8 * step + i
        stage[slot] = grads[96 * i : 96 * (i + 1)].astype(BF)
        mine = core == (i & 1)

        def put(which, slot=slot, chip=4 * step + (i >> 1)):
            pltpu.make_async_copy(stage.at[slot], outs[which].at[place_at(info, chip)], out_sem).start()

        pl.when(mine)(functools.partial(put, 0))
        pl.when(jnp.logical_not(mine))(functools.partial(put, 1))

    @pl.when(step == 3)
    def _():
        arrived(stage, out_sem)


def feed(info, second, down_in, bias, pieces):
    return pl.pallas_call(
        feed_kernel,
        grid_spec=pltpu.PrefetchScalarGridSpec(
            num_scalar_prefetch=1,
            grid=(4,),
            in_specs=[whole(ROWS, WIDTH)] * 2 + [col_tile(1, WIDTH)] + [HBM] * 8,
            out_specs=[col_tile(ROWS, WIDTH)] * 2 + [HBM] * 2,
            scratch_shapes=[
                pltpu.VMEM((WIDTH, HIDDEN), BF), PAIR_SEMS,
                pltpu.VMEM((32, 96, WIDTH), BF), pltpu.SemaphoreType.DMA,
            ],
        ),
        out_shape=[jax.ShapeDtypeStruct((ROWS, HIDDEN), BF)] * 2
        + [jax.ShapeDtypeStruct((CHIPS, 96, WIDTH), BF)] * 2,
        compiler_params=params(),
        cost_estimate=cost(4 * ROWS * WIDTH * HIDDEN, 6 * ROWS * HIDDEN + 4 * WIDTH * HIDDEN),
        name="feed",
    )(info, second, down_in, bias, *pieces)


UP_COLS = HIDDEN + WIDTH + SMALL


def spread_out(info, grads, stage):
    for device in range(32):
        value = grads[24 * device : 24 * (device + 1)].astype(BF)
        stage[info[1] ^ (device & 1), place_at(info, device >> 1)] = value


def back_kernel(info, down_in_ref, second_ref, slope_ref, gain_ref, *rest):
    att_hbm, middle_hbm, up_hbm, down_hbm = rest[:2], rest[2], rest[3], rest[4]
    up_pieces, out_pieces = rest[5:13], rest[13:21]
    outs, total_hbm, grad_att_hbm = rest[21:23], rest[23], rest[24]
    (down_store, down_sems, up_store, up_sems, out_store, att, middle, up, in_sems,
     grads, weighted, stage, out_stage, spare, total, grad_att, out_sem) = rest[25:]
    step = pl.program_id(0)
    core = info[1]
    late = [
        (att_hbm[0], att.at[:, pl.ds(0, PART_COLS)]),
        (att_hbm[1], att.at[:, pl.ds(PART_COLS, PART_COLS)]),
        (middle_hbm, middle),
        (up_hbm, up),
    ]

    @pl.when(step == 0)
    def _():
        for i in range(4):
            pltpu.make_async_copy(
                down_hbm.at[pl.ds(i * WIDTH, WIDTH)], down_store.at[i], down_sems.at[i]
            ).start()
        copies(info, up_pieces, by_half(up_store, up_sems))
        copies(info, out_pieces, one_half(out_store, in_sems.at[4]), OUT_COLS)
        for i, (source, target) in enumerate(late):
            pltpu.make_async_copy(source, target, in_sems.at[i]).start()

    arrived(down_store.at[step], down_sems.at[step])
    sums = jnp.zeros((1, WIDTH), F32)
    for i in range(ROWS // TILE):
        rows = slice(i * TILE, (i + 1) * TILE)
        value = slope_ref[rows, :].astype(F32) * mm_nt(down_in_ref[rows, :], down_store[step])
        value = value.astype(BF)
        grads[rows, :] = value
        sums += jnp.sum(value.astype(F32), axis=0, keepdims=True)
    for i in range(8):
        few = jnp.concatenate([sums[:, 96 * i : 96 * (i + 1)], jnp.zeros((1, 32), F32)], axis=1)
        few = jnp.broadcast_to(few, (24, SMALL)).astype(BF)
        spare[core ^ (i & 1), place_at(info, 4 * step + (i >> 1))] = few

    @pl.when((step & 1) == 0)
    def _():
        width = HIDDEN // 2
        cols = pl.ds(pl.multiple_of((step >> 1) * width, width), width)
        arrived(up_store.at[:, cols], up_sems.at[step >> 1])

    weights = up_store[:, pl.ds(pl.multiple_of(step * WIDTH, WIDTH), WIDTH)]

    @pl.when(step == 0)
    def _():
        weighted[...] = mm_nt(grads[...], weights)

    @pl.when(step > 0)
    def _():
        for i in range(ROWS // TILE):
            rows = slice(i * TILE, (i + 1) * TILE)
            weighted[rows, :] += mm_nt(grads[rows, :], weights)

    spread_out(info, mm_tn(second_ref[...], grads[...]), stage.at[step])
    cols = pl.ds(pl.multiple_of(step * WIDTH, 128), WIDTH)
    for which in range(2):
        pltpu.make_async_copy(
            stage.at[step, which], outs[which].at[:, :, cols], out_sem.at[0]
        ).start()

    @pl.when(step == 3)
    def _():
        for which in range(2):
            pltpu.make_async_copy(
                spare.at[which], outs[which].at[:, :, pl.ds(HIDDEN + WIDTH, SMALL)], out_sem.at[1]
            ).start()
        for i, (source, target) in enumerate(late):
            pltpu.make_async_copy(source, target, in_sems.at[i]).wait()
        arrived(out_store, in_sems.at[4])
        for i in range(ROWS // TILE):
            rows = slice(i * TILE, (i + 1) * TILE)
            inner, expanded = norm_parts(middle[rows, :])
            value = up[rows, :].astype(F32) + norm_back(
                weighted[rows, :] * gain_ref[1:2, :], inner, expanded
            )
            total[rows, :] = value
            mixed = (value - jnp.sum(value, axis=1, keepdims=True) * (1.0 / WIDTH)).astype(BF)
            grads[rows, :] = mixed
            grad_att[rows, :] = mm_nt(mixed, out_store[...]).astype(BF)
        pltpu.make_async_copy(total, total_hbm, out_sem.at[2]).start()
        pltpu.make_async_copy(grad_att, grad_att_hbm, out_sem.at[3]).start()
        spread_out(info, mm_tn(att[...], grads[...]), out_stage)
        for which in range(2):
            pltpu.make_async_copy(
                out_stage.at[which], outs[which].at[:, :, pl.ds(HIDDEN, WIDTH)], out_sem.at[4]
            ).start()
        arrived(stage, out_sem.at[0])
        arrived(spare, out_sem.at[1])
        arrived(total, out_sem.at[2])
        arrived(grad_att, out_sem.at[3])
        arrived(out_stage, out_sem.at[4])


def back(info, down_in, second, slope, gain, attended, middle, upstream, w_down, up_pieces, out_pieces):
    return pl.pallas_call(
        back_kernel,
        grid_spec=pltpu.PrefetchScalarGridSpec(
            num_scalar_prefetch=1,
            grid=(4,),
            in_specs=[whole(ROWS, WIDTH)] * 2 + [col_tile(ROWS, WIDTH), whole(8, WIDTH)] + [HBM] * 21,
            out_specs=[HBM] * 4,
            scratch_shapes=[
                pltpu.VMEM((4, WIDTH, WIDTH), BF), SLOT_SEMS,
                pltpu.VMEM((WIDTH, HIDDEN), BF), PAIR_SEMS,
                pltpu.VMEM((WIDTH, WIDTH), BF),
                pltpu.VMEM((ROWS, WIDTH), BF),
                pltpu.VMEM((ROWS, WIDTH), F32),
                pltpu.VMEM((ROWS, WIDTH), BF),
                pltpu.SemaphoreType.DMA((5,)),
                pltpu.VMEM((ROWS, WIDTH), BF),
                pltpu.VMEM((ROWS, WIDTH), F32),
                pltpu.VMEM((4, 2, CHIPS, 24, WIDTH), BF),
                pltpu.VMEM((2, CHIPS, 24, WIDTH), BF),
                pltpu.VMEM((2, CHIPS, 24, SMALL), BF),
                pltpu.VMEM((ROWS, WIDTH), F32),
                pltpu.VMEM((ROWS, WIDTH), BF),
                pltpu.SemaphoreType.DMA((5,)),
            ],
        ),
        out_shape=[jax.ShapeDtypeStruct((CHIPS, 24, UP_COLS), BF)] * 2
        + [jax.ShapeDtypeStruct((ROWS, WIDTH), F32), jax.ShapeDtypeStruct((ROWS, WIDTH), BF)],
        compiler_params=params(),
        cost_estimate=cost(6 * ROWS * WIDTH * HIDDEN + 4 * ROWS * WIDTH * WIDTH, 40000000),
        name="back",
    )(info, down_in, second, slope, gain, *attended, middle, upstream, w_down, *up_pieces, *out_pieces)


def pair_grad(q_ref, k_ref, v_ref, grad_ref, att_ref, norm_ref, prob_ref, dq_ref, dk_ref, dv_ref, key_sum, value_sum):
    factor = HEAD**-0.5
    key_sum[...] = jnp.zeros_like(key_sum)
    value_sum[...] = jnp.zeros_like(value_sum)
    for first, key_first, key_count, place in SPANS:
        rows = slice(first, first + TILE)
        keys_at = slice(key_first, key_first + key_count)
        queries = q_ref[rows, :]
        grads = (grad_ref[rows, :].astype(F32) * norm_ref[rows, :]).astype(BF)
        product = grads.astype(F32) * att_ref[rows, :].astype(F32)
        keys = k_ref[keys_at, :]
        values = v_ref[keys_at, :]
        parts = []
        for head in range(2):
            mask = head_mask(head)
            my_grads = jnp.where(mask, grads, 0)
            my_queries = jnp.where(mask, queries, 0)
            probs = prob_ref[head, :, place : place + key_count]
            inner = jnp.sum(jnp.where(mask, product, 0.0), axis=1, keepdims=True)
            slopes = probs.astype(F32) * (mm_nt(my_grads, values) - inner)
            slopes = slopes.astype(BF)
            parts.append(mm(slopes, keys))
            value_sum[:, keys_at] += mm_tn(my_grads, probs)
            key_sum[:, keys_at] += mm_tn(my_queries, slopes)
        dq_ref[rows, :] = (jnp.where(head_mask(0), parts[0], parts[1]) * factor).astype(BF)
    dk_ref[...] = (key_sum[...].T * factor).astype(BF)
    dv_ref[...] = value_sum[...].T.astype(BF)


def heads_grad_kernel(info, normed_ref, a_q, a_k, a_v, *rest):
    ins, outs = rest[:7], rest[7:10]
    keep_hbm, send_hbm, key_sum, value_sum, kept, turned, stage, out_sem = rest[10:]
    step = pl.program_id(0)

    @pl.when(step == 0)
    def _():
        turned[...] = normed_ref[...].T

    pair_grad(*ins, *outs, key_sum, value_sum)
    place = pl.ds(pl.multiple_of(step * 2 * HEAD, 2 * HEAD), 2 * HEAD)
    for i in range(3):
        kept[i, :, place] = outs[i][...]

    @pl.when(step == PART - 1)
    def _():
        for i, ref in enumerate((a_q, a_k, a_v, kept.at[0], kept.at[1], kept.at[2])):
            spread_out(info, mm(turned[...], ref[...]), stage.at[i])
            for which, target in enumerate((keep_hbm, send_hbm)):
                pltpu.make_async_copy(
                    stage.at[i, which], target.at[:, :, pl.ds(i * PART_COLS, PART_COLS)], out_sem
                ).start()
        arrived(stage, out_sem)


def attend_grad(first, qkv, grad_attended, attended, norms, probs, info=None, normed=None, parts=()):
    main = [
        pair_cols(0), pair_cols(PART), pair_cols(2 * PART),
        pair_cols(first), pair_cols(0), pair_cols(0), PROB_SPEC,
    ]
    args = [qkv, qkv, qkv, grad_attended, attended, norms, probs]
    shapes = [jax.ShapeDtypeStruct((ROWS, PART_COLS), BF)] * 3
    scratch = [pltpu.VMEM((2 * HEAD, ROWS), F32)] * 2
    if info is None:
        return pl.pallas_call(
            pair_grad,
            grid=(PART,),
            in_specs=main,
            out_specs=[pair_cols(0)] * 3,
            scratch_shapes=scratch,
            out_shape=shapes,
            compiler_params=params(),
            cost_estimate=cost(8 * 6 * 7 * TILE * TILE * 256, 8 * ROWS * WIDTH + 5505024),
            name="attend_grad",
        )(*args)
    return pl.pallas_call(
        heads_grad_kernel,
        grid_spec=pltpu.PrefetchScalarGridSpec(
            num_scalar_prefetch=1,
            grid=(PART,),
            in_specs=[whole(ROWS, WIDTH)] + [whole(ROWS, PART_COLS)] * 3 + main,
            out_specs=[pair_cols(0)] * 3 + [HBM] * 2,
            scratch_shapes=scratch
            + [
                pltpu.VMEM((3, ROWS, PART_COLS), BF),
                pltpu.VMEM((WIDTH, ROWS), BF),
                pltpu.VMEM((6, 2, CHIPS, 24, PART_COLS), BF),
                pltpu.SemaphoreType.DMA,
            ],
        ),
        out_shape=shapes + [jax.ShapeDtypeStruct((CHIPS, 24, 6 * PART_COLS), BF)] * 2,
        compiler_params=params(),
        cost_estimate=cost(
            8 * 6 * 7 * TILE * TILE * 256 + 6 * ROWS * WIDTH * WIDTH, 8 * ROWS * WIDTH + 10000000
        ),
        name="heads_grad",
    )(info, normed, *parts, *args)


def give_back(info, turned, out_ref):
    for i in range(ROWS // TILE):
        turn_back = mm(turn(first_row(info), i * TILE, TILE, False), turned[...])
        out_ref[i * TILE : (i + 1) * TILE, :] = turn_back.astype(BF)[:, : WIDTH - 1]


def token_grad_kernel(info, *rest):
    parts, (x_ref, total_ref, gain_ref) = rest[:6], rest[6:9]
    a_pieces, b_pieces = rest[9:17], rest[17:25]
    out_ref, a_store, b_store, turned, a_sems, b_sems = rest[25:]
    step = pl.program_id(0)

    @pl.when(step == 0)
    def _():
        copies(info, a_pieces, by_half(a_store, a_sems))
        copies(info, b_pieces, by_half(b_store, b_sems))
        halves_arrived(a_store, a_sems)
        halves_arrived(b_store, b_sems)

    weighted = jnp.zeros((TILE, WIDTH), F32)
    for part, store in enumerate((a_store, b_store)):
        for i in range(3):
            cols = slice(i * PART_COLS, (i + 1) * PART_COLS)
            weighted += mm_nt(parts[3 * part + i][...], store[:, cols])
    inverse, expanded = norm_parts(x_ref[...].astype(F32))
    grads = total_ref[...] + norm_back(weighted * gain_ref[0:1, :], inverse, expanded)
    turned[pl.ds(pl.multiple_of(step * TILE, TILE), TILE), :] = grads.astype(BF)

    @pl.when(step == ROWS // TILE - 1)
    def _():
        give_back(info, turned, out_ref)


def token_grad(info, parts, x, total, gain, a_pieces, b_pieces):
    return pl.pallas_call(
        token_grad_kernel,
        grid_spec=pltpu.PrefetchScalarGridSpec(
            num_scalar_prefetch=1,
            grid=(ROWS // TILE,),
            in_specs=[row_tile(PART_COLS)] * 6 + [row_tile(WIDTH)] * 2 + [whole(8, WIDTH)] + [HBM] * 16,
            out_specs=whole(ROWS, WIDTH - 1),
            scratch_shapes=[
                pltpu.VMEM((WIDTH, A_COLS), BF), pltpu.VMEM((WIDTH, B_COLS), BF),
                pltpu.VMEM((ROWS, WIDTH), BF), PAIR_SEMS, PAIR_SEMS,
            ],
        ),
        out_shape=jax.ShapeDtypeStruct((ROWS, WIDTH - 1), BF),
        compiler_params=params(),
        cost_estimate=cost(8 * ROWS * WIDTH * WIDTH, 20 * ROWS * WIDTH),
        name="token_grad",
    )(info, *parts, x, total, gain, *a_pieces, *b_pieces)


def result_kernel(info, act_ref, middle_ref, down_hbm, out_ref, store, turned, sems):
    step = pl.program_id(0)

    @pl.when(step == 0)
    def _():
        for i in range(4):
            pltpu.make_async_copy(down_hbm.at[pl.ds(i * WIDTH, WIDTH)], store.at[i], sems.at[i]).start()

    branch = jnp.zeros((TILE, WIDTH), F32)
    for i in range(4):

        @pl.when(step == 0)
        def _(i=i):
            arrived(store.at[i], sems.at[i])

        branch += mm(act_ref[:, i * WIDTH : (i + 1) * WIDTH], store[i])
    branch = branch - jnp.sum(branch, axis=1, keepdims=True) * (1.0 / WIDTH)
    turned[pl.ds(pl.multiple_of(step * TILE, TILE), TILE), :] = (middle_ref[...] + branch).astype(BF)

    @pl.when(step == ROWS // TILE - 1)
    def _():
        give_back(info, turned, out_ref)


def result(info, active, middle, w_down):
    return pl.pallas_call(
        result_kernel,
        grid_spec=pltpu.PrefetchScalarGridSpec(
            num_scalar_prefetch=1,
            grid=(ROWS // TILE,),
            in_specs=[row_tile(HIDDEN), row_tile(WIDTH), HBM],
            out_specs=whole(ROWS, WIDTH - 1),
            scratch_shapes=[
                pltpu.VMEM((4, WIDTH, WIDTH), BF), pltpu.VMEM((ROWS, WIDTH), BF), SLOT_SEMS
            ],
        ),
        out_shape=jax.ShapeDtypeStruct((ROWS, WIDTH - 1), BF),
        compiler_params=params(),
        cost_estimate=cost(2 * ROWS * WIDTH * HIDDEN, 2 * ROWS * HIDDEN + 4718592 + 10 * ROWS * WIDTH),
        name="result",
    )(info, active, middle, w_down)


WAYS = {"core": (0, 1), "x": (0, 2), "y": (1, 0), "xy": (1, 2), "z1": (2, 0), "z2": (4, 0), "z3": (6, 0)}


class Cube:
    def __init__(self, sizes):
        self.sizes = sizes
        wide, narrow = lax.axis_index("wide"), lax.axis_index("narrow")
        self.place = jnp.stack([wide * 2 + (narrow >> 1), narrow & 1]).astype(jnp.int32)

    def hop(self, value, way):
        wide, narrow = WAYS[way]
        if wide == 0:
            return lax.ppermute(value, "narrow", [(i, i ^ narrow) for i in range(self.sizes["narrow"])])
        if narrow == 0:
            return lax.ppermute(value, "wide", [(i, i ^ wide) for i in range(self.sizes["wide"])])
        bits = wide * self.sizes["narrow"] + narrow
        count = self.sizes["wide"] * self.sizes["narrow"]
        return lax.ppermute(value, AXES, [(i, i ^ bits) for i in range(count)])

    def gather(self, block):
        others = yield [self.hop(block, way) for way in ("z1", "z2", "z3")]
        near = jnp.concatenate([block] + others)
        *far, twin = yield [self.hop(near, way) for way in ("x", "y", "xy", "core")]
        twins = yield [self.hop(part, "core") for part in far]
        return [near] + far + [twin] + twins

    def blocks(self, info, shards):
        others = [self.hop(shard, "core") for shard in shards]
        return join(info, shards, others)

    def reduce(self, keep, send):
        got = yield self.hop(send, "core")
        both = [keep[4 * i : 4 * i + 4].astype(F32) + got[4 * i : 4 * i + 4].astype(F32) for i in range(4)]
        others = yield [self.hop(both[i].astype(BF), way) for i, way in ((1, "x"), (2, "y"), (3, "xy"))]
        both = sum([other.astype(F32) for other in others], both[0])
        others = yield [self.hop(both[i].astype(BF), way) for i, way in ((1, "z1"), (2, "z2"), (3, "z3"))]
        return sum([other.astype(F32) for other in others], both[0])


class Plain:
    def __init__(self):
        self.place = jnp.zeros((2,), jnp.int32)

    def blocks(self, info, shards):
        return shards

    def gather(self, shard):
        yield ()
        full = lax.all_gather(shard, AXES, axis=0, tiled=True)
        cols = full.shape[1]
        full = full.reshape(4, 4, BLOCK, cols).transpose(1, 0, 2, 3).reshape(4, 4 * BLOCK, cols)
        return [full[i, :, half * cols // 2 : (half + 1) * cols // 2] for half in range(2) for i in range(4)]

    def reduce(self, keep, send):
        yield ()
        full = jnp.stack([keep, send], axis=1).reshape(4, 4, -1, keep.shape[2])
        full = full.transpose(1, 0, 2, 3).reshape(-1, keep.shape[2])
        return lax.psum_scatter(full, AXES, scatter_dimension=0, tiled=True).astype(F32)


class Task:
    def __init__(self, steps):
        self.steps, self.flight, self.over, self.result = steps, (), False, None
        self.go(None)

    def go(self, arrived_now):
        try:
            self.flight = self.steps.send(arrived_now)
        except StopIteration as end:
            self.flight, self.over, self.result = (), True, end.value


def meet(values, *tasks):
    tasks = [task for task in tasks if not task.over]
    values, flights = lax.optimization_barrier((values, [task.flight for task in tasks]))
    for task, flight in zip(tasks, flights):
        task.go(flight)
    return values


def finish(values, *tasks):
    while not all(task.over for task in tasks):
        values = meet(values, *tasks)
    return values


def layer(sizes, tokens, lengths, gain_one, w_qkv, w_out, gain_two, w_up, b_up, w_down, cotangent):
    share, few = b_up.shape[0], gain_one.shape[0]
    links = Cube(sizes) if sizes["wide"] == 8 and sizes["narrow"] == 4 else Plain()
    info = jnp.concatenate([links.place, lengths[0]])

    a_block, b_block, up_block = links.blocks(
        info, [*pack(w_qkv, w_out, gain_one, gain_two, b_up), w_up]
    )
    group_a = Task(links.gather(a_block))
    tokens, cotangent, b_block = lax.optimization_barrier((tokens, cotangent, b_block))
    x, upstream, down_in = before(info, tokens, cotangent)
    x, b_block = meet((x, b_block), group_a)
    group_b = Task(links.gather(b_block))
    x, w_down, up_block = meet((x, w_down, up_block), group_a, group_b)
    full_down = lax.all_gather(w_down, AXES, axis=0, tiled=True)
    up = Task(links.gather(up_block))
    x = finish(x, group_a)
    normed, qkv_a, gains, att_a, norms_a, probs_a = heads_a(info, x, group_a.result)
    normed, att_a, x = meet((normed, att_a, x), group_b, up)
    normed, att_a, x = finish((normed, att_a, x), group_b)
    qkv_b, bias, middle, second, att_b, norms_b, probs_b = heads_b(
        info, normed, gains, att_a, x, group_b.result
    )
    bias = bias[: HIDDEN // WIDTH].reshape(HIDDEN // WIDTH, -1, few)
    bias = bias.transpose(1, 0, 2).reshape(1, HIDDEN)
    second = finish(second, up)
    active, slope, *grad_down = feed(info, second, down_in, bias, up.result)
    downs = Task(links.reduce(*grad_down))
    slope = meet(slope, downs)
    *grad_up, total, grad_att = back(
        info, down_in, second, slope, gains, (att_a, att_b), middle, upstream,
        full_down, up.result, group_b.result,
    )
    grad_att, grad_up = meet((grad_att, grad_up), downs)
    ups = Task(links.reduce(*grad_up))
    parts = attend_grad(0, qkv_a, grad_att, att_a, norms_a, probs_a)
    parts, grad_att = meet((parts, grad_att), downs, ups)
    *more, keep, send = attend_grad(
        PART, qkv_b, grad_att, att_b, norms_b, probs_b, info, normed, parts
    )
    heads = Task(links.reduce(keep, send))
    active, more = lax.optimization_barrier((active, more))
    output = result(info, active, middle, full_down)
    output, more = meet((output, more), heads, ups)
    grad_tokens = token_grad(
        info, list(parts) + list(more), x, total, gains, group_a.result, group_b.result
    )
    grad_tokens = finish(grad_tokens, heads, ups, downs)

    grad_up = ups.result[:, :HIDDEN]
    grad_out = ups.result[:, HIDDEN : HIDDEN + WIDTH]
    sums = ups.result[:, HIDDEN + WIDTH : HIDDEN + WIDTH + 96]
    if few >= 24:
        sums = sums[::24].reshape(-1)
    else:
        index = lax.axis_index("wide") * sizes["narrow"] + lax.axis_index("narrow")
        sums = lax.dynamic_slice_in_dim(sums[0], index % (24 // few) * share, share)
    grad_qkv = jnp.concatenate(
        [heads.result[:, (3 * part + i) * PART_COLS : (3 * part + i + 1) * PART_COLS]
         for i in range(3) for part in range(2)],
        axis=1,
    )
    return (
        output,
        grad_tokens,
        jnp.sum(w_qkv.astype(F32) * grad_qkv, axis=1) / gain_one.astype(F32),
        grad_qkv,
        grad_out,
        jnp.sum(w_up.astype(F32) * grad_up, axis=1) / gain_two.astype(F32),
        grad_up,
        sums,
        downs.result,
    )


def solution(mesh):
    rows, vector = P(AXES, None), P(AXES)
    sizes = dict(mesh.shape)
    return jax.shard_map(
        functools.partial(layer, sizes),
        mesh=mesh,
        in_specs=(rows, rows, vector, rows, rows, vector, rows, vector, rows, rows),
        out_specs=(rows, rows, vector, rows, rows, vector, rows, vector, rows),
        check_vma=False,
    )
```

```python
import functools

import jax
import jax.numpy as jnp
from jax import lax
from jax.experimental import pallas as pl
from jax.experimental.pallas import tpu as pltpu
from jax.sharding import PartitionSpec as P

AXES = ("wide", "narrow")
EPSILON = 1e-05
BF = jnp.bfloat16
F32 = jnp.float32
WIDTH = 768
HIDDEN = 3072
ROWS = 1024
TILE = 256
BIG = 768
PAIRS = 6
HEAD = 64
PROB_COLS = 1792
CHIPS = 16
BLOCK = 48
LIMIT = 56 * 1024 * 1024


def mm(left, right):
    return lax.dot_general(left, right, (((1,), (0,)), ((), ())), preferred_element_type=F32)


def mm_nt(left, right):
    return lax.dot_general(left, right, (((1,), (1,)), ((), ())), preferred_element_type=F32)


def mm_tn(left, right):
    return lax.dot_general(left, right, (((0,), (0,)), ((), ())), preferred_element_type=F32)


def lanes(width=WIDTH):
    return lax.broadcasted_iota(jnp.int32, (1, width), 1)


def norm_parts(rows):
    total = jnp.sum(rows, axis=1, keepdims=True)
    squares = jnp.sum(rows * rows, axis=1, keepdims=True)
    inverse = lax.rsqrt((squares + total * total) * (1.0 / WIDTH) + EPSILON)
    expanded = jnp.where(lanes() == WIDTH - 1, -total, rows)
    return inverse, expanded


def norm_back(weighted, inverse, expanded):
    inner = jnp.sum(weighted * expanded, axis=1, keepdims=True) * (1.0 / WIDTH)
    full = inverse * (weighted - (inverse * inverse * inner) * expanded)
    last = full[:, WIDTH - 1 :]
    return jnp.where(lanes() == WIDTH - 1, 0.0, full - last)


def turn(start, first_row, count, forward):
    rows = lax.broadcasted_iota(jnp.int32, (count, ROWS), 0) + first_row
    cols = lax.broadcasted_iota(jnp.int32, (count, ROWS), 1)
    if forward:
        source = rows + start
        source = jnp.where(source >= ROWS, source - ROWS, source)
    else:
        source = rows - start
        source = jnp.where(source < 0, source + ROWS, source)
    return jnp.where(cols == source, 1.0, 0.0).astype(BF)


def first_row(info):
    return jnp.where(info[2] == BIG, 0, jnp.where(info[3] == BIG, info[2], info[2] + info[3]))


def params(**more):
    return pltpu.CompilerParams(vmem_limit_bytes=LIMIT, **more)


def cost(flops, nbytes, transcendentals=0):
    return pl.CostEstimate(flops=flops, bytes_accessed=nbytes, transcendentals=transcendentals)


HBM = pl.BlockSpec(memory_space=pl.ANY)


def whole(*shape):
    return pl.BlockSpec(shape, lambda *i: (0,) * len(shape))


def row_tile(width, tile=TILE):
    return pl.BlockSpec((tile, width), lambda i, *s: (i, 0))


def col_tile(rows, width):
    return pl.BlockSpec((rows, width), lambda i, *s: (0, i))


def offset_of(place):
    return 4 * (place & 3) + (place >> 2)


def place_at(info, chip, half=0):
    offset = info[0] ^ chip
    x, y = offset & 1, (offset >> 1) & 1
    return (offset >> 2) + 4 * (x + 2 * y if half == 0 else y + 2 * x)


def copies(info, pieces, target, cols=None):
    for side in range(2):
        half = info[1] ^ side

        def start(side=side, half=half):
            for place in range(CHIPS):
                source = pieces[4 * side + place // 4].at[pl.ds((place % 4) * BLOCK, BLOCK)]
                if cols is not None:
                    source = source.at[:, pl.ds(*cols)]
                block = pl.multiple_of((info[0] ^ offset_of(place)) * BLOCK, 16)
                pltpu.make_async_copy(source, *target(half, block)).start()

        if cols is None:
            start()
        else:
            pl.when(half == 1)(start)


def quarter_copies(info, pieces, store, sems):
    for half in range(2):
        for side in range(2):
            quarter = 2 * (info[1] ^ side) + half
            cols = pl.ds(pl.multiple_of(quarter * WIDTH, 128), WIDTH)
            for part, first in enumerate(((0, 4, 8), (0, 8, None))[half]):
                source = pieces[6 * side + 3 * half + part]
                if half == 1 and part == 2:
                    places = [4, 5, 6, 7, 12, 13, 14, 15]
                else:
                    places = range(first, first + source.shape[0] // BLOCK)
                for i, place in enumerate(places):
                    block = pl.multiple_of((info[0] ^ offset_of(place)) * BLOCK, 16)
                    pltpu.make_async_copy(
                        source.at[pl.ds(i * BLOCK, BLOCK)], store.at[pl.ds(block, BLOCK), cols], sems.at[quarter]
                    ).start()


def by_half(store, sems):
    width = store.shape[1] // 2

    def target(half, first):
        cols = pl.ds(pl.multiple_of(half * width, 128), width)
        return store.at[pl.ds(first, BLOCK), cols], sems.at[half]

    return target


def one_half(store, semaphore):
    return lambda half, first: (store.at[pl.ds(first, BLOCK)], semaphore)


def arrived(ref, semaphore):
    pltpu.make_async_copy(ref, ref, semaphore).wait()


def halves_arrived(store, sems, halves=(0, 1)):
    width = store.shape[1] // 2
    for half in halves:
        arrived(store.at[:, pl.ds(half * width, width)], sems.at[half])


OUT_COLS = (128, WIDTH)
TURNED = pltpu.VMEM((2 * HEAD, ROWS), BF)
PAIR_SEMS = pltpu.SemaphoreType.DMA((2,))
SLOT_SEMS = pltpu.SemaphoreType.DMA((4,))
PART = 3
PART_COLS = PART * 2 * HEAD
SMALL = 128
A_COLS = 3 * PART_COLS + SMALL
B_COLS = 3 * PART_COLS + WIDTH + SMALL


def pack_kernel(qkv_ref, out_ref, one_ref, two_ref, bias_ref, a_ref, b_ref):
    few, share = one_ref.shape[1], bias_ref.shape[1]
    for part, ref in enumerate((a_ref, b_ref)):
        for i in range(3):
            first = i * WIDTH + part * PART_COLS
            ref[:, i * PART_COLS : (i + 1) * PART_COLS] = qkv_ref[:, first : first + PART_COLS]
    b_ref[:, 3 * PART_COLS : 3 * PART_COLS + WIDTH] = out_ref[...]
    place = lax.broadcasted_iota(jnp.int32, (few, SMALL), 1)

    def column(row, first):
        count = row.shape[1]
        at = lax.broadcasted_iota(jnp.int32, (few, count), 1)
        down = lax.broadcasted_iota(jnp.int32, (few, count), 0) + first
        return jnp.sum(jnp.where(at == down, row.astype(F32), 0.0), axis=1, keepdims=True)

    gains = jnp.where(place == 0, column(one_ref[...], 0), 0.0)
    gains = jnp.where(place == 1, column(two_ref[...], 0), gains)
    a_ref[:, A_COLS - SMALL :] = gains.astype(BF)
    bias = jnp.zeros((few, SMALL), F32)
    for i in range(share // few):
        bias = jnp.where(place == i, column(bias_ref[...], i * few), bias)
    b_ref[:, B_COLS - SMALL :] = bias.astype(BF)


def pack(w_qkv, w_out, gain_one, gain_two, b_up):
    few = w_qkv.shape[0]
    return pl.pallas_call(
        pack_kernel,
        out_shape=[
            jax.ShapeDtypeStruct((few, A_COLS), BF), jax.ShapeDtypeStruct((few, B_COLS), BF)
        ],
        compiler_params=params(),
        name="pack",
    )(w_qkv, w_out, gain_one[None], gain_two[None], b_up[None])


def join_kernel(info, *refs):
    own, other, outs = refs[:3], refs[3:6], refs[6:]
    first = info[1] == 0
    for mine, theirs, out in zip(own, other, outs):
        half = mine.shape[1] // 2
        cols = pl.ds(pl.multiple_of(info[1] * half, 128), half)
        mine, theirs = mine[:, cols].astype(F32), theirs[:, cols].astype(F32)
        out[...] = jnp.concatenate(
            [jnp.where(first, mine, theirs), jnp.where(first, theirs, mine)], axis=0
        ).astype(BF)


def join(info, own, other):
    shapes = [(2 * v.shape[0], v.shape[1] // 2) for v in own]
    return pl.pallas_call(
        join_kernel,
        grid_spec=pltpu.PrefetchScalarGridSpec(
            num_scalar_prefetch=1,
            grid=(1,),
            in_specs=[whole(*v.shape) for v in [*own, *other]],
            out_specs=[whole(*shape) for shape in shapes],
        ),
        out_shape=[jax.ShapeDtypeStruct(shape, BF) for shape in shapes],
        compiler_params=params(),
        name="join",
    )(info, *own, *other)


def before_kernel(info, tok_ref, cot_ref, x_ref, up_ref, down_ref, wide):
    pick = turn(first_row(info), pl.program_id(0) * TILE, TILE, True)
    wide[:, WIDTH - 128 :] = jnp.zeros((TILE, 128), F32)
    wide[:, : WIDTH - 1] = mm(pick, tok_ref[...])
    x_ref[...] = wide[...].astype(BF)
    wide[:, : WIDTH - 1] = mm(pick, cot_ref[...])
    grads = wide[...]
    up_ref[...] = grads.astype(BF)
    down_ref[...] = (grads - jnp.sum(grads, axis=1, keepdims=True) * (1.0 / WIDTH)).astype(BF)


def before(info, tokens, cotangent):
    shape = jax.ShapeDtypeStruct((ROWS, WIDTH), BF)
    return pl.pallas_call(
        before_kernel,
        grid_spec=pltpu.PrefetchScalarGridSpec(
            num_scalar_prefetch=1,
            grid=(ROWS // TILE,),
            in_specs=[whole(ROWS, WIDTH - 1)] * 2,
            out_specs=[row_tile(WIDTH)] * 3,
            scratch_shapes=[pltpu.VMEM((TILE, WIDTH), F32)],
        ),
        out_shape=[shape] * 3,
        compiler_params=params(),
        cost_estimate=cost(4 * ROWS * ROWS * WIDTH, 10 * ROWS * WIDTH),
        name="before",
    )(info, tokens, cotangent)


SPANS = ((0, 0, 256, 0), (256, 0, 512, 256), (512, 0, 768, 768), (768, 768, 256, 1536))


def tail_segments(info, axis):
    shape = (TILE, 1) if axis == 0 else (1, TILE)
    place = lax.broadcasted_iota(jnp.int32, shape, axis) + BIG + first_row(info)
    place = jnp.where(place >= ROWS, place - ROWS, place)
    found = jnp.zeros(shape, jnp.int32)
    bound = 0
    for j in range(3):
        bound = bound + info[2 + j]
        found = found + jnp.where(place >= bound, 1, 0)
    return found


def head_mask(head):
    place = lanes(2 * HEAD)
    return (place < HEAD) if head == 0 else (place >= HEAD)


def attend_pair(info, qkv, pair, out_ref, norm_ref, prob_ref, turned):
    cols = [pl.ds(pl.multiple_of(i * PART_COLS + pair * 2 * HEAD, 128), 2 * HEAD) for i in range(3)]
    causal = lax.broadcasted_iota(jnp.int32, (TILE, TILE), 0) >= lax.broadcasted_iota(
        jnp.int32, (TILE, TILE), 1
    )
    turned[...] = qkv[:, cols[1]].T
    for first, key_first, key_count, place in SPANS:
        queries = qkv[first : first + TILE, cols[0]]
        keys = turned[:, key_first : key_first + key_count]
        values = qkv[key_first : key_first + key_count, cols[2]]
        values = jnp.concatenate([values, jnp.ones_like(values)], axis=1)
        allowed = causal
        if first == BIG:
            allowed = causal & (tail_segments(info, 0) == tail_segments(info, 1))
        mixed = []
        for head in range(2):
            mine = jnp.where(head_mask(head), queries, 0) * BF(HEAD**-0.5)
            scores = mm(mine, keys)
            split = key_count - TILE
            last = jnp.where(allowed, scores[:, split:], -1e30)
            largest = jnp.max(last, axis=1, keepdims=True)
            if split:
                largest = jnp.maximum(largest, jnp.max(scores[:, :split], axis=1, keepdims=True))
            last = jnp.exp(last - largest).astype(BF)
            prob_ref[head, :, place + split : place + key_count] = last
            both = mm(last, values[split:])
            if split:
                early = jnp.exp(scores[:, :split] - largest).astype(BF)
                prob_ref[head, :, place : place + split] = early
                both += mm(early, values[:split])
            mixed.append(both)
        both = jnp.where(jnp.concatenate([head_mask(0)] * 2, axis=1), mixed[0], mixed[1])
        inverse = 1.0 / both[:, 2 * HEAD :]
        norm_ref[first : first + TILE, :] = inverse
        out_ref[first : first + TILE, :] = (both[:, : 2 * HEAD] * inverse).astype(BF)


def pair_cols(offset):
    return pl.BlockSpec((ROWS, 2 * HEAD), lambda i, *s: (0, offset + i))


PROB_SPEC = pl.BlockSpec((2, TILE, PROB_COLS), lambda i, *s: (i, 0, 0))
HEADS_SHAPES = [
    jax.ShapeDtypeStruct((ROWS, PART_COLS), BF),
    jax.ShapeDtypeStruct((ROWS, PART_COLS), F32),
    jax.ShapeDtypeStruct((2 * PART, TILE, PROB_COLS), BF),
]


def heads_a_kernel(info, x_ref, *rest):
    pieces, (normed_hbm, qkv_hbm, gains_ref, att_ref, norm_ref, prob_ref) = rest[:8], rest[8:14]
    store, normed, qkv, turned, sems, out_sems = rest[14:]
    step = pl.program_id(0)

    @pl.when(step == 0)
    def _():
        copies(info, pieces, by_half(store, sems))
        inverse, expanded = norm_parts(x_ref[...].astype(F32))
        expanded = expanded * inverse
        halves_arrived(store, sems)
        gains = store[:, 3 * PART_COLS :].astype(F32).T[:8]
        gains_ref[...] = gains
        normed[...] = (expanded * gains[:1]).astype(BF)
        pltpu.make_async_copy(normed, normed_hbm, out_sems.at[0]).start()
        for i in range(3):
            cols = slice(i * PART_COLS, (i + 1) * PART_COLS)
            qkv[:, cols] = mm(normed[...], store[:, cols]).astype(BF)
        pltpu.make_async_copy(qkv, qkv_hbm, out_sems.at[1]).start()

    attend_pair(info, qkv, step, att_ref, norm_ref, prob_ref, turned)

    @pl.when(step == PART - 1)
    def _():
        arrived(normed, out_sems.at[0])
        arrived(qkv, out_sems.at[1])


def heads_a(info, x, pieces):
    return pl.pallas_call(
        heads_a_kernel,
        grid_spec=pltpu.PrefetchScalarGridSpec(
            num_scalar_prefetch=1,
            grid=(PART,),
            in_specs=[whole(ROWS, WIDTH)] + [HBM] * 8,
            out_specs=[HBM, HBM, whole(8, WIDTH), pair_cols(0), pair_cols(0), PROB_SPEC],
            scratch_shapes=[
                pltpu.VMEM((WIDTH, A_COLS), BF), pltpu.VMEM((ROWS, WIDTH), BF),
                pltpu.VMEM((ROWS, 3 * PART_COLS), BF), TURNED, PAIR_SEMS, PAIR_SEMS,
            ],
        ),
        out_shape=[
            jax.ShapeDtypeStruct((ROWS, WIDTH), BF),
            jax.ShapeDtypeStruct((ROWS, 3 * PART_COLS), BF),
            jax.ShapeDtypeStruct((8, WIDTH), F32),
        ]
        + HEADS_SHAPES,
        compiler_params=params(),
        cost_estimate=cost(6 * ROWS * WIDTH * PART_COLS + 4 * 6 * 7 * TILE * TILE * 256, 20000000, 2752512),
        name="heads_a",
    )(info, x, *pieces)


def heads_b_kernel(info, normed_ref, gains_ref, a_att_hbm, x_hbm, *rest):
    pieces, (qkv_hbm, bias_ref, middle_hbm, second_hbm, att_ref, norm_ref, prob_ref) = rest[:8], rest[8:15]
    store, qkv, turned, att, x, middle, second, sems, in_sems, out_sems = rest[15:]
    step = pl.program_id(0)
    late = [
        pltpu.make_async_copy(a_att_hbm, att.at[:, pl.ds(0, PART_COLS)], in_sems.at[0]),
        pltpu.make_async_copy(x_hbm, x, in_sems.at[1]),
    ]

    @pl.when(step == 0)
    def _():
        copies(info, pieces, by_half(store, sems))
        for copy in late:
            copy.start()
        halves_arrived(store, sems)
        for i in range(3):
            cols = slice(i * PART_COLS, (i + 1) * PART_COLS)
            qkv[:, cols] = mm(normed_ref[...], store[:, cols]).astype(BF)
        bias_ref[...] = store[:, B_COLS - SMALL :].astype(F32).T[:8]
        pltpu.make_async_copy(qkv, qkv_hbm, out_sems.at[0]).start()

    attend_pair(info, qkv, step, att_ref, norm_ref, prob_ref, turned)
    att[:, pl.ds(pl.multiple_of(PART_COLS + step * 2 * HEAD, 128), 2 * HEAD)] = att_ref[...]

    @pl.when(step == PART - 1)
    def _():
        for copy in late:
            copy.wait()
        weights = store[:, 3 * PART_COLS : 3 * PART_COLS + WIDTH]
        for i in range(ROWS // TILE):
            rows = slice(i * TILE, (i + 1) * TILE)
            mixed = mm(att[rows, :], weights)
            mixed = mixed - jnp.sum(mixed, axis=1, keepdims=True) * (1.0 / WIDTH)
            value = x[rows, :].astype(F32) + jnp.where(lanes() == WIDTH - 1, 0.0, mixed)
            inverse, expanded = norm_parts(value)
            middle[rows, :] = value
            second[rows, :] = (expanded * inverse * gains_ref[1:2, :]).astype(BF)
            for j, (source, target) in enumerate(((middle, middle_hbm), (second, second_hbm))):
                pltpu.make_async_copy(source.at[rows], target.at[rows], out_sems.at[1 + j]).start()
        arrived(qkv, out_sems.at[0])
        arrived(middle, out_sems.at[1])
        arrived(second, out_sems.at[2])


def heads_b(info, normed, gains, a_att, x, pieces):
    return pl.pallas_call(
        heads_b_kernel,
        grid_spec=pltpu.PrefetchScalarGridSpec(
            num_scalar_prefetch=1,
            grid=(PART,),
            in_specs=[whole(ROWS, WIDTH), whole(8, WIDTH)] + [HBM] * 10,
            out_specs=[HBM, whole(8, WIDTH), HBM, HBM, pair_cols(0), pair_cols(0), PROB_SPEC],
            scratch_shapes=[
                pltpu.VMEM((WIDTH, B_COLS), BF), pltpu.VMEM((ROWS, 3 * PART_COLS), BF), TURNED,
                pltpu.VMEM((ROWS, WIDTH), BF), pltpu.VMEM((ROWS, WIDTH), BF),
                pltpu.VMEM((ROWS, WIDTH), F32), pltpu.VMEM((ROWS, WIDTH), BF),
                PAIR_SEMS, PAIR_SEMS, pltpu.SemaphoreType.DMA((3,)),
            ],
        ),
        out_shape=[
            jax.ShapeDtypeStruct((ROWS, 3 * PART_COLS), BF),
            jax.ShapeDtypeStruct((8, WIDTH), F32),
            jax.ShapeDtypeStruct((ROWS, WIDTH), F32),
            jax.ShapeDtypeStruct((ROWS, WIDTH), BF),
        ]
        + HEADS_SHAPES,
        compiler_params=params(),
        cost_estimate=cost(
            6 * ROWS * WIDTH * PART_COLS + 2 * ROWS * WIDTH * WIDTH + 4 * 6 * 7 * TILE * TILE * 256,
            25000000, 2752512,
        ),
        name="heads_b",
    )(info, normed, gains, a_att, x, *pieces)


GELU_A = 0.7978845608028654
GELU_B = 0.044715


def feed_kernel(info, second_ref, down_in_ref, bias_ref, *rest):
    pieces, outs = rest[:12], rest[14:16]
    act_ref, slope_ref = rest[12:14]
    store, sems, stage, out_sem = rest[16:]
    step = pl.program_id(0)
    core = info[1]

    @pl.when(step == 0)
    def _():
        quarter_copies(info, pieces, store, sems)

    cols = pl.ds(pl.multiple_of(step * WIDTH, WIDTH), WIDTH)
    arrived(store.at[:, cols], sems.at[step])
    weights = store[:, cols]
    for i in range(ROWS // TILE):
        rows = slice(i * TILE, (i + 1) * TILE)
        hidden = mm(second_ref[rows, :], weights) + bias_ref[...]
        square = hidden * hidden
        bent = jnp.tanh(hidden * (GELU_A + (GELU_A * GELU_B) * square))
        half = 0.5 + 0.5 * bent
        act_ref[rows, :] = (hidden * half).astype(BF)
        tilt = hidden * (0.5 * GELU_A + (1.5 * GELU_A * GELU_B) * square)
        slope_ref[rows, :] = (half + tilt * (1.0 - bent * bent)).astype(BF)
    grads = mm_tn(act_ref[...], down_in_ref[...])
    for i in range(8):
        slot = 8 * step + i
        stage[slot] = grads[96 * i : 96 * (i + 1)].astype(BF)
        mine = core == (i & 1)

        def put(which, slot=slot, chip=4 * step + (i >> 1)):
            pltpu.make_async_copy(stage.at[slot], outs[which].at[place_at(info, chip)], out_sem).start()

        pl.when(mine)(functools.partial(put, 0))
        pl.when(jnp.logical_not(mine))(functools.partial(put, 1))

    @pl.when(step == 3)
    def _():
        arrived(stage, out_sem)


def feed(info, second, down_in, bias, pieces):
    return pl.pallas_call(
        feed_kernel,
        grid_spec=pltpu.PrefetchScalarGridSpec(
            num_scalar_prefetch=1,
            grid=(4,),
            in_specs=[whole(ROWS, WIDTH)] * 2 + [col_tile(1, WIDTH)] + [HBM] * 12,
            out_specs=[col_tile(ROWS, WIDTH)] * 2 + [HBM] * 2,
            scratch_shapes=[
                pltpu.VMEM((WIDTH, HIDDEN), BF), SLOT_SEMS,
                pltpu.VMEM((32, 96, WIDTH), BF), pltpu.SemaphoreType.DMA,
            ],
        ),
        out_shape=[jax.ShapeDtypeStruct((ROWS, HIDDEN), BF)] * 2
        + [jax.ShapeDtypeStruct((CHIPS, 96, WIDTH), BF)] * 2,
        compiler_params=params(),
        cost_estimate=cost(4 * ROWS * WIDTH * HIDDEN, 6 * ROWS * HIDDEN + 4 * WIDTH * HIDDEN),
        name="feed",
    )(info, second, down_in, bias, *pieces)


UP_COLS = HIDDEN // 2 + SMALL, HIDDEN // 2


def spread_out(info, grads, stage, half=0):
    for device in range(32):
        value = grads[24 * device : 24 * (device + 1)].astype(BF)
        stage[info[1] ^ (device & 1), place_at(info, device >> 1, half)] = value


def back_kernel(info, down_in_ref, second_ref, slope_ref, down_hbm, *rest):
    pieces, outs, weighted_hbm = rest[:12], rest[12:16], rest[16]
    down_store, down_sems, up_store, up_sems, grads, weighted, stage, spare, out_sem = rest[17:]
    step = pl.program_id(0)
    core = info[1]

    @pl.when(step == 0)
    def _():
        for i in range(4):
            pltpu.make_async_copy(
                down_hbm.at[pl.ds(i * WIDTH, WIDTH)], down_store.at[i], down_sems.at[i]
            ).start()
        quarter_copies(info, pieces, up_store, up_sems)

    arrived(down_store.at[step], down_sems.at[step])
    sums = jnp.zeros((1, WIDTH), F32)
    value = mm_nt(down_in_ref[...], down_store[step])
    for i in range(ROWS // TILE):
        rows = slice(i * TILE, (i + 1) * TILE)
        part = (slope_ref[rows, :].astype(F32) * value[rows]).astype(BF)
        grads[rows, :] = part
        sums += jnp.sum(part.astype(F32), axis=0, keepdims=True)
    for i in range(8):
        few = jnp.concatenate([sums[:, 96 * i : 96 * (i + 1)], jnp.zeros((1, 32), F32)], axis=1)
        few = jnp.broadcast_to(few, (24, SMALL)).astype(BF)
        spare[core ^ (i & 1), place_at(info, 4 * step + (i >> 1))] = few
    cols = pl.ds(pl.multiple_of(step * WIDTH, WIDTH), WIDTH)
    arrived(up_store.at[:, cols], up_sems.at[step])
    weights = up_store[:, cols]

    @pl.when(step == 0)
    def _():
        weighted[...] = mm_nt(grads[...], weights)

    @pl.when(step > 0)
    def _():
        weighted[...] += mm_nt(grads[...], weights)

    @pl.when(step == 3)
    def _():
        pltpu.make_async_copy(weighted, weighted_hbm, out_sem.at[2]).start()

    found = mm_tn(second_ref[...], grads[...])
    cols = pl.ds(pl.multiple_of((step & 1) * WIDTH, 128), WIDTH)
    for half in range(2):

        @pl.when((step >> 1) == half)
        def _(half=half):
            spread_out(info, found, stage.at[step], half)
            for which in range(2):
                pltpu.make_async_copy(
                    stage.at[step, which], outs[2 * half + which].at[:, :, cols], out_sem.at[0]
                ).start()

    @pl.when(step == 3)
    def _():
        for which in range(2):
            pltpu.make_async_copy(
                spare.at[which], outs[which].at[:, :, pl.ds(HIDDEN // 2, SMALL)], out_sem.at[1]
            ).start()
        arrived(stage, out_sem.at[0])
        arrived(spare, out_sem.at[1])
        arrived(weighted, out_sem.at[2])


def back(info, down_in, second, slope, w_down, pieces):
    return pl.pallas_call(
        back_kernel,
        grid_spec=pltpu.PrefetchScalarGridSpec(
            num_scalar_prefetch=1,
            grid=(4,),
            in_specs=[whole(ROWS, WIDTH)] * 2 + [col_tile(ROWS, WIDTH)] + [HBM] * 13,
            out_specs=[HBM] * 5,
            scratch_shapes=[
                pltpu.VMEM((4, WIDTH, WIDTH), BF), SLOT_SEMS,
                pltpu.VMEM((WIDTH, HIDDEN), BF), SLOT_SEMS,
                pltpu.VMEM((ROWS, WIDTH), BF),
                pltpu.VMEM((ROWS, WIDTH), F32),
                pltpu.VMEM((4, 2, CHIPS, 24, WIDTH), BF),
                pltpu.VMEM((2, CHIPS, 24, SMALL), BF),
                pltpu.SemaphoreType.DMA((3,)),
            ],
        ),
        out_shape=[jax.ShapeDtypeStruct((CHIPS, 24, UP_COLS[i // 2]), BF) for i in range(4)]
        + [jax.ShapeDtypeStruct((ROWS, WIDTH), F32)],
        compiler_params=params(),
        cost_estimate=cost(6 * ROWS * WIDTH * HIDDEN, 35000000),
        name="back",
    )(info, down_in, second, slope, w_down, *pieces)


def middle_grad_kernel(info, weighted_ref, middle_ref, up_ref, gain_ref, *rest):
    pieces, (total_ref, mixed_ref, grad_ref, store, semaphore) = rest[:8], rest[8:]
    step = pl.program_id(0)

    @pl.when(step == 0)
    def _():
        copies(info, pieces, one_half(store, semaphore), OUT_COLS)

    inverse, expanded = norm_parts(middle_ref[...])
    total = up_ref[...].astype(F32) + norm_back(weighted_ref[...] * gain_ref[1:2, :], inverse, expanded)
    total_ref[...] = total
    mixed = (total - jnp.sum(total, axis=1, keepdims=True) * (1.0 / WIDTH)).astype(BF)
    mixed_ref[...] = mixed

    @pl.when(step == 0)
    def _():
        arrived(store, semaphore)

    grad_ref[...] = mm_nt(mixed, store[...]).astype(BF)


def middle_grad(info, weighted, middle, upstream, gains, pieces):
    return pl.pallas_call(
        middle_grad_kernel,
        grid_spec=pltpu.PrefetchScalarGridSpec(
            num_scalar_prefetch=1,
            grid=(ROWS // TILE,),
            in_specs=[row_tile(WIDTH)] * 3 + [whole(8, WIDTH)] + [HBM] * 8,
            out_specs=[row_tile(WIDTH)] * 3,
            scratch_shapes=[pltpu.VMEM((WIDTH, WIDTH), BF), pltpu.SemaphoreType.DMA],
        ),
        out_shape=[
            jax.ShapeDtypeStruct((ROWS, WIDTH), F32),
            jax.ShapeDtypeStruct((ROWS, WIDTH), BF),
            jax.ShapeDtypeStruct((ROWS, WIDTH), BF),
        ],
        compiler_params=params(),
        cost_estimate=cost(2 * ROWS * WIDTH * WIDTH, 18 * ROWS * WIDTH),
        name="middle_grad",
    )(info, weighted, middle, upstream, gains, *pieces)


def pair_grad(q_ref, k_ref, v_ref, grad_ref, att_ref, norm_ref, prob_ref, dq_ref, dk_ref, dv_ref, key_sum, value_sum, turned):
    factor = HEAD**-0.5
    turned[...] = v_ref[...].T
    key_sum[...] = jnp.zeros_like(key_sum)
    value_sum[...] = jnp.zeros_like(value_sum)
    for first, key_first, key_count, place in SPANS:
        rows = slice(first, first + TILE)
        keys_at = slice(key_first, key_first + key_count)
        queries = q_ref[rows, :]
        grads = (grad_ref[rows, :].astype(F32) * norm_ref[rows, :]).astype(BF)
        product = grads.astype(F32) * att_ref[rows, :].astype(F32)
        keys = k_ref[keys_at, :]
        values = turned[:, keys_at]
        parts = []
        for head in range(2):
            mask = head_mask(head)
            my_grads = jnp.where(mask, grads, 0)
            my_queries = jnp.where(mask, queries, 0)
            probs = prob_ref[head, :, place : place + key_count]
            inner = jnp.sum(jnp.where(mask, product, 0.0), axis=1, keepdims=True)
            slopes = probs.astype(F32) * (mm(my_grads, values) - inner)
            slopes = slopes.astype(BF)
            parts.append(mm(slopes, keys))
            value_sum[:, keys_at] += mm_tn(my_grads, probs)
            key_sum[:, keys_at] += mm_tn(my_queries, slopes)
        dq_ref[rows, :] = (jnp.where(head_mask(0), parts[0], parts[1]) * factor).astype(BF)
    dk_ref[...] = (key_sum[...].T * factor).astype(BF)
    dv_ref[...] = value_sum[...].T.astype(BF)


HEADS_COLS = 6 * PART_COLS + WIDTH


def attend_grad_kernel(info, a_att_ref, b_att_ref, mixed_ref, *rest):
    ins, outs = rest[:7], rest[7:10]
    targets, (key_sum, value_sum, values, stage, out_sem) = rest[10:12], rest[12:]
    step = pl.program_id(0)

    @pl.when(step == 0)
    def _():
        both = jnp.concatenate([a_att_ref[...], b_att_ref[...]], axis=1)
        spread_out(info, mm_tn(both, mixed_ref[...]), stage)
        for which in range(2):
            pltpu.make_async_copy(
                stage.at[which], targets[which].at[:, :, pl.ds(6 * PART_COLS, WIDTH)], out_sem
            ).start()

    pair_grad(*ins, *outs, key_sum, value_sum, values)

    @pl.when(step == PART - 1)
    def _():
        arrived(stage, out_sem)


def heads_grad_kernel(info, normed_ref, a_q, a_k, a_v, *rest):
    ins, outs = rest[:7], rest[9:12]
    targets, (key_sum, value_sum, values, kept, turned, stage, out_sem) = rest[12:14], rest[14:]
    step = pl.program_id(0)

    @pl.when(step == 0)
    def _():
        turned[...] = normed_ref[...].T

    pair_grad(*ins, *outs, key_sum, value_sum, values)
    place = pl.ds(pl.multiple_of(step * 2 * HEAD, 2 * HEAD), 2 * HEAD)
    for i in range(3):
        kept[i, :, place] = outs[i][...]

    def weights_grad(i, ref):
        spread_out(info, mm(turned[...], ref[...]), stage.at[i])
        for which, target in enumerate(targets):
            pltpu.make_async_copy(
                stage.at[i, which], target.at[:, :, pl.ds(i * PART_COLS, PART_COLS)], out_sem
            ).start()

    for i, ref in enumerate((a_q, a_k, a_v)):
        pl.when(step == i)(functools.partial(weights_grad, i, ref))

    @pl.when(step == PART - 1)
    def _():
        for i in range(3):
            weights_grad(3 + i, kept.at[i])
        arrived(stage, out_sem)


HEADS_GRADS = [jax.ShapeDtypeStruct((CHIPS, 24, HEADS_COLS), BF)] * 2


def pair_specs(first):
    return [
        pair_cols(0), pair_cols(PART), pair_cols(2 * PART),
        pair_cols(first), pair_cols(0), pair_cols(0), PROB_SPEC,
    ]


def attend_grad(info, attended, mixed, qkv, grad_attended, norms, probs):
    return pl.pallas_call(
        attend_grad_kernel,
        grid_spec=pltpu.PrefetchScalarGridSpec(
            num_scalar_prefetch=1,
            grid=(PART,),
            in_specs=[whole(ROWS, PART_COLS)] * 2 + [whole(ROWS, WIDTH)] + pair_specs(0),
            out_specs=[pair_cols(0)] * 3 + [HBM] * 2,
            scratch_shapes=[pltpu.VMEM((2 * HEAD, ROWS), F32)] * 2
            + [TURNED, pltpu.VMEM((2, CHIPS, 24, WIDTH), BF), pltpu.SemaphoreType.DMA],
        ),
        out_shape=[jax.ShapeDtypeStruct((ROWS, PART_COLS), BF)] * 3 + HEADS_GRADS,
        compiler_params=params(),
        cost_estimate=cost(8 * 6 * 7 * TILE * TILE * 256, 8 * ROWS * WIDTH + 5505024),
        name="attend_grad",
    )(info, *attended, mixed, qkv, qkv, qkv, grad_attended, attended[0], norms, probs)


def heads_grad(info, normed, parts, qkv, grad_attended, attended, norms, probs, keep, send):
    return pl.pallas_call(
        heads_grad_kernel,
        grid_spec=pltpu.PrefetchScalarGridSpec(
            num_scalar_prefetch=1,
            grid=(PART,),
            in_specs=[whole(ROWS, WIDTH)] + [whole(ROWS, PART_COLS)] * 3 + pair_specs(PART) + [HBM] * 2,
            out_specs=[pair_cols(0)] * 3 + [HBM] * 2,
            scratch_shapes=[pltpu.VMEM((2 * HEAD, ROWS), F32)] * 2
            + [
                TURNED,
                pltpu.VMEM((3, ROWS, PART_COLS), BF),
                pltpu.VMEM((WIDTH, ROWS), BF),
                pltpu.VMEM((6, 2, CHIPS, 24, PART_COLS), BF),
                pltpu.SemaphoreType.DMA,
            ],
        ),
        out_shape=[jax.ShapeDtypeStruct((ROWS, PART_COLS), BF)] * 3 + HEADS_GRADS,
        input_output_aliases={12: 3, 13: 4},
        compiler_params=params(),
        cost_estimate=cost(
            8 * 6 * 7 * TILE * TILE * 256 + 6 * ROWS * WIDTH * WIDTH, 8 * ROWS * WIDTH + 10000000
        ),
        name="heads_grad",
    )(info, normed, *parts, qkv, qkv, qkv, grad_attended, attended, norms, probs, keep, send)


def last_kernel(info, act_ref, middle_ref, gain_ref, *rest):
    parts, x_hbm, total_hbm, down_hbm = rest[:6], rest[6], rest[7], rest[8]
    a_pieces, b_pieces, (out_ref, grad_ref) = rest[9:17], rest[17:25], rest[25:27]
    down_store, down_sems, a_store, b_store, a_sems, b_sems, grads, x, total, weighted, sems = rest[27:]
    step = pl.program_id(0)
    late = [
        pltpu.make_async_copy(source, target, sems.at[i])
        for i, (source, target) in enumerate(
            [(part, grads.at[i]) for i, part in enumerate(parts)] + [(x_hbm, x), (total_hbm, total)]
        )
    ]

    @pl.when(step == 0)
    def _():
        for i in range(4):
            pltpu.make_async_copy(
                down_hbm.at[pl.ds(i * WIDTH, WIDTH)], down_store.at[i], down_sems.at[i]
            ).start()
        copies(info, a_pieces, by_half(a_store, a_sems))
        copies(info, b_pieces, by_half(b_store, b_sems))
        for copy in late:
            copy.start()
        for i in range(4):
            arrived(down_store.at[i], down_sems.at[i])

    branch = mm(act_ref[:, :WIDTH], down_store[0])
    for i in range(1, 4):
        branch += mm(act_ref[:, i * WIDTH : (i + 1) * WIDTH], down_store[i])
    branch = branch - jnp.sum(branch, axis=1, keepdims=True) * (1.0 / WIDTH)
    out_ref[...] = (middle_ref[...] + branch).astype(BF)

    for i in range(3):

        @pl.when(step == i)
        def _(i=i):
            if i == 0:
                halves_arrived(a_store, a_sems)
                halves_arrived(b_store, b_sems)
            late[i].wait()
            late[3 + i].wait()
            cols = slice(i * PART_COLS, (i + 1) * PART_COLS)
            found = mm_nt(grads[i], a_store[:, cols]) + mm_nt(grads[3 + i], b_store[:, cols])
            weighted[...] = found if i == 0 else weighted[...] + found

    @pl.when(step == 3)
    def _():
        late[6].wait()
        late[7].wait()
        for i in range(ROWS // TILE):
            rows = slice(i * TILE, (i + 1) * TILE)
            inverse, expanded = norm_parts(x[rows, :].astype(F32))
            back = norm_back(weighted[rows, :] * gain_ref[0:1, :], inverse, expanded)
            grad_ref[rows, :] = (total[rows, :] + back).astype(BF)


def last(info, active, middle, parts, x, total, gains, w_down, a_pieces, b_pieces):
    return pl.pallas_call(
        last_kernel,
        grid_spec=pltpu.PrefetchScalarGridSpec(
            num_scalar_prefetch=1,
            grid=(ROWS // TILE,),
            in_specs=[row_tile(HIDDEN), row_tile(WIDTH), whole(8, WIDTH)] + [HBM] * 25,
            out_specs=[row_tile(WIDTH), whole(ROWS, WIDTH)],
            scratch_shapes=[
                pltpu.VMEM((4, WIDTH, WIDTH), BF), SLOT_SEMS,
                pltpu.VMEM((WIDTH, A_COLS), BF), pltpu.VMEM((WIDTH, B_COLS), BF), PAIR_SEMS, PAIR_SEMS,
                pltpu.VMEM((6, ROWS, PART_COLS), BF), pltpu.VMEM((ROWS, WIDTH), BF),
                pltpu.VMEM((ROWS, WIDTH), F32), pltpu.VMEM((ROWS, WIDTH), F32),
                pltpu.SemaphoreType.DMA((8,)),
            ],
        ),
        out_shape=[jax.ShapeDtypeStruct((ROWS, WIDTH), BF)] * 2,
        compiler_params=params(),
        cost_estimate=cost(2 * ROWS * WIDTH * HIDDEN + 6 * ROWS * WIDTH * WIDTH, 30000000),
        name="last",
    )(info, active, middle, gains, *parts, x, total, w_down, *a_pieces, *b_pieces)


def turn_back_kernel(info, one_ref, two_ref, out_ref, grad_ref):
    pick = turn(first_row(info), pl.program_id(0) * TILE, TILE, False)
    out_ref[...] = mm(pick, one_ref[...]).astype(BF)[:, : WIDTH - 1]
    grad_ref[...] = mm(pick, two_ref[...]).astype(BF)[:, : WIDTH - 1]


def turn_back(info, one, two):
    return pl.pallas_call(
        turn_back_kernel,
        grid_spec=pltpu.PrefetchScalarGridSpec(
            num_scalar_prefetch=1,
            grid=(ROWS // TILE,),
            in_specs=[whole(ROWS, WIDTH)] * 2,
            out_specs=[row_tile(WIDTH - 1)] * 2,
        ),
        out_shape=[jax.ShapeDtypeStruct((ROWS, WIDTH - 1), BF)] * 2,
        compiler_params=params(),
        cost_estimate=cost(4 * ROWS * ROWS * WIDTH, 8 * ROWS * WIDTH),
        name="turn_back",
    )(info, one, two)


WAYS = {"core": (0, 1), "x": (0, 2), "y": (1, 0), "xy": (1, 2), "z1": (2, 0), "z2": (4, 0), "z3": (6, 0)}


def add_low(left, right):
    return (left.astype(F32) + right.astype(F32)).astype(BF)


class Cube:
    def __init__(self, sizes):
        self.sizes = sizes
        wide, narrow = lax.axis_index("wide"), lax.axis_index("narrow")
        self.place = jnp.stack([wide * 2 + (narrow >> 1), narrow & 1]).astype(jnp.int32)

    def hop(self, value, way):
        wide, narrow = WAYS[way]
        if wide == 0:
            return lax.ppermute(value, "narrow", [(i, i ^ narrow) for i in range(self.sizes["narrow"])])
        if narrow == 0:
            return lax.ppermute(value, "wide", [(i, i ^ wide) for i in range(self.sizes["wide"])])
        bits = wide * self.sizes["narrow"] + narrow
        count = self.sizes["wide"] * self.sizes["narrow"]
        return lax.ppermute(value, AXES, [(i, i ^ bits) for i in range(count)])

    def gather(self, block):
        others = yield [self.hop(block, way) for way in ("z1", "z2", "z3")]
        return (yield from self.across(jnp.concatenate([block] + others)))

    def gather_slowly(self, block):
        near = yield from self.along_z([block])
        return (yield from self.across(near[0]))

    def along_z(self, blocks):
        for way in ("z1", "z2"):
            others = yield [self.hop(block, way) for block in blocks]
            blocks = [jnp.concatenate(pair) for pair in zip(blocks, others)]
        return blocks

    def across(self, near):
        far = yield [self.hop(near, way) for way in ("x", "y", "xy")]
        own = [near] + far
        twins = yield [self.hop(part, "core") for part in own]
        return own + twins

    def quarters(self, block):
        block, = yield from self.along_z([block])
        near = [block[:, :WIDTH], block[:, WIDTH:]]
        far = yield [self.hop(part, way) for part, way in zip(near, ("x", "y"))]
        both = [jnp.concatenate(pair) for pair in zip(near, far)]
        *last, one, two = yield [
            self.hop(part, way) for part, way in zip(both + near, ("y", "x", "core", "core"))
        ]
        three, four, five, six = yield [self.hop(part, "core") for part in far + last]
        return [near[0], far[0], last[0], near[1], far[1], last[1], one, three, five, two, four, six]

    def blocks(self, info, shards):
        others = [self.hop(shard, "core") for shard in shards]
        return join(info, shards, others)

    def reduce_two(self, keeps, sends):
        gots = yield [self.hop(send, "core") for send in sends]
        for ways in ("yx", "xy"):
            count = keeps[0].shape[0] // 2
            sends = [add_low(keep[count:], got[count:]) for keep, got in zip(keeps, gots)]
            keeps = [add_low(keep[:count], got[:count]) for keep, got in zip(keeps, gots)]
            gots = yield [self.hop(send, way) for send, way in zip(sends, ways)]
        both = jnp.concatenate([add_low(keep, got) for keep, got in zip(keeps, gots)], axis=2)
        got = yield self.hop(both[2:], "z2")
        both = [add_low(both[i], got[i]) for i in range(2)]
        got = yield self.hop(both[1], "z1")
        return both[0].astype(F32) + got.astype(F32)

    def reduce(self, keep, send):
        got = yield self.hop(send, "core")
        both = [keep[4 * i : 4 * i + 4].astype(F32) + got[4 * i : 4 * i + 4].astype(F32) for i in range(4)]
        others = yield [self.hop(both[i].astype(BF), way) for i, way in ((1, "x"), (2, "y"), (3, "xy"))]
        both = sum([other.astype(F32) for other in others], both[0])
        others = yield [self.hop(both[i].astype(BF), way) for i, way in ((1, "z1"), (2, "z2"), (3, "z3"))]
        return sum([other.astype(F32) for other in others], both[0])


class Plain:
    def __init__(self):
        self.place = jnp.zeros((2,), jnp.int32)

    def blocks(self, info, shards):
        return shards

    def all_rows(self, shard):
        full = lax.all_gather(shard, AXES, axis=0, tiled=True)
        cols = full.shape[1]
        return full.reshape(4, 4, BLOCK, cols).transpose(1, 0, 2, 3).reshape(4, 4 * BLOCK, cols)

    def gather(self, shard):
        yield ()
        return self.split(self.all_rows(shard))

    gather_slowly = gather

    def split(self, full):
        cols = full.shape[2] // 2
        return [full[i, :, half * cols : (half + 1) * cols] for half in range(2) for i in range(4)]

    def quarters(self, shard):
        yield ()
        full, cols, pieces = self.all_rows(shard), WIDTH, []
        for i in range(4):
            part = full[:, :, i * cols : (i + 1) * cols]
            order = ((0,), (1,), (2, 3)) if i % 2 == 0 else ((0,), (2,), (1, 3))
            pieces += [jnp.concatenate([part[k] for k in some]) for some in order]
        return pieces

    def reduce_two(self, keeps, sends):
        one = yield from self.reduce(keeps[0], sends[0])
        order = jnp.arange(CHIPS).reshape(2, 2, 4).transpose(1, 0, 2).reshape(-1)
        two = yield from self.reduce(keeps[1][order], sends[1][order])
        return jnp.concatenate([one, two], axis=1)

    def reduce(self, keep, send):
        yield ()
        full = jnp.stack([keep, send], axis=1).reshape(4, 4, -1, keep.shape[2])
        full = full.transpose(1, 0, 2, 3).reshape(-1, keep.shape[2])
        return lax.psum_scatter(full, AXES, scatter_dimension=0, tiled=True).astype(F32)


class Task:
    def __init__(self, steps):
        self.steps, self.flight, self.over, self.result = steps, (), False, None
        self.go(None)

    def go(self, arrived_now):
        try:
            self.flight = self.steps.send(arrived_now)
        except StopIteration as end:
            self.flight, self.over, self.result = (), True, end.value


def meet(values, *tasks, waiting=()):
    tasks = [task for task in tasks if not task.over]
    every = tasks + list(waiting)
    values, flights = lax.optimization_barrier((values, [task.flight for task in every]))
    for task, flight in zip(every, flights):
        task.flight = flight
    for task in tasks:
        task.go(task.flight)
    return values


def finish(values, *tasks):
    while not all(task.over for task in tasks):
        values = meet(values, *tasks)
    return values


def layer(sizes, tokens, lengths, gain_one, w_qkv, w_out, gain_two, w_up, b_up, w_down, cotangent):
    share, few = b_up.shape[0], gain_one.shape[0]
    links = Cube(sizes) if sizes["wide"] == 8 and sizes["narrow"] == 4 else Plain()
    info = jnp.concatenate([links.place, lengths[0]])

    a_block, b_block, up_block = links.blocks(
        info, [*pack(w_qkv, w_out, gain_one, gain_two, b_up), w_up]
    )
    group_a, group_b = Task(links.gather(a_block)), Task(links.gather_slowly(b_block))
    tokens, cotangent, up_block = meet((tokens, cotangent, up_block), group_a, group_b)
    up = Task(links.quarters(up_block))
    x, upstream, down_in = before(info, tokens, cotangent)
    x, w_down = meet((x, w_down), group_a, waiting=(group_b, up))
    full_down = lax.all_gather(w_down, AXES, axis=0, tiled=True)
    x = meet(x, group_a, group_b, up)
    normed, qkv_a, gains, att_a, norms_a, probs_a = heads_a(info, x, group_a.result)
    normed, att_a, x = meet((normed, att_a, x), group_b, up)
    normed, att_a, x = meet((normed, att_a, x), group_b, up)
    qkv_b, bias, middle, second, att_b, norms_b, probs_b = heads_b(
        info, normed, gains, att_a, x, group_b.result
    )
    bias = bias[: HIDDEN // WIDTH].reshape(HIDDEN // WIDTH, -1, few)
    bias = bias.transpose(1, 0, 2).reshape(1, HIDDEN)
    second = finish(second, up)
    active, slope, *grad_down = feed(info, second, down_in, bias, up.result)
    downs = Task(links.reduce(*grad_down))
    slope = meet(slope, downs)
    *grad_up, weighted = back(info, down_in, second, slope, full_down, up.result)
    weighted, grad_up = meet((weighted, grad_up), downs)
    ups = Task(links.reduce_two(grad_up[::2], grad_up[1::2]))
    total, mixed, grad_att = middle_grad(info, weighted, middle, upstream, gains, group_b.result)
    total, mixed, grad_att = meet((total, mixed, grad_att), ups, downs)
    *parts, keep, send = attend_grad(info, (att_a, att_b), mixed, qkv_a, grad_att, norms_a, probs_a)
    parts, keep, send, grad_att = meet((parts, keep, send, grad_att), ups)
    *more, keep, send = heads_grad(
        info, normed, parts, qkv_b, grad_att, att_b, norms_b, probs_b, keep, send
    )
    active, more, keep, send = meet((active, more, keep, send), waiting=(ups,))
    heads = Task(links.reduce(keep, send))
    active, more = meet((active, more), heads, ups)
    output, grad_tokens = last(
        info, active, middle, list(parts) + list(more), x, total, gains, full_down,
        group_a.result, group_b.result,
    )
    output, grad_tokens = meet((output, grad_tokens), heads, ups)
    output, grad_tokens = turn_back(info, output, grad_tokens)
    output, grad_tokens = finish((output, grad_tokens), heads, ups, downs)

    first, bias_end = HIDDEN // 2, HIDDEN // 2 + SMALL
    grad_up = jnp.concatenate([ups.result[:, :first], ups.result[:, bias_end:]], axis=1)
    grad_out = heads.result[:, 6 * PART_COLS :]
    sums = ups.result[:, first : first + 96]
    if few >= 24:
        sums = sums[::24].reshape(-1)
    else:
        index = lax.axis_index("wide") * sizes["narrow"] + lax.axis_index("narrow")
        sums = lax.dynamic_slice_in_dim(sums[0], index % (24 // few) * share, share)
    grad_qkv = jnp.concatenate(
        [heads.result[:, (3 * part + i) * PART_COLS : (3 * part + i + 1) * PART_COLS]
         for i in range(3) for part in range(2)],
        axis=1,
    )
    return (
        output,
        grad_tokens,
        jnp.sum(w_qkv.astype(F32) * grad_qkv, axis=1) / gain_one.astype(F32),
        grad_qkv,
        grad_out,
        jnp.sum(w_up.astype(F32) * grad_up, axis=1) / gain_two.astype(F32),
        grad_up,
        sums,
        downs.result,
    )


def solution(mesh):
    rows, vector = P(AXES, None), P(AXES)
    sizes = dict(mesh.shape)
    return jax.shard_map(
        functools.partial(layer, sizes),
        mesh=mesh,
        in_specs=(rows, rows, vector, rows, rows, vector, rows, vector, rows, rows),
        out_specs=(rows, rows, vector, rows, rows, vector, rows, vector, rows),
        check_vma=False,
    )
```

```python
import functools

import jax
import jax.numpy as jnp
from jax import lax
from jax.experimental import pallas as pl
from jax.experimental.pallas import tpu as pltpu
from jax.sharding import PartitionSpec as P

AXES = ("wide", "narrow")
EPSILON = 1e-05
BF = jnp.bfloat16
F32 = jnp.float32
WIDTH = 768
HIDDEN = 3072
ROWS = 1024
TILE = 256
BIG = 768
PAIRS = 6
HEAD = 64
PROB_COLS = 1792
CHIPS = 16
BLOCK = 48
LIMIT = 56 * 1024 * 1024


def mm(left, right):
    return lax.dot_general(left, right, (((1,), (0,)), ((), ())), preferred_element_type=F32)


def mm_nt(left, right):
    return lax.dot_general(left, right, (((1,), (1,)), ((), ())), preferred_element_type=F32)


def mm_tn(left, right):
    return lax.dot_general(left, right, (((0,), (0,)), ((), ())), preferred_element_type=F32)


def lanes(width=WIDTH):
    return lax.broadcasted_iota(jnp.int32, (1, width), 1)


def norm_parts(rows):
    total = jnp.sum(rows, axis=1, keepdims=True)
    squares = jnp.sum(rows * rows, axis=1, keepdims=True)
    inverse = lax.rsqrt((squares + total * total) * (1.0 / WIDTH) + EPSILON)
    expanded = jnp.where(lanes() == WIDTH - 1, -total, rows)
    return inverse, expanded


def norm_back(weighted, inverse, expanded):
    inner = jnp.sum(weighted * expanded, axis=1, keepdims=True) * (1.0 / WIDTH)
    full = inverse * (weighted - (inverse * inverse * inner) * expanded)
    last = full[:, WIDTH - 1 :]
    return jnp.where(lanes() == WIDTH - 1, 0.0, full - last)


def turn(start, first_row, count, forward):
    rows = lax.broadcasted_iota(jnp.int32, (count, ROWS), 0) + first_row
    cols = lax.broadcasted_iota(jnp.int32, (count, ROWS), 1)
    if forward:
        source = rows + start
        source = jnp.where(source >= ROWS, source - ROWS, source)
    else:
        source = rows - start
        source = jnp.where(source < 0, source + ROWS, source)
    return jnp.where(cols == source, 1.0, 0.0).astype(BF)


def first_row(info):
    return jnp.where(info[2] == BIG, 0, jnp.where(info[3] == BIG, info[2], info[2] + info[3]))


def params(**more):
    return pltpu.CompilerParams(vmem_limit_bytes=LIMIT, **more)


def cost(flops, nbytes, transcendentals=0):
    return pl.CostEstimate(flops=flops, bytes_accessed=nbytes, transcendentals=transcendentals)


HBM = pl.BlockSpec(memory_space=pl.ANY)


def whole(*shape):
    return pl.BlockSpec(shape, lambda *i: (0,) * len(shape))


def row_tile(width, tile=TILE):
    return pl.BlockSpec((tile, width), lambda i, *s: (i, 0))


def col_tile(rows, width):
    return pl.BlockSpec((rows, width), lambda i, *s: (0, i))


def offset_of(place):
    return 4 * (place & 3) + (place >> 2)


def place_at(info, chip, half=0):
    offset = info[0] ^ chip
    x, y = offset & 1, (offset >> 1) & 1
    return (offset >> 2) + 4 * (x + 2 * y if half == 0 else y + 2 * x)


def copies(info, pieces, target, cols=None):
    for side in range(2):
        half = info[1] ^ side

        def start(side=side, half=half):
            for place in range(CHIPS):
                source = pieces[4 * side + place // 4].at[pl.ds((place % 4) * BLOCK, BLOCK)]
                if cols is not None:
                    source = source.at[:, pl.ds(*cols)]
                block = pl.multiple_of((info[0] ^ offset_of(place)) * BLOCK, 16)
                pltpu.make_async_copy(source, *target(half, block)).start()

        if cols is None:
            start()
        else:
            pl.when(half == 1)(start)


def quarter_copies(info, pieces, store, sems):
    for part in range(2):
        for side in range(2):
            quarter = 2 * (info[1] ^ side) + part
            cols = pl.ds(pl.multiple_of(quarter * WIDTH, 128), WIDTH)
            for place in range(CHIPS):
                source = pieces[4 * side + place // 4]
                source = source.at[pl.ds((place % 4) * BLOCK, BLOCK), pl.ds(part * WIDTH, WIDTH)]
                block = pl.multiple_of((info[0] ^ offset_of(place)) * BLOCK, 16)
                pltpu.make_async_copy(source, store.at[pl.ds(block, BLOCK), cols], sems.at[quarter]).start()


def row_copies(info, pieces, store, sems):
    for part in range(4):
        for side in range(2):
            for i in range(4):
                chip = info[0] ^ offset_of(4 * part + i)
                first = (chip & 3) * (4 * BLOCK) + (info[1] ^ side) * (2 * BLOCK)
                pltpu.make_async_copy(
                    pieces[4 * side + part].at[pl.ds(i * 2 * BLOCK, 2 * BLOCK)],
                    store.at[chip >> 2, pl.ds(pl.multiple_of(first, 16), 2 * BLOCK)],
                    sems.at[chip >> 2],
                ).start()


def by_half(store, sems):
    width = store.shape[1] // 2

    def target(half, first):
        cols = pl.ds(pl.multiple_of(half * width, 128), width)
        return store.at[pl.ds(first, BLOCK), cols], sems.at[half]

    return target


def one_half(store, semaphore):
    return lambda half, first: (store.at[pl.ds(first, BLOCK)], semaphore)


def arrived(ref, semaphore):
    pltpu.make_async_copy(ref, ref, semaphore).wait()


def halves_arrived(store, sems, halves=(0, 1)):
    width = store.shape[1] // 2
    for half in halves:
        arrived(store.at[:, pl.ds(half * width, width)], sems.at[half])


OUT_COLS = (128, WIDTH)
TURNED = pltpu.VMEM((2 * HEAD, ROWS), BF)
PAIR_SEMS = pltpu.SemaphoreType.DMA((2,))
SLOT_SEMS = pltpu.SemaphoreType.DMA((4,))
PART = 3
PART_COLS = PART * 2 * HEAD
SMALL = 128
A_COLS = 3 * PART_COLS + SMALL
B_COLS = 3 * PART_COLS + WIDTH + SMALL


def pack_kernel(qkv_ref, out_ref, one_ref, two_ref, bias_ref, a_ref, b_ref):
    few, share = one_ref.shape[1], bias_ref.shape[1]
    for part, ref in enumerate((a_ref, b_ref)):
        for i in range(3):
            first = i * WIDTH + part * PART_COLS
            ref[:, i * PART_COLS : (i + 1) * PART_COLS] = qkv_ref[:, first : first + PART_COLS]
    b_ref[:, 3 * PART_COLS : 3 * PART_COLS + WIDTH] = out_ref[...]
    place = lax.broadcasted_iota(jnp.int32, (few, SMALL), 1)

    def column(row, first):
        count = row.shape[1]
        at = lax.broadcasted_iota(jnp.int32, (few, count), 1)
        down = lax.broadcasted_iota(jnp.int32, (few, count), 0) + first
        return jnp.sum(jnp.where(at == down, row.astype(F32), 0.0), axis=1, keepdims=True)

    gains = jnp.where(place == 0, column(one_ref[...], 0), 0.0)
    gains = jnp.where(place == 1, column(two_ref[...], 0), gains)
    a_ref[:, A_COLS - SMALL :] = gains.astype(BF)
    bias = jnp.zeros((few, SMALL), F32)
    for i in range(share // few):
        bias = jnp.where(place == i, column(bias_ref[...], i * few), bias)
    b_ref[:, B_COLS - SMALL :] = bias.astype(BF)


def pack(w_qkv, w_out, gain_one, gain_two, b_up):
    few = w_qkv.shape[0]
    return pl.pallas_call(
        pack_kernel,
        out_shape=[
            jax.ShapeDtypeStruct((few, A_COLS), BF), jax.ShapeDtypeStruct((few, B_COLS), BF)
        ],
        compiler_params=params(),
        name="pack",
    )(w_qkv, w_out, gain_one[None], gain_two[None], b_up[None])


def join_kernel(info, *refs):
    own, other, outs = refs[:3], refs[3:6], refs[6:]
    first = info[1] == 0
    for mine, theirs, out in zip(own, other, outs):
        half = mine.shape[1] // 2
        cols = pl.ds(pl.multiple_of(info[1] * half, 128), half)
        mine, theirs = mine[:, cols].astype(F32), theirs[:, cols].astype(F32)
        out[...] = jnp.concatenate(
            [jnp.where(first, mine, theirs), jnp.where(first, theirs, mine)], axis=0
        ).astype(BF)


def join(info, own, other):
    shapes = [(2 * v.shape[0], v.shape[1] // 2) for v in own]
    return pl.pallas_call(
        join_kernel,
        grid_spec=pltpu.PrefetchScalarGridSpec(
            num_scalar_prefetch=1,
            grid=(1,),
            in_specs=[whole(*v.shape) for v in [*own, *other]],
            out_specs=[whole(*shape) for shape in shapes],
        ),
        out_shape=[jax.ShapeDtypeStruct(shape, BF) for shape in shapes],
        compiler_params=params(),
        name="join",
    )(info, *own, *other)


def before_kernel(info, tok_ref, cot_ref, x_ref, up_ref, down_ref, wide):
    pick = turn(first_row(info), pl.program_id(0) * TILE, TILE, True)
    wide[:, WIDTH - 128 :] = jnp.zeros((TILE, 128), F32)
    wide[:, : WIDTH - 1] = mm(pick, tok_ref[...])
    x_ref[...] = wide[...].astype(BF)
    wide[:, : WIDTH - 1] = mm(pick, cot_ref[...])
    grads = wide[...]
    up_ref[...] = grads.astype(BF)
    down_ref[...] = (grads - jnp.sum(grads, axis=1, keepdims=True) * (1.0 / WIDTH)).astype(BF)


def before(info, tokens, cotangent):
    shape = jax.ShapeDtypeStruct((ROWS, WIDTH), BF)
    return pl.pallas_call(
        before_kernel,
        grid_spec=pltpu.PrefetchScalarGridSpec(
            num_scalar_prefetch=1,
            grid=(ROWS // TILE,),
            in_specs=[whole(ROWS, WIDTH - 1)] * 2,
            out_specs=[row_tile(WIDTH)] * 3,
            scratch_shapes=[pltpu.VMEM((TILE, WIDTH), F32)],
        ),
        out_shape=[shape] * 3,
        compiler_params=params(),
        cost_estimate=cost(4 * ROWS * ROWS * WIDTH, 10 * ROWS * WIDTH),
        name="before",
    )(info, tokens, cotangent)


SPANS = ((0, 0, 256, 0), (256, 0, 512, 256), (512, 0, 768, 768), (768, 768, 256, 1536))


def tail_segments(info, axis):
    shape = (TILE, 1) if axis == 0 else (1, TILE)
    place = lax.broadcasted_iota(jnp.int32, shape, axis) + BIG + first_row(info)
    place = jnp.where(place >= ROWS, place - ROWS, place)
    found = jnp.zeros(shape, jnp.int32)
    bound = 0
    for j in range(3):
        bound = bound + info[2 + j]
        found = found + jnp.where(place >= bound, 1, 0)
    return found


def head_mask(head):
    place = lanes(2 * HEAD)
    return (place < HEAD) if head == 0 else (place >= HEAD)


def attend_pair(info, qkv, pair, out_ref, norm_ref, prob_ref, turned):
    cols = [pl.ds(pl.multiple_of(i * PART_COLS + pair * 2 * HEAD, 128), 2 * HEAD) for i in range(3)]
    causal = lax.broadcasted_iota(jnp.int32, (TILE, TILE), 0) >= lax.broadcasted_iota(
        jnp.int32, (TILE, TILE), 1
    )
    turned[...] = qkv[:, cols[1]].T
    for first, key_first, key_count, place in SPANS:
        queries = qkv[first : first + TILE, cols[0]]
        keys = turned[:, key_first : key_first + key_count]
        values = qkv[key_first : key_first + key_count, cols[2]]
        values = jnp.concatenate([values, jnp.ones_like(values)], axis=1)
        allowed = causal
        if first == BIG:
            allowed = causal & (tail_segments(info, 0) == tail_segments(info, 1))
        mixed = []
        for head in range(2):
            mine = jnp.where(head_mask(head), queries, 0) * BF(HEAD**-0.5)
            scores = mm(mine, keys)
            split = key_count - TILE
            last = jnp.where(allowed, scores[:, split:], -1e30)
            largest = jnp.max(last, axis=1, keepdims=True)
            if split:
                largest = jnp.maximum(largest, jnp.max(scores[:, :split], axis=1, keepdims=True))
            last = jnp.exp(last - largest).astype(BF)
            prob_ref[head, :, place + split : place + key_count] = last
            both = mm(last, values[split:])
            if split:
                early = jnp.exp(scores[:, :split] - largest).astype(BF)
                prob_ref[head, :, place : place + split] = early
                both += mm(early, values[:split])
            mixed.append(both)
        both = jnp.where(jnp.concatenate([head_mask(0)] * 2, axis=1), mixed[0], mixed[1])
        inverse = 1.0 / both[:, 2 * HEAD :]
        norm_ref[first : first + TILE, :] = inverse
        out_ref[first : first + TILE, :] = (both[:, : 2 * HEAD] * inverse).astype(BF)


def pair_cols(offset):
    return pl.BlockSpec((ROWS, 2 * HEAD), lambda i, *s: (0, offset + i))


PROB_SPEC = pl.BlockSpec((2, TILE, PROB_COLS), lambda i, *s: (i, 0, 0))
HEADS_SHAPES = [
    jax.ShapeDtypeStruct((ROWS, PART_COLS), BF),
    jax.ShapeDtypeStruct((ROWS, PART_COLS), F32),
    jax.ShapeDtypeStruct((2 * PART, TILE, PROB_COLS), BF),
]


def heads_a_kernel(info, x_ref, *rest):
    pieces, (normed_hbm, qkv_hbm, gains_ref, att_ref, norm_ref, prob_ref) = rest[:8], rest[8:14]
    store, normed, qkv, turned, sems, out_sems = rest[14:]
    step = pl.program_id(0)

    @pl.when(step == 0)
    def _():
        copies(info, pieces, by_half(store, sems))
        inverse, expanded = norm_parts(x_ref[...].astype(F32))
        expanded = expanded * inverse
        halves_arrived(store, sems)
        gains = store[:, 3 * PART_COLS :].astype(F32).T[:8]
        gains_ref[...] = gains
        normed[...] = (expanded * gains[:1]).astype(BF)
        pltpu.make_async_copy(normed, normed_hbm, out_sems.at[0]).start()
        for i in range(3):
            cols = slice(i * PART_COLS, (i + 1) * PART_COLS)
            qkv[:, cols] = mm(normed[...], store[:, cols]).astype(BF)
        pltpu.make_async_copy(qkv, qkv_hbm, out_sems.at[1]).start()

    attend_pair(info, qkv, step, att_ref, norm_ref, prob_ref, turned)

    @pl.when(step == PART - 1)
    def _():
        arrived(normed, out_sems.at[0])
        arrived(qkv, out_sems.at[1])


def heads_a(info, x, pieces):
    return pl.pallas_call(
        heads_a_kernel,
        grid_spec=pltpu.PrefetchScalarGridSpec(
            num_scalar_prefetch=1,
            grid=(PART,),
            in_specs=[whole(ROWS, WIDTH)] + [HBM] * 8,
            out_specs=[HBM, HBM, whole(8, WIDTH), pair_cols(0), pair_cols(0), PROB_SPEC],
            scratch_shapes=[
                pltpu.VMEM((WIDTH, A_COLS), BF), pltpu.VMEM((ROWS, WIDTH), BF),
                pltpu.VMEM((ROWS, 3 * PART_COLS), BF), TURNED, PAIR_SEMS, PAIR_SEMS,
            ],
        ),
        out_shape=[
            jax.ShapeDtypeStruct((ROWS, WIDTH), BF),
            jax.ShapeDtypeStruct((ROWS, 3 * PART_COLS), BF),
            jax.ShapeDtypeStruct((8, WIDTH), F32),
        ]
        + HEADS_SHAPES,
        compiler_params=params(),
        cost_estimate=cost(6 * ROWS * WIDTH * PART_COLS + 4 * 6 * 7 * TILE * TILE * 256, 20000000, 2752512),
        name="heads_a",
    )(info, x, *pieces)


def heads_b_kernel(info, normed_ref, gains_ref, a_att_hbm, x_hbm, *rest):
    pieces, (qkv_hbm, bias_ref, middle_hbm, second_hbm, att_ref, norm_ref, prob_ref) = rest[:8], rest[8:15]
    store, qkv, turned, att, x, middle, second, sems, in_sems, out_sems = rest[15:]
    step = pl.program_id(0)
    late = [
        pltpu.make_async_copy(a_att_hbm, att.at[:, pl.ds(0, PART_COLS)], in_sems.at[0]),
        pltpu.make_async_copy(x_hbm, x, in_sems.at[1]),
    ]

    @pl.when(step == 0)
    def _():
        copies(info, pieces, by_half(store, sems))
        for copy in late:
            copy.start()
        halves_arrived(store, sems)
        for i in range(3):
            cols = slice(i * PART_COLS, (i + 1) * PART_COLS)
            qkv[:, cols] = mm(normed_ref[...], store[:, cols]).astype(BF)
        bias_ref[...] = store[:, B_COLS - SMALL :].astype(F32).T[:8]
        pltpu.make_async_copy(qkv, qkv_hbm, out_sems.at[0]).start()

    attend_pair(info, qkv, step, att_ref, norm_ref, prob_ref, turned)
    att[:, pl.ds(pl.multiple_of(PART_COLS + step * 2 * HEAD, 128), 2 * HEAD)] = att_ref[...]

    @pl.when(step == PART - 1)
    def _():
        for copy in late:
            copy.wait()
        weights = store[:, 3 * PART_COLS : 3 * PART_COLS + WIDTH]
        for i in range(ROWS // TILE):
            rows = slice(i * TILE, (i + 1) * TILE)
            mixed = mm(att[rows, :], weights)
            mixed = mixed - jnp.sum(mixed, axis=1, keepdims=True) * (1.0 / WIDTH)
            value = x[rows, :].astype(F32) + jnp.where(lanes() == WIDTH - 1, 0.0, mixed)
            inverse, expanded = norm_parts(value)
            middle[rows, :] = value
            second[rows, :] = (expanded * inverse * gains_ref[1:2, :]).astype(BF)
            for j, (source, target) in enumerate(((middle, middle_hbm), (second, second_hbm))):
                pltpu.make_async_copy(source.at[rows], target.at[rows], out_sems.at[1 + j]).start()
        arrived(qkv, out_sems.at[0])
        arrived(middle, out_sems.at[1])
        arrived(second, out_sems.at[2])


def heads_b(info, normed, gains, a_att, x, pieces):
    return pl.pallas_call(
        heads_b_kernel,
        grid_spec=pltpu.PrefetchScalarGridSpec(
            num_scalar_prefetch=1,
            grid=(PART,),
            in_specs=[whole(ROWS, WIDTH), whole(8, WIDTH)] + [HBM] * 10,
            out_specs=[HBM, whole(8, WIDTH), HBM, HBM, pair_cols(0), pair_cols(0), PROB_SPEC],
            scratch_shapes=[
                pltpu.VMEM((WIDTH, B_COLS), BF), pltpu.VMEM((ROWS, 3 * PART_COLS), BF), TURNED,
                pltpu.VMEM((ROWS, WIDTH), BF), pltpu.VMEM((ROWS, WIDTH), BF),
                pltpu.VMEM((ROWS, WIDTH), F32), pltpu.VMEM((ROWS, WIDTH), BF),
                PAIR_SEMS, PAIR_SEMS, pltpu.SemaphoreType.DMA((3,)),
            ],
        ),
        out_shape=[
            jax.ShapeDtypeStruct((ROWS, 3 * PART_COLS), BF),
            jax.ShapeDtypeStruct((8, WIDTH), F32),
            jax.ShapeDtypeStruct((ROWS, WIDTH), F32),
            jax.ShapeDtypeStruct((ROWS, WIDTH), BF),
        ]
        + HEADS_SHAPES,
        compiler_params=params(),
        cost_estimate=cost(
            6 * ROWS * WIDTH * PART_COLS + 2 * ROWS * WIDTH * WIDTH + 4 * 6 * 7 * TILE * TILE * 256,
            25000000, 2752512,
        ),
        name="heads_b",
    )(info, normed, gains, a_att, x, *pieces)


GELU_A = 0.7978845608028654
GELU_B = 0.044715


def feed_kernel(info, second_ref, bias_ref, down_in_hbm, *rest):
    pieces, (act_ref, slope_ref, keep_hbm, send_hbm) = rest[:8], rest[8:12]
    store, sems, down_in, in_sem, stage, out_sem = rest[12:]
    step = pl.program_id(0)

    @pl.when(step == 0)
    def _():
        quarter_copies(info, pieces, store, sems)
        pltpu.make_async_copy(down_in_hbm, down_in, in_sem).start()

    cols = pl.ds(pl.multiple_of(step * WIDTH, WIDTH), WIDTH)
    arrived(store.at[:, cols], sems.at[step])
    weights = store[:, cols]
    for i in range(ROWS // TILE):
        rows = slice(i * TILE, (i + 1) * TILE)
        hidden = mm(second_ref[rows, :], weights) + bias_ref[...]
        square = hidden * hidden
        bent = jnp.tanh(hidden * (GELU_A + (GELU_A * GELU_B) * square))
        half = 0.5 + 0.5 * bent
        act_ref[rows, :] = (hidden * half).astype(BF)
        tilt = hidden * (0.5 * GELU_A + (1.5 * GELU_A * GELU_B) * square)
        slope_ref[rows, :] = (half + tilt * (1.0 - bent * bent)).astype(BF)

    @pl.when(step == 0)
    def _():
        arrived(down_in, in_sem)

    grads = mm_tn(act_ref[...], down_in[...])
    for i in range(8):
        slot = 8 * step + i
        stage[slot] = grads[96 * i : 96 * (i + 1)].astype(BF)
        place = place_at(info, 4 * step + (i >> 1))
        mine = info[1] == (i & 1)

        def put(target, slot=slot, place=place):
            pltpu.make_async_copy(stage.at[slot], target.at[place], out_sem).start()

        pl.when(mine)(functools.partial(put, keep_hbm))
        pl.when(jnp.logical_not(mine))(functools.partial(put, send_hbm))

    @pl.when(step == 3)
    def _():
        arrived(stage, out_sem)


def feed(info, second, down_in, bias, pieces):
    return pl.pallas_call(
        feed_kernel,
        grid_spec=pltpu.PrefetchScalarGridSpec(
            num_scalar_prefetch=1,
            grid=(4,),
            in_specs=[whole(ROWS, WIDTH), col_tile(1, WIDTH)] + [HBM] * 9,
            out_specs=[col_tile(ROWS, WIDTH)] * 2 + [HBM] * 2,
            scratch_shapes=[
                pltpu.VMEM((WIDTH, HIDDEN), BF), SLOT_SEMS, pltpu.VMEM((ROWS, WIDTH), BF),
                pltpu.SemaphoreType.DMA, pltpu.VMEM((32, 96, WIDTH), BF), pltpu.SemaphoreType.DMA,
            ],
        ),
        out_shape=[jax.ShapeDtypeStruct((ROWS, HIDDEN), BF)] * 2
        + [jax.ShapeDtypeStruct((CHIPS, 96, WIDTH), BF)] * 2,
        compiler_params=params(),
        cost_estimate=cost(4 * ROWS * WIDTH * HIDDEN, 6 * ROWS * HIDDEN + 4 * WIDTH * HIDDEN),
        name="feed",
    )(info, second, bias, down_in, *pieces)


UP_COLS = HIDDEN // 2 + SMALL, HIDDEN // 2


def spread_out(info, grads, stage, half=0):
    for device in range(32):
        value = grads[24 * device : 24 * (device + 1)].astype(BF)
        stage[info[1] ^ (device & 1), place_at(info, device >> 1, half)] = value


def back_kernel(info, down_in_ref, slope_ref, second_hbm, *rest):
    up_pieces, down_pieces, outs, weighted_hbm = rest[:8], rest[8:16], rest[16:20], rest[20]
    (down_store, down_sems, up_store, up_sems, second, in_sem, grads, weighted, stage, spare,
     out_sem) = rest[21:]
    step = pl.program_id(0)
    core = info[1]

    @pl.when(step == 0)
    def _():
        row_copies(info, down_pieces, down_store, down_sems)

    arrived(down_store.at[step], down_sems.at[step])

    @pl.when(step == 0)
    def _():
        quarter_copies(info, up_pieces, up_store, up_sems)
        pltpu.make_async_copy(second_hbm, second, in_sem).start()

    sums = jnp.zeros((1, WIDTH), F32)
    value = mm_nt(down_in_ref[...], down_store[step])
    for i in range(ROWS // TILE):
        rows = slice(i * TILE, (i + 1) * TILE)
        part = (slope_ref[rows, :].astype(F32) * value[rows]).astype(BF)
        grads[rows, :] = part
        sums += jnp.sum(part.astype(F32), axis=0, keepdims=True)
    for i in range(8):
        few = jnp.concatenate([sums[:, 96 * i : 96 * (i + 1)], jnp.zeros((1, 32), F32)], axis=1)
        few = jnp.broadcast_to(few, (24, SMALL)).astype(BF)
        spare[core ^ (i & 1), place_at(info, 4 * step + (i >> 1))] = few
    cols = pl.ds(pl.multiple_of(step * WIDTH, WIDTH), WIDTH)
    arrived(up_store.at[:, cols], up_sems.at[step])
    weights = up_store[:, cols]

    @pl.when(step == 0)
    def _():
        weighted[...] = mm_nt(grads[...], weights)
        arrived(second, in_sem)

    @pl.when(step > 0)
    def _():
        weighted[...] += mm_nt(grads[...], weights)

    @pl.when(step == 3)
    def _():
        pltpu.make_async_copy(weighted, weighted_hbm, out_sem.at[2]).start()

    found = mm_tn(second[...], grads[...])
    cols = pl.ds(pl.multiple_of((step & 1) * WIDTH, 128), WIDTH)
    for half in range(2):

        @pl.when((step >> 1) == half)
        def _(half=half):
            spread_out(info, found, stage.at[step], half)
            for which in range(2):
                pltpu.make_async_copy(
                    stage.at[step, which], outs[2 * half + which].at[:, :, cols], out_sem.at[0]
                ).start()

    @pl.when(step == 3)
    def _():
        for which in range(2):
            pltpu.make_async_copy(
                spare.at[which], outs[which].at[:, :, pl.ds(HIDDEN // 2, SMALL)], out_sem.at[1]
            ).start()
        arrived(stage, out_sem.at[0])
        arrived(spare, out_sem.at[1])
        arrived(weighted, out_sem.at[2])


def back(info, down_in, second, slope, up_pieces, down_pieces):
    return pl.pallas_call(
        back_kernel,
        grid_spec=pltpu.PrefetchScalarGridSpec(
            num_scalar_prefetch=1,
            grid=(4,),
            in_specs=[whole(ROWS, WIDTH), col_tile(ROWS, WIDTH)] + [HBM] * 17,
            out_specs=[HBM] * 5,
            scratch_shapes=[
                pltpu.VMEM((4, WIDTH, WIDTH), BF), SLOT_SEMS,
                pltpu.VMEM((WIDTH, HIDDEN), BF), SLOT_SEMS,
                pltpu.VMEM((ROWS, WIDTH), BF), pltpu.SemaphoreType.DMA,
                pltpu.VMEM((ROWS, WIDTH), BF),
                pltpu.VMEM((ROWS, WIDTH), F32),
                pltpu.VMEM((4, 2, CHIPS, 24, WIDTH), BF),
                pltpu.VMEM((2, CHIPS, 24, SMALL), BF),
                pltpu.SemaphoreType.DMA((3,)),
            ],
        ),
        out_shape=[jax.ShapeDtypeStruct((CHIPS, 24, UP_COLS[i // 2]), BF) for i in range(4)]
        + [jax.ShapeDtypeStruct((ROWS, WIDTH), F32)],
        compiler_params=params(),
        cost_estimate=cost(6 * ROWS * WIDTH * HIDDEN, 35000000),
        name="back",
    )(info, down_in, slope, second, *up_pieces, *down_pieces)


def middle_grad_kernel(info, weighted_ref, middle_ref, up_ref, gain_ref, *rest):
    pieces, (total_ref, mixed_ref, grad_ref, store, semaphore) = rest[:8], rest[8:]
    step = pl.program_id(0)

    @pl.when(step == 0)
    def _():
        copies(info, pieces, one_half(store, semaphore), OUT_COLS)

    inverse, expanded = norm_parts(middle_ref[...])
    total = up_ref[...].astype(F32) + norm_back(weighted_ref[...] * gain_ref[1:2, :], inverse, expanded)
    total_ref[...] = total
    mixed = (total - jnp.sum(total, axis=1, keepdims=True) * (1.0 / WIDTH)).astype(BF)
    mixed_ref[...] = mixed

    @pl.when(step == 0)
    def _():
        arrived(store, semaphore)

    grad_ref[...] = mm_nt(mixed, store[...]).astype(BF)


def middle_grad(info, weighted, middle, upstream, gains, pieces):
    return pl.pallas_call(
        middle_grad_kernel,
        grid_spec=pltpu.PrefetchScalarGridSpec(
            num_scalar_prefetch=1,
            grid=(ROWS // TILE,),
            in_specs=[row_tile(WIDTH)] * 3 + [whole(8, WIDTH)] + [HBM] * 8,
            out_specs=[row_tile(WIDTH)] * 3,
            scratch_shapes=[pltpu.VMEM((WIDTH, WIDTH), BF), pltpu.SemaphoreType.DMA],
        ),
        out_shape=[
            jax.ShapeDtypeStruct((ROWS, WIDTH), F32),
            jax.ShapeDtypeStruct((ROWS, WIDTH), BF),
            jax.ShapeDtypeStruct((ROWS, WIDTH), BF),
        ],
        compiler_params=params(),
        cost_estimate=cost(2 * ROWS * WIDTH * WIDTH, 18 * ROWS * WIDTH),
        name="middle_grad",
    )(info, weighted, middle, upstream, gains, *pieces)


def pair_grad(q_ref, k_ref, v_ref, grad_ref, att_ref, norm_ref, prob_ref, dq_ref, dk_ref, dv_ref, key_sum, value_sum, turned):
    factor = HEAD**-0.5
    turned[...] = v_ref[...].T
    key_sum[...] = jnp.zeros_like(key_sum)
    value_sum[...] = jnp.zeros_like(value_sum)
    for first, key_first, key_count, place in SPANS:
        rows = slice(first, first + TILE)
        keys_at = slice(key_first, key_first + key_count)
        queries = q_ref[rows, :]
        grads = (grad_ref[rows, :].astype(F32) * norm_ref[rows, :]).astype(BF)
        product = grads.astype(F32) * att_ref[rows, :].astype(F32)
        keys = k_ref[keys_at, :]
        values = turned[:, keys_at]
        parts = []
        for head in range(2):
            mask = head_mask(head)
            my_grads = jnp.where(mask, grads, 0)
            my_queries = jnp.where(mask, queries, 0)
            probs = prob_ref[head, :, place : place + key_count]
            inner = jnp.sum(jnp.where(mask, product, 0.0), axis=1, keepdims=True)
            slopes = probs.astype(F32) * (mm(my_grads, values) - inner)
            slopes = slopes.astype(BF)
            parts.append(mm(slopes, keys))
            value_sum[:, keys_at] += mm_tn(my_grads, probs)
            key_sum[:, keys_at] += mm_tn(my_queries, slopes)
        dq_ref[rows, :] = (jnp.where(head_mask(0), parts[0], parts[1]) * factor).astype(BF)
    dk_ref[...] = (key_sum[...].T * factor).astype(BF)
    dv_ref[...] = value_sum[...].T.astype(BF)


HEADS_COLS = 6 * PART_COLS + WIDTH


def attend_grad_kernel(info, a_att_hbm, b_att_hbm, mixed_hbm, *rest):
    ins, outs = rest[:7], rest[7:10]
    targets, (key_sum, value_sum, values, att, mixed, in_sems, stage, out_sem) = rest[10:12], rest[12:]
    step = pl.program_id(0)
    late = [
        pltpu.make_async_copy(a_att_hbm, att.at[:, pl.ds(0, PART_COLS)], in_sems.at[0]),
        pltpu.make_async_copy(b_att_hbm, att.at[:, pl.ds(PART_COLS, PART_COLS)], in_sems.at[1]),
        pltpu.make_async_copy(mixed_hbm, mixed, in_sems.at[2]),
    ]

    @pl.when(step == 0)
    def _():
        for copy in late:
            copy.start()

    pair_grad(*ins, *outs, key_sum, value_sum, values)

    @pl.when(step == 0)
    def _():
        for copy in late:
            copy.wait()
        spread_out(info, mm_tn(att[...], mixed[...]), stage)
        for which in range(2):
            pltpu.make_async_copy(
                stage.at[which], targets[which].at[:, :, pl.ds(6 * PART_COLS, WIDTH)], out_sem
            ).start()

    @pl.when(step == PART - 1)
    def _():
        arrived(stage, out_sem)


def heads_grad_kernel(info, normed_hbm, a_q, a_k, a_v, *rest):
    ins, outs = rest[:7], rest[9:12]
    targets, (key_sum, value_sum, values, kept, normed, turned, others, in_sems, stage, out_sem) = (
        rest[12:14], rest[14:]
    )
    step = pl.program_id(0)
    late = [
        pltpu.make_async_copy(source, target, in_sems.at[i])
        for i, (source, target) in enumerate(
            [(normed_hbm, normed)] + [(ref, others.at[i]) for i, ref in enumerate((a_q, a_k, a_v))]
        )
    ]

    @pl.when(step == 0)
    def _():
        for copy in late:
            copy.start()

    pair_grad(*ins, *outs, key_sum, value_sum, values)

    @pl.when(step == 0)
    def _():
        for copy in late:
            copy.wait()
        turned[...] = normed[...].T

    place = pl.ds(pl.multiple_of(step * 2 * HEAD, 2 * HEAD), 2 * HEAD)
    for i in range(3):
        kept[i, :, place] = outs[i][...]

    def weights_grad(i, ref):
        spread_out(info, mm(turned[...], ref[...]), stage.at[i])
        for which, target in enumerate(targets):
            pltpu.make_async_copy(
                stage.at[i, which], target.at[:, :, pl.ds(i * PART_COLS, PART_COLS)], out_sem
            ).start()

    for i in range(3):
        pl.when(step == i)(functools.partial(weights_grad, i, others.at[i]))

    @pl.when(step == PART - 1)
    def _():
        for i in range(3):
            weights_grad(3 + i, kept.at[i])
        arrived(stage, out_sem)


HEADS_GRADS = [jax.ShapeDtypeStruct((CHIPS, 24, HEADS_COLS), BF)] * 2


def pair_specs(first):
    return [
        pair_cols(0), pair_cols(PART), pair_cols(2 * PART),
        pair_cols(first), pair_cols(0), pair_cols(0), PROB_SPEC,
    ]


def attend_grad(info, attended, mixed, qkv, grad_attended, norms, probs):
    return pl.pallas_call(
        attend_grad_kernel,
        grid_spec=pltpu.PrefetchScalarGridSpec(
            num_scalar_prefetch=1,
            grid=(PART,),
            in_specs=[HBM] * 3 + pair_specs(0),
            out_specs=[pair_cols(0)] * 3 + [HBM] * 2,
            scratch_shapes=[pltpu.VMEM((2 * HEAD, ROWS), F32)] * 2
            + [
                TURNED, pltpu.VMEM((ROWS, WIDTH), BF), pltpu.VMEM((ROWS, WIDTH), BF),
                pltpu.SemaphoreType.DMA((3,)), pltpu.VMEM((2, CHIPS, 24, WIDTH), BF),
                pltpu.SemaphoreType.DMA,
            ],
        ),
        out_shape=[jax.ShapeDtypeStruct((ROWS, PART_COLS), BF)] * 3 + HEADS_GRADS,
        compiler_params=params(),
        cost_estimate=cost(8 * 6 * 7 * TILE * TILE * 256, 8 * ROWS * WIDTH + 5505024),
        name="attend_grad",
    )(info, *attended, mixed, qkv, qkv, qkv, grad_attended, attended[0], norms, probs)


def heads_grad(info, normed, parts, qkv, grad_attended, attended, norms, probs, keep, send):
    return pl.pallas_call(
        heads_grad_kernel,
        grid_spec=pltpu.PrefetchScalarGridSpec(
            num_scalar_prefetch=1,
            grid=(PART,),
            in_specs=[HBM] * 4 + pair_specs(PART) + [HBM] * 2,
            out_specs=[pair_cols(0)] * 3 + [HBM] * 2,
            scratch_shapes=[pltpu.VMEM((2 * HEAD, ROWS), F32)] * 2
            + [
                TURNED,
                pltpu.VMEM((3, ROWS, PART_COLS), BF),
                pltpu.VMEM((ROWS, WIDTH), BF),
                pltpu.VMEM((WIDTH, ROWS), BF),
                pltpu.VMEM((3, ROWS, PART_COLS), BF),
                pltpu.SemaphoreType.DMA((4,)),
                pltpu.VMEM((6, 2, CHIPS, 24, PART_COLS), BF),
                pltpu.SemaphoreType.DMA,
            ],
        ),
        out_shape=[jax.ShapeDtypeStruct((ROWS, PART_COLS), BF)] * 3 + HEADS_GRADS,
        input_output_aliases={12: 3, 13: 4},
        compiler_params=params(),
        cost_estimate=cost(
            8 * 6 * 7 * TILE * TILE * 256 + 6 * ROWS * WIDTH * WIDTH, 8 * ROWS * WIDTH + 10000000
        ),
        name="heads_grad",
    )(info, normed, *parts, qkv, qkv, qkv, grad_attended, attended, norms, probs, keep, send)


def last_kernel(info, act_ref, middle_ref, gain_ref, *rest):
    parts, x_hbm, total_hbm, down_pieces = rest[:6], rest[6], rest[7], rest[8:16]
    a_pieces, b_pieces, (out_ref, grad_ref) = rest[16:24], rest[24:32], rest[32:34]
    down_store, down_sems, a_store, b_store, a_sems, b_sems, grads, x, total, weighted, sems = rest[34:]
    step = pl.program_id(0)
    late = [
        pltpu.make_async_copy(source, target, sems.at[i])
        for i, (source, target) in enumerate(
            [(part, grads.at[i]) for i, part in enumerate(parts)] + [(x_hbm, x), (total_hbm, total)]
        )
    ]

    @pl.when(step == 0)
    def _():
        row_copies(info, down_pieces, down_store, down_sems)
        for i in range(4):
            arrived(down_store.at[i], down_sems.at[i])
        copies(info, a_pieces, by_half(a_store, a_sems))
        copies(info, b_pieces, by_half(b_store, b_sems))
        for copy in late:
            copy.start()

    branch = mm(act_ref[:, :WIDTH], down_store[0])
    for i in range(1, 4):
        branch += mm(act_ref[:, i * WIDTH : (i + 1) * WIDTH], down_store[i])
    branch = branch - jnp.sum(branch, axis=1, keepdims=True) * (1.0 / WIDTH)
    out_ref[...] = (middle_ref[...] + branch).astype(BF)

    for i in range(3):

        @pl.when(step == i + 1)
        def _(i=i):
            if i == 0:
                halves_arrived(a_store, a_sems)
                halves_arrived(b_store, b_sems)
            late[i].wait()
            late[3 + i].wait()
            cols = slice(i * PART_COLS, (i + 1) * PART_COLS)
            found = mm_nt(grads[i], a_store[:, cols]) + mm_nt(grads[3 + i], b_store[:, cols])
            weighted[...] = found if i == 0 else weighted[...] + found

    @pl.when(step == 3)
    def _():
        late[6].wait()
        late[7].wait()
        for i in range(ROWS // TILE):
            rows = slice(i * TILE, (i + 1) * TILE)
            inverse, expanded = norm_parts(x[rows, :].astype(F32))
            back = norm_back(weighted[rows, :] * gain_ref[0:1, :], inverse, expanded)
            grad_ref[rows, :] = (total[rows, :] + back).astype(BF)


def last(info, active, middle, parts, x, total, gains, down_pieces, a_pieces, b_pieces):
    return pl.pallas_call(
        last_kernel,
        grid_spec=pltpu.PrefetchScalarGridSpec(
            num_scalar_prefetch=1,
            grid=(ROWS // TILE,),
            in_specs=[row_tile(HIDDEN), row_tile(WIDTH), whole(8, WIDTH)] + [HBM] * 32,
            out_specs=[row_tile(WIDTH), whole(ROWS, WIDTH)],
            scratch_shapes=[
                pltpu.VMEM((4, WIDTH, WIDTH), BF), SLOT_SEMS,
                pltpu.VMEM((WIDTH, A_COLS), BF), pltpu.VMEM((WIDTH, B_COLS), BF), PAIR_SEMS, PAIR_SEMS,
                pltpu.VMEM((6, ROWS, PART_COLS), BF), pltpu.VMEM((ROWS, WIDTH), BF),
                pltpu.VMEM((ROWS, WIDTH), F32), pltpu.VMEM((ROWS, WIDTH), F32),
                pltpu.SemaphoreType.DMA((8,)),
            ],
        ),
        out_shape=[jax.ShapeDtypeStruct((ROWS, WIDTH), BF)] * 2,
        compiler_params=params(),
        cost_estimate=cost(2 * ROWS * WIDTH * HIDDEN + 6 * ROWS * WIDTH * WIDTH, 30000000),
        name="last",
    )(info, active, middle, gains, *parts, x, total, *down_pieces, *a_pieces, *b_pieces)


def turn_back_kernel(info, one_ref, two_ref, out_ref, grad_ref):
    pick = turn(first_row(info), pl.program_id(0) * TILE, TILE, False)
    out_ref[...] = mm(pick, one_ref[...]).astype(BF)[:, : WIDTH - 1]
    grad_ref[...] = mm(pick, two_ref[...]).astype(BF)[:, : WIDTH - 1]


def turn_back(info, one, two):
    return pl.pallas_call(
        turn_back_kernel,
        grid_spec=pltpu.PrefetchScalarGridSpec(
            num_scalar_prefetch=1,
            grid=(ROWS // TILE,),
            in_specs=[whole(ROWS, WIDTH)] * 2,
            out_specs=[row_tile(WIDTH - 1)] * 2,
        ),
        out_shape=[jax.ShapeDtypeStruct((ROWS, WIDTH - 1), BF)] * 2,
        compiler_params=params(),
        cost_estimate=cost(4 * ROWS * ROWS * WIDTH, 8 * ROWS * WIDTH),
        name="turn_back",
    )(info, one, two)


WAYS = {"core": (0, 1), "x": (0, 2), "y": (1, 0), "xy": (1, 2), "z1": (2, 0), "z2": (4, 0), "z3": (6, 0)}


def add_low(left, right):
    return (left.astype(F32) + right.astype(F32)).astype(BF)


class Cube:
    def __init__(self, sizes):
        self.sizes = sizes
        wide, narrow = lax.axis_index("wide"), lax.axis_index("narrow")
        self.place = jnp.stack([wide * 2 + (narrow >> 1), narrow & 1]).astype(jnp.int32)

    def hop(self, value, way):
        wide, narrow = WAYS[way]
        if wide == 0:
            return lax.ppermute(value, "narrow", [(i, i ^ narrow) for i in range(self.sizes["narrow"])])
        if narrow == 0:
            return lax.ppermute(value, "wide", [(i, i ^ wide) for i in range(self.sizes["wide"])])
        bits = wide * self.sizes["narrow"] + narrow
        count = self.sizes["wide"] * self.sizes["narrow"]
        return lax.ppermute(value, AXES, [(i, i ^ bits) for i in range(count)])

    def gather(self, block):
        others = yield [self.hop(block, way) for way in ("z1", "z2", "z3")]
        return (yield from self.across(jnp.concatenate([block] + others)))

    def gather_slowly(self, block):
        near = yield from self.along_z(block)
        return (yield from self.across(near))

    def along_z(self, block):
        for way in ("z1", "z2"):
            other = yield self.hop(block, way)
            block = jnp.concatenate([block, other])
        return block

    def across(self, near):
        far = yield [self.hop(near, way) for way in ("x", "y", "xy")]
        own = [near] + far
        twins = yield [self.hop(part, "core") for part in own]
        return own + twins

    def gather_rows(self, shard):
        near = yield from self.along_z(shard)
        return (yield from self.across(near))

    def blocks(self, info, shards):
        others = [self.hop(shard, "core") for shard in shards]
        return join(info, shards, others)

    def reduce_two(self, keeps, sends):
        gots = yield [self.hop(send, "core") for send in sends]
        for ways in ("yx", "xy"):
            count = keeps[0].shape[0] // 2
            sends = [add_low(keep[count:], got[count:]) for keep, got in zip(keeps, gots)]
            keeps = [add_low(keep[:count], got[:count]) for keep, got in zip(keeps, gots)]
            gots = yield [self.hop(send, way) for send, way in zip(sends, ways)]
        both = jnp.concatenate([add_low(keep, got) for keep, got in zip(keeps, gots)], axis=2)
        got = yield self.hop(both[2:], "z2")
        both = [add_low(both[i], got[i]) for i in range(2)]
        got = yield self.hop(both[1], "z1")
        return both[0].astype(F32) + got.astype(F32)

    def reduce(self, keep, send):
        got = yield self.hop(send, "core")
        both = [keep[4 * i : 4 * i + 4].astype(F32) + got[4 * i : 4 * i + 4].astype(F32) for i in range(4)]
        others = yield [self.hop(both[i].astype(BF), way) for i, way in ((1, "x"), (2, "y"), (3, "xy"))]
        both = sum([other.astype(F32) for other in others], both[0])
        others = yield [self.hop(both[i].astype(BF), way) for i, way in ((1, "z1"), (2, "z2"), (3, "z3"))]
        return sum([other.astype(F32) for other in others], both[0])


class Plain:
    def __init__(self):
        self.place = jnp.zeros((2,), jnp.int32)

    def blocks(self, info, shards):
        return shards

    def all_rows(self, shard):
        full = lax.all_gather(shard, AXES, axis=0, tiled=True)
        cols = full.shape[1]
        return full.reshape(4, 4, BLOCK, cols).transpose(1, 0, 2, 3).reshape(4, 4 * BLOCK, cols)

    def gather(self, shard):
        yield ()
        return self.split(self.all_rows(shard))

    gather_slowly = gather

    def gather_rows(self, shard):
        yield ()
        full = lax.all_gather(shard, AXES, axis=0, tiled=True).reshape(4, 4, 2, 2 * BLOCK, WIDTH)
        full = full.transpose(2, 1, 0, 3, 4).reshape(8, 8 * BLOCK, WIDTH)
        return [full[i] for i in range(8)]

    def split(self, full):
        cols = full.shape[2] // 2
        return [full[i, :, half * cols : (half + 1) * cols] for half in range(2) for i in range(4)]

    def reduce_two(self, keeps, sends):
        one = yield from self.reduce(keeps[0], sends[0])
        order = jnp.arange(CHIPS).reshape(2, 2, 4).transpose(1, 0, 2).reshape(-1)
        two = yield from self.reduce(keeps[1][order], sends[1][order])
        return jnp.concatenate([one, two], axis=1)

    def reduce(self, keep, send):
        yield ()
        full = jnp.stack([keep, send], axis=1).reshape(4, 4, -1, keep.shape[2])
        full = full.transpose(1, 0, 2, 3).reshape(-1, keep.shape[2])
        return lax.psum_scatter(full, AXES, scatter_dimension=0, tiled=True).astype(F32)


class Task:
    def __init__(self, steps):
        self.steps, self.flight, self.over, self.result = steps, (), False, None
        self.go(None)

    def go(self, arrived_now):
        try:
            self.flight = self.steps.send(arrived_now)
        except StopIteration as end:
            self.flight, self.over, self.result = (), True, end.value


def meet(values, *tasks, waiting=()):
    tasks = [task for task in tasks if not task.over]
    every = tasks + list(waiting)
    values, flights = lax.optimization_barrier((values, [task.flight for task in every]))
    for task, flight in zip(every, flights):
        task.flight = flight
    for task in tasks:
        task.go(task.flight)
    return values


def finish(values, *tasks):
    while not all(task.over for task in tasks):
        values = meet(values, *tasks)
    return values


def layer(sizes, tokens, lengths, gain_one, w_qkv, w_out, gain_two, w_up, b_up, w_down, cotangent):
    share, few = b_up.shape[0], gain_one.shape[0]
    links = Cube(sizes) if sizes["wide"] == 8 and sizes["narrow"] == 4 else Plain()
    info = jnp.concatenate([links.place, lengths[0]])

    a_block, b_block, up_block = links.blocks(
        info, [*pack(w_qkv, w_out, gain_one, gain_two, b_up), w_up]
    )
    group_a, group_b = Task(links.gather(a_block)), Task(links.gather_slowly(b_block))
    up = Task(links.gather_slowly(up_block))
    tokens, cotangent, w_down = meet((tokens, cotangent, w_down), group_a, group_b, waiting=(up,))
    down = Task(links.gather_rows(w_down))
    x, upstream, down_in = before(info, tokens, cotangent)
    x = meet(x, group_a, waiting=(group_b, down))
    x = meet(x, group_a, group_b, up)
    normed, qkv_a, gains, att_a, norms_a, probs_a = heads_a(info, x, group_a.result)
    normed, att_a, x = meet((normed, att_a, x), group_b, waiting=(up,))
    normed, att_a, x = meet((normed, att_a, x), group_b, up, down)
    qkv_b, bias, middle, second, att_b, norms_b, probs_b = heads_b(
        info, normed, gains, att_a, x, group_b.result
    )
    bias = bias[: HIDDEN // WIDTH].reshape(HIDDEN // WIDTH, -1, few)
    bias = bias.transpose(1, 0, 2).reshape(1, HIDDEN)
    second = meet(second, up, waiting=(down,))
    second = meet(second, up, down)
    active, slope, *grad_down = feed(info, second, down_in, bias, up.result)
    slope, grad_down = meet((slope, grad_down), down)
    downs = Task(links.reduce(*grad_down))
    slope = meet(slope, downs, down)
    *grad_up, weighted = back(info, down_in, second, slope, up.result, down.result)
    weighted, grad_up = meet((weighted, grad_up), downs)
    ups = Task(links.reduce_two(grad_up[::2], grad_up[1::2]))
    total, mixed, grad_att = middle_grad(info, weighted, middle, upstream, gains, group_b.result)
    total, mixed, grad_att = meet((total, mixed, grad_att), ups, downs)
    *parts, keep, send = attend_grad(info, (att_a, att_b), mixed, qkv_a, grad_att, norms_a, probs_a)
    parts, keep, send, grad_att = meet((parts, keep, send, grad_att), ups)
    *more, keep, send = heads_grad(
        info, normed, parts, qkv_b, grad_att, att_b, norms_b, probs_b, keep, send
    )
    active, more, keep, send = meet((active, more, keep, send), waiting=(ups,))
    heads = Task(links.reduce(keep, send))
    active, more = meet((active, more), heads, ups)
    output, grad_tokens = last(
        info, active, middle, list(parts) + list(more), x, total, gains, down.result,
        group_a.result, group_b.result,
    )
    output, grad_tokens = meet((output, grad_tokens), heads, ups)
    output, grad_tokens = turn_back(info, output, grad_tokens)
    output, grad_tokens = finish((output, grad_tokens), heads, ups, downs)

    first, bias_end = HIDDEN // 2, HIDDEN // 2 + SMALL
    grad_up = jnp.concatenate([ups.result[:, :first], ups.result[:, bias_end:]], axis=1)
    grad_out = heads.result[:, 6 * PART_COLS :]
    sums = ups.result[:, first : first + 96]
    if few >= 24:
        sums = sums[::24].reshape(-1)
    else:
        index = lax.axis_index("wide") * sizes["narrow"] + lax.axis_index("narrow")
        sums = lax.dynamic_slice_in_dim(sums[0], index % (24 // few) * share, share)
    grad_qkv = jnp.concatenate(
        [heads.result[:, (3 * part + i) * PART_COLS : (3 * part + i + 1) * PART_COLS]
         for i in range(3) for part in range(2)],
        axis=1,
    )
    return (
        output,
        grad_tokens,
        jnp.sum(w_qkv.astype(F32) * grad_qkv, axis=1) / gain_one.astype(F32),
        grad_qkv,
        grad_out,
        jnp.sum(w_up.astype(F32) * grad_up, axis=1) / gain_two.astype(F32),
        grad_up,
        sums,
        downs.result,
    )


def solution(mesh):
    rows, vector = P(AXES, None), P(AXES)
    sizes = dict(mesh.shape)
    return jax.shard_map(
        functools.partial(layer, sizes),
        mesh=mesh,
        in_specs=(rows, rows, vector, rows, rows, vector, rows, vector, rows, rows),
        out_specs=(rows, rows, vector, rows, rows, vector, rows, vector, rows),
        check_vma=False,
    )
```

```python
import functools

import jax
import jax.numpy as jnp
from jax import lax
from jax.experimental import pallas as pl
from jax.experimental.pallas import tpu as pltpu
from jax.sharding import PartitionSpec as P

AXES = ("wide", "narrow")
EPSILON = 1e-05
BF = jnp.bfloat16
F32 = jnp.float32
WIDTH = 768
HIDDEN = 3072
ROWS = 1024
TILE = 256
BIG = 768
PAIRS = 6
HEAD = 64
PROB_COLS = 1792
CHIPS = 16
BLOCK = 48
SHARE = 96
MINE = 1536
LIMIT = 56 * 1024 * 1024


def mm(left, right):
    return lax.dot_general(left, right, (((1,), (0,)), ((), ())), preferred_element_type=F32)


def mm_nt(left, right):
    return lax.dot_general(left, right, (((1,), (1,)), ((), ())), preferred_element_type=F32)


def mm_tn(left, right):
    return lax.dot_general(left, right, (((0,), (0,)), ((), ())), preferred_element_type=F32)


def lanes(width=WIDTH):
    return lax.broadcasted_iota(jnp.int32, (1, width), 1)


def norm_parts(rows):
    total = jnp.sum(rows, axis=1, keepdims=True)
    squares = jnp.sum(rows * rows, axis=1, keepdims=True)
    inverse = lax.rsqrt((squares + total * total) * (1.0 / WIDTH) + EPSILON)
    expanded = jnp.where(lanes() == WIDTH - 1, -total, rows)
    return inverse, expanded


def norm_back(weighted, inverse, expanded):
    inner = jnp.sum(weighted * expanded, axis=1, keepdims=True) * (1.0 / WIDTH)
    full = inverse * (weighted - (inverse * inverse * inner) * expanded)
    last = full[:, WIDTH - 1 :]
    return jnp.where(lanes() == WIDTH - 1, 0.0, full - last)


def turn(start, first_row, count, forward):
    rows = lax.broadcasted_iota(jnp.int32, (count, ROWS), 0) + first_row
    cols = lax.broadcasted_iota(jnp.int32, (count, ROWS), 1)
    if forward:
        source = rows + start
        source = jnp.where(source >= ROWS, source - ROWS, source)
    else:
        source = rows - start
        source = jnp.where(source < 0, source + ROWS, source)
    return jnp.where(cols == source, 1.0, 0.0).astype(BF)


def first_row(info):
    return jnp.where(info[2] == BIG, 0, jnp.where(info[3] == BIG, info[2], info[2] + info[3]))


def params(**more):
    return pltpu.CompilerParams(vmem_limit_bytes=LIMIT, **more)


def cost(flops, nbytes, transcendentals=0):
    return pl.CostEstimate(flops=flops, bytes_accessed=nbytes, transcendentals=transcendentals)


HBM = pl.BlockSpec(memory_space=pl.ANY)


def whole(*shape):
    return pl.BlockSpec(shape, lambda *i: (0,) * len(shape))


def row_tile(width, tile=TILE):
    return pl.BlockSpec((tile, width), lambda i, *s: (i, 0))


def col_tile(rows, width):
    return pl.BlockSpec((rows, width), lambda i, *s: (0, i))


def offset_of(place):
    return 4 * (place & 3) + (place >> 2)


def place_at(info, chip, half=0):
    offset = info[0] ^ chip
    x, y = offset & 1, (offset >> 1) & 1
    return (offset >> 2) + 4 * (x + 2 * y if half == 0 else y + 2 * x)


def copies(info, pieces, target, cols=None):
    for side in range(2):
        half = info[1] ^ side

        def start(side=side, half=half):
            for place in range(CHIPS):
                source = pieces[4 * side + place // 4].at[pl.ds((place % 4) * BLOCK, BLOCK)]
                if cols is not None:
                    source = source.at[:, pl.ds(*cols)]
                block = pl.multiple_of((info[0] ^ offset_of(place)) * BLOCK, 16)
                pltpu.make_async_copy(source, *target(half, block)).start()

        if cols is None:
            start()
        else:
            pl.when(half == 1)(start)


def up_copies(info, pieces, store, sems):
    for part in range(2):
        cols = pl.ds(part * WIDTH, WIDTH)
        for place in range(CHIPS):
            source = pieces[place // 4].at[pl.ds((place % 4) * BLOCK, BLOCK), cols]
            block = pl.multiple_of((info[0] ^ offset_of(place)) * BLOCK, 16)
            pltpu.make_async_copy(source, store.at[pl.ds(block, BLOCK), cols], sems.at[part]).start()


def down_copies(info, pieces, store, sems):
    for place in range(CHIPS):
        chip = info[0] ^ offset_of(place)
        first = pl.multiple_of((chip & 7) * SHARE, 16)
        pltpu.make_async_copy(
            pieces[place // 4].at[pl.ds((place % 4) * SHARE, SHARE)],
            store.at[chip >> 3, pl.ds(first, SHARE)],
            sems.at[chip >> 3],
        ).start()


def by_half(store, sems):
    width = store.shape[1] // 2

    def target(half, first):
        cols = pl.ds(pl.multiple_of(half * width, 128), width)
        return store.at[pl.ds(first, BLOCK), cols], sems.at[half]

    return target


def one_half(store, semaphore):
    return lambda half, first: (store.at[pl.ds(first, BLOCK)], semaphore)


def arrived(ref, semaphore):
    pltpu.make_async_copy(ref, ref, semaphore).wait()


def halves_arrived(store, sems, halves=(0, 1)):
    width = store.shape[1] // 2
    for half in halves:
        arrived(store.at[:, pl.ds(half * width, width)], sems.at[half])


OUT_COLS = (128, WIDTH)
TURNED = pltpu.VMEM((2 * HEAD, ROWS), BF)
PAIR_SEMS = pltpu.SemaphoreType.DMA((2,))
SLOT_SEMS = pltpu.SemaphoreType.DMA((4,))
PART = 3
PART_COLS = PART * 2 * HEAD
SMALL = 128
A_COLS = 3 * PART_COLS + SMALL
B_COLS = 3 * PART_COLS + WIDTH + SMALL


def pack_kernel(qkv_ref, out_ref, one_ref, two_ref, bias_ref, w_up_ref, a_ref, b_ref, up_ref):
    few, share = one_ref.shape[1], bias_ref.shape[1]
    for part, ref in enumerate((a_ref, b_ref)):
        for i in range(3):
            first = i * WIDTH + part * PART_COLS
            ref[:, i * PART_COLS : (i + 1) * PART_COLS] = qkv_ref[:, first : first + PART_COLS]
    b_ref[:, 3 * PART_COLS : 3 * PART_COLS + WIDTH] = out_ref[...]
    place = lax.broadcasted_iota(jnp.int32, (few, SMALL), 1)

    def column(row, first):
        count = row.shape[1]
        at = lax.broadcasted_iota(jnp.int32, (few, count), 1)
        down = lax.broadcasted_iota(jnp.int32, (few, count), 0) + first
        return jnp.sum(jnp.where(at == down, row.astype(F32), 0.0), axis=1, keepdims=True)

    gains = jnp.where(place == 0, column(one_ref[...], 0), 0.0)
    gains = jnp.where(place == 1, column(two_ref[...], 0), gains)
    a_ref[:, A_COLS - SMALL :] = gains.astype(BF)
    bias = jnp.zeros((few, SMALL), F32)
    for i in range(share // few):
        bias = jnp.where(place == i, column(bias_ref[...], i * few), bias)
    b_ref[:, B_COLS - SMALL :] = bias.astype(BF)
    weights = w_up_ref[...].astype(F32)
    for core in range(2):
        blocks = [weights[:, SHARE * (2 * i + core) : SHARE * (2 * i + core + 1)] for i in range(CHIPS)]
        up_ref[:, core * MINE : (core + 1) * MINE] = jnp.concatenate(blocks, axis=1).astype(BF)


def pack(w_qkv, w_out, gain_one, gain_two, b_up, w_up):
    few = w_qkv.shape[0]
    return pl.pallas_call(
        pack_kernel,
        out_shape=[
            jax.ShapeDtypeStruct((few, cols), BF) for cols in (A_COLS, B_COLS, HIDDEN)
        ],
        compiler_params=params(),
        name="pack",
    )(w_qkv, w_out, gain_one[None], gain_two[None], b_up[None], w_up)


def join_kernel(info, *refs):
    own, other, outs = refs[:3], refs[3:6], refs[6:]
    first = info[1] == 0
    for mine, theirs, out in zip(own, other, outs):
        half = mine.shape[1] // 2
        cols = pl.ds(pl.multiple_of(info[1] * half, 128), half)
        mine, theirs = mine[:, cols].astype(F32), theirs[:, cols].astype(F32)
        out[...] = jnp.concatenate(
            [jnp.where(first, mine, theirs), jnp.where(first, theirs, mine)], axis=0
        ).astype(BF)


def join(info, own, other):
    shapes = [(2 * v.shape[0], v.shape[1] // 2) for v in own]
    return pl.pallas_call(
        join_kernel,
        grid_spec=pltpu.PrefetchScalarGridSpec(
            num_scalar_prefetch=1,
            grid=(1,),
            in_specs=[whole(*v.shape) for v in [*own, *other]],
            out_specs=[whole(*shape) for shape in shapes],
        ),
        out_shape=[jax.ShapeDtypeStruct(shape, BF) for shape in shapes],
        compiler_params=params(),
        name="join",
    )(info, *own, *other)


def before_kernel(info, tok_ref, cot_ref, x_ref, up_ref, down_ref, wide):
    pick = turn(first_row(info), pl.program_id(0) * TILE, TILE, True)
    wide[:, WIDTH - 128 :] = jnp.zeros((TILE, 128), F32)
    wide[:, : WIDTH - 1] = mm(pick, tok_ref[...])
    x_ref[...] = wide[...].astype(BF)
    wide[:, : WIDTH - 1] = mm(pick, cot_ref[...])
    grads = wide[...]
    up_ref[...] = grads.astype(BF)
    down_ref[...] = (grads - jnp.sum(grads, axis=1, keepdims=True) * (1.0 / WIDTH)).astype(BF)


def before(info, tokens, cotangent):
    shape = jax.ShapeDtypeStruct((ROWS, WIDTH), BF)
    return pl.pallas_call(
        before_kernel,
        grid_spec=pltpu.PrefetchScalarGridSpec(
            num_scalar_prefetch=1,
            grid=(ROWS // TILE,),
            in_specs=[whole(ROWS, WIDTH - 1)] * 2,
            out_specs=[row_tile(WIDTH)] * 3,
            scratch_shapes=[pltpu.VMEM((TILE, WIDTH), F32)],
        ),
        out_shape=[shape] * 3,
        compiler_params=params(),
        cost_estimate=cost(4 * ROWS * ROWS * WIDTH, 10 * ROWS * WIDTH),
        name="before",
    )(info, tokens, cotangent)


SPANS = ((0, 0, 256, 0), (256, 0, 512, 256), (512, 0, 768, 768), (768, 768, 256, 1536))


def tail_segments(info, axis):
    shape = (TILE, 1) if axis == 0 else (1, TILE)
    place = lax.broadcasted_iota(jnp.int32, shape, axis) + BIG + first_row(info)
    place = jnp.where(place >= ROWS, place - ROWS, place)
    found = jnp.zeros(shape, jnp.int32)
    bound = 0
    for j in range(3):
        bound = bound + info[2 + j]
        found = found + jnp.where(place >= bound, 1, 0)
    return found


def head_mask(head):
    place = lanes(2 * HEAD)
    return (place < HEAD) if head == 0 else (place >= HEAD)


def attend_pair(info, qkv, pair, out_ref, norm_ref, prob_ref, turned):
    cols = [pl.ds(pl.multiple_of(i * PART_COLS + pair * 2 * HEAD, 128), 2 * HEAD) for i in range(3)]
    causal = lax.broadcasted_iota(jnp.int32, (TILE, TILE), 0) >= lax.broadcasted_iota(
        jnp.int32, (TILE, TILE), 1
    )
    turned[...] = qkv[:, cols[1]].T
    for first, key_first, key_count, place in SPANS:
        queries = qkv[first : first + TILE, cols[0]]
        keys = turned[:, key_first : key_first + key_count]
        values = qkv[key_first : key_first + key_count, cols[2]]
        values = jnp.concatenate([values, jnp.ones_like(values)], axis=1)
        allowed = causal
        if first == BIG:
            allowed = causal & (tail_segments(info, 0) == tail_segments(info, 1))
        mixed = []
        for head in range(2):
            mine = jnp.where(head_mask(head), queries, 0) * BF(HEAD**-0.5)
            scores = mm(mine, keys)
            split = key_count - TILE
            last = jnp.where(allowed, scores[:, split:], -1e30)
            largest = jnp.max(last, axis=1, keepdims=True)
            if split:
                largest = jnp.maximum(largest, jnp.max(scores[:, :split], axis=1, keepdims=True))
            last = jnp.exp(last - largest).astype(BF)
            prob_ref[head, :, place + split : place + key_count] = last
            both = mm(last, values[split:])
            if split:
                early = jnp.exp(scores[:, :split] - largest).astype(BF)
                prob_ref[head, :, place : place + split] = early
                both += mm(early, values[:split])
            mixed.append(both)
        both = jnp.where(jnp.concatenate([head_mask(0)] * 2, axis=1), mixed[0], mixed[1])
        inverse = 1.0 / both[:, 2 * HEAD :]
        norm_ref[first : first + TILE, :] = inverse
        out_ref[first : first + TILE, :] = (both[:, : 2 * HEAD] * inverse).astype(BF)


def pair_cols(offset):
    return pl.BlockSpec((ROWS, 2 * HEAD), lambda i, *s: (0, offset + i))


PROB_SPEC = pl.BlockSpec((2, TILE, PROB_COLS), lambda i, *s: (i, 0, 0))
HEADS_SHAPES = [
    jax.ShapeDtypeStruct((ROWS, PART_COLS), BF),
    jax.ShapeDtypeStruct((ROWS, PART_COLS), F32),
    jax.ShapeDtypeStruct((2 * PART, TILE, PROB_COLS), BF),
]


def heads_a_kernel(info, x_ref, *rest):
    pieces, (normed_hbm, qkv_hbm, gains_ref, att_ref, norm_ref, prob_ref) = rest[:8], rest[8:14]
    store, normed, qkv, turned, sems, out_sems = rest[14:]
    step = pl.program_id(0)

    @pl.when(step == 0)
    def _():
        copies(info, pieces, by_half(store, sems))
        inverse, expanded = norm_parts(x_ref[...].astype(F32))
        expanded = expanded * inverse
        halves_arrived(store, sems)
        gains = store[:, 3 * PART_COLS :].astype(F32).T[:8]
        gains_ref[...] = gains
        normed[...] = (expanded * gains[:1]).astype(BF)
        pltpu.make_async_copy(normed, normed_hbm, out_sems.at[0]).start()
        for i in range(3):
            cols = slice(i * PART_COLS, (i + 1) * PART_COLS)
            qkv[:, cols] = mm(normed[...], store[:, cols]).astype(BF)
        pltpu.make_async_copy(qkv, qkv_hbm, out_sems.at[1]).start()

    attend_pair(info, qkv, step, att_ref, norm_ref, prob_ref, turned)

    @pl.when(step == PART - 1)
    def _():
        arrived(normed, out_sems.at[0])
        arrived(qkv, out_sems.at[1])


def heads_a(info, x, pieces):
    return pl.pallas_call(
        heads_a_kernel,
        grid_spec=pltpu.PrefetchScalarGridSpec(
            num_scalar_prefetch=1,
            grid=(PART,),
            in_specs=[whole(ROWS, WIDTH)] + [HBM] * 8,
            out_specs=[HBM, HBM, whole(8, WIDTH), pair_cols(0), pair_cols(0), PROB_SPEC],
            scratch_shapes=[
                pltpu.VMEM((WIDTH, A_COLS), BF), pltpu.VMEM((ROWS, WIDTH), BF),
                pltpu.VMEM((ROWS, 3 * PART_COLS), BF), TURNED, PAIR_SEMS, PAIR_SEMS,
            ],
        ),
        out_shape=[
            jax.ShapeDtypeStruct((ROWS, WIDTH), BF),
            jax.ShapeDtypeStruct((ROWS, 3 * PART_COLS), BF),
            jax.ShapeDtypeStruct((8, WIDTH), F32),
        ]
        + HEADS_SHAPES,
        compiler_params=params(),
        cost_estimate=cost(6 * ROWS * WIDTH * PART_COLS + 4 * 6 * 7 * TILE * TILE * 256, 20000000, 2752512),
        name="heads_a",
    )(info, x, *pieces)


def heads_b_kernel(info, normed_ref, gains_ref, a_att_hbm, x_hbm, *rest):
    pieces, (qkv_hbm, bias_ref, middle_hbm, second_hbm, att_ref, norm_ref, prob_ref) = rest[:8], rest[8:15]
    store, qkv, turned, att, x, middle, second, sems, in_sems, out_sems = rest[15:]
    step = pl.program_id(0)
    late = [
        pltpu.make_async_copy(a_att_hbm, att.at[:, pl.ds(0, PART_COLS)], in_sems.at[0]),
        pltpu.make_async_copy(x_hbm, x, in_sems.at[1]),
    ]

    @pl.when(step == 0)
    def _():
        copies(info, pieces, by_half(store, sems))
        for copy in late:
            copy.start()
        halves_arrived(store, sems)
        for i in range(3):
            cols = slice(i * PART_COLS, (i + 1) * PART_COLS)
            qkv[:, cols] = mm(normed_ref[...], store[:, cols]).astype(BF)
        bias_ref[...] = store[:, B_COLS - SMALL :].astype(F32).T[:8]
        pltpu.make_async_copy(qkv, qkv_hbm, out_sems.at[0]).start()

    attend_pair(info, qkv, step, att_ref, norm_ref, prob_ref, turned)
    att[:, pl.ds(pl.multiple_of(PART_COLS + step * 2 * HEAD, 128), 2 * HEAD)] = att_ref[...]

    @pl.when(step == PART - 1)
    def _():
        for copy in late:
            copy.wait()
        weights = store[:, 3 * PART_COLS : 3 * PART_COLS + WIDTH]
        for i in range(ROWS // TILE):
            rows = slice(i * TILE, (i + 1) * TILE)
            mixed = mm(att[rows, :], weights)
            mixed = mixed - jnp.sum(mixed, axis=1, keepdims=True) * (1.0 / WIDTH)
            value = x[rows, :].astype(F32) + jnp.where(lanes() == WIDTH - 1, 0.0, mixed)
            inverse, expanded = norm_parts(value)
            middle[rows, :] = value
            second[rows, :] = (expanded * inverse * gains_ref[1:2, :]).astype(BF)
            for j, (source, target) in enumerate(((middle, middle_hbm), (second, second_hbm))):
                pltpu.make_async_copy(source.at[rows], target.at[rows], out_sems.at[1 + j]).start()
        arrived(qkv, out_sems.at[0])
        arrived(middle, out_sems.at[1])
        arrived(second, out_sems.at[2])


def heads_b(info, normed, gains, a_att, x, pieces):
    return pl.pallas_call(
        heads_b_kernel,
        grid_spec=pltpu.PrefetchScalarGridSpec(
            num_scalar_prefetch=1,
            grid=(PART,),
            in_specs=[whole(ROWS, WIDTH), whole(8, WIDTH)] + [HBM] * 10,
            out_specs=[HBM, whole(8, WIDTH), HBM, HBM, pair_cols(0), pair_cols(0), PROB_SPEC],
            scratch_shapes=[
                pltpu.VMEM((WIDTH, B_COLS), BF), pltpu.VMEM((ROWS, 3 * PART_COLS), BF), TURNED,
                pltpu.VMEM((ROWS, WIDTH), BF), pltpu.VMEM((ROWS, WIDTH), BF),
                pltpu.VMEM((ROWS, WIDTH), F32), pltpu.VMEM((ROWS, WIDTH), BF),
                PAIR_SEMS, PAIR_SEMS, pltpu.SemaphoreType.DMA((3,)),
            ],
        ),
        out_shape=[
            jax.ShapeDtypeStruct((ROWS, 3 * PART_COLS), BF),
            jax.ShapeDtypeStruct((8, WIDTH), F32),
            jax.ShapeDtypeStruct((ROWS, WIDTH), F32),
            jax.ShapeDtypeStruct((ROWS, WIDTH), BF),
        ]
        + HEADS_SHAPES,
        compiler_params=params(),
        cost_estimate=cost(
            6 * ROWS * WIDTH * PART_COLS + 2 * ROWS * WIDTH * WIDTH + 4 * 6 * 7 * TILE * TILE * 256,
            25000000, 2752512,
        ),
        name="heads_b",
    )(info, normed, gains, a_att, x, *pieces)


GELU_A = 0.7978845608028654
GELU_B = 0.044715


def tokens_copies(refs, second, down_in, sems):
    return [
        pltpu.make_async_copy(ref, (second, down_in)[i // 2].at[i % 2], sems.at[i])
        for i, ref in enumerate(refs)
    ]


def feed_kernel(info, bias_ref, *rest):
    ins, pieces, (act_hbm, slope_hbm, grad_hbm) = rest[:4], rest[4:8], rest[8:11]
    store, sems, second, down_in, in_sems, act, slope, stage, out_sems = rest[11:]
    late = tokens_copies(ins, second, down_in, in_sems)
    late[0].start()
    up_copies(info, pieces, store, sems)
    for i in (2, 1, 3):
        late[i].start()
    late[0].wait()
    sums = [None, None]
    for side in range(2):
        if side == 1:
            late[1].wait()
        for part in range(2):
            cols = slice(part * WIDTH, (part + 1) * WIDTH)
            if side == 0:
                arrived(store.at[:, pl.ds(part * WIDTH, WIDTH)], sems.at[part])
            slot = 2 * side + part
            for i in range(ROWS // TILE):
                rows = slice(i * TILE, (i + 1) * TILE)
                hidden = mm(second[side, rows, :], store[:, cols]) + bias_ref[:, cols]
                square = hidden * hidden
                bent = jnp.tanh(hidden * (GELU_A + (GELU_A * GELU_B) * square))
                half = 0.5 + 0.5 * bent
                act[slot, rows, :] = (hidden * half).astype(BF)
                tilt = hidden * (0.5 * GELU_A + (1.5 * GELU_A * GELU_B) * square)
                slope[slot, rows, :] = (half + tilt * (1.0 - bent * bent)).astype(BF)
            for source, target, which in ((act, act_hbm, 0), (slope, slope_hbm, 1)):
                pltpu.make_async_copy(source.at[slot], target.at[slot], out_sems.at[which]).start()
            if part == 0:
                late[2 + side].wait()
            found = mm_tn(act[slot], down_in[side])
            if side == 0:
                sums[part] = found
                continue
            total = sums[part] + found
            for i in range(8):
                slot = 8 * part + i
                stage[slot] = total[SHARE * i : SHARE * (i + 1)].astype(BF)
                place = place_at(info, slot)
                pltpu.make_async_copy(stage.at[slot], grad_hbm.at[place], out_sems.at[2]).start()
    arrived(act, out_sems.at[0])
    arrived(slope, out_sems.at[1])
    arrived(stage, out_sems.at[2])


BOTH = pltpu.VMEM((2, ROWS, WIDTH), BF)
FOUR = pltpu.VMEM((4, ROWS, WIDTH), BF)


def feed(info, second, other_second, down_in, other_down_in, bias, pieces):
    return pl.pallas_call(
        feed_kernel,
        grid_spec=pltpu.PrefetchScalarGridSpec(
            num_scalar_prefetch=1,
            grid=(1,),
            in_specs=[whole(1, MINE)] + [HBM] * 8,
            out_specs=[HBM] * 3,
            scratch_shapes=[
                pltpu.VMEM((WIDTH, MINE), BF), PAIR_SEMS, BOTH, BOTH, SLOT_SEMS, FOUR, FOUR,
                pltpu.VMEM((CHIPS, SHARE, WIDTH), BF), pltpu.SemaphoreType.DMA((3,)),
            ],
        ),
        out_shape=[jax.ShapeDtypeStruct((4, ROWS, WIDTH), BF)] * 2
        + [jax.ShapeDtypeStruct((CHIPS, SHARE, WIDTH), BF)],
        compiler_params=params(),
        cost_estimate=cost(4 * ROWS * WIDTH * HIDDEN, 6 * ROWS * HIDDEN + 4 * WIDTH * HIDDEN),
        name="feed",
    )(info, bias, second, other_second, down_in, other_down_in, *pieces)


UP_COLS = WIDTH + SMALL, WIDTH


def spread_out(info, grads, stage, half=0):
    for device in range(32):
        value = grads[24 * device : 24 * (device + 1)].astype(BF)
        stage[info[1] ^ (device & 1), place_at(info, device >> 1, half)] = value


def back_kernel(info, *rest):
    slope_hbm, ins, up_pieces, down_pieces = rest[0], rest[1:5], rest[5:9], rest[9:13]
    outs, own_hbm, other_hbm = rest[13:15], rest[15], rest[16]
    (down_store, down_sems, up_store, up_sems, second, down_in, in_sems, slope, slope_sems, grads,
     weighted, other, stage, spare, out_sems) = rest[17:]
    late = tokens_copies(ins, second, down_in, in_sems)
    slopes = [pltpu.make_async_copy(slope_hbm.at[i], slope.at[i], slope_sems.at[i]) for i in range(4)]
    late[2].start()
    down_copies(info, down_pieces, down_store, down_sems)
    slopes[0].start()
    up_copies(info, up_pieces, up_store, up_sems)
    for copy in (late[0], late[3], slopes[2], late[1], slopes[1], slopes[3]):
        copy.start()
    for part in range(2):
        cols = slice(part * WIDTH, (part + 1) * WIDTH)
        arrived(down_store.at[part], down_sems.at[part])
        for side in range(2):
            if part == 0:
                late[2 + side].wait()
            value = mm_nt(down_in[side], down_store[part])
            slopes[2 * side + part].wait()
            bias = jnp.zeros((1, WIDTH), F32)
            for i in range(ROWS // TILE):
                rows = slice(i * TILE, (i + 1) * TILE)
                few = (slope[2 * side + part, rows, :].astype(F32) * value[rows]).astype(BF)
                grads[side, rows, :] = few
                bias += jnp.sum(few.astype(F32), axis=0, keepdims=True)
            if side == 0:
                arrived(up_store.at[:, pl.ds(part * WIDTH, WIDTH)], up_sems.at[part])
            if part == 0:
                weighted[side] = mm_nt(grads[side], up_store[:, cols])
            elif side == 0:
                weighted[0] += mm_nt(grads[0], up_store[:, cols])
                pltpu.make_async_copy(weighted.at[0], own_hbm, out_sems.at[0]).start()
            else:
                other[...] = (weighted[1] + mm_nt(grads[1], up_store[:, cols])).astype(BF)
                pltpu.make_async_copy(other, other_hbm, out_sems.at[1]).start()
            if part == 0:
                late[side].wait()
            found = mm_tn(second[side], grads[side])
            if side == 0:
                sums, biases = found, bias
        total = sums + found
        for chip in range(CHIPS):
            block = total[BLOCK * chip : BLOCK * (chip + 1)].astype(BF)
            stage[part, place_at(info, chip, part)] = block
        pltpu.make_async_copy(
            stage.at[part], outs[part].at[:, :, pl.ds(0, WIDTH)], out_sems.at[2]
        ).start()
        row = biases + bias
        for i in range(8):
            few = jnp.concatenate(
                [row[:, SHARE * i : SHARE * (i + 1)], jnp.zeros((1, SMALL - SHARE), F32)], axis=1
            )
            spare[place_at(info, 8 * part + i)] = jnp.broadcast_to(few, (BLOCK, SMALL)).astype(BF)
    pltpu.make_async_copy(spare, outs[0].at[:, :, pl.ds(WIDTH, SMALL)], out_sems.at[3]).start()
    arrived(weighted.at[0], out_sems.at[0])
    arrived(other, out_sems.at[1])
    arrived(stage, out_sems.at[2])
    arrived(spare, out_sems.at[3])


def back(info, second, other_second, down_in, other_down_in, slope, up_pieces, down_pieces):
    return pl.pallas_call(
        back_kernel,
        grid_spec=pltpu.PrefetchScalarGridSpec(
            num_scalar_prefetch=1,
            grid=(1,),
            in_specs=[HBM] * 13,
            out_specs=[HBM] * 4,
            scratch_shapes=[
                pltpu.VMEM((2, WIDTH, WIDTH), BF), PAIR_SEMS, pltpu.VMEM((WIDTH, MINE), BF), PAIR_SEMS,
                BOTH, BOTH, SLOT_SEMS, FOUR, SLOT_SEMS, BOTH,
                pltpu.VMEM((2, ROWS, WIDTH), F32),
                pltpu.VMEM((ROWS, WIDTH), BF),
                pltpu.VMEM((2, CHIPS, BLOCK, WIDTH), BF),
                pltpu.VMEM((CHIPS, BLOCK, SMALL), BF),
                SLOT_SEMS,
            ],
        ),
        out_shape=[jax.ShapeDtypeStruct((CHIPS, BLOCK, cols), BF) for cols in UP_COLS]
        + [jax.ShapeDtypeStruct((ROWS, WIDTH), F32), jax.ShapeDtypeStruct((ROWS, WIDTH), BF)],
        compiler_params=params(),
        cost_estimate=cost(6 * ROWS * WIDTH * HIDDEN, 35000000),
        name="back",
    )(info, slope, second, other_second, down_in, other_down_in, *up_pieces, *down_pieces)


def middle_grad_kernel(info, weighted_ref, other_ref, middle_ref, up_ref, gain_ref, *rest):
    pieces, (total_ref, mixed_ref, grad_ref, store, semaphore) = rest[:8], rest[8:]
    step = pl.program_id(0)

    @pl.when(step == 0)
    def _():
        copies(info, pieces, one_half(store, semaphore), OUT_COLS)

    inverse, expanded = norm_parts(middle_ref[...])
    weighted = (weighted_ref[...] + other_ref[...].astype(F32)) * gain_ref[1:2, :]
    total = up_ref[...].astype(F32) + norm_back(weighted, inverse, expanded)
    total_ref[...] = total
    mixed = (total - jnp.sum(total, axis=1, keepdims=True) * (1.0 / WIDTH)).astype(BF)
    mixed_ref[...] = mixed

    @pl.when(step == 0)
    def _():
        arrived(store, semaphore)

    grad_ref[...] = mm_nt(mixed, store[...]).astype(BF)


def middle_grad(info, weighted, other, middle, upstream, gains, pieces):
    return pl.pallas_call(
        middle_grad_kernel,
        grid_spec=pltpu.PrefetchScalarGridSpec(
            num_scalar_prefetch=1,
            grid=(ROWS // TILE,),
            in_specs=[row_tile(WIDTH)] * 4 + [whole(8, WIDTH)] + [HBM] * 8,
            out_specs=[row_tile(WIDTH)] * 3,
            scratch_shapes=[pltpu.VMEM((WIDTH, WIDTH), BF), pltpu.SemaphoreType.DMA],
        ),
        out_shape=[
            jax.ShapeDtypeStruct((ROWS, WIDTH), F32),
            jax.ShapeDtypeStruct((ROWS, WIDTH), BF),
            jax.ShapeDtypeStruct((ROWS, WIDTH), BF),
        ],
        compiler_params=params(),
        cost_estimate=cost(2 * ROWS * WIDTH * WIDTH, 18 * ROWS * WIDTH),
        name="middle_grad",
    )(info, weighted, other, middle, upstream, gains, *pieces)


def pair_grad(q_ref, k_ref, v_ref, grad_ref, att_ref, norm_ref, prob_ref, dq_ref, dk_ref, dv_ref, key_sum, value_sum, turned):
    factor = HEAD**-0.5
    turned[...] = v_ref[...].T
    key_sum[...] = jnp.zeros_like(key_sum)
    value_sum[...] = jnp.zeros_like(value_sum)
    for first, key_first, key_count, place in SPANS:
        rows = slice(first, first + TILE)
        keys_at = slice(key_first, key_first + key_count)
        queries = q_ref[rows, :]
        grads = (grad_ref[rows, :].astype(F32) * norm_ref[rows, :]).astype(BF)
        product = grads.astype(F32) * att_ref[rows, :].astype(F32)
        keys = k_ref[keys_at, :]
        values = turned[:, keys_at]
        parts = []
        for head in range(2):
            mask = head_mask(head)
            my_grads = jnp.where(mask, grads, 0)
            my_queries = jnp.where(mask, queries, 0)
            probs = prob_ref[head, :, place : place + key_count]
            inner = jnp.sum(jnp.where(mask, product, 0.0), axis=1, keepdims=True)
            slopes = probs.astype(F32) * (mm(my_grads, values) - inner)
            slopes = slopes.astype(BF)
            parts.append(mm(slopes, keys))
            value_sum[:, keys_at] += mm_tn(my_grads, probs)
            key_sum[:, keys_at] += mm_tn(my_queries, slopes)
        dq_ref[rows, :] = (jnp.where(head_mask(0), parts[0], parts[1]) * factor).astype(BF)
    dk_ref[...] = (key_sum[...].T * factor).astype(BF)
    dv_ref[...] = value_sum[...].T.astype(BF)


HEADS_COLS = 6 * PART_COLS + WIDTH


def attend_grad_kernel(info, a_att_hbm, b_att_hbm, mixed_hbm, *rest):
    ins, outs = rest[:7], rest[7:10]
    targets, (key_sum, value_sum, values, att, mixed, in_sems, stage, out_sem) = rest[10:12], rest[12:]
    step = pl.program_id(0)
    late = [
        pltpu.make_async_copy(a_att_hbm, att.at[:, pl.ds(0, PART_COLS)], in_sems.at[0]),
        pltpu.make_async_copy(b_att_hbm, att.at[:, pl.ds(PART_COLS, PART_COLS)], in_sems.at[1]),
        pltpu.make_async_copy(mixed_hbm, mixed, in_sems.at[2]),
    ]

    @pl.when(step == 0)
    def _():
        for copy in late:
            copy.start()

    pair_grad(*ins, *outs, key_sum, value_sum, values)

    @pl.when(step == 0)
    def _():
        for copy in late:
            copy.wait()
        spread_out(info, mm_tn(att[...], mixed[...]), stage)
        for which in range(2):
            pltpu.make_async_copy(
                stage.at[which], targets[which].at[:, :, pl.ds(6 * PART_COLS, WIDTH)], out_sem
            ).start()

    @pl.when(step == PART - 1)
    def _():
        arrived(stage, out_sem)


def heads_grad_kernel(info, normed_hbm, a_q, a_k, a_v, *rest):
    ins, outs = rest[:7], rest[9:12]
    targets, (key_sum, value_sum, values, kept, normed, turned, others, in_sems, stage, out_sem) = (
        rest[12:14], rest[14:]
    )
    step = pl.program_id(0)
    late = [
        pltpu.make_async_copy(source, target, in_sems.at[i])
        for i, (source, target) in enumerate(
            [(normed_hbm, normed)] + [(ref, others.at[i]) for i, ref in enumerate((a_q, a_k, a_v))]
        )
    ]

    @pl.when(step == 0)
    def _():
        for copy in late:
            copy.start()

    pair_grad(*ins, *outs, key_sum, value_sum, values)

    @pl.when(step == 0)
    def _():
        for copy in late:
            copy.wait()
        turned[...] = normed[...].T

    place = pl.ds(pl.multiple_of(step * 2 * HEAD, 2 * HEAD), 2 * HEAD)
    for i in range(3):
        kept[i, :, place] = outs[i][...]

    def weights_grad(i, ref):
        spread_out(info, mm(turned[...], ref[...]), stage.at[i])
        for which, target in enumerate(targets):
            pltpu.make_async_copy(
                stage.at[i, which], target.at[:, :, pl.ds(i * PART_COLS, PART_COLS)], out_sem
            ).start()

    for i in range(3):
        pl.when(step == i)(functools.partial(weights_grad, i, others.at[i]))

    @pl.when(step == PART - 1)
    def _():
        for i in range(3):
            weights_grad(3 + i, kept.at[i])
        arrived(stage, out_sem)


HEADS_GRADS = [jax.ShapeDtypeStruct((CHIPS, 24, HEADS_COLS), BF)] * 2


def pair_specs(first):
    return [
        pair_cols(0), pair_cols(PART), pair_cols(2 * PART),
        pair_cols(first), pair_cols(0), pair_cols(0), PROB_SPEC,
    ]


def attend_grad(info, attended, mixed, qkv, grad_attended, norms, probs):
    return pl.pallas_call(
        attend_grad_kernel,
        grid_spec=pltpu.PrefetchScalarGridSpec(
            num_scalar_prefetch=1,
            grid=(PART,),
            in_specs=[HBM] * 3 + pair_specs(0),
            out_specs=[pair_cols(0)] * 3 + [HBM] * 2,
            scratch_shapes=[pltpu.VMEM((2 * HEAD, ROWS), F32)] * 2
            + [
                TURNED, pltpu.VMEM((ROWS, WIDTH), BF), pltpu.VMEM((ROWS, WIDTH), BF),
                pltpu.SemaphoreType.DMA((3,)), pltpu.VMEM((2, CHIPS, 24, WIDTH), BF),
                pltpu.SemaphoreType.DMA,
            ],
        ),
        out_shape=[jax.ShapeDtypeStruct((ROWS, PART_COLS), BF)] * 3 + HEADS_GRADS,
        compiler_params=params(),
        cost_estimate=cost(8 * 6 * 7 * TILE * TILE * 256, 8 * ROWS * WIDTH + 5505024),
        name="attend_grad",
    )(info, *attended, mixed, qkv, qkv, qkv, grad_attended, attended[0], norms, probs)


def heads_grad(info, normed, parts, qkv, grad_attended, attended, norms, probs, keep, send):
    return pl.pallas_call(
        heads_grad_kernel,
        grid_spec=pltpu.PrefetchScalarGridSpec(
            num_scalar_prefetch=1,
            grid=(PART,),
            in_specs=[HBM] * 4 + pair_specs(PART) + [HBM] * 2,
            out_specs=[pair_cols(0)] * 3 + [HBM] * 2,
            scratch_shapes=[pltpu.VMEM((2 * HEAD, ROWS), F32)] * 2
            + [
                TURNED,
                pltpu.VMEM((3, ROWS, PART_COLS), BF),
                pltpu.VMEM((ROWS, WIDTH), BF),
                pltpu.VMEM((WIDTH, ROWS), BF),
                pltpu.VMEM((3, ROWS, PART_COLS), BF),
                pltpu.SemaphoreType.DMA((4,)),
                pltpu.VMEM((6, 2, CHIPS, 24, PART_COLS), BF),
                pltpu.SemaphoreType.DMA,
            ],
        ),
        out_shape=[jax.ShapeDtypeStruct((ROWS, PART_COLS), BF)] * 3 + HEADS_GRADS,
        input_output_aliases={12: 3, 13: 4},
        compiler_params=params(),
        cost_estimate=cost(
            8 * 6 * 7 * TILE * TILE * 256 + 6 * ROWS * WIDTH * WIDTH, 8 * ROWS * WIDTH + 10000000
        ),
        name="heads_grad",
    )(info, normed, *parts, qkv, qkv, qkv, grad_attended, attended, norms, probs, keep, send)


def centred(branch):
    return branch - jnp.sum(branch, axis=1, keepdims=True) * (1.0 / WIDTH)


def last_kernel(info, act_ref, middle_ref, gain_ref, *rest):
    parts, x_hbm, total_hbm, down_pieces = rest[:6], rest[6], rest[7], rest[8:12]
    a_pieces, b_pieces, (out_ref, other_ref, grad_ref) = rest[12:20], rest[20:28], rest[28:31]
    down_store, down_sems, a_store, b_store, a_sems, b_sems, grads, x, total, weighted, sems = rest[31:]
    step = pl.program_id(0)
    late = [
        pltpu.make_async_copy(source, target, sems.at[i])
        for i, (source, target) in enumerate(
            [(part, grads.at[i]) for i, part in enumerate(parts)] + [(x_hbm, x), (total_hbm, total)]
        )
    ]

    @pl.when(step == 0)
    def _():
        down_copies(info, down_pieces, down_store, down_sems)
        for i in range(2):
            arrived(down_store.at[i], down_sems.at[i])
        copies(info, a_pieces, by_half(a_store, a_sems))
        copies(info, b_pieces, by_half(b_store, b_sems))
        for copy in late:
            copy.start()

    branch = mm(act_ref[0], down_store[0]) + mm(act_ref[1], down_store[1])
    out_ref[...] = middle_ref[...] + centred(branch)
    branch = mm(act_ref[2], down_store[0]) + mm(act_ref[3], down_store[1])
    other_ref[...] = centred(branch).astype(BF)

    for i in range(3):

        @pl.when(step == i + 1)
        def _(i=i):
            if i == 0:
                halves_arrived(a_store, a_sems)
                halves_arrived(b_store, b_sems)
            late[i].wait()
            late[3 + i].wait()
            cols = slice(i * PART_COLS, (i + 1) * PART_COLS)
            found = mm_nt(grads[i], a_store[:, cols]) + mm_nt(grads[3 + i], b_store[:, cols])
            weighted[...] = found if i == 0 else weighted[...] + found

    @pl.when(step == 3)
    def _():
        late[6].wait()
        late[7].wait()
        for i in range(ROWS // TILE):
            rows = slice(i * TILE, (i + 1) * TILE)
            inverse, expanded = norm_parts(x[rows, :].astype(F32))
            back = norm_back(weighted[rows, :] * gain_ref[0:1, :], inverse, expanded)
            grad_ref[rows, :] = (total[rows, :] + back).astype(BF)


def last(info, active, middle, parts, x, total, gains, down_pieces, a_pieces, b_pieces):
    act_tile = pl.BlockSpec((4, TILE, WIDTH), lambda i, *s: (0, i, 0))
    return pl.pallas_call(
        last_kernel,
        grid_spec=pltpu.PrefetchScalarGridSpec(
            num_scalar_prefetch=1,
            grid=(ROWS // TILE,),
            in_specs=[act_tile, row_tile(WIDTH), whole(8, WIDTH)] + [HBM] * 28,
            out_specs=[row_tile(WIDTH)] * 2 + [whole(ROWS, WIDTH)],
            scratch_shapes=[
                pltpu.VMEM((2, WIDTH, WIDTH), BF), PAIR_SEMS,
                pltpu.VMEM((WIDTH, A_COLS), BF), pltpu.VMEM((WIDTH, B_COLS), BF), PAIR_SEMS, PAIR_SEMS,
                pltpu.VMEM((6, ROWS, PART_COLS), BF), pltpu.VMEM((ROWS, WIDTH), BF),
                pltpu.VMEM((ROWS, WIDTH), F32), pltpu.VMEM((ROWS, WIDTH), F32),
                pltpu.SemaphoreType.DMA((8,)),
            ],
        ),
        out_shape=[jax.ShapeDtypeStruct((ROWS, WIDTH), dtype) for dtype in (F32, BF, BF)],
        compiler_params=params(),
        cost_estimate=cost(2 * ROWS * WIDTH * HIDDEN + 6 * ROWS * WIDTH * WIDTH, 30000000),
        name="last",
    )(info, active, middle, gains, *parts, x, total, *down_pieces, *a_pieces, *b_pieces)


def turn_back_kernel(info, own_ref, other_ref, two_ref, out_ref, grad_ref, one):
    step = pl.program_id(0)

    @pl.when(step == 0)
    def _():
        one[...] = (own_ref[...] + other_ref[...].astype(F32)).astype(BF)

    pick = turn(first_row(info), step * TILE, TILE, False)
    out_ref[...] = mm(pick, one[...]).astype(BF)[:, : WIDTH - 1]
    grad_ref[...] = mm(pick, two_ref[...]).astype(BF)[:, : WIDTH - 1]


def turn_back(info, own, other, two):
    return pl.pallas_call(
        turn_back_kernel,
        grid_spec=pltpu.PrefetchScalarGridSpec(
            num_scalar_prefetch=1,
            grid=(ROWS // TILE,),
            in_specs=[whole(ROWS, WIDTH)] * 3,
            out_specs=[row_tile(WIDTH - 1)] * 2,
            scratch_shapes=[pltpu.VMEM((ROWS, WIDTH), BF)],
        ),
        out_shape=[jax.ShapeDtypeStruct((ROWS, WIDTH - 1), BF)] * 2,
        compiler_params=params(),
        cost_estimate=cost(4 * ROWS * ROWS * WIDTH, 8 * ROWS * WIDTH),
        name="turn_back",
    )(info, own, other, two)


WAYS = {"core": (0, 1), "x": (0, 2), "y": (1, 0), "xy": (1, 2), "z1": (2, 0), "z2": (4, 0), "z3": (6, 0)}


def add_low(left, right):
    return (left.astype(F32) + right.astype(F32)).astype(BF)


class Cube:
    def __init__(self, sizes):
        self.sizes = sizes
        wide, narrow = lax.axis_index("wide"), lax.axis_index("narrow")
        self.place = jnp.stack([wide * 2 + (narrow >> 1), narrow & 1]).astype(jnp.int32)

    def hop(self, value, way):
        wide, narrow = WAYS[way]
        if wide == 0:
            return lax.ppermute(value, "narrow", [(i, i ^ narrow) for i in range(self.sizes["narrow"])])
        if narrow == 0:
            return lax.ppermute(value, "wide", [(i, i ^ wide) for i in range(self.sizes["wide"])])
        bits = wide * self.sizes["narrow"] + narrow
        count = self.sizes["wide"] * self.sizes["narrow"]
        return lax.ppermute(value, AXES, [(i, i ^ bits) for i in range(count)])

    def gather(self, block):
        others = yield [self.hop(block, way) for way in ("z1", "z2", "z3")]
        return (yield from self.across(jnp.concatenate([block] + others)))

    def gather_slowly(self, block):
        near = yield from self.along_z(block)
        return (yield from self.across(near))

    def along_z(self, block):
        for way in ("z1", "z2"):
            other = yield self.hop(block, way)
            block = jnp.concatenate([block, other])
        return block

    def across(self, near):
        own = yield from self.plane(near)
        twins = yield [self.hop(part, "core") for part in own]
        return own + twins

    def plane(self, near):
        far = yield [self.hop(near, way) for way in ("x", "y", "xy")]
        return [near] + far

    def gather_mine(self, block):
        near = yield from self.along_z(block)
        return (yield from self.plane(near))

    def exchange(self, value):
        return (yield self.hop(value, "core"))

    def blocks(self, info, shards):
        others = [self.hop(shard, "core") for shard in shards]
        return join(info, shards, others)

    def reduce_up(self, keeps):
        for ways in ("yx", "xy"):
            count = keeps[0].shape[0] // 2
            gots = yield [self.hop(keep[count:], way) for keep, way in zip(keeps, ways)]
            keeps = [add_low(keep[:count], got) for keep, got in zip(keeps, gots)]
        both = jnp.concatenate(keeps, axis=2)
        got = yield self.hop(both[2:], "z2")
        both = add_low(both[:2], got)
        got = yield self.hop(both[1], "z1")
        total = both[0].astype(F32) + got.astype(F32)
        sums = total[0, WIDTH : WIDTH + SHARE]
        total = jnp.concatenate([total[:, :WIDTH], total[:, WIDTH + SMALL :]], axis=1)
        total = total.reshape(2, -1, MINE)
        core = self.place[1]
        mine = lax.dynamic_index_in_dim(total, core, 0, False)
        got = yield self.hop(lax.dynamic_index_in_dim(total, 1 - core, 0, False), "core")
        first = core == 0
        return jnp.concatenate([jnp.where(first, mine, got), jnp.where(first, got, mine)], axis=1), sums

    def reduce_mine(self, keep):
        both = [keep[4 * i : 4 * i + 4] for i in range(4)]
        others = yield [self.hop(both[i], way) for i, way in ((1, "x"), (2, "y"), (3, "xy"))]
        return (yield from self.sum_z(sum([other.astype(F32) for other in others], both[0].astype(F32))))

    def sum_z(self, both):
        others = yield [self.hop(both[i].astype(BF), way) for i, way in ((1, "z1"), (2, "z2"), (3, "z3"))]
        return sum([other.astype(F32) for other in others], both[0])

    def reduce(self, keep, send):
        got = yield self.hop(send, "core")
        both = [keep[4 * i : 4 * i + 4].astype(F32) + got[4 * i : 4 * i + 4].astype(F32) for i in range(4)]
        others = yield [self.hop(both[i].astype(BF), way) for i, way in ((1, "x"), (2, "y"), (3, "xy"))]
        return (yield from self.sum_z(sum([other.astype(F32) for other in others], both[0])))


class Plain:
    def __init__(self, sizes):
        self.sizes = sizes
        self.core = (lax.axis_index("narrow") & 1).astype(jnp.int32)
        self.place = jnp.stack([jnp.zeros_like(self.core), self.core])

    def exchange(self, value):
        count = self.sizes["narrow"]
        other = lax.ppermute(value, "narrow", [(i, i ^ 1) for i in range(count)])
        yield ()
        return other

    def blocks(self, info, shards):
        return shards

    def by_place(self, rows):
        return rows.reshape(4, 4, -1, rows.shape[1]).transpose(1, 0, 2, 3).reshape(4, -1, rows.shape[1])

    def by_chip(self, blocks):
        return blocks.reshape(4, 4, *blocks.shape[1:]).swapaxes(0, 1).reshape(blocks.shape)

    def mine_first(self, one, two):
        first = self.core == 0
        return jnp.where(first, one, two), jnp.where(first, two, one)

    def gather(self, shard):
        yield ()
        full = self.by_place(lax.all_gather(shard, AXES, axis=0, tiled=True))
        cols = full.shape[2] // 2
        halves = self.mine_first(full[:, :, :cols], full[:, :, cols:])
        return [half[i] for half in halves for i in range(4)]

    gather_slowly = gather

    def gather_mine(self, shard):
        yield ()
        full = lax.all_gather(shard, AXES, axis=0, tiled=True)
        if full.shape[0] == WIDTH:
            one, two = full[:, :MINE], full[:, MINE:]
        else:
            one, two = [
                full.reshape(CHIPS, 2, SHARE, WIDTH)[:, i].reshape(MINE, WIDTH) for i in range(2)
            ]
        full = self.by_place(self.mine_first(one, two)[0])
        return [full[i] for i in range(4)]

    def scatter(self, full):
        return lax.psum_scatter(full, AXES, scatter_dimension=0, tiled=True).astype(F32)

    def apart(self, value):
        return self.mine_first(value, jnp.zeros_like(value))

    def reduce_up(self, keeps):
        yield ()
        order = jnp.arange(CHIPS).reshape(2, 2, 4).transpose(1, 0, 2).reshape(-1)
        one, two = self.by_chip(keeps[0]), self.by_chip(keeps[1][order])
        sums = jnp.stack(self.apart(one[:, 0, WIDTH : WIDTH + SHARE].astype(F32)), axis=1)
        both = jnp.concatenate([one[:, :, :WIDTH], two], axis=2).reshape(WIDTH, MINE)
        both = jnp.concatenate(self.apart(both), axis=1)
        return self.scatter(both), self.scatter(sums.reshape(HIDDEN, 1))[:, 0]

    def reduce_mine(self, keep):
        yield ()
        full = jnp.stack(self.apart(self.by_chip(keep)), axis=1)
        return self.scatter(full.reshape(HIDDEN, WIDTH))

    def reduce(self, keep, send):
        yield ()
        full = jnp.stack(self.mine_first(self.by_chip(keep), self.by_chip(send)), axis=1)
        return self.scatter(full.reshape(WIDTH, -1))


class Task:
    def __init__(self, steps):
        self.steps, self.flight, self.over, self.result = steps, (), False, None
        self.go(None)

    def go(self, arrived_now):
        try:
            self.flight = self.steps.send(arrived_now)
        except StopIteration as end:
            self.flight, self.over, self.result = (), True, end.value


def meet(values, *tasks, waiting=()):
    tasks = [task for task in tasks if not task.over]
    every = tasks + list(waiting)
    values, flights = lax.optimization_barrier((values, [task.flight for task in every]))
    for task, flight in zip(every, flights):
        task.flight = flight
    for task in tasks:
        task.go(task.flight)
    return values


def finish(values, *tasks):
    while not all(task.over for task in tasks):
        values = meet(values, *tasks)
    return values


def layer(sizes, tokens, lengths, gain_one, w_qkv, w_out, gain_two, w_up, b_up, w_down, cotangent):
    share, few = b_up.shape[0], gain_one.shape[0]
    links = (Cube if sizes["wide"] == 8 and sizes["narrow"] == 4 else Plain)(sizes)
    info = jnp.concatenate([links.place, lengths[0]])
    core = info[1]

    a_block, b_block, up_block = links.blocks(info, pack(w_qkv, w_out, gain_one, gain_two, b_up, w_up))
    group_a, group_b = Task(links.gather(a_block)), Task(links.gather_slowly(b_block))
    up = Task(links.gather_mine(up_block))
    tokens, cotangent, w_down = meet((tokens, cotangent, w_down), group_a, group_b, waiting=(up,))
    down = Task(links.gather_mine(w_down))
    x, upstream, down_in = before(info, tokens, cotangent)
    x = meet(x, group_a, waiting=(group_b, down))
    x, down_in = meet((x, down_in), group_a, group_b, up)
    other_down_in = Task(links.exchange(down_in))
    normed, qkv_a, gains, att_a, norms_a, probs_a = heads_a(info, x, group_a.result)
    normed, att_a, x = meet((normed, att_a, x), group_b, other_down_in, waiting=(up,))
    normed, att_a, x = meet((normed, att_a, x), group_b, up, down)
    qkv_b, bias, middle, second, att_b, norms_b, probs_b = heads_b(
        info, normed, gains, att_a, x, group_b.result
    )
    bias = bias[: share // few].reshape(share // few, -1, few).transpose(1, 0, 2)
    bias = bias.reshape(CHIPS, 2, SHARE)
    bias = jnp.where(core == 0, bias[:, 0], bias[:, 1]).reshape(1, MINE)
    bias, second = meet((bias, second), up, waiting=(down,))
    other_second = Task(links.exchange(second))
    bias = meet(bias, other_second, down)
    inputs = second, other_second.result, down_in, other_down_in.result
    active, slope, grad_down = feed(info, *inputs, bias, up.result)
    slope, grad_down = meet((slope, grad_down), down)
    downs = Task(links.reduce_mine(grad_down))
    *grad_up, weighted, other_weighted = back(info, *inputs, slope, up.result, down.result)
    weighted, other_weighted, grad_up = meet((weighted, other_weighted, grad_up), downs)
    other_weighted = Task(links.exchange(other_weighted))
    ups = Task(links.reduce_up(grad_up))
    weighted = finish(weighted, other_weighted)
    total, mixed, grad_att = middle_grad(
        info, weighted, other_weighted.result, middle, upstream, gains, group_b.result
    )
    total, mixed, grad_att = meet((total, mixed, grad_att), downs)
    *parts, keep, send = attend_grad(info, (att_a, att_b), mixed, qkv_a, grad_att, norms_a, probs_a)
    parts, keep, send, grad_att = meet((parts, keep, send, grad_att), ups)
    *more, keep, send = heads_grad(
        info, normed, parts, qkv_b, grad_att, att_b, norms_b, probs_b, keep, send
    )
    active, more, keep, send = meet((active, more, keep, send), waiting=(ups,))
    heads = Task(links.reduce(keep, send))
    active, more = meet((active, more), heads, ups)
    output, other_output, grad_tokens = last(
        info, active, middle, list(parts) + list(more), x, total, gains, down.result,
        group_a.result, group_b.result,
    )
    output, grad_tokens, other_output = meet((output, grad_tokens, other_output), heads, ups)
    other_output = Task(links.exchange(other_output))
    output, grad_tokens = meet((output, grad_tokens), other_output)
    output, grad_tokens = turn_back(info, output, other_output.result, grad_tokens)
    output, grad_tokens = finish((output, grad_tokens), heads, ups, downs)

    grad_up, sums = ups.result
    grad_up = grad_up.reshape(few, 2, CHIPS, SHARE).transpose(0, 2, 1, 3).reshape(few, HIDDEN)
    grad_out = heads.result[:, 6 * PART_COLS :]
    grad_qkv = jnp.concatenate(
        [heads.result[:, (3 * part + i) * PART_COLS : (3 * part + i + 1) * PART_COLS]
         for i in range(3) for part in range(2)],
        axis=1,
    )
    return (
        output,
        grad_tokens,
        jnp.sum(w_qkv.astype(F32) * grad_qkv, axis=1) / gain_one.astype(F32),
        grad_qkv,
        grad_out,
        jnp.sum(w_up.astype(F32) * grad_up, axis=1) / gain_two.astype(F32),
        grad_up,
        sums,
        downs.result,
    )


def solution(mesh):
    rows, vector = P(AXES, None), P(AXES)
    sizes = dict(mesh.shape)
    return jax.shard_map(
        functools.partial(layer, sizes),
        mesh=mesh,
        in_specs=(rows, rows, vector, rows, rows, vector, rows, vector, rows, rows),
        out_specs=(rows, rows, vector, rows, rows, vector, rows, vector, rows),
        check_vma=False,
    )
```

```python
import functools

import jax
import jax.numpy as jnp
from jax import lax
from jax.experimental import pallas as pl
from jax.experimental.pallas import tpu as pltpu
from jax.sharding import PartitionSpec as P

AXES = ("wide", "narrow")
EPSILON = 1e-05
BF = jnp.bfloat16
F32 = jnp.float32
WIDTH = 768
HIDDEN = 3072
ROWS = 1024
TILE = 256
BIG = 768
PAIRS = 6
HEAD = 64
PROB_COLS = 1792
CHIPS = 16
BLOCK = 48
SHARE = 96
MINE = 1536
LIMIT = 56 * 1024 * 1024


def mm(left, right):
    return lax.dot_general(left, right, (((1,), (0,)), ((), ())), preferred_element_type=F32)


def mm_nt(left, right):
    return lax.dot_general(left, right, (((1,), (1,)), ((), ())), preferred_element_type=F32)


def mm_tn(left, right):
    return lax.dot_general(left, right, (((0,), (0,)), ((), ())), preferred_element_type=F32)


def lanes(width=WIDTH):
    return lax.broadcasted_iota(jnp.int32, (1, width), 1)


def norm_parts(rows):
    total = jnp.sum(rows, axis=1, keepdims=True)
    squares = jnp.sum(rows * rows, axis=1, keepdims=True)
    inverse = lax.rsqrt((squares + total * total) * (1.0 / WIDTH) + EPSILON)
    expanded = jnp.where(lanes() == WIDTH - 1, -total, rows)
    return inverse, expanded


def norm_back(weighted, inverse, expanded):
    inner = jnp.sum(weighted * expanded, axis=1, keepdims=True) * (1.0 / WIDTH)
    full = inverse * (weighted - (inverse * inverse * inner) * expanded)
    last = full[:, WIDTH - 1 :]
    return jnp.where(lanes() == WIDTH - 1, 0.0, full - last)


def turn(start, first_row, count, forward):
    rows = lax.broadcasted_iota(jnp.int32, (count, ROWS), 0) + first_row
    cols = lax.broadcasted_iota(jnp.int32, (count, ROWS), 1)
    if forward:
        source = rows + start
        source = jnp.where(source >= ROWS, source - ROWS, source)
    else:
        source = rows - start
        source = jnp.where(source < 0, source + ROWS, source)
    return jnp.where(cols == source, 1.0, 0.0).astype(BF)


def first_row(info):
    return jnp.where(info[2] == BIG, 0, jnp.where(info[3] == BIG, info[2], info[2] + info[3]))


def params(**more):
    return pltpu.CompilerParams(vmem_limit_bytes=LIMIT, **more)


def cost(flops, nbytes, transcendentals=0):
    return pl.CostEstimate(flops=flops, bytes_accessed=nbytes, transcendentals=transcendentals)


HBM = pl.BlockSpec(memory_space=pl.ANY)


def whole(*shape):
    return pl.BlockSpec(shape, lambda *i: (0,) * len(shape))


def row_tile(width, tile=TILE):
    return pl.BlockSpec((tile, width), lambda i, *s: (i, 0))


def col_tile(rows, width):
    return pl.BlockSpec((rows, width), lambda i, *s: (0, i))


def offset_of(place):
    return 4 * (place & 3) + (place >> 2)


def place_at(info, chip, half=0):
    offset = info[0] ^ chip
    x, y = offset & 1, (offset >> 1) & 1
    return (offset >> 2) + 4 * (x + 2 * y if half == 0 else y + 2 * x)


def copies(info, pieces, target, cols=None):
    for side in range(2):
        half = info[1] ^ side

        def start(side=side, half=half):
            for place in range(CHIPS):
                source = pieces[4 * side + place // 4].at[pl.ds((place % 4) * BLOCK, BLOCK)]
                if cols is not None:
                    source = source.at[:, pl.ds(*cols)]
                block = pl.multiple_of((info[0] ^ offset_of(place)) * BLOCK, 16)
                pltpu.make_async_copy(source, *target(half, block)).start()

        if cols is None:
            start()
        else:
            pl.when(half == 1)(start)


def up_copies(info, pieces, store, sems):
    for part in range(2):
        cols = pl.ds(part * WIDTH, WIDTH)
        for place in range(CHIPS):
            source = pieces[place // 4].at[pl.ds((place % 4) * BLOCK, BLOCK), cols]
            block = pl.multiple_of((info[0] ^ offset_of(place)) * BLOCK, 16)
            pltpu.make_async_copy(source, store.at[pl.ds(block, BLOCK), cols], sems.at[part]).start()


def down_copies(info, pieces, store, sems):
    for place in range(CHIPS):
        chip = info[0] ^ offset_of(place)
        first = pl.multiple_of((chip & 7) * SHARE, 16)
        pltpu.make_async_copy(
            pieces[place // 4].at[pl.ds((place % 4) * SHARE, SHARE)],
            store.at[chip >> 3, pl.ds(first, SHARE)],
            sems.at[chip >> 3],
        ).start()


def by_half(store, sems):
    width = store.shape[1] // 2

    def target(half, first):
        cols = pl.ds(pl.multiple_of(half * width, 128), width)
        return store.at[pl.ds(first, BLOCK), cols], sems.at[half]

    return target


def one_half(store, semaphore):
    return lambda half, first: (store.at[pl.ds(first, BLOCK)], semaphore)


def arrived(ref, semaphore):
    pltpu.make_async_copy(ref, ref, semaphore).wait()


def halves_arrived(store, sems, halves=(0, 1)):
    width = store.shape[1] // 2
    for half in halves:
        arrived(store.at[:, pl.ds(half * width, width)], sems.at[half])


OUT_COLS = (128, WIDTH)
TURNED = pltpu.VMEM((2 * HEAD, ROWS), BF)
PAIR_SEMS = pltpu.SemaphoreType.DMA((2,))
SLOT_SEMS = pltpu.SemaphoreType.DMA((4,))
PART = 3
PART_COLS = PART * 2 * HEAD
SMALL = 128
A_COLS = 3 * PART_COLS + SMALL
B_COLS = 3 * PART_COLS + WIDTH + SMALL


def pack_kernel(qkv_ref, out_ref, one_ref, two_ref, bias_ref, w_up_ref, a_ref, b_ref, up_ref):
    few, share = one_ref.shape[1], bias_ref.shape[1]
    for part, ref in enumerate((a_ref, b_ref)):
        for i in range(3):
            first = i * WIDTH + part * PART_COLS
            ref[:, i * PART_COLS : (i + 1) * PART_COLS] = qkv_ref[:, first : first + PART_COLS]
    b_ref[:, 3 * PART_COLS : 3 * PART_COLS + WIDTH] = out_ref[...]
    place = lax.broadcasted_iota(jnp.int32, (few, SMALL), 1)

    def column(row, first):
        count = row.shape[1]
        at = lax.broadcasted_iota(jnp.int32, (few, count), 1)
        down = lax.broadcasted_iota(jnp.int32, (few, count), 0) + first
        return jnp.sum(jnp.where(at == down, row.astype(F32), 0.0), axis=1, keepdims=True)

    gains = jnp.where(place == 0, column(one_ref[...], 0), 0.0)
    gains = jnp.where(place == 1, column(two_ref[...], 0), gains)
    a_ref[:, A_COLS - SMALL :] = gains.astype(BF)
    bias = jnp.zeros((few, SMALL), F32)
    for i in range(share // few):
        bias = jnp.where(place == i, column(bias_ref[...], i * few), bias)
    b_ref[:, B_COLS - SMALL :] = bias.astype(BF)
    weights = w_up_ref[...].astype(F32)
    for core in range(2):
        blocks = [weights[:, SHARE * (2 * i + core) : SHARE * (2 * i + core + 1)] for i in range(CHIPS)]
        up_ref[:, core * MINE : (core + 1) * MINE] = jnp.concatenate(blocks, axis=1).astype(BF)


def pack(w_qkv, w_out, gain_one, gain_two, b_up, w_up):
    few = w_qkv.shape[0]
    return pl.pallas_call(
        pack_kernel,
        out_shape=[
            jax.ShapeDtypeStruct((few, cols), BF) for cols in (A_COLS, B_COLS, HIDDEN)
        ],
        compiler_params=params(),
        name="pack",
    )(w_qkv, w_out, gain_one[None], gain_two[None], b_up[None], w_up)


def join_kernel(info, *refs):
    own, other, outs = refs[:3], refs[3:6], refs[6:]
    first = info[1] == 0
    for mine, theirs, out in zip(own, other, outs):
        half = mine.shape[1] // 2
        cols = pl.ds(pl.multiple_of(info[1] * half, 128), half)
        mine, theirs = mine[:, cols].astype(F32), theirs[:, cols].astype(F32)
        out[...] = jnp.concatenate(
            [jnp.where(first, mine, theirs), jnp.where(first, theirs, mine)], axis=0
        ).astype(BF)


def join(info, own, other):
    shapes = [(2 * v.shape[0], v.shape[1] // 2) for v in own]
    return pl.pallas_call(
        join_kernel,
        grid_spec=pltpu.PrefetchScalarGridSpec(
            num_scalar_prefetch=1,
            grid=(1,),
            in_specs=[whole(*v.shape) for v in [*own, *other]],
            out_specs=[whole(*shape) for shape in shapes],
        ),
        out_shape=[jax.ShapeDtypeStruct(shape, BF) for shape in shapes],
        compiler_params=pltpu.CompilerParams(vmem_limit_bytes=8 * 1024 * 1024),
        name="join",
    )(info, *own, *other)


def before_kernel(info, tok_ref, cot_ref, x_ref, up_ref, down_ref, wide):
    pick = turn(first_row(info), pl.program_id(0) * TILE, TILE, True)
    wide[:, WIDTH - 128 :] = jnp.zeros((TILE, 128), F32)
    wide[:, : WIDTH - 1] = mm(pick, tok_ref[...])
    x_ref[...] = wide[...].astype(BF)
    wide[:, : WIDTH - 1] = mm(pick, cot_ref[...])
    grads = wide[...]
    up_ref[...] = grads.astype(BF)
    down_ref[...] = (grads - jnp.sum(grads, axis=1, keepdims=True) * (1.0 / WIDTH)).astype(BF)


def before(info, tokens, cotangent):
    shape = jax.ShapeDtypeStruct((ROWS, WIDTH), BF)
    return pl.pallas_call(
        before_kernel,
        grid_spec=pltpu.PrefetchScalarGridSpec(
            num_scalar_prefetch=1,
            grid=(ROWS // TILE,),
            in_specs=[whole(ROWS, WIDTH - 1)] * 2,
            out_specs=[row_tile(WIDTH)] * 3,
            scratch_shapes=[pltpu.VMEM((TILE, WIDTH), F32)],
        ),
        out_shape=[shape] * 3,
        compiler_params=params(),
        cost_estimate=cost(4 * ROWS * ROWS * WIDTH, 10 * ROWS * WIDTH),
        name="before",
    )(info, tokens, cotangent)


SPANS = ((0, 0, 256, 0), (256, 0, 512, 256), (512, 0, 768, 768), (768, 768, 256, 1536))


def tail_segments(info, axis):
    shape = (TILE, 1) if axis == 0 else (1, TILE)
    place = lax.broadcasted_iota(jnp.int32, shape, axis) + BIG + first_row(info)
    place = jnp.where(place >= ROWS, place - ROWS, place)
    found = jnp.zeros(shape, jnp.int32)
    bound = 0
    for j in range(3):
        bound = bound + info[2 + j]
        found = found + jnp.where(place >= bound, 1, 0)
    return found


def head_mask(head):
    place = lanes(2 * HEAD)
    return (place < HEAD) if head == 0 else (place >= HEAD)


def attend_pair(info, qkv, pair, out_ref, norm_ref, prob_ref, turned):
    cols = [pl.ds(pl.multiple_of(i * PART_COLS + pair * 2 * HEAD, 128), 2 * HEAD) for i in range(3)]
    causal = lax.broadcasted_iota(jnp.int32, (TILE, TILE), 0) >= lax.broadcasted_iota(
        jnp.int32, (TILE, TILE), 1
    )
    turned[...] = qkv[:, cols[1]].T
    for first, key_first, key_count, place in SPANS:
        queries = qkv[first : first + TILE, cols[0]]
        keys = turned[:, key_first : key_first + key_count]
        values = qkv[key_first : key_first + key_count, cols[2]]
        values = jnp.concatenate([values, jnp.ones_like(values)], axis=1)
        allowed = causal
        if first == BIG:
            allowed = causal & (tail_segments(info, 0) == tail_segments(info, 1))
        mixed = []
        for head in range(2):
            mine = jnp.where(head_mask(head), queries, 0) * BF(HEAD**-0.5)
            scores = mm(mine, keys)
            split = key_count - TILE
            last = jnp.where(allowed, scores[:, split:], -1e30)
            largest = jnp.max(last, axis=1, keepdims=True)
            if split:
                largest = jnp.maximum(largest, jnp.max(scores[:, :split], axis=1, keepdims=True))
            last = jnp.exp(last - largest).astype(BF)
            prob_ref[head, :, place + split : place + key_count] = last
            both = mm(last, values[split:])
            if split:
                early = jnp.exp(scores[:, :split] - largest).astype(BF)
                prob_ref[head, :, place : place + split] = early
                both += mm(early, values[:split])
            mixed.append(both)
        both = jnp.where(jnp.concatenate([head_mask(0)] * 2, axis=1), mixed[0], mixed[1])
        inverse = 1.0 / both[:, 2 * HEAD :]
        norm_ref[first : first + TILE, :] = inverse
        out_ref[first : first + TILE, :] = (both[:, : 2 * HEAD] * inverse).astype(BF)


def pair_cols(offset):
    return pl.BlockSpec((ROWS, 2 * HEAD), lambda i, *s: (0, offset + i))


PROB_SPEC = pl.BlockSpec((2, TILE, PROB_COLS), lambda i, *s: (i, 0, 0))
HEADS_SHAPES = [
    jax.ShapeDtypeStruct((ROWS, PART_COLS), BF),
    jax.ShapeDtypeStruct((ROWS, PART_COLS), F32),
    jax.ShapeDtypeStruct((2 * PART, TILE, PROB_COLS), BF),
]


def heads_a_kernel(info, x_ref, *rest):
    pieces, (normed_hbm, qkv_hbm, gains_ref, att_ref, norm_ref, prob_ref) = rest[:8], rest[8:14]
    store, normed, qkv, turned, sems, out_sems = rest[14:]
    step = pl.program_id(0)

    @pl.when(step == 0)
    def _():
        copies(info, pieces, by_half(store, sems))
        inverse, expanded = norm_parts(x_ref[...].astype(F32))
        expanded = expanded * inverse
        halves_arrived(store, sems)
        gains = store[:, 3 * PART_COLS :].astype(F32).T[:8]
        gains_ref[...] = gains
        normed[...] = (expanded * gains[:1]).astype(BF)
        pltpu.make_async_copy(normed, normed_hbm, out_sems.at[0]).start()
        for i in range(3):
            cols = slice(i * PART_COLS, (i + 1) * PART_COLS)
            qkv[:, cols] = mm(normed[...], store[:, cols]).astype(BF)
        pltpu.make_async_copy(qkv, qkv_hbm, out_sems.at[1]).start()

    attend_pair(info, qkv, step, att_ref, norm_ref, prob_ref, turned)

    @pl.when(step == PART - 1)
    def _():
        arrived(normed, out_sems.at[0])
        arrived(qkv, out_sems.at[1])


def heads_a(info, x, pieces):
    return pl.pallas_call(
        heads_a_kernel,
        grid_spec=pltpu.PrefetchScalarGridSpec(
            num_scalar_prefetch=1,
            grid=(PART,),
            in_specs=[whole(ROWS, WIDTH)] + [HBM] * 8,
            out_specs=[HBM, HBM, whole(8, WIDTH), pair_cols(0), pair_cols(0), PROB_SPEC],
            scratch_shapes=[
                pltpu.VMEM((WIDTH, A_COLS), BF), pltpu.VMEM((ROWS, WIDTH), BF),
                pltpu.VMEM((ROWS, 3 * PART_COLS), BF), TURNED, PAIR_SEMS, PAIR_SEMS,
            ],
        ),
        out_shape=[
            jax.ShapeDtypeStruct((ROWS, WIDTH), BF),
            jax.ShapeDtypeStruct((ROWS, 3 * PART_COLS), BF),
            jax.ShapeDtypeStruct((8, WIDTH), F32),
        ]
        + HEADS_SHAPES,
        compiler_params=params(),
        cost_estimate=cost(6 * ROWS * WIDTH * PART_COLS + 4 * 6 * 7 * TILE * TILE * 256, 20000000, 2752512),
        name="heads_a",
    )(info, x, *pieces)


def heads_b_kernel(info, normed_ref, gains_ref, a_att_hbm, x_hbm, *rest):
    pieces, (qkv_hbm, bias_ref, middle_hbm, second_hbm, att_ref, norm_ref, prob_ref) = rest[:8], rest[8:15]
    store, qkv, turned, att, x, middle, second, sems, in_sems, out_sems = rest[15:]
    step = pl.program_id(0)
    late = [
        pltpu.make_async_copy(a_att_hbm, att.at[:, pl.ds(0, PART_COLS)], in_sems.at[0]),
        pltpu.make_async_copy(x_hbm, x, in_sems.at[1]),
    ]

    @pl.when(step == 0)
    def _():
        copies(info, pieces, by_half(store, sems))
        for copy in late:
            copy.start()
        halves_arrived(store, sems)
        for i in range(3):
            cols = slice(i * PART_COLS, (i + 1) * PART_COLS)
            qkv[:, cols] = mm(normed_ref[...], store[:, cols]).astype(BF)
        bias_ref[...] = store[:, B_COLS - SMALL :].astype(F32).T[:8]
        pltpu.make_async_copy(qkv, qkv_hbm, out_sems.at[0]).start()

    attend_pair(info, qkv, step, att_ref, norm_ref, prob_ref, turned)
    att[:, pl.ds(pl.multiple_of(PART_COLS + step * 2 * HEAD, 128), 2 * HEAD)] = att_ref[...]

    @pl.when(step == PART - 1)
    def _():
        for copy in late:
            copy.wait()
        weights = store[:, 3 * PART_COLS : 3 * PART_COLS + WIDTH]
        for i in range(ROWS // TILE):
            rows = slice(i * TILE, (i + 1) * TILE)
            mixed = mm(att[rows, :], weights)
            mixed = mixed - jnp.sum(mixed, axis=1, keepdims=True) * (1.0 / WIDTH)
            value = x[rows, :].astype(F32) + jnp.where(lanes() == WIDTH - 1, 0.0, mixed)
            inverse, expanded = norm_parts(value)
            middle[rows, :] = value
            second[rows, :] = (expanded * inverse * gains_ref[1:2, :]).astype(BF)
            for j, (source, target) in enumerate(((middle, middle_hbm), (second, second_hbm))):
                pltpu.make_async_copy(source.at[rows], target.at[rows], out_sems.at[1 + j]).start()
        arrived(qkv, out_sems.at[0])
        arrived(middle, out_sems.at[1])
        arrived(second, out_sems.at[2])


def heads_b(info, normed, gains, a_att, x, pieces):
    return pl.pallas_call(
        heads_b_kernel,
        grid_spec=pltpu.PrefetchScalarGridSpec(
            num_scalar_prefetch=1,
            grid=(PART,),
            in_specs=[whole(ROWS, WIDTH), whole(8, WIDTH)] + [HBM] * 10,
            out_specs=[HBM, whole(8, WIDTH), HBM, HBM, pair_cols(0), pair_cols(0), PROB_SPEC],
            scratch_shapes=[
                pltpu.VMEM((WIDTH, B_COLS), BF), pltpu.VMEM((ROWS, 3 * PART_COLS), BF), TURNED,
                pltpu.VMEM((ROWS, WIDTH), BF), pltpu.VMEM((ROWS, WIDTH), BF),
                pltpu.VMEM((ROWS, WIDTH), F32), pltpu.VMEM((ROWS, WIDTH), BF),
                PAIR_SEMS, PAIR_SEMS, pltpu.SemaphoreType.DMA((3,)),
            ],
        ),
        out_shape=[
            jax.ShapeDtypeStruct((ROWS, 3 * PART_COLS), BF),
            jax.ShapeDtypeStruct((8, WIDTH), F32),
            jax.ShapeDtypeStruct((ROWS, WIDTH), F32),
            jax.ShapeDtypeStruct((ROWS, WIDTH), BF),
        ]
        + HEADS_SHAPES,
        compiler_params=params(),
        cost_estimate=cost(
            6 * ROWS * WIDTH * PART_COLS + 2 * ROWS * WIDTH * WIDTH + 4 * 6 * 7 * TILE * TILE * 256,
            25000000, 2752512,
        ),
        name="heads_b",
    )(info, normed, gains, a_att, x, *pieces)


GELU_A = 0.7978845608028654
GELU_B = 0.044715


def tokens_copies(refs, second, down_in, sems):
    return [
        pltpu.make_async_copy(ref, (second, down_in)[i // 2].at[i % 2], sems.at[i])
        for i, ref in enumerate(refs)
    ]


def feed_kernel(info, bias_ref, *rest):
    ins, pieces, (act_hbm, slope_hbm, *grads) = rest[:4], rest[4:8], rest[8:14]
    store, sems, second, down_in, in_sems, act, slope, stage, out_sems = rest[14:]
    late = tokens_copies(ins, second, down_in, in_sems)
    late[0].start()
    up_copies(info, pieces, store, sems)
    for i in (2, 1, 3):
        late[i].start()
    late[0].wait()
    sums = [None, None]
    for side in range(2):
        if side == 1:
            late[1].wait()
        for part in range(2):
            cols = slice(part * WIDTH, (part + 1) * WIDTH)
            if side == 0:
                arrived(store.at[:, pl.ds(part * WIDTH, WIDTH)], sems.at[part])
            slot = 2 * side + part
            for i in range(ROWS // TILE):
                rows = slice(i * TILE, (i + 1) * TILE)
                hidden = mm(second[side, rows, :], store[:, cols]) + bias_ref[:, cols]
                square = hidden * hidden
                bent = jnp.tanh(hidden * (GELU_A + (GELU_A * GELU_B) * square))
                half = 0.5 + 0.5 * bent
                act[slot, rows, :] = (hidden * half).astype(BF)
                tilt = hidden * (0.5 * GELU_A + (1.5 * GELU_A * GELU_B) * square)
                slope[slot, rows, :] = (half + tilt * (1.0 - bent * bent)).astype(BF)
            for source, target, which in ((act, act_hbm, 0), (slope, slope_hbm, 1)):
                pltpu.make_async_copy(source.at[slot], target.at[slot], out_sems.at[which]).start()
            if part == 0:
                late[2 + side].wait()
            found = mm_tn(act[slot], down_in[side])
            if side == 0:
                sums[part] = found
                continue
            total = sums[part] + found
            for i in range(8):
                block = total[SHARE * i : SHARE * (i + 1)].astype(BF)
                stage[place_at(info, 8 * part + i)] = block
    for i, target in enumerate(grads):
        pltpu.make_async_copy(stage.at[pl.ds(4 * i, 4)], target, out_sems.at[2]).start()
    arrived(act, out_sems.at[0])
    arrived(slope, out_sems.at[1])
    arrived(stage, out_sems.at[2])


BOTH = pltpu.VMEM((2, ROWS, WIDTH), BF)
FOUR = pltpu.VMEM((4, ROWS, WIDTH), BF)


def feed(info, second, other_second, down_in, other_down_in, bias, pieces):
    return pl.pallas_call(
        feed_kernel,
        grid_spec=pltpu.PrefetchScalarGridSpec(
            num_scalar_prefetch=1,
            grid=(1,),
            in_specs=[whole(1, MINE)] + [HBM] * 8,
            out_specs=[HBM] * 6,
            scratch_shapes=[
                pltpu.VMEM((WIDTH, MINE), BF), PAIR_SEMS, BOTH, BOTH, SLOT_SEMS, FOUR, FOUR,
                pltpu.VMEM((CHIPS, SHARE, WIDTH), BF), pltpu.SemaphoreType.DMA((3,)),
            ],
        ),
        out_shape=[jax.ShapeDtypeStruct((4, ROWS, WIDTH), BF)] * 2
        + [jax.ShapeDtypeStruct((4, SHARE, WIDTH), BF)] * 4,
        compiler_params=params(),
        cost_estimate=cost(4 * ROWS * WIDTH * HIDDEN, 6 * ROWS * HIDDEN + 4 * WIDTH * HIDDEN),
        name="feed",
    )(info, bias, second, other_second, down_in, other_down_in, *pieces)


UP_COLS = WIDTH + SMALL, WIDTH


def spread_out(info, grads, stage, half=0):
    for device in range(32):
        value = grads[24 * device : 24 * (device + 1)].astype(BF)
        stage[info[1] ^ (device & 1), place_at(info, device >> 1, half)] = value


def back_kernel(info, *rest):
    slope_hbm, ins, up_pieces, down_pieces = rest[0], rest[1:5], rest[5:9], rest[9:13]
    outs, own_hbm, other_hbm = rest[13:17], rest[17], rest[18]
    (down_store, down_sems, up_store, up_sems, second, down_in, in_sems, slope, slope_sems, grads,
     weighted, other, stage, spare, out_sems) = rest[19:]
    late = tokens_copies(ins, second, down_in, in_sems)
    slopes = [pltpu.make_async_copy(slope_hbm.at[i], slope.at[i], slope_sems.at[i]) for i in range(4)]
    late[2].start()
    down_copies(info, down_pieces, down_store, down_sems)
    slopes[0].start()
    up_copies(info, up_pieces, up_store, up_sems)
    for copy in (late[0], late[3], slopes[2], late[1], slopes[1], slopes[3]):
        copy.start()
    for part in range(2):
        cols = slice(part * WIDTH, (part + 1) * WIDTH)
        arrived(down_store.at[part], down_sems.at[part])
        for side in range(2):
            if part == 0:
                late[2 + side].wait()
            value = mm_nt(down_in[side], down_store[part])
            slopes[2 * side + part].wait()
            bias = jnp.zeros((1, WIDTH), F32)
            for i in range(ROWS // TILE):
                rows = slice(i * TILE, (i + 1) * TILE)
                few = (slope[2 * side + part, rows, :].astype(F32) * value[rows]).astype(BF)
                grads[side, rows, :] = few
                bias += jnp.sum(few.astype(F32), axis=0, keepdims=True)
            if side == 0:
                arrived(up_store.at[:, pl.ds(part * WIDTH, WIDTH)], up_sems.at[part])
            if part == 0:
                weighted[side] = mm_nt(grads[side], up_store[:, cols])
            elif side == 0:
                weighted[0] += mm_nt(grads[0], up_store[:, cols])
                pltpu.make_async_copy(weighted.at[0], own_hbm, out_sems.at[0]).start()
            else:
                other[...] = (weighted[1] + mm_nt(grads[1], up_store[:, cols])).astype(BF)
                pltpu.make_async_copy(other, other_hbm, out_sems.at[1]).start()
            if part == 0:
                late[side].wait()
            found = mm_tn(second[side], grads[side])
            if side == 0:
                sums, biases = found, bias
        total = sums + found
        for chip in range(CHIPS):
            block = total[BLOCK * chip : BLOCK * (chip + 1)].astype(BF)
            stage[part, place_at(info, chip, part)] = block
        for i in range(2):
            pltpu.make_async_copy(
                stage.at[part, pl.ds(8 * i, 8)], outs[2 * part + i].at[:, :, pl.ds(0, WIDTH)], out_sems.at[2]
            ).start()
        row = biases + bias
        for i in range(8):
            few = jnp.concatenate(
                [row[:, SHARE * i : SHARE * (i + 1)], jnp.zeros((1, SMALL - SHARE), F32)], axis=1
            )
            spare[place_at(info, 8 * part + i)] = jnp.broadcast_to(few, (BLOCK, SMALL)).astype(BF)
    for i in range(2):
        pltpu.make_async_copy(
            spare.at[pl.ds(8 * i, 8)], outs[i].at[:, :, pl.ds(WIDTH, SMALL)], out_sems.at[3]
        ).start()
    arrived(weighted.at[0], out_sems.at[0])
    arrived(other, out_sems.at[1])
    arrived(stage, out_sems.at[2])
    arrived(spare, out_sems.at[3])


def back(info, second, other_second, down_in, other_down_in, slope, up_pieces, down_pieces):
    return pl.pallas_call(
        back_kernel,
        grid_spec=pltpu.PrefetchScalarGridSpec(
            num_scalar_prefetch=1,
            grid=(1,),
            in_specs=[HBM] * 13,
            out_specs=[HBM] * 6,
            scratch_shapes=[
                pltpu.VMEM((2, WIDTH, WIDTH), BF), PAIR_SEMS, pltpu.VMEM((WIDTH, MINE), BF), PAIR_SEMS,
                BOTH, BOTH, SLOT_SEMS, FOUR, SLOT_SEMS, BOTH,
                pltpu.VMEM((2, ROWS, WIDTH), F32),
                pltpu.VMEM((ROWS, WIDTH), BF),
                pltpu.VMEM((2, CHIPS, BLOCK, WIDTH), BF),
                pltpu.VMEM((CHIPS, BLOCK, SMALL), BF),
                SLOT_SEMS,
            ],
        ),
        out_shape=[jax.ShapeDtypeStruct((CHIPS // 2, BLOCK, UP_COLS[i // 2]), BF) for i in range(4)]
        + [jax.ShapeDtypeStruct((ROWS, WIDTH), F32), jax.ShapeDtypeStruct((ROWS, WIDTH), BF)],
        compiler_params=params(),
        cost_estimate=cost(6 * ROWS * WIDTH * HIDDEN, 35000000),
        name="back",
    )(info, slope, second, other_second, down_in, other_down_in, *up_pieces, *down_pieces)


def pair_grad(q_ref, k_ref, v_ref, grad_ref, att_ref, norm_ref, prob_ref, dq_ref, dk_ref, dv_ref,
              key_sum, value_sum, values, scaled, turned):
    factor = HEAD**-0.5
    values[...] = v_ref[...].T
    turned[0] = q_ref[...].T
    scaled[...] = (grad_ref[...].astype(F32) * norm_ref[...]).astype(BF)
    turned[1] = scaled[...].T
    key_sum[...] = jnp.zeros_like(key_sum)
    value_sum[...] = jnp.zeros_like(value_sum)
    for first, key_first, key_count, place in SPANS:
        rows = slice(first, first + TILE)
        keys_at = slice(key_first, key_first + key_count)
        grads = scaled[rows, :]
        product = grads.astype(F32) * att_ref[rows, :].astype(F32)
        keys = k_ref[keys_at, :]
        parts = []
        for head in range(2):
            mask = head_mask(head)
            mine = slice(HEAD * head, HEAD * (head + 1))
            probs = prob_ref[head, :, place : place + key_count]
            inner = jnp.sum(jnp.where(mask, product, 0.0), axis=1, keepdims=True)
            slopes = mm(jnp.where(mask, grads, 0), values[:, keys_at]) - inner
            slopes = (probs.astype(F32) * slopes).astype(BF)
            parts.append(mm(slopes, keys))
            value_sum[mine, keys_at] += mm(turned[1, mine, rows], probs)
            key_sum[mine, keys_at] += mm(turned[0, mine, rows], slopes)
        dq_ref[rows, :] = (jnp.where(head_mask(0), parts[0], parts[1]) * factor).astype(BF)
    dk_ref[...] = (key_sum[...].T * factor).astype(BF)
    dv_ref[...] = value_sum[...].T.astype(BF)


PAIR_SCRATCH = [
    pltpu.VMEM((2 * HEAD, ROWS), F32), pltpu.VMEM((2 * HEAD, ROWS), F32), TURNED,
    pltpu.VMEM((ROWS, 2 * HEAD), BF), pltpu.VMEM((2, 2 * HEAD, ROWS), BF),
]


HEADS_COLS = 6 * PART_COLS + WIDTH


def attend_grad_kernel(info, gain_ref, weighted_hbm, other_hbm, middle_hbm, up_hbm, a_att_hbm, b_att_hbm, *rest):
    pieces, (q_ref, k_ref, v_ref, att_ref, norm_ref, prob_ref), outs = rest[:8], rest[8:14], rest[14:17]
    targets, total_hbm, grad_hbm, pair_scratch = rest[17:19], rest[19], rest[20], rest[21:26]
    (weighted, other, middle, up, in_sems, store, semaphore, total, mixed, grad_att, att, att_sems, stage,
     out_sems) = rest[26:]
    step = pl.program_id(0)
    late = [
        pltpu.make_async_copy(a_att_hbm, att.at[:, pl.ds(0, PART_COLS)], att_sems.at[0]),
        pltpu.make_async_copy(b_att_hbm, att.at[:, pl.ds(PART_COLS, PART_COLS)], att_sems.at[1]),
    ]

    @pl.when(step == 0)
    def _():
        early = []
        for i in range(ROWS // TILE):
            rows = pl.ds(i * TILE, TILE)
            early.append([
                pltpu.make_async_copy(source.at[rows], target.at[rows], in_sems.at[4 * i + j])
                for j, (source, target) in enumerate(
                    ((middle_hbm, middle), (weighted_hbm, weighted), (other_hbm, other), (up_hbm, up))
                )
            ])
            for copy in early[-1]:
                copy.start()
        copies(info, pieces, one_half(store, semaphore), OUT_COLS)
        for copy in late:
            copy.start()
        for i in range(ROWS // TILE):
            rows = slice(i * TILE, (i + 1) * TILE)
            for copy in early[i]:
                copy.wait()
            inverse, expanded = norm_parts(middle[rows, :])
            value = (weighted[rows, :] + other[rows, :].astype(F32)) * gain_ref[1:2, :]
            value = up[rows, :].astype(F32) + norm_back(value, inverse, expanded)
            total[rows, :] = value
            mixed[rows, :] = centred(value).astype(BF)
        pltpu.make_async_copy(total, total_hbm, out_sems.at[1]).start()
        arrived(store, semaphore)
        grad_att[...] = mm_nt(mixed[...], store[...]).astype(BF)
        pltpu.make_async_copy(grad_att, grad_hbm, out_sems.at[2]).start()

    place = pl.ds(pl.multiple_of(step * 2 * HEAD, 2 * HEAD), 2 * HEAD)
    pair_grad(
        q_ref, k_ref, v_ref, grad_att.at[:, place], att_ref, norm_ref, prob_ref, *outs, *pair_scratch
    )

    @pl.when(step == 0)
    def _():
        for copy in late:
            copy.wait()
        spread_out(info, mm_tn(att[...], mixed[...]), stage)
        for which in range(2):
            pltpu.make_async_copy(
                stage.at[which], targets[which].at[:, :, pl.ds(6 * PART_COLS, WIDTH)], out_sems.at[0]
            ).start()

    @pl.when(step == PART - 1)
    def _():
        arrived(stage, out_sems.at[0])
        arrived(total, out_sems.at[1])
        arrived(grad_att, out_sems.at[2])


def centred(branch):
    return branch - jnp.sum(branch, axis=1, keepdims=True) * (1.0 / WIDTH)


def heads_grad_kernel(info, normed_hbm, a_q, a_k, a_v, *rest):
    ins, outs, targets, pair_scratch = rest[:7], rest[9:12], rest[12:14], rest[14:19]
    kept, normed, turned, others, in_sems, stage, out_sem = rest[19:]
    step = pl.program_id(0)
    late = [
        pltpu.make_async_copy(source, target, in_sems.at[i])
        for i, (source, target) in enumerate(
            [(normed_hbm, normed)] + [(ref, others.at[i]) for i, ref in enumerate((a_q, a_k, a_v))]
        )
    ]

    def weights_grad(i, value):
        spread_out(info, mm(turned[...], value), stage.at[i])
        cols = pl.ds(pl.multiple_of(i * PART_COLS, 128), PART_COLS)
        for which, target in enumerate(targets):
            pltpu.make_async_copy(stage.at[i, which], target.at[:, :, cols], out_sem).start()

    @pl.when(step == 0)
    def _():
        for copy in late:
            copy.start()

    pair_grad(*ins, *outs, *pair_scratch)

    @pl.when(step == 0)
    def _():
        for copy in late:
            copy.wait()
        turned[...] = normed[...].T

    weights_grad(step, others[step])
    place = pl.ds(pl.multiple_of(step * 2 * HEAD, 2 * HEAD), 2 * HEAD)
    for i in range(3):
        kept[i, :, place] = outs[i][...]

    @pl.when(step == PART - 1)
    def _():
        for i in range(3):
            weights_grad(3 + i, kept[i])
        arrived(stage, out_sem)


HEADS_GRADS = [jax.ShapeDtypeStruct((CHIPS, 24, HEADS_COLS), BF)] * 2


def pair_specs(first):
    return [
        pair_cols(0), pair_cols(PART), pair_cols(2 * PART),
        pair_cols(first), pair_cols(0), pair_cols(0), PROB_SPEC,
    ]


def attend_grad(info, weighted, other, middle, upstream, gains, attended, qkv, norms, probs, pieces):
    specs = pair_specs(0)
    return pl.pallas_call(
        attend_grad_kernel,
        grid_spec=pltpu.PrefetchScalarGridSpec(
            num_scalar_prefetch=1,
            grid=(PART,),
            in_specs=[whole(8, WIDTH)] + [HBM] * 14 + specs[:3] + specs[4:],
            out_specs=[pair_cols(0)] * 3 + [HBM] * 4,
            scratch_shapes=PAIR_SCRATCH
            + [
                pltpu.VMEM((ROWS, WIDTH), F32), pltpu.VMEM((ROWS, WIDTH), BF),
                pltpu.VMEM((ROWS, WIDTH), F32), pltpu.VMEM((ROWS, WIDTH), BF),
                pltpu.SemaphoreType.DMA((16,)),
                pltpu.VMEM((WIDTH, WIDTH), BF), pltpu.SemaphoreType.DMA,
                pltpu.VMEM((ROWS, WIDTH), F32), pltpu.VMEM((ROWS, WIDTH), BF),
                pltpu.VMEM((ROWS, WIDTH), BF), pltpu.VMEM((ROWS, WIDTH), BF), PAIR_SEMS,
                pltpu.VMEM((2, CHIPS, 24, WIDTH), BF), pltpu.SemaphoreType.DMA((3,)),
            ],
        ),
        out_shape=[jax.ShapeDtypeStruct((ROWS, PART_COLS), BF)] * 3
        + HEADS_GRADS
        + [jax.ShapeDtypeStruct((ROWS, WIDTH), F32), jax.ShapeDtypeStruct((ROWS, WIDTH), BF)],
        compiler_params=params(),
        cost_estimate=cost(8 * 6 * 7 * TILE * TILE * 256, 8 * ROWS * WIDTH + 5505024),
        name="attend_grad",
    )(info, gains, weighted, other, middle, upstream, *attended, *pieces, qkv, qkv, qkv, attended[0], norms, probs)


def heads_grad(info, normed, parts, qkv, grad_attended, attended, norms, probs, keep, send):
    return pl.pallas_call(
        heads_grad_kernel,
        grid_spec=pltpu.PrefetchScalarGridSpec(
            num_scalar_prefetch=1,
            grid=(PART,),
            in_specs=[HBM] * 4 + pair_specs(PART) + [HBM] * 2,
            out_specs=[pair_cols(0)] * 3 + [HBM] * 2,
            scratch_shapes=PAIR_SCRATCH
            + [
                pltpu.VMEM((3, ROWS, PART_COLS), BF),
                pltpu.VMEM((ROWS, WIDTH), BF),
                pltpu.VMEM((WIDTH, ROWS), BF),
                pltpu.VMEM((3, ROWS, PART_COLS), BF),
                SLOT_SEMS,
                pltpu.VMEM((6, 2, CHIPS, 24, PART_COLS), BF),
                pltpu.SemaphoreType.DMA,
            ],
        ),
        out_shape=[jax.ShapeDtypeStruct((ROWS, PART_COLS), BF)] * 3 + HEADS_GRADS,
        input_output_aliases={12: 3, 13: 4},
        compiler_params=params(),
        cost_estimate=cost(
            8 * 6 * 7 * TILE * TILE * 256 + 6 * ROWS * WIDTH * WIDTH, 8 * ROWS * WIDTH + 10000000
        ),
        name="heads_grad",
    )(info, normed, *parts, qkv, qkv, qkv, grad_attended, attended, norms, probs, keep, send)


def last_kernel(info, act_ref, middle_ref, gain_ref, *rest):
    parts, x_hbm, total_hbm, down_pieces = rest[:6], rest[6], rest[7], rest[8:12]
    a_pieces, b_pieces, (out_ref, other_ref, grad_ref) = rest[12:20], rest[20:28], rest[28:31]
    down_store, down_sems, a_store, b_store, a_sems, b_sems, grads, x, total, weighted, sems = rest[31:]
    step = pl.program_id(0)
    late = [
        pltpu.make_async_copy(source, target, sems.at[i])
        for i, (source, target) in enumerate(
            [(part, grads.at[i]) for i, part in enumerate(parts)] + [(x_hbm, x), (total_hbm, total)]
        )
    ]

    @pl.when(step == 0)
    def _():
        down_copies(info, down_pieces, down_store, down_sems)
        for i in range(2):
            arrived(down_store.at[i], down_sems.at[i])
        copies(info, a_pieces, by_half(a_store, a_sems))
        copies(info, b_pieces, by_half(b_store, b_sems))
        for copy in late:
            copy.start()

    branch = mm(act_ref[0], down_store[0]) + mm(act_ref[1], down_store[1])
    out_ref[...] = middle_ref[...] + centred(branch)
    branch = mm(act_ref[2], down_store[0]) + mm(act_ref[3], down_store[1])
    other_ref[...] = centred(branch).astype(BF)

    for i in range(3):

        @pl.when(step == i + 1)
        def _(i=i):
            if i == 0:
                halves_arrived(a_store, a_sems)
                halves_arrived(b_store, b_sems)
            late[i].wait()
            late[3 + i].wait()
            cols = slice(i * PART_COLS, (i + 1) * PART_COLS)
            found = mm_nt(grads[i], a_store[:, cols]) + mm_nt(grads[3 + i], b_store[:, cols])
            weighted[...] = found if i == 0 else weighted[...] + found

    @pl.when(step == 3)
    def _():
        late[6].wait()
        late[7].wait()
        for i in range(ROWS // TILE):
            rows = slice(i * TILE, (i + 1) * TILE)
            inverse, expanded = norm_parts(x[rows, :].astype(F32))
            back = norm_back(weighted[rows, :] * gain_ref[0:1, :], inverse, expanded)
            grad_ref[rows, :] = (total[rows, :] + back).astype(BF)


def last(info, active, middle, parts, x, total, gains, down_pieces, a_pieces, b_pieces):
    act_tile = pl.BlockSpec((4, TILE, WIDTH), lambda i, *s: (0, i, 0))
    return pl.pallas_call(
        last_kernel,
        grid_spec=pltpu.PrefetchScalarGridSpec(
            num_scalar_prefetch=1,
            grid=(ROWS // TILE,),
            in_specs=[act_tile, row_tile(WIDTH), whole(8, WIDTH)] + [HBM] * 28,
            out_specs=[row_tile(WIDTH)] * 2 + [whole(ROWS, WIDTH)],
            scratch_shapes=[
                pltpu.VMEM((2, WIDTH, WIDTH), BF), PAIR_SEMS,
                pltpu.VMEM((WIDTH, A_COLS), BF), pltpu.VMEM((WIDTH, B_COLS), BF), PAIR_SEMS, PAIR_SEMS,
                pltpu.VMEM((6, ROWS, PART_COLS), BF), pltpu.VMEM((ROWS, WIDTH), BF),
                pltpu.VMEM((ROWS, WIDTH), F32), pltpu.VMEM((ROWS, WIDTH), F32),
                pltpu.SemaphoreType.DMA((8,)),
            ],
        ),
        out_shape=[jax.ShapeDtypeStruct((ROWS, WIDTH), dtype) for dtype in (F32, BF, BF)],
        compiler_params=params(),
        cost_estimate=cost(2 * ROWS * WIDTH * HIDDEN + 6 * ROWS * WIDTH * WIDTH, 30000000),
        name="last",
    )(info, active, middle, gains, *parts, x, total, *down_pieces, *a_pieces, *b_pieces)


def turn_back_kernel(info, own_ref, other_ref, two_ref, out_ref, grad_ref, one):
    step = pl.program_id(0)

    @pl.when(step == 0)
    def _():
        one[...] = (own_ref[...] + other_ref[...].astype(F32)).astype(BF)

    pick = turn(first_row(info), step * TILE, TILE, False)
    out_ref[...] = mm(pick, one[...]).astype(BF)[:, : WIDTH - 1]
    grad_ref[...] = mm(pick, two_ref[...]).astype(BF)[:, : WIDTH - 1]


def turn_back(info, own, other, two):
    return pl.pallas_call(
        turn_back_kernel,
        grid_spec=pltpu.PrefetchScalarGridSpec(
            num_scalar_prefetch=1,
            grid=(ROWS // TILE,),
            in_specs=[whole(ROWS, WIDTH)] * 3,
            out_specs=[row_tile(WIDTH - 1)] * 2,
            scratch_shapes=[pltpu.VMEM((ROWS, WIDTH), BF)],
        ),
        out_shape=[jax.ShapeDtypeStruct((ROWS, WIDTH - 1), BF)] * 2,
        compiler_params=params(),
        cost_estimate=cost(4 * ROWS * ROWS * WIDTH, 8 * ROWS * WIDTH),
        name="turn_back",
    )(info, own, other, two)


WAYS = {"core": (0, 1), "x": (0, 2), "y": (1, 0), "xy": (1, 2), "z1": (2, 0), "z2": (4, 0), "z3": (6, 0)}


def add_low(left, right):
    return (left.astype(F32) + right.astype(F32)).astype(BF)


class Cube:
    def __init__(self, sizes):
        self.sizes = sizes
        wide, narrow = lax.axis_index("wide"), lax.axis_index("narrow")
        self.place = jnp.stack([wide * 2 + (narrow >> 1), narrow & 1]).astype(jnp.int32)

    def hop(self, value, way):
        wide, narrow = WAYS[way]
        if wide == 0:
            return lax.ppermute(value, "narrow", [(i, i ^ narrow) for i in range(self.sizes["narrow"])])
        if narrow == 0:
            return lax.ppermute(value, "wide", [(i, i ^ wide) for i in range(self.sizes["wide"])])
        bits = wide * self.sizes["narrow"] + narrow
        count = self.sizes["wide"] * self.sizes["narrow"]
        return lax.ppermute(value, AXES, [(i, i ^ bits) for i in range(count)])

    def gather(self, block):
        others = yield [self.hop(block, way) for way in ("z1", "z2", "z3")]
        return (yield from self.across(jnp.concatenate([block] + others)))

    def gather_slowly(self, block):
        near = yield from self.along_z(block)
        return (yield from self.across(near))

    def along_z(self, block):
        for way in ("z1", "z2"):
            other = yield self.hop(block, way)
            block = jnp.concatenate([block, other])
        return block

    def across(self, near):
        own = yield from self.plane(near)
        twins = yield [self.hop(part, "core") for part in own]
        return own + twins

    def plane(self, near):
        far = yield [self.hop(near, way) for way in ("x", "y", "xy")]
        return [near] + far

    def gather_mine(self, block):
        near = yield from self.along_z(block)
        return (yield from self.plane(near))

    def exchange(self, value):
        return (yield self.hop(value, "core"))

    def blocks(self, info, shards):
        others = [self.hop(shard, "core") for shard in shards]
        return join(info, shards, others)

    def reduce_up(self, keeps):
        gots = yield [self.hop(send, way) for send, way in zip(keeps[1::2], "yx")]
        sends = [add_low(keep[4:], got[4:]) for keep, got in zip(keeps[::2], gots)]
        keeps = [add_low(keep[:4], got[:4]) for keep, got in zip(keeps[::2], gots)]
        gots = yield [self.hop(send, way) for send, way in zip(sends, "xy")]
        both = jnp.concatenate([add_low(keep, got) for keep, got in zip(keeps, gots)], axis=2)
        got = yield self.hop(both[2:], "z2")
        both = add_low(both[:2], got)
        got = yield self.hop(both[1], "z1")
        total = both[0].astype(F32) + got.astype(F32)
        sums = total[0, WIDTH : WIDTH + SHARE]
        total = jnp.concatenate([total[:, :WIDTH], total[:, WIDTH + SMALL :]], axis=1)
        total = total.reshape(2, -1, MINE)
        core = self.place[1]
        mine = lax.dynamic_index_in_dim(total, core, 0, False)
        got = yield self.hop(lax.dynamic_index_in_dim(total, 1 - core, 0, False), "core")
        first = core == 0
        return jnp.concatenate([jnp.where(first, mine, got), jnp.where(first, got, mine)], axis=1), sums

    def reduce_mine(self, keep):
        others = yield [self.hop(quad, way) for quad, way in zip(keep[1:], ("x", "y", "xy"))]
        return (yield from self.sum_z(sum([other.astype(F32) for other in others], keep[0].astype(F32))))

    def sum_z(self, both):
        others = yield [self.hop(both[i].astype(BF), way) for i, way in ((1, "z1"), (2, "z2"), (3, "z3"))]
        return sum([other.astype(F32) for other in others], both[0])

    def reduce(self, keep, send):
        got = yield self.hop(send, "core")
        both = [keep[4 * i : 4 * i + 4].astype(F32) + got[4 * i : 4 * i + 4].astype(F32) for i in range(4)]
        others = yield [self.hop(both[i].astype(BF), way) for i, way in ((1, "x"), (2, "y"), (3, "xy"))]
        return (yield from self.sum_z(sum([other.astype(F32) for other in others], both[0])))


class Plain:
    def __init__(self, sizes):
        self.sizes = sizes
        self.core = (lax.axis_index("narrow") & 1).astype(jnp.int32)
        self.place = jnp.stack([jnp.zeros_like(self.core), self.core])

    def exchange(self, value):
        count = self.sizes["narrow"]
        other = lax.ppermute(value, "narrow", [(i, i ^ 1) for i in range(count)])
        yield ()
        return other

    def blocks(self, info, shards):
        return shards

    def by_place(self, rows):
        return rows.reshape(4, 4, -1, rows.shape[1]).transpose(1, 0, 2, 3).reshape(4, -1, rows.shape[1])

    def by_chip(self, blocks):
        return blocks.reshape(4, 4, *blocks.shape[1:]).swapaxes(0, 1).reshape(blocks.shape)

    def mine_first(self, one, two):
        first = self.core == 0
        return jnp.where(first, one, two), jnp.where(first, two, one)

    def gather(self, shard):
        yield ()
        full = self.by_place(lax.all_gather(shard, AXES, axis=0, tiled=True))
        cols = full.shape[2] // 2
        halves = self.mine_first(full[:, :, :cols], full[:, :, cols:])
        return [half[i] for half in halves for i in range(4)]

    gather_slowly = gather

    def gather_mine(self, shard):
        yield ()
        full = lax.all_gather(shard, AXES, axis=0, tiled=True)
        if full.shape[0] == WIDTH:
            one, two = full[:, :MINE], full[:, MINE:]
        else:
            one, two = [
                full.reshape(CHIPS, 2, SHARE, WIDTH)[:, i].reshape(MINE, WIDTH) for i in range(2)
            ]
        full = self.by_place(self.mine_first(one, two)[0])
        return [full[i] for i in range(4)]

    def scatter(self, full):
        return lax.psum_scatter(full, AXES, scatter_dimension=0, tiled=True).astype(F32)

    def apart(self, value):
        return self.mine_first(value, jnp.zeros_like(value))

    def reduce_up(self, keeps):
        yield ()
        order = jnp.arange(CHIPS).reshape(2, 2, 4).transpose(1, 0, 2).reshape(-1)
        one, two = jnp.concatenate(keeps[:2]), jnp.concatenate(keeps[2:])
        one, two = self.by_chip(one), self.by_chip(two[order])
        sums = jnp.stack(self.apart(one[:, 0, WIDTH : WIDTH + SHARE].astype(F32)), axis=1)
        both = jnp.concatenate([one[:, :, :WIDTH], two], axis=2).reshape(WIDTH, MINE)
        both = jnp.concatenate(self.apart(both), axis=1)
        return self.scatter(both), self.scatter(sums.reshape(HIDDEN, 1))[:, 0]

    def reduce_mine(self, keep):
        yield ()
        full = jnp.stack(self.apart(self.by_chip(jnp.concatenate(keep))), axis=1)
        return self.scatter(full.reshape(HIDDEN, WIDTH))

    def reduce(self, keep, send):
        yield ()
        full = jnp.stack(self.mine_first(self.by_chip(keep), self.by_chip(send)), axis=1)
        return self.scatter(full.reshape(WIDTH, -1))


class Task:
    def __init__(self, steps):
        self.steps, self.flight, self.over, self.result = steps, (), False, None
        self.go(None)

    def go(self, arrived_now):
        try:
            self.flight = self.steps.send(arrived_now)
        except StopIteration as end:
            self.flight, self.over, self.result = (), True, end.value


def meet(values, *tasks, waiting=()):
    tasks = [task for task in tasks if not task.over]
    every = tasks + list(waiting)
    values, flights = lax.optimization_barrier((values, [task.flight for task in every]))
    for task, flight in zip(every, flights):
        task.flight = flight
    for task in tasks:
        task.go(task.flight)
    return values


def finish(values, *tasks):
    while not all(task.over for task in tasks):
        values = meet(values, *tasks)
    return values


def layer(sizes, tokens, lengths, gain_one, w_qkv, w_out, gain_two, w_up, b_up, w_down, cotangent):
    share, few = b_up.shape[0], gain_one.shape[0]
    links = (Cube if sizes["wide"] == 8 and sizes["narrow"] == 4 else Plain)(sizes)
    info = jnp.concatenate([links.place, lengths[0]])
    core = info[1]

    a_block, b_block, up_block = links.blocks(info, pack(w_qkv, w_out, gain_one, gain_two, b_up, w_up))
    group_a, group_b = Task(links.gather(a_block)), Task(links.gather_slowly(b_block))
    up = Task(links.gather_mine(up_block))
    tokens, cotangent, w_down = meet((tokens, cotangent, w_down), group_a, group_b, waiting=(up,))
    down = Task(links.gather_mine(w_down))
    x, upstream, down_in = before(info, tokens, cotangent)
    x = meet(x, group_a, waiting=(group_b, down))
    x, down_in = meet((x, down_in), group_a, group_b, up)
    other_down_in = Task(links.exchange(down_in))
    normed, qkv_a, gains, att_a, norms_a, probs_a = heads_a(info, x, group_a.result)
    normed, att_a, x = meet((normed, att_a, x), group_b, other_down_in, waiting=(up,))
    normed, att_a, x = meet((normed, att_a, x), group_b, up, down)
    qkv_b, bias, middle, second, att_b, norms_b, probs_b = heads_b(
        info, normed, gains, att_a, x, group_b.result
    )
    bias = bias[: share // few].reshape(share // few, -1, few).transpose(1, 0, 2)
    bias = bias.reshape(CHIPS, 2, SHARE)
    bias = jnp.where(core == 0, bias[:, 0], bias[:, 1]).reshape(1, MINE)
    bias, second = meet((bias, second), up, waiting=(down,))
    other_second = Task(links.exchange(second))
    bias = meet(bias, other_second, down)
    inputs = second, other_second.result, down_in, other_down_in.result
    active, slope, *grad_down = feed(info, *inputs, bias, up.result)
    slope, grad_down = meet((slope, grad_down), down)
    downs = Task(links.reduce_mine(grad_down))
    *grad_up, weighted, other_weighted = back(info, *inputs, slope, up.result, down.result)
    weighted, other_weighted, grad_up = meet((weighted, other_weighted, grad_up), downs)
    other_weighted = Task(links.exchange(other_weighted))
    ups = Task(links.reduce_up(grad_up))
    weighted = finish(weighted, other_weighted)
    *parts, keep, send, total, grad_att = attend_grad(
        info, weighted, other_weighted.result, middle, upstream, gains, (att_a, att_b), qkv_a, norms_a,
        probs_a, group_b.result,
    )
    parts, keep, send, grad_att = meet((parts, keep, send, grad_att), ups, downs)
    *more, keep, send = heads_grad(
        info, normed, parts, qkv_b, grad_att, att_b, norms_b, probs_b, keep, send
    )
    active, more, keep, send = meet((active, more, keep, send), waiting=(ups,))
    heads = Task(links.reduce(keep, send))
    active, more = meet((active, more), heads, ups)
    output, other_output, grad_tokens = last(
        info, active, middle, list(parts) + list(more), x, total, gains, down.result,
        group_a.result, group_b.result,
    )
    output, grad_tokens, other_output = meet((output, grad_tokens, other_output), heads, ups)
    other_output = Task(links.exchange(other_output))
    output, grad_tokens = meet((output, grad_tokens), other_output, ups)
    output, grad_tokens = turn_back(info, output, other_output.result, grad_tokens)
    output, grad_tokens = finish((output, grad_tokens), heads, ups, downs)

    grad_up, sums = ups.result
    grad_up = grad_up.reshape(few, 2, CHIPS, SHARE).transpose(0, 2, 1, 3).reshape(few, HIDDEN)
    grad_out = heads.result[:, 6 * PART_COLS :]
    grad_qkv = jnp.concatenate(
        [heads.result[:, (3 * part + i) * PART_COLS : (3 * part + i + 1) * PART_COLS]
         for i in range(3) for part in range(2)],
        axis=1,
    )
    return (
        output,
        grad_tokens,
        jnp.sum(w_qkv.astype(F32) * grad_qkv, axis=1) / gain_one.astype(F32),
        grad_qkv,
        grad_out,
        jnp.sum(w_up.astype(F32) * grad_up, axis=1) / gain_two.astype(F32),
        grad_up,
        sums,
        downs.result,
    )


def solution(mesh):
    rows, vector = P(AXES, None), P(AXES)
    sizes = dict(mesh.shape)
    return jax.shard_map(
        functools.partial(layer, sizes),
        mesh=mesh,
        in_specs=(rows, rows, vector, rows, rows, vector, rows, vector, rows, rows),
        out_specs=(rows, rows, vector, rows, rows, vector, rows, vector, rows),
        check_vma=False,
    )
```

```python
import functools

import jax
import jax.numpy as jnp
from jax import lax
from jax.experimental import pallas as pl
from jax.experimental.pallas import tpu as pltpu
from jax.sharding import PartitionSpec as P

AXES = ("wide", "narrow")
EPSILON = 1e-05
BF = jnp.bfloat16
F32 = jnp.float32
WIDTH = 768
HIDDEN = 3072
ROWS = 1024
TILE = 256
BIG = 768
PAIRS = 6
HEAD = 64
PROB_COLS = 1792
CHIPS = 16
BLOCK = 48
SHARE = 96
MINE = 1536
LIMIT = 56 * 1024 * 1024


def mm(left, right):
    return lax.dot_general(left, right, (((1,), (0,)), ((), ())), preferred_element_type=F32)


def mm_nt(left, right):
    return lax.dot_general(left, right, (((1,), (1,)), ((), ())), preferred_element_type=F32)


def mm_tn(left, right):
    return lax.dot_general(left, right, (((0,), (0,)), ((), ())), preferred_element_type=F32)


def lanes(width=WIDTH):
    return lax.broadcasted_iota(jnp.int32, (1, width), 1)


def norm_parts(rows):
    total = jnp.sum(rows, axis=1, keepdims=True)
    squares = jnp.sum(rows * rows, axis=1, keepdims=True)
    inverse = lax.rsqrt((squares + total * total) * (1.0 / WIDTH) + EPSILON)
    expanded = jnp.where(lanes() == WIDTH - 1, -total, rows)
    return inverse, expanded


def norm_back(weighted, inverse, expanded):
    inner = jnp.sum(weighted * expanded, axis=1, keepdims=True) * (1.0 / WIDTH)
    full = inverse * (weighted - (inverse * inverse * inner) * expanded)
    last = full[:, WIDTH - 1 :]
    return jnp.where(lanes() == WIDTH - 1, 0.0, full - last)


def turn(start, forward):
    rows = lax.broadcasted_iota(jnp.int32, (TILE, 2 * TILE), 0)
    cols = lax.broadcasted_iota(jnp.int32, (TILE, 2 * TILE), 1)
    source = rows + start if forward else rows + TILE - start
    return jnp.where(cols == source, 1.0, 0.0).astype(BF)


def first_row(info):
    return jnp.where(info[2] == BIG, 0, jnp.where(info[3] == BIG, info[2], info[2] + info[3]))


def params(**more):
    return pltpu.CompilerParams(vmem_limit_bytes=LIMIT, **more)


def cost(flops, nbytes, transcendentals=0):
    return pl.CostEstimate(flops=flops, bytes_accessed=nbytes, transcendentals=transcendentals)


HBM = pl.BlockSpec(memory_space=pl.ANY)


def whole(*shape):
    return pl.BlockSpec(shape, lambda *i: (0,) * len(shape))


def row_tile(width, tile=TILE):
    return pl.BlockSpec((tile, width), lambda i, *s: (i, 0))


def col_tile(rows, width):
    return pl.BlockSpec((rows, width), lambda i, *s: (0, i))


def offset_of(place):
    return 4 * (place & 3) + (place >> 2)


def place_at(info, chip):
    offset = info[0] ^ chip
    return (offset >> 2) + 4 * (offset & 3)


def copies(info, pieces, target, cols=None):
    for side in range(2):
        half = info[1] ^ side

        def start(side=side, half=half):
            for place in range(CHIPS):
                source = pieces[4 * side + place // 4].at[pl.ds((place % 4) * BLOCK, BLOCK)]
                if cols is not None:
                    source = source.at[:, pl.ds(*cols)]
                block = pl.multiple_of((info[0] ^ offset_of(place)) * BLOCK, 16)
                pltpu.make_async_copy(source, *target(half, block)).start()

        if cols is None:
            start()
        else:
            pl.when(half == 1)(start)


def up_copies(info, pieces, store, sems):
    for part in range(2):
        cols = pl.ds(part * WIDTH, WIDTH)
        for place in range(CHIPS):
            source = pieces[place // 4].at[pl.ds((place % 4) * BLOCK, BLOCK), cols]
            block = pl.multiple_of((info[0] ^ offset_of(place)) * BLOCK, 16)
            pltpu.make_async_copy(source, store.at[pl.ds(block, BLOCK), cols], sems.at[part]).start()


def down_copies(info, pieces, store, sems):
    for place in range(CHIPS):
        chip = info[0] ^ offset_of(place)
        first = pl.multiple_of((chip & 7) * SHARE, 16)
        pltpu.make_async_copy(
            pieces[place // 4].at[pl.ds((place % 4) * SHARE, SHARE)],
            store.at[chip >> 3, pl.ds(first, SHARE)],
            sems.at[chip >> 3],
        ).start()


def by_half(store, sems):
    width = store.shape[1] // 2

    def target(half, first):
        cols = pl.ds(pl.multiple_of(half * width, 128), width)
        return store.at[pl.ds(first, BLOCK), cols], sems.at[half]

    return target


def one_half(store, semaphore):
    return lambda half, first: (store.at[pl.ds(first, BLOCK)], semaphore)


def arrived(ref, semaphore):
    pltpu.make_async_copy(ref, ref, semaphore).wait()


def halves_arrived(store, sems, halves=(0, 1)):
    width = store.shape[1] // 2
    for half in halves:
        arrived(store.at[:, pl.ds(half * width, width)], sems.at[half])


OUT_COLS = (128, WIDTH)
TURNED = pltpu.VMEM((2 * HEAD, ROWS), BF)
PAIR_SEMS = pltpu.SemaphoreType.DMA((2,))
SLOT_SEMS = pltpu.SemaphoreType.DMA((4,))
PART = 3
PART_COLS = PART * 2 * HEAD
SMALL = 128
A_COLS = 3 * PART_COLS + SMALL
B_COLS = 3 * PART_COLS + WIDTH + SMALL


def pack_kernel(qkv_ref, out_ref, one_ref, two_ref, bias_ref, w_up_ref, a_ref, b_ref, up_ref):
    few, share = one_ref.shape[1], bias_ref.shape[1]
    for part, ref in enumerate((a_ref, b_ref)):
        for i in range(3):
            first = i * WIDTH + part * PART_COLS
            ref[:, i * PART_COLS : (i + 1) * PART_COLS] = qkv_ref[:, first : first + PART_COLS]
    b_ref[:, 3 * PART_COLS : 3 * PART_COLS + WIDTH] = out_ref[...]
    place = lax.broadcasted_iota(jnp.int32, (few, SMALL), 1)

    def column(row, first):
        count = row.shape[1]
        at = lax.broadcasted_iota(jnp.int32, (few, count), 1)
        down = lax.broadcasted_iota(jnp.int32, (few, count), 0) + first
        return jnp.sum(jnp.where(at == down, row.astype(F32), 0.0), axis=1, keepdims=True)

    gains = jnp.where(place == 0, column(one_ref[...], 0), 0.0)
    gains = jnp.where(place == 1, column(two_ref[...], 0), gains)
    a_ref[:, A_COLS - SMALL :] = gains.astype(BF)
    bias = jnp.zeros((few, SMALL), F32)
    for i in range(share // few):
        bias = jnp.where(place == i, column(bias_ref[...], i * few), bias)
    b_ref[:, B_COLS - SMALL :] = bias.astype(BF)
    weights = w_up_ref[...].astype(F32)
    for core in range(2):
        blocks = [weights[:, SHARE * (2 * i + core) : SHARE * (2 * i + core + 1)] for i in range(CHIPS)]
        up_ref[:, core * MINE : (core + 1) * MINE] = jnp.concatenate(blocks, axis=1).astype(BF)


def pack(w_qkv, w_out, gain_one, gain_two, b_up, w_up):
    few = w_qkv.shape[0]
    return pl.pallas_call(
        pack_kernel,
        out_shape=[
            jax.ShapeDtypeStruct((few, cols), BF) for cols in (A_COLS, B_COLS, HIDDEN)
        ],
        compiler_params=params(),
        name="pack",
    )(w_qkv, w_out, gain_one[None], gain_two[None], b_up[None], w_up)


def join_kernel(info, *refs):
    own, other, outs = refs[:3], refs[3:6], refs[6:]
    first = info[1] == 0
    for mine, theirs, out in zip(own, other, outs):
        half = mine.shape[1] // 2
        cols = pl.ds(pl.multiple_of(info[1] * half, 128), half)
        mine, theirs = mine[:, cols].astype(F32), theirs[:, cols].astype(F32)
        out[...] = jnp.concatenate(
            [jnp.where(first, mine, theirs), jnp.where(first, theirs, mine)], axis=0
        ).astype(BF)


def join(info, own, other):
    shapes = [(2 * v.shape[0], v.shape[1] // 2) for v in own]
    return pl.pallas_call(
        join_kernel,
        grid_spec=pltpu.PrefetchScalarGridSpec(
            num_scalar_prefetch=1,
            grid=(1,),
            in_specs=[whole(*v.shape) for v in [*own, *other]],
            out_specs=[whole(*shape) for shape in shapes],
        ),
        out_shape=[jax.ShapeDtypeStruct(shape, BF) for shape in shapes],
        compiler_params=pltpu.CompilerParams(vmem_limit_bytes=8 * 1024 * 1024),
        name="join",
    )(info, *own, *other)


def before_kernel(info, tok_ref, cot_ref, x_ref, up_ref, down_ref, both, wide):
    step = pl.program_id(0)
    both[:, :TILE] = both[:, TILE:]
    both[0, TILE:, : WIDTH - 1] = tok_ref[...]
    both[1, TILE:, : WIDTH - 1] = cot_ref[...]

    @pl.when(step > 0)
    def _():
        pick = turn(first_row(info), True)
        wide[...] = mm(pick, both[0])
        x_ref[...] = jnp.where(lanes() == WIDTH - 1, 0.0, wide[...]).astype(BF)
        grads = jnp.where(lanes() == WIDTH - 1, 0.0, mm(pick, both[1]))
        up_ref[...] = grads.astype(BF)
        down_ref[...] = centred(grads).astype(BF)


def before(info, tokens, cotangent):
    shape = jax.ShapeDtypeStruct((ROWS, WIDTH), BF)
    tiles = ROWS // TILE
    source = pl.BlockSpec((TILE, WIDTH - 1), lambda i, *s: (lax.rem(i, tiles), 0))
    target = pl.BlockSpec((TILE, WIDTH), lambda i, *s: (jnp.maximum(i - 1, 0), 0))
    return pl.pallas_call(
        before_kernel,
        grid_spec=pltpu.PrefetchScalarGridSpec(
            num_scalar_prefetch=1,
            grid=(tiles + 1,),
            in_specs=[source] * 2,
            out_specs=[target] * 3,
            scratch_shapes=[pltpu.VMEM((2, 2 * TILE, WIDTH), BF), pltpu.VMEM((TILE, WIDTH), F32)],
        ),
        out_shape=[shape] * 3,
        compiler_params=params(),
        cost_estimate=cost(4 * ROWS * ROWS * WIDTH, 10 * ROWS * WIDTH),
        name="before",
    )(info, tokens, cotangent)


SPANS = ((0, 0, 256, 0), (256, 0, 512, 256), (512, 0, 768, 768), (768, 768, 256, 1536))


def tail_segments(info, axis):
    shape = (TILE, 1) if axis == 0 else (1, TILE)
    place = lax.broadcasted_iota(jnp.int32, shape, axis) + BIG + first_row(info)
    place = jnp.where(place >= ROWS, place - ROWS, place)
    found = jnp.zeros(shape, jnp.int32)
    bound = 0
    for j in range(3):
        bound = bound + info[2 + j]
        found = found + jnp.where(place >= bound, 1, 0)
    return found


def head_mask(head):
    place = lanes(2 * HEAD)
    return (place < HEAD) if head == 0 else (place >= HEAD)


def attend_pair(info, qkv, pair, out_ref, norm_ref, prob_ref, turned):
    cols = [pl.ds(pl.multiple_of(i * PART_COLS + pair * 2 * HEAD, 128), 2 * HEAD) for i in range(3)]
    causal = lax.broadcasted_iota(jnp.int32, (TILE, TILE), 0) >= lax.broadcasted_iota(
        jnp.int32, (TILE, TILE), 1
    )
    turned[...] = qkv[:, cols[1]].T
    for first, key_first, key_count, place in SPANS:
        queries = qkv[first : first + TILE, cols[0]]
        keys = turned[:, key_first : key_first + key_count]
        values = qkv[key_first : key_first + key_count, cols[2]]
        values = jnp.concatenate([values, jnp.ones_like(values)], axis=1)
        allowed = causal
        if first == BIG:
            allowed = causal & (tail_segments(info, 0) == tail_segments(info, 1))
        mixed = []
        for head in range(2):
            mine = jnp.where(head_mask(head), queries, 0) * BF(HEAD**-0.5)
            scores = mm(mine, keys)
            split = key_count - TILE
            last = jnp.where(allowed, scores[:, split:], -1e30)
            largest = jnp.max(last, axis=1, keepdims=True)
            if split:
                largest = jnp.maximum(largest, jnp.max(scores[:, :split], axis=1, keepdims=True))
            last = jnp.exp(last - largest).astype(BF)
            prob_ref[head, :, place + split : place + key_count] = last
            both = mm(last, values[split:])
            if split:
                early = jnp.exp(scores[:, :split] - largest).astype(BF)
                prob_ref[head, :, place : place + split] = early
                both += mm(early, values[:split])
            mixed.append(both)
        both = jnp.where(jnp.concatenate([head_mask(0)] * 2, axis=1), mixed[0], mixed[1])
        inverse = 1.0 / both[:, 2 * HEAD :]
        norm_ref[first : first + TILE, :] = inverse
        out_ref[first : first + TILE, :] = (both[:, : 2 * HEAD] * inverse).astype(BF)


def pair_cols(offset):
    return pl.BlockSpec((ROWS, 2 * HEAD), lambda i, *s: (0, offset + i))


PROB_SPEC = pl.BlockSpec((2, TILE, PROB_COLS), lambda i, *s: (i, 0, 0))
HEADS_SHAPES = [
    jax.ShapeDtypeStruct((ROWS, PART_COLS), BF),
    jax.ShapeDtypeStruct((ROWS, PART_COLS), F32),
    jax.ShapeDtypeStruct((2 * PART, TILE, PROB_COLS), BF),
]


def heads_a_kernel(info, x_ref, *rest):
    pieces, (normed_hbm, qkv_hbm, gains_ref, att_ref, norm_ref, prob_ref) = rest[:8], rest[8:14]
    store, normed, qkv, turned, sems, out_sems = rest[14:]
    step = pl.program_id(0)

    @pl.when(step == 0)
    def _():
        copies(info, pieces, by_half(store, sems))
        inverse, expanded = norm_parts(x_ref[...].astype(F32))
        expanded = expanded * inverse
        halves_arrived(store, sems)
        gains = store[:, 3 * PART_COLS :].astype(F32).T[:8]
        gains_ref[...] = gains
        normed[...] = (expanded * gains[:1]).astype(BF)
        pltpu.make_async_copy(normed, normed_hbm, out_sems.at[0]).start()
        for i in range(3):
            cols = slice(i * PART_COLS, (i + 1) * PART_COLS)
            qkv[:, cols] = mm(normed[...], store[:, cols]).astype(BF)
        pltpu.make_async_copy(qkv, qkv_hbm, out_sems.at[1]).start()

    attend_pair(info, qkv, step, att_ref, norm_ref, prob_ref, turned)

    @pl.when(step == PART - 1)
    def _():
        arrived(normed, out_sems.at[0])
        arrived(qkv, out_sems.at[1])


def heads_a(info, x, pieces):
    return pl.pallas_call(
        heads_a_kernel,
        grid_spec=pltpu.PrefetchScalarGridSpec(
            num_scalar_prefetch=1,
            grid=(PART,),
            in_specs=[whole(ROWS, WIDTH)] + [HBM] * 8,
            out_specs=[HBM, HBM, whole(8, WIDTH), pair_cols(0), pair_cols(0), PROB_SPEC],
            scratch_shapes=[
                pltpu.VMEM((WIDTH, A_COLS), BF), pltpu.VMEM((ROWS, WIDTH), BF),
                pltpu.VMEM((ROWS, 3 * PART_COLS), BF), TURNED, PAIR_SEMS, PAIR_SEMS,
            ],
        ),
        out_shape=[
            jax.ShapeDtypeStruct((ROWS, WIDTH), BF),
            jax.ShapeDtypeStruct((ROWS, 3 * PART_COLS), BF),
            jax.ShapeDtypeStruct((8, WIDTH), F32),
        ]
        + HEADS_SHAPES,
        compiler_params=params(),
        cost_estimate=cost(6 * ROWS * WIDTH * PART_COLS + 4 * 6 * 7 * TILE * TILE * 256, 20000000, 2752512),
        name="heads_a",
    )(info, x, *pieces)


def heads_b_kernel(info, normed_ref, gains_ref, a_att_hbm, x_hbm, *rest):
    pieces, (qkv_hbm, bias_ref, middle_hbm, second_hbm, att_ref, norm_ref, prob_ref) = rest[:8], rest[8:15]
    store, qkv, turned, att, x, middle, second, sems, in_sems, out_sems = rest[15:]
    step = pl.program_id(0)
    late = [
        pltpu.make_async_copy(a_att_hbm, att.at[:, pl.ds(0, PART_COLS)], in_sems.at[0]),
        pltpu.make_async_copy(x_hbm, x, in_sems.at[1]),
    ]

    @pl.when(step == 0)
    def _():
        copies(info, pieces, by_half(store, sems))
        for copy in late:
            copy.start()
        halves_arrived(store, sems)
        for i in range(3):
            cols = slice(i * PART_COLS, (i + 1) * PART_COLS)
            qkv[:, cols] = mm(normed_ref[...], store[:, cols]).astype(BF)
        bias_ref[...] = store[:, B_COLS - SMALL :].astype(F32).T[:8]
        pltpu.make_async_copy(qkv, qkv_hbm, out_sems.at[0]).start()

    attend_pair(info, qkv, step, att_ref, norm_ref, prob_ref, turned)
    att[:, pl.ds(pl.multiple_of(PART_COLS + step * 2 * HEAD, 128), 2 * HEAD)] = att_ref[...]

    @pl.when(step == PART - 1)
    def _():
        for copy in late:
            copy.wait()
        weights = store[:, 3 * PART_COLS : 3 * PART_COLS + WIDTH]
        for i in range(ROWS // TILE):
            rows = slice(i * TILE, (i + 1) * TILE)
            mixed = mm(att[rows, :], weights)
            mixed = mixed - jnp.sum(mixed, axis=1, keepdims=True) * (1.0 / WIDTH)
            value = x[rows, :].astype(F32) + jnp.where(lanes() == WIDTH - 1, 0.0, mixed)
            inverse, expanded = norm_parts(value)
            middle[rows, :] = value
            second[rows, :] = (expanded * inverse * gains_ref[1:2, :]).astype(BF)
            for j, (source, target) in enumerate(((middle, middle_hbm), (second, second_hbm))):
                pltpu.make_async_copy(source.at[rows], target.at[rows], out_sems.at[1 + j]).start()
        arrived(qkv, out_sems.at[0])
        arrived(middle, out_sems.at[1])
        arrived(second, out_sems.at[2])


def heads_b(info, normed, gains, a_att, x, pieces):
    return pl.pallas_call(
        heads_b_kernel,
        grid_spec=pltpu.PrefetchScalarGridSpec(
            num_scalar_prefetch=1,
            grid=(PART,),
            in_specs=[whole(ROWS, WIDTH), whole(8, WIDTH)] + [HBM] * 10,
            out_specs=[HBM, whole(8, WIDTH), HBM, HBM, pair_cols(0), pair_cols(0), PROB_SPEC],
            scratch_shapes=[
                pltpu.VMEM((WIDTH, B_COLS), BF), pltpu.VMEM((ROWS, 3 * PART_COLS), BF), TURNED,
                pltpu.VMEM((ROWS, WIDTH), BF), pltpu.VMEM((ROWS, WIDTH), BF),
                pltpu.VMEM((ROWS, WIDTH), F32), pltpu.VMEM((ROWS, WIDTH), BF),
                PAIR_SEMS, PAIR_SEMS, pltpu.SemaphoreType.DMA((3,)),
            ],
        ),
        out_shape=[
            jax.ShapeDtypeStruct((ROWS, 3 * PART_COLS), BF),
            jax.ShapeDtypeStruct((8, WIDTH), F32),
            jax.ShapeDtypeStruct((ROWS, WIDTH), F32),
            jax.ShapeDtypeStruct((ROWS, WIDTH), BF),
        ]
        + HEADS_SHAPES,
        compiler_params=params(),
        cost_estimate=cost(
            6 * ROWS * WIDTH * PART_COLS + 2 * ROWS * WIDTH * WIDTH + 4 * 6 * 7 * TILE * TILE * 256,
            25000000, 2752512,
        ),
        name="heads_b",
    )(info, normed, gains, a_att, x, *pieces)


GELU_A = 0.7978845608028654
GELU_B = 0.044715


def tokens_copies(refs, second, down_in, sems):
    return [
        pltpu.make_async_copy(ref, (second, down_in)[i // 2].at[i % 2], sems.at[i])
        for i, ref in enumerate(refs)
    ]


def feed_kernel(info, bias_ref, *rest):
    ins, pieces, (act_hbm, slope_hbm, *grads) = rest[:4], rest[4:8], rest[8:14]
    store, sems, second, down_in, in_sems, act, slope, stage, out_sems = rest[14:]
    late = tokens_copies(ins, second, down_in, in_sems)
    late[0].start()
    up_copies(info, pieces, store, sems)
    for i in (2, 1, 3):
        late[i].start()
    late[0].wait()
    sums = [None, None]
    for side in range(2):
        if side == 1:
            late[1].wait()
        for part in range(2):
            cols = slice(part * WIDTH, (part + 1) * WIDTH)
            if side == 0:
                arrived(store.at[:, pl.ds(part * WIDTH, WIDTH)], sems.at[part])
            slot = 2 * side + part
            for i in range(ROWS // TILE):
                rows = slice(i * TILE, (i + 1) * TILE)
                hidden = mm(second[side, rows, :], store[:, cols]) + bias_ref[:, cols]
                square = hidden * hidden
                bent = jnp.tanh(hidden * (GELU_A + (GELU_A * GELU_B) * square))
                half = 0.5 + 0.5 * bent
                act[slot, rows, :] = (hidden * half).astype(BF)
                tilt = hidden * (0.5 * GELU_A + (1.5 * GELU_A * GELU_B) * square)
                slope[slot, rows, :] = (half + tilt * (1.0 - bent * bent)).astype(BF)
            for source, target, which in ((act, act_hbm, 0), (slope, slope_hbm, 1)):
                pltpu.make_async_copy(source.at[slot], target.at[slot], out_sems.at[which]).start()
            if part == 0:
                late[2 + side].wait()
            found = mm_tn(act[slot], down_in[side])
            if side == 0:
                sums[part] = found
                continue
            total = sums[part] + found
            for i in range(8):
                block = total[SHARE * i : SHARE * (i + 1)].astype(BF)
                stage[place_at(info, 8 * part + i)] = block
    for i, target in enumerate(grads):
        pltpu.make_async_copy(stage.at[pl.ds(4 * i, 4)], target, out_sems.at[2]).start()
    arrived(act, out_sems.at[0])
    arrived(slope, out_sems.at[1])
    arrived(stage, out_sems.at[2])


BOTH = pltpu.VMEM((2, ROWS, WIDTH), BF)
FOUR = pltpu.VMEM((4, ROWS, WIDTH), BF)


def feed(info, second, other_second, down_in, other_down_in, bias, pieces):
    return pl.pallas_call(
        feed_kernel,
        grid_spec=pltpu.PrefetchScalarGridSpec(
            num_scalar_prefetch=1,
            grid=(1,),
            in_specs=[whole(1, MINE)] + [HBM] * 8,
            out_specs=[HBM] * 6,
            scratch_shapes=[
                pltpu.VMEM((WIDTH, MINE), BF), PAIR_SEMS, BOTH, BOTH, SLOT_SEMS, FOUR, FOUR,
                pltpu.VMEM((CHIPS, SHARE, WIDTH), BF), pltpu.SemaphoreType.DMA((3,)),
            ],
        ),
        out_shape=[jax.ShapeDtypeStruct((4, ROWS, WIDTH), BF)] * 2
        + [jax.ShapeDtypeStruct((4, SHARE, WIDTH), BF)] * 4,
        compiler_params=params(),
        cost_estimate=cost(4 * ROWS * WIDTH * HIDDEN, 6 * ROWS * HIDDEN + 4 * WIDTH * HIDDEN),
        name="feed",
    )(info, bias, second, other_second, down_in, other_down_in, *pieces)


UP_COLS = MINE + SMALL


def spread_out(info, grads, stage):
    for device in range(32):
        value = grads[24 * device : 24 * (device + 1)].astype(BF)
        stage[info[1] ^ (device & 1), place_at(info, device >> 1)] = value


def back_kernel(info, *rest):
    slope_hbm, ins, up_pieces, down_pieces = rest[0], rest[1:5], rest[5:9], rest[9:13]
    outs, own_hbm, other_hbm = rest[13:17], rest[17], rest[18]
    (down_store, down_sems, up_store, up_sems, second, down_in, in_sems, slope, slope_sems, grads,
     weighted, other, stage, spare, out_sems) = rest[19:]
    late = tokens_copies(ins, second, down_in, in_sems)
    slopes = [pltpu.make_async_copy(slope_hbm.at[i], slope.at[i], slope_sems.at[i]) for i in range(4)]
    late[2].start()
    down_copies(info, down_pieces, down_store, down_sems)
    slopes[0].start()
    up_copies(info, up_pieces, up_store, up_sems)
    for copy in (late[0], late[3], slopes[2], late[1], slopes[1], slopes[3]):
        copy.start()
    for part in range(2):
        cols = slice(part * WIDTH, (part + 1) * WIDTH)
        arrived(down_store.at[part], down_sems.at[part])
        for side in range(2):
            if part == 0:
                late[2 + side].wait()
            value = mm_nt(down_in[side], down_store[part])
            slopes[2 * side + part].wait()
            bias = jnp.zeros((1, WIDTH), F32)
            for i in range(ROWS // TILE):
                rows = slice(i * TILE, (i + 1) * TILE)
                few = (slope[2 * side + part, rows, :].astype(F32) * value[rows]).astype(BF)
                grads[side, rows, :] = few
                bias += jnp.sum(few.astype(F32), axis=0, keepdims=True)
            if side == 0:
                arrived(up_store.at[:, pl.ds(part * WIDTH, WIDTH)], up_sems.at[part])
            if part == 0:
                weighted[side] = mm_nt(grads[side], up_store[:, cols])
            elif side == 0:
                weighted[0] += mm_nt(grads[0], up_store[:, cols])
                pltpu.make_async_copy(weighted.at[0], own_hbm, out_sems.at[0]).start()
            else:
                other[...] = (weighted[1] + mm_nt(grads[1], up_store[:, cols])).astype(BF)
                pltpu.make_async_copy(other, other_hbm, out_sems.at[1]).start()
            if part == 0:
                late[side].wait()
            found = mm_tn(second[side], grads[side])
            if side == 0:
                sums, biases = found, bias
        total = sums + found
        for chip in range(CHIPS):
            block = total[BLOCK * chip : BLOCK * (chip + 1)].astype(BF)
            stage[part, place_at(info, chip)] = block
        for i, target in enumerate(outs):
            pltpu.make_async_copy(
                stage.at[part, pl.ds(4 * i, 4)], target.at[:, :, pl.ds(part * WIDTH, WIDTH)], out_sems.at[2]
            ).start()
        row = biases + bias
        for i in range(8):
            few = jnp.concatenate(
                [row[:, SHARE * i : SHARE * (i + 1)], jnp.zeros((1, SMALL - SHARE), F32)], axis=1
            )
            spare[place_at(info, 8 * part + i)] = jnp.broadcast_to(few, (BLOCK, SMALL)).astype(BF)
    for i, target in enumerate(outs):
        pltpu.make_async_copy(
            spare.at[pl.ds(4 * i, 4)], target.at[:, :, pl.ds(MINE, SMALL)], out_sems.at[3]
        ).start()
    arrived(weighted.at[0], out_sems.at[0])
    arrived(other, out_sems.at[1])
    arrived(stage, out_sems.at[2])
    arrived(spare, out_sems.at[3])


def back(info, second, other_second, down_in, other_down_in, slope, up_pieces, down_pieces):
    return pl.pallas_call(
        back_kernel,
        grid_spec=pltpu.PrefetchScalarGridSpec(
            num_scalar_prefetch=1,
            grid=(1,),
            in_specs=[HBM] * 13,
            out_specs=[HBM] * 6,
            scratch_shapes=[
                pltpu.VMEM((2, WIDTH, WIDTH), BF), PAIR_SEMS, pltpu.VMEM((WIDTH, MINE), BF), PAIR_SEMS,
                BOTH, BOTH, SLOT_SEMS, FOUR, SLOT_SEMS, BOTH,
                pltpu.VMEM((2, ROWS, WIDTH), F32),
                pltpu.VMEM((ROWS, WIDTH), BF),
                pltpu.VMEM((2, CHIPS, BLOCK, WIDTH), BF),
                pltpu.VMEM((CHIPS, BLOCK, SMALL), BF),
                SLOT_SEMS,
            ],
        ),
        out_shape=[jax.ShapeDtypeStruct((4, BLOCK, UP_COLS), BF)] * 4
        + [jax.ShapeDtypeStruct((ROWS, WIDTH), F32), jax.ShapeDtypeStruct((ROWS, WIDTH), BF)],
        compiler_params=params(),
        cost_estimate=cost(6 * ROWS * WIDTH * HIDDEN, 35000000),
        name="back",
    )(info, slope, second, other_second, down_in, other_down_in, *up_pieces, *down_pieces)


def pair_grad(q_ref, k_ref, v_ref, grad_ref, att_ref, norm_ref, prob_ref, dq_ref, dk_ref, dv_ref,
              key_sum, value_sum, values, scaled, turned):
    factor = HEAD**-0.5
    values[...] = v_ref[...].T
    turned[0] = q_ref[...].T
    scaled[...] = (grad_ref[...].astype(F32) * norm_ref[...]).astype(BF)
    turned[1] = scaled[...].T
    key_sum[...] = jnp.zeros_like(key_sum)
    value_sum[...] = jnp.zeros_like(value_sum)
    for first, key_first, key_count, place in SPANS:
        rows = slice(first, first + TILE)
        keys_at = slice(key_first, key_first + key_count)
        grads = scaled[rows, :]
        product = grads.astype(F32) * att_ref[rows, :].astype(F32)
        keys = k_ref[keys_at, :]
        parts = []
        for head in range(2):
            mask = head_mask(head)
            mine = slice(HEAD * head, HEAD * (head + 1))
            probs = prob_ref[head, :, place : place + key_count]
            inner = jnp.sum(jnp.where(mask, product, 0.0), axis=1, keepdims=True)
            slopes = mm(jnp.where(mask, grads, 0), values[:, keys_at]) - inner
            slopes = (probs.astype(F32) * slopes).astype(BF)
            parts.append(mm(slopes, keys))
            value_sum[mine, keys_at] += mm(turned[1, mine, rows], probs)
            key_sum[mine, keys_at] += mm(turned[0, mine, rows], slopes)
        dq_ref[rows, :] = (jnp.where(head_mask(0), parts[0], parts[1]) * factor).astype(BF)
    dk_ref[...] = (key_sum[...].T * factor).astype(BF)
    dv_ref[...] = value_sum[...].T.astype(BF)


PAIR_SCRATCH = [
    pltpu.VMEM((2 * HEAD, ROWS), F32), pltpu.VMEM((2 * HEAD, ROWS), F32), TURNED,
    pltpu.VMEM((ROWS, 2 * HEAD), BF), pltpu.VMEM((2, 2 * HEAD, ROWS), BF),
]


HEADS_COLS = 4 * WIDTH


def attend_grad_kernel(info, gain_ref, weighted_hbm, other_hbm, middle_hbm, up_hbm, a_att_hbm, b_att_hbm,
                       normed_hbm, *rest):
    pieces, groups, outs = rest[:8], (rest[8:14], rest[14:20]), rest[20:23]
    targets, total_hbm, pair_scratch = rest[23:25], rest[25], rest[26:31]
    (weighted, other, middle, up, in_sems, store, semaphore, total, mixed, grad_att, att, normed, late_sems,
     turned, kept, stage, out_sems) = rest[31:]
    step = pl.program_id(0)
    late = [
        pltpu.make_async_copy(a_att_hbm, att.at[:, pl.ds(0, PART_COLS)], late_sems.at[0]),
        pltpu.make_async_copy(b_att_hbm, att.at[:, pl.ds(PART_COLS, PART_COLS)], late_sems.at[1]),
        pltpu.make_async_copy(normed_hbm, normed, late_sems.at[2]),
    ]

    def weights_grad(i, value):
        spread_out(info, value, stage.at[i])
        for which, target in enumerate(targets):
            pltpu.make_async_copy(
                stage.at[i, which], target.at[:, :, pl.ds(i * WIDTH, WIDTH)], out_sems.at[0]
            ).start()

    @pl.when(step == 0)
    def _():
        early = []
        for i in range(ROWS // TILE):
            rows = pl.ds(i * TILE, TILE)
            early.append([
                pltpu.make_async_copy(source.at[rows], target.at[rows], in_sems.at[4 * i + j])
                for j, (source, target) in enumerate(
                    ((middle_hbm, middle), (weighted_hbm, weighted), (other_hbm, other), (up_hbm, up))
                )
            ])
            for copy in early[-1]:
                copy.start()
        copies(info, pieces, one_half(store, semaphore), OUT_COLS)
        for copy in late:
            copy.start()
        for i in range(ROWS // TILE):
            rows = slice(i * TILE, (i + 1) * TILE)
            for copy in early[i]:
                copy.wait()
            inverse, expanded = norm_parts(middle[rows, :])
            value = (weighted[rows, :] + other[rows, :].astype(F32)) * gain_ref[1:2, :]
            value = up[rows, :].astype(F32) + norm_back(value, inverse, expanded)
            total[rows, :] = value
            mixed[rows, :] = centred(value).astype(BF)
        pltpu.make_async_copy(total, total_hbm, out_sems.at[1]).start()
        arrived(store, semaphore)
        grad_att[...] = mm_nt(mixed[...], store[...]).astype(BF)

    place = pl.ds(pl.multiple_of(step * 2 * HEAD, 2 * HEAD), 2 * HEAD)
    for group, (q_ref, k_ref, v_ref, att_ref, norm_ref, prob_ref) in enumerate(groups):

        @pl.when((step < PART) if group == 0 else (step >= PART))
        def _(q_ref=q_ref, k_ref=k_ref, v_ref=v_ref, att_ref=att_ref, norm_ref=norm_ref, prob_ref=prob_ref):
            pair_grad(
                q_ref, k_ref, v_ref, grad_att.at[:, place], att_ref, norm_ref, prob_ref, *outs, *pair_scratch
            )

    for i in range(3):
        kept[i, :, place] = outs[i][...]

    @pl.when(step == 0)
    def _():
        for copy in late:
            copy.wait()
        weights_grad(3, mm_tn(att[...], mixed[...]))
        turned[...] = normed[...].T

    @pl.when(step == PAIRS - 1)
    def _():
        for i in range(3):
            weights_grad(i, mm(turned[...], kept[i]))
        arrived(stage, out_sems.at[0])
        arrived(total, out_sems.at[1])


def centred(branch):
    return branch - jnp.sum(branch, axis=1, keepdims=True) * (1.0 / WIDTH)


def group_specs(group):
    def at(i):
        return jnp.clip(i - PART * group, 0, PART - 1)

    def cols(offset):
        return pl.BlockSpec((ROWS, 2 * HEAD), lambda i, *s: (0, offset + at(i)))

    probs = pl.BlockSpec((2, TILE, PROB_COLS), lambda i, *s: (at(i), 0, 0))
    return [cols(0), cols(PART), cols(2 * PART), cols(0), cols(0), probs]


def attend_grad(info, weighted, other, middle, upstream, gains, normed, group_a, group_b, pieces):
    attended = [group[1] for group in (group_a, group_b)]
    blocks = [v for qkv, *others in (group_a, group_b) for v in [qkv, qkv, qkv, *others]]
    return pl.pallas_call(
        attend_grad_kernel,
        grid_spec=pltpu.PrefetchScalarGridSpec(
            num_scalar_prefetch=1,
            grid=(PAIRS,),
            in_specs=[whole(8, WIDTH)] + [HBM] * 15 + group_specs(0) + group_specs(1),
            out_specs=[pair_cols(0)] * 3 + [HBM] * 3,
            scratch_shapes=PAIR_SCRATCH
            + [
                pltpu.VMEM((ROWS, WIDTH), F32), pltpu.VMEM((ROWS, WIDTH), BF),
                pltpu.VMEM((ROWS, WIDTH), F32), pltpu.VMEM((ROWS, WIDTH), BF),
                pltpu.SemaphoreType.DMA((16,)),
                pltpu.VMEM((WIDTH, WIDTH), BF), pltpu.SemaphoreType.DMA,
                pltpu.VMEM((ROWS, WIDTH), F32), pltpu.VMEM((ROWS, WIDTH), BF),
                pltpu.VMEM((ROWS, WIDTH), BF), pltpu.VMEM((ROWS, WIDTH), BF),
                pltpu.VMEM((ROWS, WIDTH), BF), pltpu.SemaphoreType.DMA((3,)),
                pltpu.VMEM((WIDTH, ROWS), BF), pltpu.VMEM((3, ROWS, WIDTH), BF),
                pltpu.VMEM((4, 2, CHIPS, 24, WIDTH), BF), PAIR_SEMS,
            ],
        ),
        out_shape=[jax.ShapeDtypeStruct((ROWS, WIDTH), BF)] * 3
        + [jax.ShapeDtypeStruct((CHIPS, 24, HEADS_COLS), BF)] * 2
        + [jax.ShapeDtypeStruct((ROWS, WIDTH), F32)],
        compiler_params=params(),
        cost_estimate=cost(16 * 6 * 7 * TILE * TILE * 256 + 8 * ROWS * WIDTH * WIDTH, 45000000),
        name="attend_grad",
    )(info, gains, weighted, other, middle, upstream, *attended, normed, *pieces, *blocks)


def last_kernel(info, act_ref, middle_ref, gain_ref, *rest):
    parts, x_hbm, total_hbm, down_pieces = rest[:3], rest[3], rest[4], rest[5:9]
    a_pieces, b_pieces, (out_ref, other_ref, grad_ref) = rest[9:17], rest[17:25], rest[25:28]
    down_store, down_sems, a_store, b_store, a_sems, b_sems, grads, x, total, weighted, sems = rest[28:]
    step = pl.program_id(0)
    late = [
        pltpu.make_async_copy(source, target, sems.at[i])
        for i, (source, target) in enumerate(
            [(part, grads.at[i]) for i, part in enumerate(parts)] + [(x_hbm, x), (total_hbm, total)]
        )
    ]

    @pl.when(step == 0)
    def _():
        down_copies(info, down_pieces, down_store, down_sems)
        for i in range(2):
            arrived(down_store.at[i], down_sems.at[i])
        copies(info, a_pieces, by_half(a_store, a_sems))
        copies(info, b_pieces, by_half(b_store, b_sems))
        for copy in late:
            copy.start()

    branch = mm(act_ref[0], down_store[0]) + mm(act_ref[1], down_store[1])
    out_ref[...] = middle_ref[...] + centred(branch)
    branch = mm(act_ref[2], down_store[0]) + mm(act_ref[3], down_store[1])
    other_ref[...] = centred(branch).astype(BF)

    for i in range(3):

        @pl.when(step == i + 1)
        def _(i=i):
            if i == 0:
                halves_arrived(a_store, a_sems)
                halves_arrived(b_store, b_sems)
            late[i].wait()
            cols = slice(i * PART_COLS, (i + 1) * PART_COLS)
            found = mm_nt(grads[i, :, :PART_COLS], a_store[:, cols])
            found += mm_nt(grads[i, :, PART_COLS:], b_store[:, cols])
            weighted[...] = found if i == 0 else weighted[...] + found

    @pl.when(step == 3)
    def _():
        late[3].wait()
        late[4].wait()
        for i in range(ROWS // TILE):
            rows = slice(i * TILE, (i + 1) * TILE)
            inverse, expanded = norm_parts(x[rows, :].astype(F32))
            back = norm_back(weighted[rows, :] * gain_ref[0:1, :], inverse, expanded)
            grad_ref[rows, :] = (total[rows, :] + back).astype(BF)


def last(info, active, middle, parts, x, total, gains, down_pieces, a_pieces, b_pieces):
    act_tile = pl.BlockSpec((4, TILE, WIDTH), lambda i, *s: (0, i, 0))
    return pl.pallas_call(
        last_kernel,
        grid_spec=pltpu.PrefetchScalarGridSpec(
            num_scalar_prefetch=1,
            grid=(ROWS // TILE,),
            in_specs=[act_tile, row_tile(WIDTH), whole(8, WIDTH)] + [HBM] * 25,
            out_specs=[row_tile(WIDTH)] * 2 + [whole(ROWS, WIDTH)],
            scratch_shapes=[
                pltpu.VMEM((2, WIDTH, WIDTH), BF), PAIR_SEMS,
                pltpu.VMEM((WIDTH, A_COLS), BF), pltpu.VMEM((WIDTH, B_COLS), BF), PAIR_SEMS, PAIR_SEMS,
                pltpu.VMEM((3, ROWS, WIDTH), BF), pltpu.VMEM((ROWS, WIDTH), BF),
                pltpu.VMEM((ROWS, WIDTH), F32), pltpu.VMEM((ROWS, WIDTH), F32),
                pltpu.SemaphoreType.DMA((5,)),
            ],
        ),
        out_shape=[jax.ShapeDtypeStruct((ROWS, WIDTH), dtype) for dtype in (F32, BF, BF)],
        compiler_params=params(),
        cost_estimate=cost(2 * ROWS * WIDTH * HIDDEN + 6 * ROWS * WIDTH * WIDTH, 30000000),
        name="last",
    )(info, active, middle, gains, *parts, x, total, *down_pieces, *a_pieces, *b_pieces)


def turn_back_kernel(info, own_ref, other_ref, two_ref, out_ref, grad_ref, both):
    step = pl.program_id(0)
    both[:, :TILE] = both[:, TILE:]
    both[0, TILE:] = (own_ref[...] + other_ref[...].astype(F32)).astype(BF)
    both[1, TILE:] = two_ref[...]

    @pl.when(step > 0)
    def _():
        pick = turn(first_row(info), False)
        out_ref[...] = mm(pick, both[0]).astype(BF)[:, : WIDTH - 1]
        grad_ref[...] = mm(pick, both[1]).astype(BF)[:, : WIDTH - 1]


def turn_back(info, own, other, two):
    tiles = ROWS // TILE
    source = pl.BlockSpec((TILE, WIDTH), lambda i, *s: (lax.rem(i + tiles - 1, tiles), 0))
    target = pl.BlockSpec((TILE, WIDTH - 1), lambda i, *s: (jnp.maximum(i - 1, 0), 0))
    return pl.pallas_call(
        turn_back_kernel,
        grid_spec=pltpu.PrefetchScalarGridSpec(
            num_scalar_prefetch=1,
            grid=(tiles + 1,),
            in_specs=[source] * 3,
            out_specs=[target] * 2,
            scratch_shapes=[pltpu.VMEM((2, 2 * TILE, WIDTH), BF)],
        ),
        out_shape=[jax.ShapeDtypeStruct((ROWS, WIDTH - 1), BF)] * 2,
        compiler_params=pltpu.CompilerParams(vmem_limit_bytes=24 * 1024 * 1024),
        cost_estimate=cost(4 * ROWS * ROWS * WIDTH, 8 * ROWS * WIDTH),
        name="turn_back",
    )(info, own, other, two)


def heads_sum_kernel(first_ref, *rest):
    others, (weights_ref, gain_ref), (grad_ref, out_ref, norm_ref) = rest[:-5], rest[-5:-3], rest[-3:]
    total = first_ref[...]
    for ref in others:
        total += ref[...].astype(F32)
    grads = total[:, : 3 * WIDTH]
    grad_ref[...] = grads
    out_ref[...] = total[:, 3 * WIDTH :]
    found = jnp.sum(weights_ref[...].astype(F32) * grads, axis=1, keepdims=True)
    place = lax.broadcasted_iota(jnp.int32, (found.shape[0],) * 2, 0)
    across = lax.broadcasted_iota(jnp.int32, (found.shape[0],) * 2, 1)
    row = jnp.sum(jnp.where(place == across, found, 0.0), axis=0, keepdims=True)
    norm_ref[...] = row / gain_ref[...].astype(F32)


def heads_sum(terms, w_qkv, gain):
    few = gain.shape[0]
    grad_qkv, grad_out, grad_gain = pl.pallas_call(
        heads_sum_kernel,
        out_shape=[jax.ShapeDtypeStruct((few, cols), F32) for cols in (3 * WIDTH, WIDTH, few)][:2]
        + [jax.ShapeDtypeStruct((1, few), F32)],
        compiler_params=params(),
        name="heads_sum",
    )(*terms, w_qkv, gain[None])
    return grad_qkv, grad_out, grad_gain.reshape(few)


WAYS = {"core": (0, 1), "x": (0, 2), "y": (1, 0), "xy": (1, 2), "z1": (2, 0), "z2": (4, 0), "z3": (6, 0)}


def add_low(left, right):
    return (left.astype(F32) + right.astype(F32)).astype(BF)


class Cube:
    def __init__(self, sizes):
        self.sizes = sizes
        wide, narrow = lax.axis_index("wide"), lax.axis_index("narrow")
        self.place = jnp.stack([wide * 2 + (narrow >> 1), narrow & 1]).astype(jnp.int32)

    def hop(self, value, way):
        wide, narrow = WAYS[way]
        if wide == 0:
            return lax.ppermute(value, "narrow", [(i, i ^ narrow) for i in range(self.sizes["narrow"])])
        if narrow == 0:
            return lax.ppermute(value, "wide", [(i, i ^ wide) for i in range(self.sizes["wide"])])
        bits = wide * self.sizes["narrow"] + narrow
        count = self.sizes["wide"] * self.sizes["narrow"]
        return lax.ppermute(value, AXES, [(i, i ^ bits) for i in range(count)])

    def gather(self, block):
        others = yield [self.hop(block, way) for way in ("z1", "z2", "z3")]
        return (yield from self.across(jnp.concatenate([block] + others)))

    def gather_slowly(self, block):
        near = yield from self.along_z(block)
        return (yield from self.across(near))

    def along_z(self, block):
        for way in ("z1", "z2"):
            other = yield self.hop(block, way)
            block = jnp.concatenate([block, other])
        return block

    def across(self, near):
        own = yield from self.plane(near)
        twins = yield [self.hop(part, "core") for part in own]
        return own + twins

    def plane(self, near):
        far = yield [self.hop(near, way) for way in ("x", "y", "xy")]
        return [near] + far

    def gather_mine(self, block):
        near = yield from self.along_z(block)
        return (yield from self.plane(near))

    def exchange(self, value):
        return (yield self.hop(value, "core"))

    def blocks(self, info, shards):
        others = [self.hop(shard, "core") for shard in shards]
        return join(info, shards, others)

    def sum_plane(self, keep):
        others = yield [self.hop(quad, way) for quad, way in zip(keep[1:], ("x", "y", "xy"))]
        return sum([other.astype(F32) for other in others], keep[0].astype(F32))

    def sum_z_slowly(self, both):
        got = yield self.hop(both[2:].astype(BF), "z2")
        both = both[:2] + got.astype(F32)
        got = yield self.hop(both[1].astype(BF), "z1")
        return both[0] + got.astype(F32)

    def reduce_up(self, keep):
        both = yield from self.sum_plane(keep)
        total = yield from self.sum_z_slowly(both)
        sums = total[0, MINE : MINE + SHARE]
        total = total[:, :MINE].reshape(2, -1, MINE)
        core = self.place[1]
        mine = lax.dynamic_index_in_dim(total, core, 0, False)
        got = yield self.hop(lax.dynamic_index_in_dim(total, 1 - core, 0, False), "core")
        first = core == 0
        return jnp.concatenate([jnp.where(first, mine, got), jnp.where(first, got, mine)], axis=1), sums

    def reduce_mine(self, keep):
        both = yield from self.sum_plane(keep)
        return (yield from self.sum_z_slowly(both))

    def reduce(self, keep, send):
        got = yield self.hop(send, "core")
        both = [keep[4 * i : 4 * i + 4].astype(F32) + got[4 * i : 4 * i + 4].astype(F32) for i in range(4)]
        others = yield [self.hop(both[i].astype(BF), way) for i, way in ((1, "x"), (2, "y"), (3, "xy"))]
        both = sum([other.astype(F32) for other in others], both[0])
        others = yield [self.hop(both[i].astype(BF), way) for i, way in ((1, "z1"), (2, "z2"), (3, "z3"))]
        return [both[0]] + others


class Plain:
    def __init__(self, sizes):
        self.sizes = sizes
        self.core = (lax.axis_index("narrow") & 1).astype(jnp.int32)
        self.place = jnp.stack([jnp.zeros_like(self.core), self.core])

    def exchange(self, value):
        count = self.sizes["narrow"]
        other = lax.ppermute(value, "narrow", [(i, i ^ 1) for i in range(count)])
        yield ()
        return other

    def blocks(self, info, shards):
        return shards

    def by_place(self, rows):
        return rows.reshape(4, 4, -1, rows.shape[1]).transpose(1, 0, 2, 3).reshape(4, -1, rows.shape[1])

    def by_chip(self, blocks):
        return blocks.reshape(4, 4, *blocks.shape[1:]).swapaxes(0, 1).reshape(blocks.shape)

    def mine_first(self, one, two):
        first = self.core == 0
        return jnp.where(first, one, two), jnp.where(first, two, one)

    def gather(self, shard):
        yield ()
        full = self.by_place(lax.all_gather(shard, AXES, axis=0, tiled=True))
        cols = full.shape[2] // 2
        halves = self.mine_first(full[:, :, :cols], full[:, :, cols:])
        return [half[i] for half in halves for i in range(4)]

    gather_slowly = gather

    def gather_mine(self, shard):
        yield ()
        full = lax.all_gather(shard, AXES, axis=0, tiled=True)
        if full.shape[0] == WIDTH:
            one, two = full[:, :MINE], full[:, MINE:]
        else:
            one, two = [
                full.reshape(CHIPS, 2, SHARE, WIDTH)[:, i].reshape(MINE, WIDTH) for i in range(2)
            ]
        full = self.by_place(self.mine_first(one, two)[0])
        return [full[i] for i in range(4)]

    def scatter(self, full):
        return lax.psum_scatter(full, AXES, scatter_dimension=0, tiled=True).astype(F32)

    def apart(self, value):
        return self.mine_first(value, jnp.zeros_like(value))

    def reduce_up(self, keep):
        yield ()
        full = self.by_chip(jnp.concatenate(keep))
        sums = jnp.stack(self.apart(full[:, 0, MINE : MINE + SHARE].astype(F32)), axis=1)
        both = jnp.concatenate(self.apart(full[:, :, :MINE].reshape(WIDTH, MINE)), axis=1)
        return self.scatter(both), self.scatter(sums.reshape(HIDDEN, 1))[:, 0]

    def reduce_mine(self, keep):
        yield ()
        full = jnp.stack(self.apart(self.by_chip(jnp.concatenate(keep))), axis=1)
        return self.scatter(full.reshape(HIDDEN, WIDTH))

    def reduce(self, keep, send):
        yield ()
        full = jnp.stack(self.mine_first(self.by_chip(keep), self.by_chip(send)), axis=1)
        return [self.scatter(full.reshape(WIDTH, -1))]


class Task:
    def __init__(self, steps):
        self.steps, self.flight, self.over, self.result = steps, (), False, None
        self.go(None)

    def go(self, arrived_now):
        try:
            self.flight = self.steps.send(arrived_now)
        except StopIteration as end:
            self.flight, self.over, self.result = (), True, end.value


def meet(values, *tasks, waiting=()):
    tasks = [task for task in tasks if not task.over]
    every = tasks + list(waiting)
    values, flights = lax.optimization_barrier((values, [task.flight for task in every]))
    for task, flight in zip(every, flights):
        task.flight = flight
    for task in tasks:
        task.go(task.flight)
    return values


def finish(values, *tasks):
    while not all(task.over for task in tasks):
        values = meet(values, *tasks)
    return values


def layer(sizes, tokens, lengths, gain_one, w_qkv, w_out, gain_two, w_up, b_up, w_down, cotangent):
    share, few = b_up.shape[0], gain_one.shape[0]
    links = (Cube if sizes["wide"] == 8 and sizes["narrow"] == 4 else Plain)(sizes)
    info = jnp.concatenate([links.place, lengths[0]])
    core = info[1]

    a_block, b_block, up_block = links.blocks(info, pack(w_qkv, w_out, gain_one, gain_two, b_up, w_up))
    group_a, group_b = Task(links.gather(a_block)), Task(links.gather_slowly(b_block))
    tokens, cotangent, up_block = meet((tokens, cotangent, up_block), group_a, group_b)
    up = Task(links.gather_mine(up_block))
    x, upstream, down_in = before(info, tokens, cotangent)
    x = meet(x, group_a, waiting=(group_b, up))
    x, w_down = meet((x, w_down), group_a, group_b, up)
    down = Task(links.gather_mine(w_down))
    normed, qkv_a, gains, att_a, norms_a, probs_a = heads_a(info, x, group_a.result)
    normed, att_a, x = meet((normed, att_a, x), group_b, waiting=(up, down))
    normed, att_a, x, down_in = meet((normed, att_a, x, down_in), group_b, up, down)
    other_down_in = Task(links.exchange(down_in))
    qkv_b, bias, middle, second, att_b, norms_b, probs_b = heads_b(
        info, normed, gains, att_a, x, group_b.result
    )
    bias = bias[: share // few].reshape(share // few, -1, few).transpose(1, 0, 2)
    bias = bias.reshape(CHIPS, 2, SHARE)
    bias = jnp.where(core == 0, bias[:, 0], bias[:, 1]).reshape(1, MINE)
    bias, second = meet((bias, second), up, other_down_in, waiting=(down,))
    other_second = Task(links.exchange(second))
    bias = meet(bias, other_second, down)
    inputs = second, other_second.result, down_in, other_down_in.result
    active, slope, *grad_down = feed(info, *inputs, bias, up.result)
    slope, grad_down = meet((slope, grad_down), down)
    downs = Task(links.reduce_mine(grad_down))
    *grad_up, weighted, other_weighted = back(info, *inputs, slope, up.result, down.result)
    weighted, other_weighted, grad_up = meet((weighted, other_weighted, grad_up), downs)
    other_weighted = Task(links.exchange(other_weighted))
    ups = Task(links.reduce_up(grad_up))
    weighted = finish(weighted, other_weighted)
    *parts, keep, send, total = attend_grad(
        info, weighted, other_weighted.result, middle, upstream, gains, normed,
        (qkv_a, att_a, norms_a, probs_a), (qkv_b, att_b, norms_b, probs_b), group_b.result,
    )
    active, parts, keep, send = meet((active, parts, keep, send), waiting=(ups, downs))
    heads = Task(links.reduce(keep, send))
    active, parts = meet((active, parts), heads, ups, downs)
    output, other_output, grad_tokens = last(
        info, active, middle, parts, x, total, gains, down.result, group_a.result, group_b.result,
    )
    output, grad_tokens, other_output = meet((output, grad_tokens, other_output), heads, ups, downs)
    other_output = Task(links.exchange(other_output))
    output, grad_tokens = meet((output, grad_tokens), other_output, ups)
    output, grad_tokens = turn_back(info, output, other_output.result, grad_tokens)
    output, grad_tokens = finish((output, grad_tokens), heads, ups, downs)

    grad_up, sums = ups.result
    grad_up = grad_up.reshape(few, 2, CHIPS, SHARE).transpose(0, 2, 1, 3).reshape(few, HIDDEN)
    grad_qkv, grad_out, grad_gain = heads_sum(heads.result, w_qkv, gain_one)
    return (
        output,
        grad_tokens,
        grad_gain,
        grad_qkv,
        grad_out,
        jnp.sum(w_up.astype(F32) * grad_up, axis=1) / gain_two.astype(F32),
        grad_up,
        sums,
        downs.result,
    )


def solution(mesh):
    rows, vector = P(AXES, None), P(AXES)
    sizes = dict(mesh.shape)
    return jax.shard_map(
        functools.partial(layer, sizes),
        mesh=mesh,
        in_specs=(rows, rows, vector, rows, rows, vector, rows, vector, rows, rows),
        out_specs=(rows, rows, vector, rows, rows, vector, rows, vector, rows),
        check_vma=False,
    )
```

```python
import functools

import jax
import jax.numpy as jnp
from jax import lax
from jax.experimental import pallas as pl
from jax.experimental.pallas import tpu as pltpu
from jax.sharding import PartitionSpec as P

AXES = ("wide", "narrow")
EPSILON = 1e-05
BF = jnp.bfloat16
F32 = jnp.float32
WIDTH = 768
HIDDEN = 3072
ROWS = 1024
TILE = 256
BIG = 768
PAIRS = 6
HEAD = 64
PROB_COLS = 1792
CHIPS = 16
BLOCK = 48
SHARE = 96
MINE = 1536
LIMIT = 56 * 1024 * 1024


def mm(left, right):
    return lax.dot_general(left, right, (((1,), (0,)), ((), ())), preferred_element_type=F32)


def mm_nt(left, right):
    return lax.dot_general(left, right, (((1,), (1,)), ((), ())), preferred_element_type=F32)


def mm_tn(left, right):
    return lax.dot_general(left, right, (((0,), (0,)), ((), ())), preferred_element_type=F32)


def lanes(width=WIDTH):
    return lax.broadcasted_iota(jnp.int32, (1, width), 1)


def norm_parts(rows):
    total = jnp.sum(rows, axis=1, keepdims=True)
    squares = jnp.sum(rows * rows, axis=1, keepdims=True)
    inverse = lax.rsqrt((squares + total * total) * (1.0 / WIDTH) + EPSILON)
    expanded = jnp.where(lanes() == WIDTH - 1, -total, rows)
    return inverse, expanded


def norm_back(weighted, inverse, expanded):
    inner = jnp.sum(weighted * expanded, axis=1, keepdims=True) * (1.0 / WIDTH)
    full = inverse * (weighted - (inverse * inverse * inner) * expanded)
    last = full[:, WIDTH - 1 :]
    return jnp.where(lanes() == WIDTH - 1, 0.0, full - last)


def turn(start, forward):
    rows = lax.broadcasted_iota(jnp.int32, (TILE, 2 * TILE), 0)
    cols = lax.broadcasted_iota(jnp.int32, (TILE, 2 * TILE), 1)
    source = rows + start if forward else rows + TILE - start
    return jnp.where(cols == source, 1.0, 0.0).astype(BF)


def first_row(info):
    return jnp.where(info[2] == BIG, 0, jnp.where(info[3] == BIG, info[2], info[2] + info[3]))


def params(**more):
    return pltpu.CompilerParams(vmem_limit_bytes=LIMIT, **more)


def cost(flops, nbytes, transcendentals=0):
    return pl.CostEstimate(flops=flops, bytes_accessed=nbytes, transcendentals=transcendentals)


HBM = pl.BlockSpec(memory_space=pl.ANY)


def whole(*shape):
    return pl.BlockSpec(shape, lambda *i: (0,) * len(shape))


def row_tile(width, tile=TILE):
    return pl.BlockSpec((tile, width), lambda i, *s: (i, 0))


def col_tile(rows, width):
    return pl.BlockSpec((rows, width), lambda i, *s: (0, i))


def offset_of(place):
    return 4 * (place & 3) + (place >> 2)


def place_at(info, chip):
    offset = info[0] ^ chip
    return (offset >> 2) + 4 * (offset & 3)


def copies(info, pieces, target, cols=None):
    for side in range(2):
        half = info[1] ^ side

        def start(side=side, half=half):
            for place in range(CHIPS):
                source = pieces[4 * side + place // 4].at[pl.ds((place % 4) * BLOCK, BLOCK)]
                if cols is not None:
                    source = source.at[:, pl.ds(*cols)]
                block = pl.multiple_of((info[0] ^ offset_of(place)) * BLOCK, 16)
                pltpu.make_async_copy(source, *target(half, block)).start()

        if cols is None:
            start()
        else:
            pl.when(half == 1)(start)


def up_copies(info, pieces, store, sems):
    for part in range(2):
        cols = pl.ds(part * WIDTH, WIDTH)
        for place in range(CHIPS):
            source = pieces[place // 4].at[pl.ds((place % 4) * BLOCK, BLOCK), cols]
            block = pl.multiple_of((info[0] ^ offset_of(place)) * BLOCK, 16)
            pltpu.make_async_copy(source, store.at[pl.ds(block, BLOCK), cols], sems.at[part]).start()


def down_copies(info, pieces, store, sems):
    for place in range(CHIPS):
        chip = info[0] ^ offset_of(place)
        first = pl.multiple_of((chip & 7) * SHARE, 16)
        pltpu.make_async_copy(
            pieces[place // 4].at[pl.ds((place % 4) * SHARE, SHARE)],
            store.at[chip >> 3, pl.ds(first, SHARE)],
            sems.at[chip >> 3],
        ).start()


def by_half(store, sems):
    width = store.shape[1] // 2

    def target(half, first):
        cols = pl.ds(pl.multiple_of(half * width, 128), width)
        return store.at[pl.ds(first, BLOCK), cols], sems.at[half]

    return target


def one_half(store, semaphore):
    return lambda half, first: (store.at[pl.ds(first, BLOCK)], semaphore)


def arrived(ref, semaphore):
    pltpu.make_async_copy(ref, ref, semaphore).wait()


def halves_arrived(store, sems, halves=(0, 1)):
    width = store.shape[1] // 2
    for half in halves:
        arrived(store.at[:, pl.ds(half * width, width)], sems.at[half])


OUT_COLS = (128, WIDTH)
TURNED = pltpu.VMEM((2 * HEAD, ROWS), BF)
PAIR_SEMS = pltpu.SemaphoreType.DMA((2,))
SLOT_SEMS = pltpu.SemaphoreType.DMA((4,))
PART = 3
PART_COLS = PART * 2 * HEAD
SMALL = 128
A_COLS = 3 * PART_COLS + SMALL
B_COLS = 3 * PART_COLS + WIDTH + SMALL


def pack_kernel(qkv_ref, out_ref, one_ref, two_ref, bias_ref, w_up_ref, a_ref, b_ref, up_ref):
    few, share = one_ref.shape[1], bias_ref.shape[1]
    for part, ref in enumerate((a_ref, b_ref)):
        for i in range(3):
            first = i * WIDTH + part * PART_COLS
            ref[:, i * PART_COLS : (i + 1) * PART_COLS] = qkv_ref[:, first : first + PART_COLS]
    b_ref[:, 3 * PART_COLS : 3 * PART_COLS + WIDTH] = out_ref[...]
    place = lax.broadcasted_iota(jnp.int32, (few, SMALL), 1)

    def column(row, first):
        count = row.shape[1]
        at = lax.broadcasted_iota(jnp.int32, (few, count), 1)
        down = lax.broadcasted_iota(jnp.int32, (few, count), 0) + first
        return jnp.sum(jnp.where(at == down, row.astype(F32), 0.0), axis=1, keepdims=True)

    gains = jnp.where(place == 0, column(one_ref[...], 0), 0.0)
    gains = jnp.where(place == 1, column(two_ref[...], 0), gains)
    a_ref[:, A_COLS - SMALL :] = gains.astype(BF)
    bias = jnp.zeros((few, SMALL), F32)
    for i in range(share // few):
        bias = jnp.where(place == i, column(bias_ref[...], i * few), bias)
    b_ref[:, B_COLS - SMALL :] = bias.astype(BF)
    weights = w_up_ref[...].astype(F32)
    for core in range(2):
        blocks = [weights[:, SHARE * (2 * i + core) : SHARE * (2 * i + core + 1)] for i in range(CHIPS)]
        up_ref[:, core * MINE : (core + 1) * MINE] = jnp.concatenate(blocks, axis=1).astype(BF)


def pack(w_qkv, w_out, gain_one, gain_two, b_up, w_up):
    few = w_qkv.shape[0]
    return pl.pallas_call(
        pack_kernel,
        out_shape=[
            jax.ShapeDtypeStruct((few, cols), BF) for cols in (A_COLS, B_COLS, HIDDEN)
        ],
        compiler_params=params(),
        name="pack",
    )(w_qkv, w_out, gain_one[None], gain_two[None], b_up[None], w_up)


def join_kernel(info, *refs):
    own, other, outs = refs[:3], refs[3:6], refs[6:]
    first = info[1] == 0
    for mine, theirs, out in zip(own, other, outs):
        half = mine.shape[1] // 2
        cols = pl.ds(pl.multiple_of(info[1] * half, 128), half)
        mine, theirs = mine[:, cols].astype(F32), theirs[:, cols].astype(F32)
        out[...] = jnp.concatenate(
            [jnp.where(first, mine, theirs), jnp.where(first, theirs, mine)], axis=0
        ).astype(BF)


def join(info, own, other):
    shapes = [(2 * v.shape[0], v.shape[1] // 2) for v in own]
    return pl.pallas_call(
        join_kernel,
        grid_spec=pltpu.PrefetchScalarGridSpec(
            num_scalar_prefetch=1,
            grid=(1,),
            in_specs=[whole(*v.shape) for v in [*own, *other]],
            out_specs=[whole(*shape) for shape in shapes],
        ),
        out_shape=[jax.ShapeDtypeStruct(shape, BF) for shape in shapes],
        compiler_params=pltpu.CompilerParams(vmem_limit_bytes=8 * 1024 * 1024),
        name="join",
    )(info, *own, *other)


def before_kernel(info, tok_ref, cot_ref, x_ref, up_ref, down_ref, both, wide):
    step = pl.program_id(0)
    both[:, :TILE] = both[:, TILE:]
    both[0, TILE:, : WIDTH - 1] = tok_ref[...]
    both[1, TILE:, : WIDTH - 1] = cot_ref[...]

    @pl.when(step > 0)
    def _():
        pick = turn(first_row(info), True)
        wide[...] = mm(pick, both[0])
        x_ref[...] = jnp.where(lanes() == WIDTH - 1, 0.0, wide[...]).astype(BF)
        grads = jnp.where(lanes() == WIDTH - 1, 0.0, mm(pick, both[1]))
        up_ref[...] = grads.astype(BF)
        down_ref[...] = centred(grads).astype(BF)


def before(info, tokens, cotangent):
    shape = jax.ShapeDtypeStruct((ROWS, WIDTH), BF)
    tiles = ROWS // TILE
    source = pl.BlockSpec((TILE, WIDTH - 1), lambda i, *s: (lax.rem(i, tiles), 0))
    target = pl.BlockSpec((TILE, WIDTH), lambda i, *s: (jnp.maximum(i - 1, 0), 0))
    return pl.pallas_call(
        before_kernel,
        grid_spec=pltpu.PrefetchScalarGridSpec(
            num_scalar_prefetch=1,
            grid=(tiles + 1,),
            in_specs=[source] * 2,
            out_specs=[target] * 3,
            scratch_shapes=[pltpu.VMEM((2, 2 * TILE, WIDTH), BF), pltpu.VMEM((TILE, WIDTH), F32)],
        ),
        out_shape=[shape] * 3,
        compiler_params=params(),
        cost_estimate=cost(4 * ROWS * ROWS * WIDTH, 10 * ROWS * WIDTH),
        name="before",
    )(info, tokens, cotangent)


SPANS = ((0, 0, 256, 0), (256, 0, 512, 256), (512, 0, 768, 768), (768, 768, 256, 1536))


def tail_segments(info, axis):
    shape = (TILE, 1) if axis == 0 else (1, TILE)
    place = lax.broadcasted_iota(jnp.int32, shape, axis) + BIG + first_row(info)
    place = jnp.where(place >= ROWS, place - ROWS, place)
    found = jnp.zeros(shape, jnp.int32)
    bound = 0
    for j in range(3):
        bound = bound + info[2 + j]
        found = found + jnp.where(place >= bound, 1, 0)
    return found


def head_mask(head):
    place = lanes(2 * HEAD)
    return (place < HEAD) if head == 0 else (place >= HEAD)


def attend_pair(info, qkv, pair, out_ref, norm_ref, prob_ref, turned):
    cols = [pl.ds(pl.multiple_of(i * PART_COLS + pair * 2 * HEAD, 128), 2 * HEAD) for i in range(3)]
    causal = lax.broadcasted_iota(jnp.int32, (TILE, TILE), 0) >= lax.broadcasted_iota(
        jnp.int32, (TILE, TILE), 1
    )
    turned[...] = qkv[:, cols[1]].T
    for first, key_first, key_count, place in SPANS:
        queries = qkv[first : first + TILE, cols[0]]
        keys = turned[:, key_first : key_first + key_count]
        values = qkv[key_first : key_first + key_count, cols[2]]
        values = jnp.concatenate([values, jnp.ones_like(values)], axis=1)
        allowed = causal
        if first == BIG:
            allowed = causal & (tail_segments(info, 0) == tail_segments(info, 1))
        mixed = []
        for head in range(2):
            mine = jnp.where(head_mask(head), queries, 0) * BF(HEAD**-0.5)
            scores = mm(mine, keys)
            split = key_count - TILE
            last = jnp.where(allowed, scores[:, split:], -1e30)
            largest = jnp.max(last, axis=1, keepdims=True)
            if split:
                largest = jnp.maximum(largest, jnp.max(scores[:, :split], axis=1, keepdims=True))
            last = jnp.exp(last - largest).astype(BF)
            prob_ref[head, :, place + split : place + key_count] = last
            both = mm(last, values[split:])
            if split:
                early = jnp.exp(scores[:, :split] - largest).astype(BF)
                prob_ref[head, :, place : place + split] = early
                both += mm(early, values[:split])
            mixed.append(both)
        both = jnp.where(jnp.concatenate([head_mask(0)] * 2, axis=1), mixed[0], mixed[1])
        inverse = 1.0 / both[:, 2 * HEAD :]
        norm_ref[first : first + TILE, :] = inverse.astype(BF)
        out_ref[first : first + TILE, :] = (both[:, : 2 * HEAD] * inverse).astype(BF)


def pair_cols(offset):
    return pl.BlockSpec((ROWS, 2 * HEAD), lambda i, *s: (0, offset + i))


PROB_SPEC = pl.BlockSpec((2, TILE, PROB_COLS), lambda i, *s: (i, 0, 0))
HEADS_SHAPES = [
    jax.ShapeDtypeStruct((ROWS, PART_COLS), BF),
    jax.ShapeDtypeStruct((ROWS, PART_COLS), BF),
    jax.ShapeDtypeStruct((2 * PART, TILE, PROB_COLS), BF),
]


def heads_a_kernel(info, x_ref, *rest):
    pieces, (normed_hbm, qkv_hbm, gains_ref, att_ref, norm_ref, prob_ref) = rest[:8], rest[8:14]
    store, normed, qkv, turned, sems, out_sems = rest[14:]
    step = pl.program_id(0)

    @pl.when(step == 0)
    def _():
        copies(info, pieces, by_half(store, sems))
        inverse, expanded = norm_parts(x_ref[...].astype(F32))
        expanded = expanded * inverse
        halves_arrived(store, sems)
        gains = store[:, 3 * PART_COLS :].astype(F32).T[:8]
        gains_ref[...] = gains
        normed[...] = (expanded * gains[:1]).astype(BF)
        pltpu.make_async_copy(normed, normed_hbm, out_sems.at[0]).start()
        for i in range(3):
            cols = slice(i * PART_COLS, (i + 1) * PART_COLS)
            qkv[:, cols] = mm(normed[...], store[:, cols]).astype(BF)
        pltpu.make_async_copy(qkv, qkv_hbm, out_sems.at[1]).start()

    attend_pair(info, qkv, step, att_ref, norm_ref, prob_ref, turned)

    @pl.when(step == PART - 1)
    def _():
        arrived(normed, out_sems.at[0])
        arrived(qkv, out_sems.at[1])


def heads_a(info, x, pieces):
    return pl.pallas_call(
        heads_a_kernel,
        grid_spec=pltpu.PrefetchScalarGridSpec(
            num_scalar_prefetch=1,
            grid=(PART,),
            in_specs=[whole(ROWS, WIDTH)] + [HBM] * 8,
            out_specs=[HBM, HBM, whole(8, WIDTH), pair_cols(0), pair_cols(0), PROB_SPEC],
            scratch_shapes=[
                pltpu.VMEM((WIDTH, A_COLS), BF), pltpu.VMEM((ROWS, WIDTH), BF),
                pltpu.VMEM((ROWS, 3 * PART_COLS), BF), TURNED, PAIR_SEMS, PAIR_SEMS,
            ],
        ),
        out_shape=[
            jax.ShapeDtypeStruct((ROWS, WIDTH), BF),
            jax.ShapeDtypeStruct((ROWS, 3 * PART_COLS), BF),
            jax.ShapeDtypeStruct((8, WIDTH), F32),
        ]
        + HEADS_SHAPES,
        compiler_params=params(),
        cost_estimate=cost(6 * ROWS * WIDTH * PART_COLS + 4 * 6 * 7 * TILE * TILE * 256, 20000000, 2752512),
        name="heads_a",
    )(info, x, *pieces)


def heads_b_kernel(info, normed_ref, gains_ref, a_att_hbm, x_hbm, *rest):
    pieces, (qkv_hbm, bias_ref, middle_hbm, low_hbm, second_hbm, *pair_refs) = rest[:8], rest[8:16]
    att_ref, norm_ref, prob_ref = pair_refs
    store, qkv, turned, att, x, middle, low, second, sems, in_sems, out_sems = rest[16:]
    step = pl.program_id(0)
    late = [
        pltpu.make_async_copy(a_att_hbm, att.at[:, pl.ds(0, PART_COLS)], in_sems.at[0]),
        pltpu.make_async_copy(x_hbm, x, in_sems.at[1]),
    ]

    @pl.when(step == 0)
    def _():
        copies(info, pieces, by_half(store, sems))
        for copy in late:
            copy.start()
        halves_arrived(store, sems)
        for i in range(3):
            cols = slice(i * PART_COLS, (i + 1) * PART_COLS)
            qkv[:, cols] = mm(normed_ref[...], store[:, cols]).astype(BF)
        bias_ref[...] = store[:, B_COLS - SMALL :].astype(F32).T[:8]
        pltpu.make_async_copy(qkv, qkv_hbm, out_sems.at[0]).start()

    attend_pair(info, qkv, step, att_ref, norm_ref, prob_ref, turned)
    att[:, pl.ds(pl.multiple_of(PART_COLS + step * 2 * HEAD, 128), 2 * HEAD)] = att_ref[...]

    @pl.when(step == PART - 1)
    def _():
        for copy in late:
            copy.wait()
        weights = store[:, 3 * PART_COLS : 3 * PART_COLS + WIDTH]
        for i in range(ROWS // TILE):
            rows = slice(i * TILE, (i + 1) * TILE)
            mixed = mm(att[rows, :], weights)
            mixed = mixed - jnp.sum(mixed, axis=1, keepdims=True) * (1.0 / WIDTH)
            value = x[rows, :].astype(F32) + jnp.where(lanes() == WIDTH - 1, 0.0, mixed)
            inverse, expanded = norm_parts(value)
            middle[rows, :] = value
            low[rows, :] = value.astype(BF)
            second[rows, :] = (expanded * inverse * gains_ref[1:2, :]).astype(BF)
            for j, (source, target) in enumerate(
                ((middle, middle_hbm), (second, second_hbm), (low, low_hbm))
            ):
                pltpu.make_async_copy(source.at[rows], target.at[rows], out_sems.at[1 + j]).start()
        arrived(qkv, out_sems.at[0])
        arrived(middle, out_sems.at[1])
        arrived(second, out_sems.at[2])
        arrived(low, out_sems.at[3])


def heads_b(info, normed, gains, a_att, x, pieces):
    return pl.pallas_call(
        heads_b_kernel,
        grid_spec=pltpu.PrefetchScalarGridSpec(
            num_scalar_prefetch=1,
            grid=(PART,),
            in_specs=[whole(ROWS, WIDTH), whole(8, WIDTH)] + [HBM] * 10,
            out_specs=[HBM, whole(8, WIDTH), HBM, HBM, HBM, pair_cols(0), pair_cols(0), PROB_SPEC],
            scratch_shapes=[
                pltpu.VMEM((WIDTH, B_COLS), BF), pltpu.VMEM((ROWS, 3 * PART_COLS), BF), TURNED,
                pltpu.VMEM((ROWS, WIDTH), BF), pltpu.VMEM((ROWS, WIDTH), BF),
                pltpu.VMEM((ROWS, WIDTH), F32), pltpu.VMEM((ROWS, WIDTH), BF),
                pltpu.VMEM((ROWS, WIDTH), BF), PAIR_SEMS, PAIR_SEMS, SLOT_SEMS,
            ],
        ),
        out_shape=[
            jax.ShapeDtypeStruct((ROWS, 3 * PART_COLS), BF),
            jax.ShapeDtypeStruct((8, WIDTH), F32),
            jax.ShapeDtypeStruct((ROWS, WIDTH), F32),
            jax.ShapeDtypeStruct((ROWS, WIDTH), BF),
            jax.ShapeDtypeStruct((ROWS, WIDTH), BF),
        ]
        + HEADS_SHAPES,
        compiler_params=params(),
        cost_estimate=cost(
            6 * ROWS * WIDTH * PART_COLS + 2 * ROWS * WIDTH * WIDTH + 4 * 6 * 7 * TILE * TILE * 256,
            25000000, 2752512,
        ),
        name="heads_b",
    )(info, normed, gains, a_att, x, *pieces)


GELU_A = 0.7978845608028654
GELU_B = 0.044715


def tokens_copies(refs, second, down_in, sems):
    return [
        pltpu.make_async_copy(ref, (second, down_in)[i // 2].at[i % 2], sems.at[i])
        for i, ref in enumerate(refs)
    ]


def feed_kernel(info, bias_ref, *rest):
    ins, pieces, (act_hbm, slope_hbm, *grads) = rest[:4], rest[4:8], rest[8:14]
    store, sems, second, down_in, in_sems, act, slope, stage, out_sems = rest[14:]
    late = tokens_copies(ins, second, down_in, in_sems)
    late[0].start()
    up_copies(info, pieces, store, sems)
    for i in (2, 1, 3):
        late[i].start()
    late[0].wait()
    sums = [None, None]
    for side in range(2):
        if side == 1:
            late[1].wait()
        for part in range(2):
            cols = slice(part * WIDTH, (part + 1) * WIDTH)
            if side == 0:
                arrived(store.at[:, pl.ds(part * WIDTH, WIDTH)], sems.at[part])
            slot = 2 * side + part
            for i in range(ROWS // TILE):
                rows = slice(i * TILE, (i + 1) * TILE)
                hidden = mm(second[side, rows, :], store[:, cols]) + bias_ref[:, cols]
                square = hidden * hidden
                bent = jnp.tanh(hidden * (GELU_A + (GELU_A * GELU_B) * square))
                half = 0.5 + 0.5 * bent
                act[slot, rows, :] = (hidden * half).astype(BF)
                tilt = hidden * (0.5 * GELU_A + (1.5 * GELU_A * GELU_B) * square)
                slope[slot, rows, :] = (half + tilt * (1.0 - bent * bent)).astype(BF)
            for source, target, which in ((act, act_hbm, 0), (slope, slope_hbm, 1)):
                pltpu.make_async_copy(source.at[slot], target.at[slot], out_sems.at[which]).start()
            if part == 0:
                late[2 + side].wait()
            found = mm_tn(act[slot], down_in[side])
            if side == 0:
                sums[part] = found
                continue
            total = sums[part] + found
            for i in range(8):
                block = total[SHARE * i : SHARE * (i + 1)].astype(BF)
                stage[place_at(info, 8 * part + i)] = block
    for i, target in enumerate(grads):
        pltpu.make_async_copy(stage.at[pl.ds(4 * i, 4)], target, out_sems.at[2]).start()
    arrived(act, out_sems.at[0])
    arrived(slope, out_sems.at[1])
    arrived(stage, out_sems.at[2])


BOTH = pltpu.VMEM((2, ROWS, WIDTH), BF)
FOUR = pltpu.VMEM((4, ROWS, WIDTH), BF)


def feed(info, second, other_second, down_in, other_down_in, bias, pieces):
    return pl.pallas_call(
        feed_kernel,
        grid_spec=pltpu.PrefetchScalarGridSpec(
            num_scalar_prefetch=1,
            grid=(1,),
            in_specs=[whole(1, MINE)] + [HBM] * 8,
            out_specs=[HBM] * 6,
            scratch_shapes=[
                pltpu.VMEM((WIDTH, MINE), BF), PAIR_SEMS, BOTH, BOTH, SLOT_SEMS, FOUR, FOUR,
                pltpu.VMEM((CHIPS, SHARE, WIDTH), BF), pltpu.SemaphoreType.DMA((3,)),
            ],
        ),
        out_shape=[jax.ShapeDtypeStruct((4, ROWS, WIDTH), BF)] * 2
        + [jax.ShapeDtypeStruct((4, SHARE, WIDTH), BF)] * 4,
        compiler_params=params(),
        cost_estimate=cost(4 * ROWS * WIDTH * HIDDEN, 6 * ROWS * HIDDEN + 4 * WIDTH * HIDDEN),
        name="feed",
    )(info, bias, second, other_second, down_in, other_down_in, *pieces)


UP_COLS = MINE + SMALL


def spread_out(info, grads, stage):
    for device in range(32):
        value = grads[24 * device : 24 * (device + 1)].astype(BF)
        stage[info[1] ^ (device & 1), place_at(info, device >> 1)] = value


def back_kernel(info, *rest):
    slope_hbm, ins, up_pieces, down_pieces = rest[0], rest[1:5], rest[5:9], rest[9:13]
    outs, own_hbm, other_hbm = rest[13:17], rest[17], rest[18]
    (down_store, down_sems, up_store, up_sems, second, down_in, in_sems, slope, slope_sems, grads,
     weighted, other, stage, spare, out_sems) = rest[19:]
    late = tokens_copies(ins, second, down_in, in_sems)
    slopes = [pltpu.make_async_copy(slope_hbm.at[i], slope.at[i], slope_sems.at[i]) for i in range(4)]
    late[2].start()
    down_copies(info, down_pieces, down_store, down_sems)
    slopes[0].start()
    up_copies(info, up_pieces, up_store, up_sems)
    for copy in (late[0], late[3], slopes[2], late[1], slopes[1], slopes[3]):
        copy.start()
    for part in range(2):
        cols = slice(part * WIDTH, (part + 1) * WIDTH)
        arrived(down_store.at[part], down_sems.at[part])
        for side in range(2):
            if part == 0:
                late[2 + side].wait()
            value = mm_nt(down_in[side], down_store[part])
            slopes[2 * side + part].wait()
            bias = jnp.zeros((1, WIDTH), F32)
            for i in range(ROWS // TILE):
                rows = slice(i * TILE, (i + 1) * TILE)
                few = (slope[2 * side + part, rows, :].astype(F32) * value[rows]).astype(BF)
                grads[side, rows, :] = few
                bias += jnp.sum(few.astype(F32), axis=0, keepdims=True)
            if side == 0:
                arrived(up_store.at[:, pl.ds(part * WIDTH, WIDTH)], up_sems.at[part])
            if part == 0:
                weighted[side] = mm_nt(grads[side], up_store[:, cols])
            elif side == 0:
                weighted[0] += mm_nt(grads[0], up_store[:, cols])
                pltpu.make_async_copy(weighted.at[0], own_hbm, out_sems.at[0]).start()
            else:
                other[...] = (weighted[1] + mm_nt(grads[1], up_store[:, cols])).astype(BF)
                pltpu.make_async_copy(other, other_hbm, out_sems.at[1]).start()
            if part == 0:
                late[side].wait()
            found = mm_tn(second[side], grads[side])
            if side == 0:
                sums, biases = found, bias
        total = sums + found
        for chip in range(CHIPS):
            block = total[BLOCK * chip : BLOCK * (chip + 1)].astype(BF)
            stage[part, place_at(info, chip)] = block
        for i, target in enumerate(outs):
            pltpu.make_async_copy(
                stage.at[part, pl.ds(4 * i, 4)], target.at[:, :, pl.ds(part * WIDTH, WIDTH)], out_sems.at[2]
            ).start()
        row = biases + bias
        for i in range(8):
            few = jnp.concatenate(
                [row[:, SHARE * i : SHARE * (i + 1)], jnp.zeros((1, SMALL - SHARE), F32)], axis=1
            )
            spare[place_at(info, 8 * part + i)] = jnp.broadcast_to(few, (BLOCK, SMALL)).astype(BF)
    for i, target in enumerate(outs):
        pltpu.make_async_copy(
            spare.at[pl.ds(4 * i, 4)], target.at[:, :, pl.ds(MINE, SMALL)], out_sems.at[3]
        ).start()
    arrived(weighted.at[0], out_sems.at[0])
    arrived(other, out_sems.at[1])
    arrived(stage, out_sems.at[2])
    arrived(spare, out_sems.at[3])


def back(info, second, other_second, down_in, other_down_in, slope, up_pieces, down_pieces):
    return pl.pallas_call(
        back_kernel,
        grid_spec=pltpu.PrefetchScalarGridSpec(
            num_scalar_prefetch=1,
            grid=(1,),
            in_specs=[HBM] * 13,
            out_specs=[HBM] * 6,
            scratch_shapes=[
                pltpu.VMEM((2, WIDTH, WIDTH), BF), PAIR_SEMS, pltpu.VMEM((WIDTH, MINE), BF), PAIR_SEMS,
                BOTH, BOTH, SLOT_SEMS, FOUR, SLOT_SEMS, BOTH,
                pltpu.VMEM((2, ROWS, WIDTH), F32),
                pltpu.VMEM((ROWS, WIDTH), BF),
                pltpu.VMEM((2, CHIPS, BLOCK, WIDTH), BF),
                pltpu.VMEM((CHIPS, BLOCK, SMALL), BF),
                SLOT_SEMS,
            ],
        ),
        out_shape=[jax.ShapeDtypeStruct((4, BLOCK, UP_COLS), BF)] * 4
        + [jax.ShapeDtypeStruct((ROWS, WIDTH), F32), jax.ShapeDtypeStruct((ROWS, WIDTH), BF)],
        compiler_params=params(),
        cost_estimate=cost(6 * ROWS * WIDTH * HIDDEN, 35000000),
        name="back",
    )(info, slope, second, other_second, down_in, other_down_in, *up_pieces, *down_pieces)


def pair_grad(q_ref, k_ref, v_ref, grad_ref, att_ref, norm_ref, prob_ref, dq_ref, dk_ref, dv_ref,
              key_sum, value_sum, values, scaled, turned):
    factor = HEAD**-0.5
    values[...] = v_ref[...].T
    turned[0] = q_ref[...].T
    scaled[...] = grad_ref[...] * norm_ref[...]
    turned[1] = scaled[...].T
    key_sum[...] = jnp.zeros_like(key_sum)
    value_sum[...] = jnp.zeros_like(value_sum)
    for first, key_first, key_count, place in SPANS:
        rows = slice(first, first + TILE)
        keys_at = slice(key_first, key_first + key_count)
        grads = scaled[rows, :]
        product = grads.astype(F32) * att_ref[rows, :].astype(F32)
        keys = k_ref[keys_at, :]
        parts = []
        for head in range(2):
            mask = head_mask(head)
            mine = slice(HEAD * head, HEAD * (head + 1))
            probs = prob_ref[head, :, place : place + key_count]
            inner = jnp.sum(jnp.where(mask, product, 0.0), axis=1, keepdims=True)
            slopes = mm(jnp.where(mask, grads, 0), values[:, keys_at]) - inner
            slopes = (probs.astype(F32) * slopes).astype(BF)
            parts.append(mm(slopes, keys))
            value_sum[mine, keys_at] += mm(turned[1, mine, rows], probs)
            key_sum[mine, keys_at] += mm(turned[0, mine, rows], slopes)
        dq_ref[rows, :] = (jnp.where(head_mask(0), parts[0], parts[1]) * factor).astype(BF)
    dk_ref[...] = (key_sum[...].T * factor).astype(BF)
    dv_ref[...] = value_sum[...].T.astype(BF)


PAIR_SCRATCH = [
    pltpu.VMEM((2 * HEAD, ROWS), F32), pltpu.VMEM((2 * HEAD, ROWS), F32), TURNED,
    pltpu.VMEM((ROWS, 2 * HEAD), BF), pltpu.VMEM((2, 2 * HEAD, ROWS), BF),
]


HEADS_COLS = 4 * WIDTH


def attend_grad_kernel(info, gain_ref, weighted_hbm, other_hbm, middle_hbm, up_hbm, normed_hbm, *rest):
    pieces, groups, grads_hbm = rest[:8], (rest[8:12], rest[12:16]), rest[16:19]
    targets, total_hbm, pair_scratch = rest[19:23], rest[23], rest[24:29]
    (total, other, middle, up, in_sems, store, semaphore, mixed, grad_att, att, normed, qkv, norms, late_sems,
     probs, prob_sems, turned, kept, stage, out_sems) = rest[29:]
    step = pl.program_id(0)
    late = [
        pltpu.make_async_copy(source, target, late_sems.at[i])
        for i, (source, target) in enumerate([
            (groups[0][0], qkv.at[0]),
            (groups[0][1], att.at[:, pl.ds(0, PART_COLS)]),
            (groups[0][2], norms.at[0]),
            (groups[1][1], att.at[:, pl.ds(PART_COLS, PART_COLS)]),
            (normed_hbm, normed),
            (groups[1][0], qkv.at[1]),
            (groups[1][2], norms.at[1]),
        ])
    ]

    def weights_grad(i, value):
        spread_out(info, value, stage.at[i])
        for which in range(2):
            for half, places in enumerate((pl.ds(0, 4), pl.ds(4, 12))):
                pltpu.make_async_copy(
                    stage.at[i, which, places],
                    targets[2 * which + half].at[:, :, pl.ds(i * WIDTH, WIDTH)],
                    out_sems.at[0],
                ).start()

    def fetch_probs(pair):
        slot = lax.rem(pair, 2)
        for group in range(2):

            @pl.when((pair < PART) if group == 0 else (pair >= PART))
            def _(group=group):
                source = groups[group][3].at[pl.ds(2 * (pair - PART * group), 2)]
                pltpu.make_async_copy(source, probs.at[slot], prob_sems.at[slot]).start()

    @pl.when(step == 0)
    def _():
        early = []
        for i in range(ROWS // TILE):
            rows = pl.ds(i * TILE, TILE)
            early.append([
                pltpu.make_async_copy(source.at[rows], target.at[rows], in_sems.at[4 * i + j])
                for j, (source, target) in enumerate(
                    ((middle_hbm, middle), (weighted_hbm, total), (other_hbm, other), (up_hbm, up))
                )
            ])
            for copy in early[-1]:
                copy.start()
        copies(info, pieces, one_half(store, semaphore), OUT_COLS)
        for copy in late[:3]:
            copy.start()
        fetch_probs(step)
        for copy in late[3:]:
            copy.start()
        for i in range(ROWS // TILE):
            rows = slice(i * TILE, (i + 1) * TILE)
            for copy in early[i]:
                copy.wait()
            inverse, expanded = norm_parts(middle[rows, :].astype(F32))
            value = (total[rows, :] + other[rows, :].astype(F32)) * gain_ref[1:2, :]
            value = up[rows, :].astype(F32) + norm_back(value, inverse, expanded)
            total[rows, :] = value
            mixed[rows, :] = centred(value).astype(BF)
        pltpu.make_async_copy(total, total_hbm, out_sems.at[1]).start()
        arrived(store, semaphore)
        grad_att[...] = mm_nt(mixed[...], store[...]).astype(BF)
        for copy in late[:3]:
            copy.wait()

    @pl.when(step == PART)
    def _():
        for copy in late[5:]:
            copy.wait()

    @pl.when(step < PAIRS - 1)
    def _():
        fetch_probs(step + 1)

    slot = lax.rem(step, 2)
    arrived(probs.at[slot], prob_sems.at[slot])
    group = step // PART
    pair = step - PART * group
    place = pl.ds(pl.multiple_of(step * 2 * HEAD, 2 * HEAD), 2 * HEAD)
    cols = [pl.ds(pl.multiple_of(i * PART_COLS + pair * 2 * HEAD, 2 * HEAD), 2 * HEAD) for i in range(3)]
    pair_grad(
        *[qkv.at[group, :, at] for at in cols], grad_att.at[:, place], att.at[:, place],
        norms.at[group, :, cols[0]], probs.at[slot], *[kept.at[i, :, place] for i in range(3)], *pair_scratch
    )
    for i in range(3):
        pltpu.make_async_copy(kept.at[i, :, place], grads_hbm[i].at[:, place], out_sems.at[2]).start()

    @pl.when(step == 0)
    def _():
        for copy in late[3:5]:
            copy.wait()
        weights_grad(3, mm_tn(att[...], mixed[...]))
        turned[...] = normed[...].T

    @pl.when(step == PAIRS - 1)
    def _():
        for i in range(3):
            weights_grad(i, mm(turned[...], kept[i]))
        arrived(total, out_sems.at[1])
        arrived(kept, out_sems.at[2])
        arrived(stage, out_sems.at[0])


def centred(branch):
    return branch - jnp.sum(branch, axis=1, keepdims=True) * (1.0 / WIDTH)


def attend_grad(info, weighted, other, middle, upstream, gains, normed, group_a, group_b, pieces):
    return pl.pallas_call(
        attend_grad_kernel,
        grid_spec=pltpu.PrefetchScalarGridSpec(
            num_scalar_prefetch=1,
            grid=(PAIRS,),
            in_specs=[whole(8, WIDTH)] + [HBM] * 21,
            out_specs=[HBM] * 8,
            scratch_shapes=PAIR_SCRATCH
            + [
                pltpu.VMEM((ROWS, WIDTH), F32), pltpu.VMEM((ROWS, WIDTH), BF),
                pltpu.VMEM((ROWS, WIDTH), BF), pltpu.VMEM((ROWS, WIDTH), BF),
                pltpu.SemaphoreType.DMA((16,)),
                pltpu.VMEM((WIDTH, WIDTH), BF), pltpu.SemaphoreType.DMA,
                pltpu.VMEM((ROWS, WIDTH), BF), pltpu.VMEM((ROWS, WIDTH), BF),
                pltpu.VMEM((ROWS, WIDTH), BF), pltpu.VMEM((ROWS, WIDTH), BF),
                pltpu.VMEM((2, ROWS, 3 * PART_COLS), BF), pltpu.VMEM((2, ROWS, PART_COLS), BF),
                pltpu.SemaphoreType.DMA((7,)),
                pltpu.VMEM((2, 2, TILE, PROB_COLS), BF), PAIR_SEMS,
                pltpu.VMEM((WIDTH, ROWS), BF), pltpu.VMEM((3, ROWS, WIDTH), BF),
                pltpu.VMEM((4, 2, CHIPS, 24, WIDTH), BF), pltpu.SemaphoreType.DMA((3,)),
            ],
        ),
        out_shape=[jax.ShapeDtypeStruct((ROWS, WIDTH), BF)] * 3
        + [jax.ShapeDtypeStruct((count, 24, HEADS_COLS), BF) for count in (4, 12, 4, 12)]
        + [jax.ShapeDtypeStruct((ROWS, WIDTH), F32)],
        compiler_params=params(),
        cost_estimate=cost(16 * 6 * 7 * TILE * TILE * 256 + 8 * ROWS * WIDTH * WIDTH, 45000000),
        name="attend_grad",
    )(info, gains, weighted, other, middle, upstream, normed, *pieces, *group_a, *group_b)


def last_kernel(info, act_ref, middle_ref, gain_ref, *rest):
    parts, x_hbm, total_hbm, down_pieces = rest[:3], rest[3], rest[4], rest[5:9]
    a_pieces, b_pieces, (out_ref, other_ref, grad_ref) = rest[9:17], rest[17:25], rest[25:28]
    down_store, down_sems, a_store, b_store, a_sems, b_sems, grads, x, total, weighted, sems = rest[28:]
    step = pl.program_id(0)
    late = [
        pltpu.make_async_copy(source, target, sems.at[i])
        for i, (source, target) in enumerate(
            [(part, grads.at[i]) for i, part in enumerate(parts)] + [(x_hbm, x), (total_hbm, total)]
        )
    ]

    @pl.when(step == 0)
    def _():
        down_copies(info, down_pieces, down_store, down_sems)
        for i in range(2):
            arrived(down_store.at[i], down_sems.at[i])
        copies(info, a_pieces, by_half(a_store, a_sems))
        copies(info, b_pieces, by_half(b_store, b_sems))
        for copy in late:
            copy.start()

    branch = mm(act_ref[0], down_store[0]) + mm(act_ref[1], down_store[1])
    out_ref[...] = middle_ref[...] + centred(branch)
    branch = mm(act_ref[2], down_store[0]) + mm(act_ref[3], down_store[1])
    other_ref[...] = centred(branch).astype(BF)

    for i in range(3):

        @pl.when(step == i + 1)
        def _(i=i):
            if i == 0:
                halves_arrived(a_store, a_sems)
                halves_arrived(b_store, b_sems)
            late[i].wait()
            cols = slice(i * PART_COLS, (i + 1) * PART_COLS)
            found = mm_nt(grads[i, :, :PART_COLS], a_store[:, cols])
            found += mm_nt(grads[i, :, PART_COLS:], b_store[:, cols])
            weighted[...] = found if i == 0 else weighted[...] + found

    @pl.when(step == 3)
    def _():
        late[3].wait()
        late[4].wait()
        for i in range(ROWS // TILE):
            rows = slice(i * TILE, (i + 1) * TILE)
            inverse, expanded = norm_parts(x[rows, :].astype(F32))
            back = norm_back(weighted[rows, :] * gain_ref[0:1, :], inverse, expanded)
            grad_ref[rows, :] = (total[rows, :] + back).astype(BF)


def last(info, active, middle, parts, x, total, gains, down_pieces, a_pieces, b_pieces):
    act_tile = pl.BlockSpec((4, TILE, WIDTH), lambda i, *s: (0, i, 0))
    return pl.pallas_call(
        last_kernel,
        grid_spec=pltpu.PrefetchScalarGridSpec(
            num_scalar_prefetch=1,
            grid=(ROWS // TILE,),
            in_specs=[act_tile, row_tile(WIDTH), whole(8, WIDTH)] + [HBM] * 25,
            out_specs=[row_tile(WIDTH)] * 2 + [whole(ROWS, WIDTH)],
            scratch_shapes=[
                pltpu.VMEM((2, WIDTH, WIDTH), BF), PAIR_SEMS,
                pltpu.VMEM((WIDTH, A_COLS), BF), pltpu.VMEM((WIDTH, B_COLS), BF), PAIR_SEMS, PAIR_SEMS,
                pltpu.VMEM((3, ROWS, WIDTH), BF), pltpu.VMEM((ROWS, WIDTH), BF),
                pltpu.VMEM((ROWS, WIDTH), F32), pltpu.VMEM((ROWS, WIDTH), F32),
                pltpu.SemaphoreType.DMA((5,)),
            ],
        ),
        out_shape=[jax.ShapeDtypeStruct((ROWS, WIDTH), dtype) for dtype in (F32, BF, BF)],
        compiler_params=params(),
        cost_estimate=cost(2 * ROWS * WIDTH * HIDDEN + 6 * ROWS * WIDTH * WIDTH, 30000000),
        name="last",
    )(info, active, middle, gains, *parts, x, total, *down_pieces, *a_pieces, *b_pieces)


def turn_back_kernel(info, own_ref, other_ref, two_ref, out_ref, grad_ref, both):
    step = pl.program_id(0)
    both[:, :TILE] = both[:, TILE:]
    both[0, TILE:] = (own_ref[...] + other_ref[...].astype(F32)).astype(BF)
    both[1, TILE:] = two_ref[...]

    @pl.when(step > 0)
    def _():
        pick = turn(first_row(info), False)
        out_ref[...] = mm(pick, both[0]).astype(BF)[:, : WIDTH - 1]
        grad_ref[...] = mm(pick, both[1]).astype(BF)[:, : WIDTH - 1]


def turn_back(info, own, other, two):
    tiles = ROWS // TILE
    source = pl.BlockSpec((TILE, WIDTH), lambda i, *s: (lax.rem(i + tiles - 1, tiles), 0))
    target = pl.BlockSpec((TILE, WIDTH - 1), lambda i, *s: (jnp.maximum(i - 1, 0), 0))
    return pl.pallas_call(
        turn_back_kernel,
        grid_spec=pltpu.PrefetchScalarGridSpec(
            num_scalar_prefetch=1,
            grid=(tiles + 1,),
            in_specs=[source] * 3,
            out_specs=[target] * 2,
            scratch_shapes=[pltpu.VMEM((2, 2 * TILE, WIDTH), BF)],
        ),
        out_shape=[jax.ShapeDtypeStruct((ROWS, WIDTH - 1), BF)] * 2,
        compiler_params=pltpu.CompilerParams(vmem_limit_bytes=24 * 1024 * 1024),
        cost_estimate=cost(4 * ROWS * ROWS * WIDTH, 8 * ROWS * WIDTH),
        name="turn_back",
    )(info, own, other, two)


def along(column):
    shape = (column.shape[0],) * 2
    same = lax.broadcasted_iota(jnp.int32, shape, 0) == lax.broadcasted_iota(jnp.int32, shape, 1)
    return jnp.sum(jnp.where(same, column, 0.0), axis=0, keepdims=True)


def sums_kernel(count, info, *rest):
    terms, (mine_ref, got_ref, qkv_ref, up_ref, one_ref, two_ref), outs = (
        rest[:count], rest[count : count + 6], rest[count + 6 :]
    )
    total = terms[0][...]
    for ref in terms[1:]:
        total += ref[...].astype(F32)
    grads = total[:, : 3 * WIDTH]
    outs[0][...] = grads
    outs[1][...] = total[:, 3 * WIDTH :]
    found = jnp.sum(qkv_ref[...].astype(F32) * grads, axis=1, keepdims=True)
    outs[2][...] = along(found) / one_ref[...].astype(F32)
    first = info[1] == 0
    mine, got = mine_ref[...], got_ref[...]
    both = jnp.where(first, mine, got), jnp.where(first, got, mine)
    grads = jnp.concatenate(
        [both[core][:, SHARE * i : SHARE * (i + 1)] for i in range(CHIPS) for core in range(2)], axis=1
    )
    outs[3][...] = grads
    found = jnp.sum(up_ref[...].astype(F32) * grads, axis=1, keepdims=True)
    outs[4][...] = along(found) / two_ref[...].astype(F32)


def sums(info, terms, mine, got, w_qkv, w_up, gain_one, gain_two):
    few = gain_one.shape[0]
    ins = [*terms, mine, got, w_qkv, w_up, gain_one[None], gain_two[None]]
    shapes = [(few, 3 * WIDTH), (few, WIDTH), (1, few), (few, HIDDEN), (1, few)]
    found = pl.pallas_call(
        functools.partial(sums_kernel, len(terms)),
        grid_spec=pltpu.PrefetchScalarGridSpec(
            num_scalar_prefetch=1,
            grid=(1,),
            in_specs=[whole(*v.shape) for v in ins],
            out_specs=[whole(*shape) for shape in shapes],
        ),
        out_shape=[jax.ShapeDtypeStruct(shape, F32) for shape in shapes],
        compiler_params=pltpu.CompilerParams(vmem_limit_bytes=24 * 1024 * 1024),
        name="sums",
    )(info, *ins)
    return [v.reshape(few) if v.shape == (1, few) else v for v in found]


WAYS = {"core": (0, 1), "x": (0, 2), "y": (1, 0), "xy": (1, 2), "z1": (2, 0), "z2": (4, 0), "z3": (6, 0)}


def add_low(left, right):
    return (left.astype(F32) + right.astype(F32)).astype(BF)


class Cube:
    def __init__(self, sizes):
        self.sizes = sizes
        wide, narrow = lax.axis_index("wide"), lax.axis_index("narrow")
        self.place = jnp.stack([wide * 2 + (narrow >> 1), narrow & 1]).astype(jnp.int32)

    def hop(self, value, way):
        wide, narrow = WAYS[way]
        if wide == 0:
            return lax.ppermute(value, "narrow", [(i, i ^ narrow) for i in range(self.sizes["narrow"])])
        if narrow == 0:
            return lax.ppermute(value, "wide", [(i, i ^ wide) for i in range(self.sizes["wide"])])
        bits = wide * self.sizes["narrow"] + narrow
        count = self.sizes["wide"] * self.sizes["narrow"]
        return lax.ppermute(value, AXES, [(i, i ^ bits) for i in range(count)])

    def gather(self, block):
        others = yield [self.hop(block, way) for way in ("z1", "z2", "z3")]
        return (yield from self.across(jnp.concatenate([block] + others)))

    def gather_slowly(self, block):
        near = yield from self.along_z(block)
        return (yield from self.across(near))

    def along_z(self, block):
        for way in ("z1", "z2"):
            other = yield self.hop(block, way)
            block = jnp.concatenate([block, other])
        return block

    def across(self, near):
        own = yield from self.plane(near)
        twins = yield [self.hop(part, "core") for part in own]
        return own + twins

    def plane(self, near):
        far = yield [self.hop(near, way) for way in ("x", "y", "xy")]
        return [near] + far

    def gather_mine(self, block):
        near = yield from self.along_z(block)
        return (yield from self.plane(near))

    def exchange(self, value):
        return (yield self.hop(value, "core"))

    def blocks(self, info, shards):
        others = [self.hop(shard, "core") for shard in shards]
        return join(info, shards, others)

    def sum_plane(self, keep):
        others = yield [self.hop(quad, way) for quad, way in zip(keep[1:], ("x", "y", "xy"))]
        return sum([other.astype(F32) for other in others], keep[0].astype(F32))

    def sum_z_slowly(self, both):
        got = yield self.hop(both[2:].astype(BF), "z2")
        both = both[:2] + got.astype(F32)
        got = yield self.hop(both[1].astype(BF), "z1")
        return both[0] + got.astype(F32)

    def reduce_up(self, keep):
        both = yield from self.sum_plane(keep)
        total = yield from self.sum_z_slowly(both)
        sums = total[0, MINE : MINE + SHARE]
        total = total[:, :MINE].reshape(2, -1, MINE)
        core = self.place[1]
        mine = lax.dynamic_index_in_dim(total, core, 0, False)
        got = yield self.hop(lax.dynamic_index_in_dim(total, 1 - core, 0, False), "core")
        return mine, got, sums

    def reduce_mine(self, keep):
        both = yield from self.sum_plane(keep)
        return (yield from self.sum_z_slowly(both))

    def reduce(self, keep, send):
        got = yield self.hop(send[1], "core")
        sends = [add_low(keep[1][4 * i : 4 * i + 4], got[4 * i : 4 * i + 4]) for i in range(3)]
        *others, keep, got = yield [
            self.hop(part, way) for part, way in zip(sends, ("x", "y", "xy"))
        ] + [keep[0], self.hop(send[0], "core")]
        both = sum([other.astype(F32) for other in [got] + others], keep.astype(F32))
        others = yield [self.hop(both[i].astype(BF), way) for i, way in ((1, "z1"), (2, "z2"), (3, "z3"))]
        return [both[0]] + others


class Plain:
    def __init__(self, sizes):
        self.sizes = sizes
        self.core = (lax.axis_index("narrow") & 1).astype(jnp.int32)
        self.place = jnp.stack([jnp.zeros_like(self.core), self.core])

    def exchange(self, value):
        count = self.sizes["narrow"]
        other = lax.ppermute(value, "narrow", [(i, i ^ 1) for i in range(count)])
        yield ()
        return other

    def blocks(self, info, shards):
        return shards

    def by_place(self, rows):
        return rows.reshape(4, 4, -1, rows.shape[1]).transpose(1, 0, 2, 3).reshape(4, -1, rows.shape[1])

    def by_chip(self, blocks):
        return blocks.reshape(4, 4, *blocks.shape[1:]).swapaxes(0, 1).reshape(blocks.shape)

    def mine_first(self, one, two):
        first = self.core == 0
        return jnp.where(first, one, two), jnp.where(first, two, one)

    def gather(self, shard):
        yield ()
        full = self.by_place(lax.all_gather(shard, AXES, axis=0, tiled=True))
        cols = full.shape[2] // 2
        halves = self.mine_first(full[:, :, :cols], full[:, :, cols:])
        return [half[i] for half in halves for i in range(4)]

    gather_slowly = gather

    def gather_mine(self, shard):
        yield ()
        full = lax.all_gather(shard, AXES, axis=0, tiled=True)
        if full.shape[0] == WIDTH:
            one, two = full[:, :MINE], full[:, MINE:]
        else:
            one, two = [
                full.reshape(CHIPS, 2, SHARE, WIDTH)[:, i].reshape(MINE, WIDTH) for i in range(2)
            ]
        full = self.by_place(self.mine_first(one, two)[0])
        return [full[i] for i in range(4)]

    def scatter(self, full):
        return lax.psum_scatter(full, AXES, scatter_dimension=0, tiled=True).astype(F32)

    def apart(self, value):
        return self.mine_first(value, jnp.zeros_like(value))

    def reduce_up(self, keep):
        yield ()
        full = self.by_chip(jnp.concatenate(keep))
        sums = jnp.stack(self.apart(full[:, 0, MINE : MINE + SHARE].astype(F32)), axis=1)
        both = jnp.concatenate(self.apart(full[:, :, :MINE].reshape(WIDTH, MINE)), axis=1)
        both = self.scatter(both)
        both = self.mine_first(both[:, :MINE], both[:, MINE:])
        return *both, self.scatter(sums.reshape(HIDDEN, 1))[:, 0]

    def reduce_mine(self, keep):
        yield ()
        full = jnp.stack(self.apart(self.by_chip(jnp.concatenate(keep))), axis=1)
        return self.scatter(full.reshape(HIDDEN, WIDTH))

    def reduce(self, keep, send):
        yield ()
        keep, send = [self.by_chip(jnp.concatenate(parts)) for parts in (keep, send)]
        full = jnp.stack(self.mine_first(keep, send), axis=1)
        return [self.scatter(full.reshape(WIDTH, -1))]


class Task:
    def __init__(self, steps):
        self.steps, self.flight, self.over, self.result = steps, (), False, None
        self.go(None)

    def go(self, arrived_now):
        try:
            self.flight = self.steps.send(arrived_now)
        except StopIteration as end:
            self.flight, self.over, self.result = (), True, end.value


def meet(values, *tasks, waiting=()):
    tasks = [task for task in tasks if not task.over]
    every = tasks + list(waiting)
    values, flights = lax.optimization_barrier((values, [task.flight for task in every]))
    for task, flight in zip(every, flights):
        task.flight = flight
    for task in tasks:
        task.go(task.flight)
    return values


def finish(values, *tasks):
    while not all(task.over for task in tasks):
        values = meet(values, *tasks)
    return values


def layer(sizes, tokens, lengths, gain_one, w_qkv, w_out, gain_two, w_up, b_up, w_down, cotangent):
    share, few = b_up.shape[0], gain_one.shape[0]
    links = (Cube if sizes["wide"] == 8 and sizes["narrow"] == 4 else Plain)(sizes)
    info = jnp.concatenate([links.place, lengths[0]])
    core = info[1]

    a_block, b_block, up_block = links.blocks(info, pack(w_qkv, w_out, gain_one, gain_two, b_up, w_up))
    group_a, group_b = Task(links.gather(a_block)), Task(links.gather_slowly(b_block))
    tokens, cotangent, up_block = meet((tokens, cotangent, up_block), group_a, group_b)
    up = Task(links.gather_mine(up_block))
    x, upstream, down_in = before(info, tokens, cotangent)
    x = meet(x, group_a, waiting=(group_b, up))
    x, w_down = meet((x, w_down), group_a, group_b, up)
    down = Task(links.gather_mine(w_down))
    normed, qkv_a, gains, att_a, norms_a, probs_a = heads_a(info, x, group_a.result)
    normed, att_a, x = meet((normed, att_a, x), group_b, waiting=(up, down))
    normed, att_a, x, down_in = meet((normed, att_a, x, down_in), group_b, up, down)
    other_down_in = Task(links.exchange(down_in))
    qkv_b, bias, middle, middle_low, second, att_b, norms_b, probs_b = heads_b(
        info, normed, gains, att_a, x, group_b.result
    )
    bias = bias[: share // few].reshape(share // few, -1, few).transpose(1, 0, 2)
    bias = bias.reshape(CHIPS, 2, SHARE)
    bias = jnp.where(core == 0, bias[:, 0], bias[:, 1]).reshape(1, MINE)
    bias, second = meet((bias, second), up, other_down_in, waiting=(down,))
    other_second = Task(links.exchange(second))
    bias = meet(bias, other_second, down)
    inputs = second, other_second.result, down_in, other_down_in.result
    active, slope, *grad_down = feed(info, *inputs, bias, up.result)
    slope, grad_down = meet((slope, grad_down), down)
    downs = Task(links.reduce_mine(grad_down))
    *grad_up, weighted, other_weighted = back(info, *inputs, slope, up.result, down.result)
    weighted, other_weighted, grad_up = meet((weighted, other_weighted, grad_up), downs)
    other_weighted = Task(links.exchange(other_weighted))
    ups = Task(links.reduce_up(grad_up))
    weighted = finish(weighted, other_weighted)
    *parts, keep, keep_more, send, send_more, total = attend_grad(
        info, weighted, other_weighted.result, middle_low, upstream, gains, normed,
        (qkv_a, att_a, norms_a, probs_a), (qkv_b, att_b, norms_b, probs_b), group_b.result,
    )
    keep, send = [keep, keep_more], [send, send_more]
    active, parts, keep, send = meet((active, parts, keep, send), waiting=(ups, downs))
    heads = Task(links.reduce(keep, send))
    active, parts = meet((active, parts), heads, ups, downs)
    output, other_output, grad_tokens = last(
        info, active, middle, parts, x, total, gains, down.result, group_a.result, group_b.result,
    )
    output, grad_tokens, other_output = meet((output, grad_tokens, other_output), heads, ups, downs)
    other_output = Task(links.exchange(other_output))
    output, grad_tokens = meet((output, grad_tokens), other_output, ups)
    output, grad_tokens = turn_back(info, output, other_output.result, grad_tokens)
    output, grad_tokens = finish((output, grad_tokens), heads, ups, downs)

    mine, got, grad_bias = ups.result
    grad_qkv, grad_out, grad_one, grad_up, grad_two = sums(
        info, heads.result, mine, got, w_qkv, w_up, gain_one, gain_two
    )
    return (
        output,
        grad_tokens,
        grad_one,
        grad_qkv,
        grad_out,
        grad_two,
        grad_up,
        grad_bias,
        downs.result,
    )


def solution(mesh):
    rows, vector = P(AXES, None), P(AXES)
    sizes = dict(mesh.shape)
    return jax.shard_map(
        functools.partial(layer, sizes),
        mesh=mesh,
        in_specs=(rows, rows, vector, rows, rows, vector, rows, vector, rows, rows),
        out_specs=(rows, rows, vector, rows, rows, vector, rows, vector, rows),
        check_vma=False,
    )
```
